512 devices in a mesh: gx: 8 (over y), gy: 4 (over z_hi), gz: 16 (over x, z_lo, core).
Axes of the slice: x: 4, y: 8, z: 8 (z_hi: 4, z_lo: 2; z = z_hi * 2 + z_lo), core: 2. Of those that a mesh axis runs over, the one named last changes fastest.
Arguments:
- rhs: float32 [16, 8, 64, 256], P('gx', 'gy', 'gz'), may hold values from -12 to 12
- diagonal: float32 [16, 8, 64, 16], P('gx', 'gy', 'gz'), may hold values from 1 to 3
- blocks: float32 [16, 8, 64, 16, 432], P('gx', 'gy', 'gz'), may hold values from -0.09 to 0.09
- neighbours: int32 [16, 8, 64, 27], P('gx', 'gy', 'gz'), may hold values from 0 to 8191, as said below
Outputs:
- solution: float32 [16, 8, 64, 256], P('gx', 'gy', 'gz')
The draws below stay inside these ranges and needn't reach their ends.
Inputs may be any that keep to these rules, and one draw needn't show every extreme that they name: `neighbours`: entry k of an atom's list is the flat index of an atom whose three lattice coordinates each differ from the atom's own by at most one, periodically; every list names the atom itself at least once, and entries may repeat, their blocks then adding.
All inputs are finite; a program needn't handle non-finite values.
Results may differ from the reference program's by a relative error of at most 0.0003.
Values sent between devices are 32-bit elements; how exact they have to be, the bound alone decides.
No kernel may reach another device: no remote copies, remote signals or barrier semaphores. Data moves between devices by JAX's collectives and lax.ppermute only.
A program may use at most 64 MiB of HBM per device.

```python
import math
import jax
import jax.numpy as jnp
from jax import lax

LM = 16
RHS = 16
SLOTS = 27
ITERS = 2
NX = 16
NY = 8
NZ = 64


def draw_rhs(key, part):
    key = jax.random.fold_in(key, 9)
    along = jnp.arange(NX, dtype=jnp.float32) / max(NX - 1, 1)
    ramp = (1.0 + 2.0 * along).reshape(NX, 1, 1, 1)
    base = jnp.clip(jax.random.normal(key, (NX, NY, NZ, LM * RHS), jnp.float32), -4.0, 4.0)
    return base * ramp


def draw_neighbours(key, part):
    key = jax.random.fold_in(key, 5)
    first_key, second_key = jax.random.split(key)
    atom_count = NX * NY * NZ
    scores = jax.random.randint(first_key, (atom_count, SLOTS), 0, 1 << 20) * 32 + jnp.arange(SLOTS, dtype=jnp.int32)[None, :]
    ordering = jnp.argsort(scores, axis=1, stable=True).astype(jnp.int32)
    keeping = jax.random.randint(second_key, (atom_count, SLOTS), 0, 5) > 0
    chosen = jnp.where(keeping | (ordering == 13), ordering, 13)
    flat_index = jnp.arange(atom_count, dtype=jnp.int32)
    along_x = flat_index // (NY * NZ)
    along_y = flat_index // NZ % NY
    along_z = flat_index % NZ
    near_x = (along_x[:, None] + chosen // 9 - 1) % NX
    near_y = (along_y[:, None] + chosen // 3 % 3 - 1) % NY
    near_z = (along_z[:, None] + chosen % 3 - 1) % NZ
    result = (near_x * NY + near_y) * NZ + near_z
    return result.reshape(NX, NY, NZ, SLOTS).astype(jnp.int32)


def block_scale(rng, extent, cuts, low, largest):
    gain, own = 1.0, jax.random.fold_in(rng, 6)
    for position, blocks in cuts:
        heights = jnp.exp(jax.random.uniform(jax.random.fold_in(own, position), (blocks,), jnp.float32, low / len(cuts), largest / len(cuts)))
        gain = gain * jnp.repeat(heights, extent[position] // blocks).reshape([-1 if axis == position else 1 for axis in range(len(extent))])
    return gain


def noise(own_key, extent, scale, bound, cuts=(), held_as=jnp.bfloat16):
    factor_of = block_scale(own_key, extent, cuts, -0.22, 0.18) if cuts else 1.0
    array = jax.random.normal(own_key, extent, jnp.float32) * scale * factor_of
    return jnp.minimum(jnp.maximum(array, -bound), bound).astype(held_as)


def setup_inputs(seed: int = 0) -> dict:
    key_list = jax.random.split(jax.random.key(seed), 5)
    rhs = draw_rhs(jax.random.fold_in(key_list[4], 71), 0)
    diagonal = jnp.clip(jnp.exp(math.log(3.0) - 1.0986123 * jax.random.uniform(key_list[1], (NX, NY, NZ, LM), jnp.float32) ** block_scale(key_list[1], (NX, NY, NZ, LM), ((0, 8), (1, 4), (2, 16)), -0.2, 0.2)), 1.0, 3.0)
    blocks = noise(key_list[2], (NX, NY, NZ, LM, SLOTS * LM), 0.018, 0.09, ((0, 8), (1, 4), (2, 16)), jnp.float32)
    neighbours = draw_neighbours(jax.random.fold_in(key_list[4], 71), 0)
    return {"rhs": rhs, "diagonal": diagonal, "blocks": blocks, "neighbours": neighbours}


def column_dot(first, second, components):
    return lax.optimization_barrier(jnp.sum((first * second).reshape(-1, components, first.shape[-1] // components), axis=(0, 1)))

def broaden(values, components):
    return jnp.tile(values, components)

def shrink_step(quasi_norm, ratio_step, step_size):
    damping = 1.0 / (1.0 + ratio_step * ratio_step)
    return (quasi_norm * ratio_step * jnp.sqrt(damping), damping * step_size)

def operate(field, diagonal, blocks, neighbours):
    components = diagonal.shape[-1]
    width = field.shape[-1]
    columns = width // components
    slot_count = neighbours.shape[-1]
    flattened = field.reshape(-1, width)

    def slab(pieces):
        coupling, indices = pieces
        nearby = jnp.take(flattened, indices.astype(jnp.int32), axis=0)
        nearby = nearby.reshape(indices.shape[0], indices.shape[1], slot_count * components, columns)
        summed = jnp.einsum('bclk,bckr->bclr', coupling, nearby, precision=lax.Precision.HIGHEST, preferred_element_type=jnp.float32)
        return summed.reshape(indices.shape[0], indices.shape[1], width)
    coupled = lax.map(slab, (blocks, neighbours))
    return jnp.repeat(diagonal, columns, axis=-1) * field - coupled

def reference(rhs, diagonal, blocks, neighbours):
    components = diagonal.shape[-1]

    def apply_op(field):
        return operate(field, diagonal, blocks, neighbours)
    image = apply_op(rhs)
    inner_now = column_dot(rhs, rhs, components)
    quasi_norm = jnp.sqrt(inner_now)
    solution = jnp.zeros_like(rhs)
    quasi_resid = rhs
    search = rhs
    direction = jnp.zeros_like(rhs)
    ratio_step = jnp.zeros_like(inner_now)
    weight_step = jnp.zeros_like(inner_now)
    for iteration in range(ITERS):
        curvature = column_dot(image, rhs, components)
        step_size = inner_now / curvature
        spread_step = broaden(step_size, components)
        quasi_resid = quasi_resid - spread_step * image
        direction = search + broaden(ratio_step * ratio_step * weight_step / step_size, components) * direction
        ratio_step = jnp.sqrt(column_dot(quasi_resid, quasi_resid, components)) / quasi_norm
        quasi_norm, weight_step = shrink_step(quasi_norm, ratio_step, step_size)
        solution = solution + broaden(weight_step, components) * direction
        search_odd = search - spread_step * image
        image_odd = apply_op(search_odd)
        quasi_resid = quasi_resid - spread_step * image_odd
        direction = search_odd + broaden(ratio_step * ratio_step * weight_step / step_size, components) * direction
        ratio_step = jnp.sqrt(column_dot(quasi_resid, quasi_resid, components)) / quasi_norm
        quasi_norm, weight_step = shrink_step(quasi_norm, ratio_step, step_size)
        solution = solution + broaden(weight_step, components) * direction
        if iteration + 1 < ITERS:
            inner_next = column_dot(quasi_resid, rhs, components)
            mix_ratio = inner_next / inner_now
            spread_mix = broaden(mix_ratio, components)
            search = quasi_resid + spread_mix * search_odd
            image = apply_op(search) + spread_mix * (image_odd + spread_mix * image)
            inner_now = inner_next
    return solution
```

```python
import jax
import jax.numpy as jnp
from jax import lax
from jax.experimental import pallas as pl
from jax.experimental.pallas import tpu as pltpu
from jax.sharding import PartitionSpec as P

ITERS = 2
DEGREE = 2 * ITERS
SHIFT = 2.0
LANES = 128
PAIRS = [(i, j) for i in range(DEGREE + 1) for j in range(i, DEGREE + 1)]
VMEM = pl.BlockSpec(memory_space=pltpu.VMEM)


def two_sum(a, b):
    total = a + b
    part = total - a
    return total, (a - (total - part)) + (b - part)


def quick_sum(a, b):
    total = a + b
    return total, b - (total - a)


def split(a):
    scaled = 4097.0 * a
    head = scaled - (scaled - a)
    return head, a - head


def two_prod(a, b):
    product = a * b
    a_head, a_tail = split(a)
    b_head, b_tail = split(b)
    rest = ((a_head * b_head - product) + a_head * b_tail + a_tail * b_head) + a_tail * b_tail
    return product, rest


def pair_add(a, b):
    head, tail = two_sum(a[0], b[0])
    return quick_sum(head, tail + (a[1] + b[1]))


def pair_mul(a, b):
    head, tail = two_prod(a[0], b[0])
    return quick_sum(head, tail + (a[0] * b[1] + a[1] * b[0]))


def pair_scale(a, factor):
    head, tail = two_prod(a[0], factor)
    return quick_sum(head, tail + a[1] * factor)


def roll_pair(a, amount, axis):
    return pltpu.roll(a[0], amount, axis), pltpu.roll(a[1], amount, axis)


def iota(shape, axis):
    return lax.broadcasted_iota(jnp.int32, shape, axis)


def gram_kernel(fields, out):
    columns = 16
    diagonal_mask = iota((8, LANES), 0) == iota((8, LANES), 1) // columns
    rows = []
    parts = [split(field) for field in fields]
    for i, j in PAIRS:
        product = fields[i] * fields[j]
        (a_head, a_tail), (b_head, b_tail) = parts[i], parts[j]
        rest = ((a_head * b_head - product) + a_head * b_tail + a_tail * b_head) + a_tail * b_tail
        pieces = [
            (product[s : s + 8, t : t + LANES], rest[s : s + 8, t : t + LANES])
            for s in range(0, product.shape[0], 8)
            for t in range(0, product.shape[1], LANES)
        ]
        while len(pieces) > 1:
            pieces = [pair_add(pieces[q], pieces[q + 1]) for q in range(0, len(pieces), 2)]
        total = pieces[0]
        for amount in (4, 2, 1):
            total = pair_add(total, roll_pair(total, amount, 0))
        rows.append((total[0][0:1], total[1][0:1]))
    rows += [(jnp.zeros((1, LANES), jnp.float32),) * 2] * (16 - len(rows))
    packed = [[], []]
    for start in (0, 8):
        total = tuple(
            jnp.concatenate([row[part] for row in rows[start : start + 8]], axis=0)
            for part in (0, 1)
        )
        for amount in (64, 32, 16):
            total = pair_add(total, roll_pair(total, amount, 1))
        for part in (0, 1):
            packed[part].append(
                jnp.sum(jnp.where(diagonal_mask, total[part], 0.0), axis=0, keepdims=True)
            )
    message = jnp.concatenate(packed[0] + packed[1], axis=0)
    for q in range(out.shape[0]):
        out[q] = message


def sum_messages(ref):
    terms = [(ref[q], None) for q in range(ref.shape[0])]
    while len(terms) > 1:
        merged = []
        for q in range(0, len(terms), 2):
            (a, a_rest), (b, b_rest) = terms[q], terms[q + 1]
            total, rest = two_sum(a, b)
            if a_rest is not None:
                rest = rest + (a_rest + b_rest)
            merged.append((total, rest))
        terms = merged
    total, rest = terms[0]
    return quick_sum(total[0:2], rest[0:2] + (total[2:4] + rest[2:4]))


def relay_kernel(ref, out):
    head, tail = sum_messages(ref)
    message = jnp.concatenate([head, tail], axis=0)
    for q in range(out.shape[0]):
        out[q] = message


def finish_kernel(ref, *refs):
    fields, out = refs[:-1], refs[-1]
    columns = 16
    shape = (8, LANES)
    row = iota(shape, 0)
    diagonal_mask = row == iota(shape, 1) // columns
    packed = sum_messages(ref)
    unpacked = []
    for part in (0, 1):
        halves = []
        for half in (0, 1):
            value = jnp.where(
                diagonal_mask, jnp.broadcast_to(packed[part][half : half + 1], shape), 0.0
            )
            for amount in (64, 32, 16):
                value = value + pltpu.roll(value, amount, 1)
            halves.append(value)
        unpacked.append(halves)

    def entry(part, i, j):
        place = PAIRS.index((min(i, j), max(i, j)))
        half = unpacked[part][place // 8]
        return jnp.broadcast_to(half[place % 8 : place % 8 + 1], shape)

    gram = []
    for j in range(DEGREE + 1):
        column = []
        for part in (0, 1):
            value = jnp.zeros(shape, jnp.float32)
            for i in range(DEGREE + 1):
                value = jnp.where(row == i, entry(part, i, j), value)
            column.append(value)
        gram.append(tuple(column))

    def total_rows(a):
        for amount in (4, 2, 1):
            a = pair_add(a, roll_pair(a, amount, 0))
        return a[0]

    def with_start(a):
        return total_rows(pair_mul(gram[0], a))

    def square(a, degree):
        acc = None
        for j in range(degree + 1):
            factor = tuple(jnp.broadcast_to(part[j : j + 1], shape) for part in a)
            term = pair_mul(gram[j], factor)
            acc = term if acc is None else pair_add(acc, term)
        return total_rows(pair_mul(acc, a))

    def apply(a):
        return pair_add((SHIFT * a[0], SHIFT * a[1]), roll_pair(a, 1, 0))

    def shrink(quasi_norm, ratio, step):
        damping = 1.0 / (1.0 + ratio * ratio)
        return quasi_norm * ratio * jnp.sqrt(damping), damping * step

    zero = jnp.zeros(shape, jnp.float32)
    start = (jnp.where(row == 0, 1.0, 0.0), zero)
    inner = entry(0, 0, 0)
    quasi_norm = jnp.sqrt(inner)
    image = apply(start)
    resid = search = start
    direction = total = (zero, zero)
    ratio = weight = zero
    for iteration in range(ITERS):
        step = inner / with_start(image)
        resid = pair_add(resid, pair_scale(image, -step))
        direction = pair_add(search, pair_scale(direction, ratio * ratio * weight / step))
        ratio = jnp.sqrt(square(resid, 2 * iteration + 1)) / quasi_norm
        quasi_norm, weight = shrink(quasi_norm, ratio, step)
        total = pair_add(total, pair_scale(direction, weight))
        search_odd = pair_add(search, pair_scale(image, -step))
        image_odd = apply(search_odd)
        resid = pair_add(resid, pair_scale(image_odd, -step))
        direction = pair_add(search_odd, pair_scale(direction, ratio * ratio * weight / step))
        ratio = jnp.sqrt(square(resid, 2 * iteration + 2)) / quasi_norm
        quasi_norm, weight = shrink(quasi_norm, ratio, step)
        total = pair_add(total, pair_scale(direction, weight))
        if iteration + 1 < ITERS:
            inner_next = with_start(resid)
            mix = inner_next / inner
            search = pair_add(resid, pair_scale(search_odd, mix))
            image = pair_add(
                apply(search), pair_scale(pair_add(image_odd, pair_scale(image, mix)), mix)
            )
            inner = inner_next
    coefficients = total[0] + total[1]
    height, width = out.shape
    acc = None
    for i, field in enumerate(fields):
        factor = jnp.broadcast_to(coefficients[i : i + 1], (height, LANES))
        factor = jnp.concatenate([factor] * (width // LANES), axis=1)
        term = factor * field[...]
        acc = term if acc is None else acc + term
    out[...] = acc


SLOT_ROWS = 16
WIDE = 512
SELF = 27
CODE = 448
REACH = 3
HIGH = lax.Precision.HIGHEST


def third_of(value):
    return (value * 11) >> 5


def offsets_of(code):
    first = (code * 57) >> 9
    rest = code - 9 * first
    second = third_of(rest)
    return first - 1, second - 1, rest - 3 * second - 1


def far_atom(row):
    column = (row * 205) >> 11
    return 1 + (column >> 1), 1 + (column & 1), row - 10 * column - 3


def near_atom(row):
    column = row >> 3
    return column >> 1, column & 1, (row & 7) - 2


def bricks_place(x, y, z):
    brick = ((z + 4) >> 2) * 4 + (x >> 1) * 2 + (y >> 1)
    return (brick * 2 + (x & 1)) * 8 + (y & 1) * 4 + ((z + 4) & 3)


def pieces_place(origin, run, low):
    def place(x, y, z):
        x, y = x - origin, y - origin
        piece = (x >> 1) * 2 + (y >> 1)
        return (piece * 4 + (x & 1) * 2 + (y & 1)) * run + z - low

    return place


def find_places(matrix, count, atom, place, staged, places, sem):
    rows = [q * SLOT_ROWS for q in range(count)]
    code = jnp.concatenate([matrix[row : row + 1, CODE - 64 : CODE + 64] for row in rows], axis=0)
    code = pltpu.roll(code, 64, 1).astype(jnp.int32)
    x, y, z = atom(iota(code.shape, 0))
    dx, dy, dz = offsets_of(code)
    staged[...] = place(x + dx, y + dy, z + dz)
    copy = pltpu.make_async_copy(staged, places, sem)
    copy.start()
    copy.wait()


def couple(matrix, groups, field, places, gathered):
    lane_slot = iota((SLOT_ROWS, LANES), 1) >> 4
    gathered[pl.ds(CODE, WIDE - CODE), :] = jnp.zeros((WIDE - CODE, LANES), jnp.float32)
    tiles = []
    for group in groups:

        def gather(k, carry):
            acc = None
            for slot, atom in enumerate(group):
                place = places[atom, k]
                tile = pltpu.roll(field[place >> 3], ((slot - place) & 7) * SLOT_ROWS, 1)
                acc = tile if acc is None else jnp.where(lane_slot == slot, tile, acc)
            gathered[pl.ds(pl.multiple_of(k * SLOT_ROWS, SLOT_ROWS), SLOT_ROWS), :] = acc
            return carry

        lax.fori_loop(0, SELF + 1, gather, 0)
        left, start = [], 0
        for q in range(1, 9):
            if q == 8 or group[q] != group[q - 1] + 1:
                left.append(matrix[group[start] * SLOT_ROWS : (group[q - 1] + 1) * SLOT_ROWS, :])
                start = q
        left = left[0] if len(left) == 1 else jnp.concatenate(left, axis=0)
        product = jnp.dot(
            left, gathered[...], precision=HIGH, preferred_element_type=jnp.float32
        )
        acc = product[0:SLOT_ROWS]
        for slot in range(1, 8):
            piece = product[slot * SLOT_ROWS : (slot + 1) * SLOT_ROWS]
            acc = jnp.where(lane_slot == slot, piece, acc)
        tiles.append(-acc)
    return tiles


def pick_own(field, place):
    lane_slot = iota((SLOT_ROWS, LANES), 1) >> 4
    tiles = []
    for x in (0, 1):
        acc = None
        for slot in range(8):
            where = place(x, slot >> 2, slot & 3)
            tile = field[where >> 3]
            amount = ((slot - where) & 7) * SLOT_ROWS
            tile = pltpu.roll(tile, amount, 1) if amount else tile
            acc = tile if acc is None else jnp.where(lane_slot == slot, tile, acc)
        tiles.append(acc)
    return jnp.concatenate(tiles, axis=1)


def pack_bricks(field):
    return jnp.concatenate([field[0:8], field[8:16]], axis=1)


def pack_kernel(blocks, diagonal, codes, start, matrix, to_x, to_y, to_xy):
    matrix[:, 0:432] = blocks[...]
    matrix[:, 432:WIDE] = jnp.zeros((matrix.shape[0], WIDE - 432), jnp.float32)
    eye = iota((SLOT_ROWS, SLOT_ROWS), 0) == iota((SLOT_ROWS, SLOT_ROWS), 1)
    for x in range(2):
        for y in range(2):
            for z in range(4):
                row = ((x * 2 + y) * 4 + z) * SLOT_ROWS
                own = SHIFT - jnp.broadcast_to(diagonal[x, y, z : z + 1], eye.shape)
                matrix[row : row + SLOT_ROWS, 432:448] = jnp.where(eye, own, 0.0)
                matrix[row : row + 1, CODE : CODE + SELF] = codes[x, y, z : z + 1]
                matrix[row : row + 1, CODE + SELF : CODE + SELF + 1] = jnp.full(
                    (1, 1), 13.0, jnp.float32
                )
    bricks = pack_bricks(start[...])
    for out, row in ((to_x, 64), (to_y, 128), (to_xy, 0)):
        out[0:64] = matrix[row : row + 64]
        out[64:72] = bricks


def spread_kernel(matrix, from_x, from_y, from_xy, start, up, down):
    far = ((matrix, 192), (from_y, 0), (from_x, 0), (from_xy, 0))
    for q, (ref, row) in enumerate(far):
        up[q * 48 : q * 48 + 48] = ref[row + 16 : row + 64]
        down[q * 48 : q * 48 + 48] = ref[row : row + 48]
    for q in range(3):
        up[192 + q * 32 : 224 + q * 32] = matrix[q * 64 + 32 : q * 64 + 64]
        down[192 + q * 32 : 224 + q * 32] = matrix[q * 64 : q * 64 + 32]
    bricks = [pack_bricks(start[...])] + [ref[64:72] for ref in (from_y, from_x, from_xy)]
    for q, brick in enumerate(bricks):
        up[288 + q * 8 : 296 + q * 8] = brick
        down[288 + q * 8 : 296 + q * 8] = brick


def far_kernel(
    matrix, from_x, from_y, from_xy, start, low, high,
    out, wide, field, gathered, staged, places, sem,
):
    for q, (ref, row) in enumerate(
        ((matrix, 192), (from_y, 0), (from_x, 0), (from_xy, 0))
    ):
        wide[q * 160 : q * 160 + 48] = low[q * 48 : q * 48 + 48]
        wide[q * 160 + 48 : q * 160 + 112] = ref[row : row + 64]
        wide[q * 160 + 112 : q * 160 + 160] = high[q * 48 : q * 48 + 48]
    bricks = [low[288 + q * 8 : 296 + q * 8] for q in range(4)]
    bricks += [pack_bricks(start[...])] + [ref[64:72] for ref in (from_y, from_x, from_xy)]
    bricks += [high[288 + q * 8 : 296 + q * 8] for q in range(4)]
    for q, brick in enumerate(bricks):
        for half in (0, 1):
            for part in (0, 1):
                lanes = brick[:, (part * 2 + half) * LANES : (part * 2 + half + 1) * LANES]
                field[q * 2 + half, part * 8 : part * 8 + 8] = lanes
    find_places(wide, 40, far_atom, bricks_place, staged, places, sem)
    groups = [list(range(q * 8, q * 8 + 8)) for q in range(5)]
    for q, tile in enumerate(couple(wide, groups, field, places, gathered)):
        out[:, q * LANES : (q + 1) * LANES] = tile


def near_matrix_kernel(matrix, low, high, out):
    for q in range(4):
        lo, hi = (192 + q * 32, 192 + q * 32) if q < 3 else (16, 0)
        out[q * 128 : q * 128 + 32] = low[lo : lo + 32]
        out[q * 128 + 32 : q * 128 + 96] = matrix[q * 64 : q * 64 + 64]
        out[q * 128 + 96 : q * 128 + 128] = high[hi : hi + 32]


def load_pieces(pieces, field):
    count = pieces[0].shape[1] // LANES
    for q, piece in enumerate(pieces):
        for t in range(count):
            field[q * count + t] = piece[:, t * LANES : (t + 1) * LANES]


def second_kernel(
    matrix, own, from_x, from_y, from_xy, out, first_own, second_own,
    field, gathered, staged, places, sem,
):
    place = pieces_place(-1, 10, -3)
    load_pieces((from_xy, from_x, from_y, own), field)
    find_places(matrix, 32, near_atom, place, staged, places, sem)
    groups = [list(range(q * 8, q * 8 + 8)) for q in range(4)]
    tiles = couple(matrix, groups, field, places, gathered)
    for q, tile in enumerate(tiles):
        out[:, q * LANES : (q + 1) * LANES] = tile
    first_own[...] = pick_own(field, place)
    second_own[...] = pick_own(tiles, lambda x, y, z: (x * 2 + y) * 8 + z + 2)


def third_kernel(
    matrix, own, from_x, from_y, from_xy, out, field, gathered, staged, places, sem
):
    load_pieces((own, from_y, from_x, from_xy), field)
    find_places(matrix, 40, far_atom, pieces_place(0, 8, -2), staged, places, sem)
    atoms = [c * 10 + z + 3 for c in range(4) for z in range(-1, 5)]
    groups = [atoms[q * 8 : q * 8 + 8] for q in range(3)]
    for q, tile in enumerate(couple(matrix, groups, field, places, gathered)):
        out[:, q * LANES : (q + 1) * LANES] = tile


def fourth_kernel(
    matrix, own, from_x, from_y, from_xy, start, first, second, third_own, out,
    field, gathered, staged, places, sem,
):
    place = pieces_place(-1, 6, -1)
    load_pieces((from_xy, from_x, from_y, own), field)
    find_places(matrix, 32, near_atom, place, staged, places, sem)
    atoms = [c * 8 + z + 2 for c in range(4) for z in range(4)]
    groups = [atoms[q * 8 : q * 8 + 8] for q in range(2)]
    fourth = jnp.concatenate(couple(matrix, groups, field, places, gathered), axis=1)
    third = pick_own(field, place)
    third_own[...] = third
    gram_kernel([start[...], first[...], second[...], third, fourth], out)


def call(kernel, shapes, *operands, scratch=()):
    shapes = [jax.ShapeDtypeStruct(shape, jnp.float32) for shape in shapes]
    out = pl.pallas_call(
        kernel,
        out_shape=shapes,
        in_specs=[VMEM] * len(operands),
        out_specs=[VMEM] * len(shapes),
        scratch_shapes=list(scratch),
        compiler_params=pltpu.CompilerParams(vmem_limit_bytes=32 * 1024 * 1024),
    )(*operands)
    return out


def scratch_for(tiles, rows):
    return (
        pltpu.VMEM((tiles, SLOT_ROWS, LANES), jnp.float32),
        pltpu.VMEM((WIDE, LANES), jnp.float32),
        pltpu.VMEM((rows, LANES), jnp.int32),
        pltpu.SMEM((rows, LANES), jnp.int32),
        pltpu.SemaphoreType.DMA,
    )


def fetch(value, first, second, third):
    axes = ("gx", "gy", "gz")
    sizes = [lax.axis_size(axis) for axis in axes]
    pairs = []
    for a in range(sizes[0]):
        for b in range(sizes[1]):
            for c in range(sizes[2]):
                near = (a + first) % sizes[0], (b + second) % sizes[1], (c + third) % sizes[2]
                source = (near[0] * sizes[1] + near[1]) * sizes[2] + near[2]
                pairs.append((source, (a * sizes[1] + b) * sizes[2] + c))
    return lax.ppermute(value, axes, pairs)


def fetch_three(to_x, to_y, to_xy, sign):
    return fetch(to_x, sign, 0, 0), fetch(to_y, 0, sign, 0), fetch(to_xy, sign, sign, 0)


def body(rhs, diagonal, blocks, neighbours):
    first_len, second_len, third_len, width = rhs.shape
    components = diagonal.shape[-1]
    columns = width // components
    lengths = (first_len, second_len, third_len)
    totals = [n * lax.axis_size(axis) for n, axis in zip(lengths, ("gx", "gy", "gz"))]
    coords = (
        neighbours // (totals[1] * totals[2]),
        neighbours // totals[2] % totals[1],
        neighbours % totals[2],
    )
    codes = 0
    for dim, axis in enumerate(("gx", "gy", "gz")):
        here = iota(neighbours.shape, dim) + lax.axis_index(axis) * lengths[dim]
        codes = codes * 3 + (coords[dim] - here + 1 + totals[dim]) % totals[dim]
    codes = codes.astype(jnp.float32)
    atoms = first_len * second_len * third_len
    start = rhs.reshape(atoms, components, columns).transpose(1, 0, 2).reshape(components, -1)

    matrix, *out = call(
        pack_kernel,
        [(atoms * SLOT_ROWS, WIDE)] + [(72, WIDE)] * 3,
        blocks.reshape(atoms * components, -1),
        diagonal,
        codes,
        start,
    )
    sides = fetch_three(*out, 1)
    up, down = call(spread_kernel, [(320, WIDE)] * 2, matrix, *sides, start)
    low, high = fetch(up, 0, 0, -1), fetch(down, 0, 0, 1)
    first, far_matrix = call(
        far_kernel,
        [(components, 5 * LANES), (640, WIDE)],
        matrix, *sides, start, low, high,
        scratch=scratch_for(24, 40),
    )
    (near_matrix,) = call(near_matrix_kernel, [(512, WIDE)], matrix, low, high)
    second, first_own, second_own = call(
        second_kernel,
        [(components, 4 * LANES)] + [(components, width)] * 2,
        near_matrix, first, *fetch_three(first, first, first, -1),
        scratch=scratch_for(20, 32),
    )
    (third,) = call(
        third_kernel,
        [(components, 3 * LANES)],
        far_matrix, second, *fetch_three(second, second, second, 1),
        scratch=scratch_for(16, 40),
    )
    third_own, message = call(
        fourth_kernel,
        [(components, width), (lax.axis_size("gx"), 4, LANES)],
        near_matrix, third, *fetch_three(third, third, third, -1), start, first_own, second_own,
        scratch=scratch_for(12, 32),
    )
    rest = lax.axis_size("gy") * lax.axis_size("gz")
    message = lax.all_to_all(message, "gx", 0, 0, tiled=True)
    (message,) = call(relay_kernel, [(rest, 4, LANES)], message)
    message = lax.all_to_all(message, ("gy", "gz"), 0, 0, tiled=True)
    (result,) = call(
        finish_kernel, [start.shape], message, start, first_own, second_own, third_own
    )
    result = result.reshape(components, atoms, columns).transpose(1, 0, 2)
    return result.reshape(rhs.shape)


def solution(mesh):
    return jax.shard_map(
        body,
        mesh=mesh,
        in_specs=(
            P("gx", "gy", "gz", None),
            P("gx", "gy", "gz", None),
            P("gx", "gy", "gz", None, None),
            P("gx", "gy", "gz", None),
        ),
        out_specs=P("gx", "gy", "gz", None),
        check_vma=False,
    )
```

```python
import jax
import jax.numpy as jnp
from jax import lax
from jax.experimental import pallas as pl
from jax.experimental.pallas import tpu as pltpu
from jax.sharding import PartitionSpec as P

ITERS = 2
DEGREE = 2 * ITERS
SHIFT = 2.0
LANES = 128
PAIRS = [(i, j) for i in range(DEGREE + 1) for j in range(i, DEGREE + 1)]
VMEM = pl.BlockSpec(memory_space=pltpu.VMEM)


def two_sum(a, b):
    total = a + b
    part = total - a
    return total, (a - (total - part)) + (b - part)


def quick_sum(a, b):
    total = a + b
    return total, b - (total - a)


def split(a):
    scaled = 4097.0 * a
    head = scaled - (scaled - a)
    return head, a - head


def two_prod(a, b):
    product = a * b
    a_head, a_tail = split(a)
    b_head, b_tail = split(b)
    rest = ((a_head * b_head - product) + a_head * b_tail + a_tail * b_head) + a_tail * b_tail
    return product, rest


def pair_add(a, b):
    head, tail = two_sum(a[0], b[0])
    return quick_sum(head, tail + (a[1] + b[1]))


def pair_mul(a, b):
    head, tail = two_prod(a[0], b[0])
    return quick_sum(head, tail + (a[0] * b[1] + a[1] * b[0]))


def pair_scale(a, factor):
    head, tail = two_prod(a[0], factor)
    return quick_sum(head, tail + a[1] * factor)


def roll_pair(a, amount, axis):
    return pltpu.roll(a[0], amount, axis), pltpu.roll(a[1], amount, axis)


def iota(shape, axis):
    return lax.broadcasted_iota(jnp.int32, shape, axis)


def gram_kernel(fields, out):
    columns = 16
    diagonal_mask = iota((8, LANES), 0) == iota((8, LANES), 1) // columns
    rows = []
    parts = [split(field) for field in fields]
    for i, j in PAIRS:
        product = fields[i] * fields[j]
        (a_head, a_tail), (b_head, b_tail) = parts[i], parts[j]
        rest = ((a_head * b_head - product) + a_head * b_tail + a_tail * b_head) + a_tail * b_tail
        pieces = [
            (product[s : s + 8, t : t + LANES], rest[s : s + 8, t : t + LANES])
            for s in range(0, product.shape[0], 8)
            for t in range(0, product.shape[1], LANES)
        ]
        while len(pieces) > 1:
            pieces = [pair_add(pieces[q], pieces[q + 1]) for q in range(0, len(pieces), 2)]
        total = pieces[0]
        for amount in (4, 2, 1):
            total = pair_add(total, roll_pair(total, amount, 0))
        rows.append((total[0][0:1], total[1][0:1]))
    rows += [(jnp.zeros((1, LANES), jnp.float32),) * 2] * (16 - len(rows))
    packed = [[], []]
    for start in (0, 8):
        total = tuple(
            jnp.concatenate([row[part] for row in rows[start : start + 8]], axis=0)
            for part in (0, 1)
        )
        for amount in (64, 32, 16):
            total = pair_add(total, roll_pair(total, amount, 1))
        for part in (0, 1):
            packed[part].append(
                jnp.sum(jnp.where(diagonal_mask, total[part], 0.0), axis=0, keepdims=True)
            )
    message = jnp.concatenate(packed[0] + packed[1], axis=0)
    for q in range(out.shape[0]):
        out[q] = message


def sum_messages(ref):
    terms = [(ref[q], None) for q in range(ref.shape[0])]
    while len(terms) > 1:
        merged = []
        for q in range(0, len(terms), 2):
            (a, a_rest), (b, b_rest) = terms[q], terms[q + 1]
            total, rest = two_sum(a, b)
            if a_rest is not None:
                rest = rest + (a_rest + b_rest)
            merged.append((total, rest))
        terms = merged
    total, rest = terms[0]
    return quick_sum(total[0:2], rest[0:2] + (total[2:4] + rest[2:4]))


def relay_kernel(ref, out):
    head, tail = sum_messages(ref)
    message = jnp.concatenate([head, tail], axis=0)
    for q in range(out.shape[0]):
        out[q] = message


def finish_kernel(ref, *refs):
    fields, out = refs[:-1], refs[-1]
    columns = 16
    shape = (8, LANES)
    row = iota(shape, 0)
    diagonal_mask = row == iota(shape, 1) // columns
    packed = sum_messages(ref)
    unpacked = []
    for part in (0, 1):
        halves = []
        for half in (0, 1):
            value = jnp.where(
                diagonal_mask, jnp.broadcast_to(packed[part][half : half + 1], shape), 0.0
            )
            for amount in (64, 32, 16):
                value = value + pltpu.roll(value, amount, 1)
            halves.append(value)
        unpacked.append(halves)

    def entry(part, i, j):
        place = PAIRS.index((min(i, j), max(i, j)))
        half = unpacked[part][place // 8]
        return jnp.broadcast_to(half[place % 8 : place % 8 + 1], shape)

    gram = []
    for j in range(DEGREE + 1):
        column = []
        for part in (0, 1):
            value = jnp.zeros(shape, jnp.float32)
            for i in range(DEGREE + 1):
                value = jnp.where(row == i, entry(part, i, j), value)
            column.append(value)
        gram.append(tuple(column))

    def total_rows(a):
        for amount in (4, 2, 1):
            a = pair_add(a, roll_pair(a, amount, 0))
        return a[0]

    def with_start(a):
        return total_rows(pair_mul(gram[0], a))

    def square(a, degree):
        acc = None
        for j in range(degree + 1):
            factor = tuple(jnp.broadcast_to(part[j : j + 1], shape) for part in a)
            term = pair_mul(gram[j], factor)
            acc = term if acc is None else pair_add(acc, term)
        return total_rows(pair_mul(acc, a))

    def apply(a):
        return pair_add((SHIFT * a[0], SHIFT * a[1]), roll_pair(a, 1, 0))

    def shrink(quasi_norm, ratio, step):
        damping = 1.0 / (1.0 + ratio * ratio)
        return quasi_norm * ratio * jnp.sqrt(damping), damping * step

    zero = jnp.zeros(shape, jnp.float32)
    start = (jnp.where(row == 0, 1.0, 0.0), zero)
    inner = entry(0, 0, 0)
    quasi_norm = jnp.sqrt(inner)
    image = apply(start)
    resid = search = start
    direction = total = (zero, zero)
    ratio = weight = zero
    for iteration in range(ITERS):
        step = inner / with_start(image)
        resid = pair_add(resid, pair_scale(image, -step))
        direction = pair_add(search, pair_scale(direction, ratio * ratio * weight / step))
        ratio = jnp.sqrt(square(resid, 2 * iteration + 1)) / quasi_norm
        quasi_norm, weight = shrink(quasi_norm, ratio, step)
        total = pair_add(total, pair_scale(direction, weight))
        search_odd = pair_add(search, pair_scale(image, -step))
        image_odd = apply(search_odd)
        resid = pair_add(resid, pair_scale(image_odd, -step))
        direction = pair_add(search_odd, pair_scale(direction, ratio * ratio * weight / step))
        ratio = jnp.sqrt(square(resid, 2 * iteration + 2)) / quasi_norm
        quasi_norm, weight = shrink(quasi_norm, ratio, step)
        total = pair_add(total, pair_scale(direction, weight))
        if iteration + 1 < ITERS:
            inner_next = with_start(resid)
            mix = inner_next / inner
            search = pair_add(resid, pair_scale(search_odd, mix))
            image = pair_add(
                apply(search), pair_scale(pair_add(image_odd, pair_scale(image, mix)), mix)
            )
            inner = inner_next
    coefficients = total[0] + total[1]
    height, width = out.shape
    acc = None
    for i, field in enumerate(fields):
        factor = jnp.broadcast_to(coefficients[i : i + 1], (height, LANES))
        factor = jnp.concatenate([factor] * (width // LANES), axis=1)
        term = factor * field[...]
        acc = term if acc is None else acc + term
    out[...] = acc


SLOT_ROWS = 16
WIDE = 512
SELF = 27
CODE = 448
REACH = 3
HIGH = lax.Precision.HIGHEST


def third_of(value):
    return (value * 11) >> 5


def offsets_of(code):
    first = (code * 57) >> 9
    rest = code - 9 * first
    second = third_of(rest)
    return first - 1, second - 1, rest - 3 * second - 1


def far_atom(row):
    column = (row * 205) >> 11
    return 1 + (column >> 1), 1 + (column & 1), row - 10 * column - 3


def near_atom(row):
    column = row >> 3
    return column >> 1, column & 1, (row & 7) - 2


def far_slot(run, low):
    return lambda x, y, z: (((x - 1) * 2 + y - 1) * run + z - low) & 7


def near_slot(run, low):
    return lambda x, y, z: ((x * 2 + y) * run + z - low) & 7


def bricks_place(x, y, z):
    brick = ((z + 4) >> 2) * 4 + (x >> 1) * 2 + (y >> 1)
    return (brick * 2 + (x & 1)) * 8 + (y & 1) * 4 + ((z + 4) & 3)


def pieces_place(origin, run, low):
    def place(x, y, z):
        x, y = x - origin, y - origin
        piece = (x >> 1) * 2 + (y >> 1)
        return (piece * 4 + (x & 1) * 2 + (y & 1)) * run + z - low

    return place


def find_places(matrix, count, atom, place, slot, staged, places, sem):
    rows = [q * SLOT_ROWS for q in range(count)]
    code = jnp.concatenate([matrix[row : row + 1, CODE - 64 : CODE + 64] for row in rows], axis=0)
    code = pltpu.roll(code, 64, 1).astype(jnp.int32)
    x, y, z = atom(iota(code.shape, 0))
    dx, dy, dz = offsets_of(code)
    where = place(x + dx, y + dy, z + dz)
    staged[...] = (where & ~7) + ((slot(x, y, z) - where) & 7)
    copy = pltpu.make_async_copy(staged, places, sem)
    copy.start()
    copy.wait()


def set_tile(field, index, tile):
    for turn in range(8):
        field[index * 8 + turn] = pltpu.roll(tile, turn * SLOT_ROWS, 1) if turn else tile


def couple(matrix, groups, field, places, gathered):
    lane_slot = iota((SLOT_ROWS, LANES), 1) >> 4

    def gather(k, carry):
        for q, group in enumerate(groups):
            acc = None
            for slot, atom in enumerate(group):
                tile = field[places[atom, k]]
                acc = tile if acc is None else jnp.where(lane_slot == slot, tile, acc)
            gathered[q, pl.ds(pl.multiple_of(k * SLOT_ROWS, SLOT_ROWS), SLOT_ROWS), :] = acc
        return carry

    lax.fori_loop(0, SELF + 1, gather, 0, unroll=4)
    tiles = []
    for q, group in enumerate(groups):
        gathered[q, CODE:WIDE, :] = jnp.zeros((WIDE - CODE, LANES), jnp.float32)
        left, start = [], 0
        for r in range(1, 9):
            if r == 8 or group[r] != group[r - 1] + 1:
                left.append(matrix[group[start] * SLOT_ROWS : (group[r - 1] + 1) * SLOT_ROWS, :])
                start = r
        left = left[0] if len(left) == 1 else jnp.concatenate(left, axis=0)
        product = jnp.dot(
            left, gathered[q], precision=HIGH, preferred_element_type=jnp.float32
        )
        acc = product[0:SLOT_ROWS]
        for slot in range(1, 8):
            piece = product[slot * SLOT_ROWS : (slot + 1) * SLOT_ROWS]
            acc = jnp.where(lane_slot == slot, piece, acc)
        tiles.append(-acc)
    return tiles


def pick_own(field, place):
    lane_slot = iota((SLOT_ROWS, LANES), 1) >> 4
    tiles = []
    for x in (0, 1):
        acc = None
        for slot in range(8):
            where = place(x, slot >> 2, slot & 3)
            tile = field[(where & ~7) + ((slot - where) & 7)]
            acc = tile if acc is None else jnp.where(lane_slot == slot, tile, acc)
        tiles.append(acc)
    return jnp.concatenate(tiles, axis=1)


def pack_bricks(field):
    return jnp.concatenate([field[0:8], field[8:16]], axis=1)


def pack_kernel(blocks, diagonal, codes, start, matrix, to_x, to_y, to_xy):
    matrix[:, 0:432] = blocks[...]
    matrix[:, 432:WIDE] = jnp.zeros((matrix.shape[0], WIDE - 432), jnp.float32)
    eye = iota((SLOT_ROWS, SLOT_ROWS), 0) == iota((SLOT_ROWS, SLOT_ROWS), 1)
    for x in range(2):
        for y in range(2):
            for z in range(4):
                row = ((x * 2 + y) * 4 + z) * SLOT_ROWS
                own = SHIFT - jnp.broadcast_to(diagonal[x, y, z : z + 1], eye.shape)
                matrix[row : row + SLOT_ROWS, 432:448] = jnp.where(eye, own, 0.0)
                matrix[row : row + 1, CODE : CODE + SELF] = codes[x, y, z : z + 1]
                matrix[row : row + 1, CODE + SELF : CODE + SELF + 1] = jnp.full(
                    (1, 1), 13.0, jnp.float32
                )
    bricks = pack_bricks(start[...])
    for out, row in ((to_x, 64), (to_y, 128), (to_xy, 0)):
        out[0:64] = matrix[row : row + 64]
        out[64:72] = bricks


def spread_kernel(matrix, from_x, from_y, from_xy, start, up, down):
    far = ((matrix, 192), (from_y, 0), (from_x, 0), (from_xy, 0))
    for q, (ref, row) in enumerate(far):
        up[q * 48 : q * 48 + 48] = ref[row + 16 : row + 64]
        down[q * 48 : q * 48 + 48] = ref[row : row + 48]
    for q in range(3):
        up[192 + q * 32 : 224 + q * 32] = matrix[q * 64 + 32 : q * 64 + 64]
        down[192 + q * 32 : 224 + q * 32] = matrix[q * 64 : q * 64 + 32]
    bricks = [pack_bricks(start[...])] + [ref[64:72] for ref in (from_y, from_x, from_xy)]
    for q, brick in enumerate(bricks):
        up[288 + q * 8 : 296 + q * 8] = brick
        down[288 + q * 8 : 296 + q * 8] = brick


def far_kernel(
    matrix, from_x, from_y, from_xy, start, low, high,
    out, wide, field, gathered, staged, places, sem,
):
    for q, (ref, row) in enumerate(
        ((matrix, 192), (from_y, 0), (from_x, 0), (from_xy, 0))
    ):
        wide[q * 160 : q * 160 + 48] = low[q * 48 : q * 48 + 48]
        wide[q * 160 + 48 : q * 160 + 112] = ref[row : row + 64]
        wide[q * 160 + 112 : q * 160 + 160] = high[q * 48 : q * 48 + 48]
    bricks = [low[288 + q * 8 : 296 + q * 8] for q in range(4)]
    bricks += [pack_bricks(start[...])] + [ref[64:72] for ref in (from_y, from_x, from_xy)]
    bricks += [high[288 + q * 8 : 296 + q * 8] for q in range(4)]
    for q, brick in enumerate(bricks):
        for half in (0, 1):
            lanes = [brick[:, r * LANES : (r + 1) * LANES] for r in (half, half + 2)]
            set_tile(field, q * 2 + half, jnp.concatenate(lanes, axis=0))
    find_places(wide, 40, far_atom, bricks_place, far_slot(10, -3), staged, places, sem)
    groups = [list(range(q * 8, q * 8 + 8)) for q in range(5)]
    for q, tile in enumerate(couple(wide, groups, field, places, gathered)):
        out[:, q * LANES : (q + 1) * LANES] = tile


def near_matrix_kernel(matrix, low, high, out):
    for q in range(4):
        lo, hi = (192 + q * 32, 192 + q * 32) if q < 3 else (16, 0)
        out[q * 128 : q * 128 + 32] = low[lo : lo + 32]
        out[q * 128 + 32 : q * 128 + 96] = matrix[q * 64 : q * 64 + 64]
        out[q * 128 + 96 : q * 128 + 128] = high[hi : hi + 32]


def load_pieces(pieces, field):
    count = pieces[0].shape[1] // LANES
    for q, piece in enumerate(pieces):
        for t in range(count):
            set_tile(field, q * count + t, piece[:, t * LANES : (t + 1) * LANES])


def second_kernel(
    matrix, own, from_x, from_y, from_xy, out, first_own, second_own,
    field, gathered, staged, places, sem,
):
    place = pieces_place(-1, 10, -3)
    load_pieces((from_xy, from_x, from_y, own), field)
    find_places(matrix, 32, near_atom, place, near_slot(8, -2), staged, places, sem)
    groups = [list(range(q * 8, q * 8 + 8)) for q in range(4)]
    tiles = couple(matrix, groups, field, places, gathered)
    for q, tile in enumerate(tiles):
        out[:, q * LANES : (q + 1) * LANES] = tile
    first_own[...] = pick_own(field, place)
    turned = [pltpu.roll(tile, turn * SLOT_ROWS, 1) if turn else tile for tile in tiles for turn in range(8)]
    second_own[...] = pick_own(turned, lambda x, y, z: (x * 2 + y) * 8 + z + 2)


def third_kernel(
    matrix, own, from_x, from_y, from_xy, out, field, gathered, staged, places, sem
):
    load_pieces((own, from_y, from_x, from_xy), field)
    find_places(
        matrix, 40, far_atom, pieces_place(0, 8, -2), far_slot(6, -1), staged, places, sem
    )
    atoms = [c * 10 + z + 3 for c in range(4) for z in range(-1, 5)]
    groups = [atoms[q * 8 : q * 8 + 8] for q in range(3)]
    for q, tile in enumerate(couple(matrix, groups, field, places, gathered)):
        out[:, q * LANES : (q + 1) * LANES] = tile


def fourth_kernel(
    matrix, own, from_x, from_y, from_xy, start, first, second, third_own, out,
    field, gathered, staged, places, sem,
):
    place = pieces_place(-1, 6, -1)
    load_pieces((from_xy, from_x, from_y, own), field)
    find_places(matrix, 32, near_atom, place, near_slot(4, 0), staged, places, sem)
    atoms = [c * 8 + z + 2 for c in range(4) for z in range(4)]
    groups = [atoms[q * 8 : q * 8 + 8] for q in range(2)]
    fourth = jnp.concatenate(couple(matrix, groups, field, places, gathered), axis=1)
    third = pick_own(field, place)
    third_own[...] = third
    gram_kernel([start[...], first[...], second[...], third, fourth], out)


def call(kernel, shapes, *operands, scratch=()):
    shapes = [jax.ShapeDtypeStruct(shape, jnp.float32) for shape in shapes]
    out = pl.pallas_call(
        kernel,
        out_shape=shapes,
        in_specs=[VMEM] * len(operands),
        out_specs=[VMEM] * len(shapes),
        scratch_shapes=list(scratch),
        compiler_params=pltpu.CompilerParams(vmem_limit_bytes=32 * 1024 * 1024),
    )(*operands)
    return out


def scratch_for(tiles, groups, rows):
    return (
        pltpu.VMEM((tiles * 8, SLOT_ROWS, LANES), jnp.float32),
        pltpu.VMEM((groups, WIDE, LANES), jnp.float32),
        pltpu.VMEM((rows, LANES), jnp.int32),
        pltpu.SMEM((rows, LANES), jnp.int32),
        pltpu.SemaphoreType.DMA,
    )


def fetch(value, first, second, third):
    axes = ("gx", "gy", "gz")
    sizes = [lax.axis_size(axis) for axis in axes]
    pairs = []
    for a in range(sizes[0]):
        for b in range(sizes[1]):
            for c in range(sizes[2]):
                near = (a + first) % sizes[0], (b + second) % sizes[1], (c + third) % sizes[2]
                source = (near[0] * sizes[1] + near[1]) * sizes[2] + near[2]
                pairs.append((source, (a * sizes[1] + b) * sizes[2] + c))
    return lax.ppermute(value, axes, pairs)


def fetch_three(to_x, to_y, to_xy, sign):
    return fetch(to_x, sign, 0, 0), fetch(to_y, 0, sign, 0), fetch(to_xy, sign, sign, 0)


def body(rhs, diagonal, blocks, neighbours):
    first_len, second_len, third_len, width = rhs.shape
    components = diagonal.shape[-1]
    columns = width // components
    lengths = (first_len, second_len, third_len)
    totals = [n * lax.axis_size(axis) for n, axis in zip(lengths, ("gx", "gy", "gz"))]
    coords = (
        neighbours // (totals[1] * totals[2]),
        neighbours // totals[2] % totals[1],
        neighbours % totals[2],
    )
    codes = 0
    for dim, axis in enumerate(("gx", "gy", "gz")):
        here = iota(neighbours.shape, dim) + lax.axis_index(axis) * lengths[dim]
        codes = codes * 3 + (coords[dim] - here + 1 + totals[dim]) % totals[dim]
    codes = codes.astype(jnp.float32)
    atoms = first_len * second_len * third_len
    start = rhs.reshape(atoms, components, columns).transpose(1, 0, 2).reshape(components, -1)

    matrix, *out = call(
        pack_kernel,
        [(atoms * SLOT_ROWS, WIDE)] + [(72, WIDE)] * 3,
        blocks.reshape(atoms * components, -1),
        diagonal,
        codes,
        start,
    )
    sides = fetch_three(*out, 1)
    up, down = call(spread_kernel, [(320, WIDE)] * 2, matrix, *sides, start)
    low, high = fetch(up, 0, 0, -1), fetch(down, 0, 0, 1)
    first, far_matrix = call(
        far_kernel,
        [(components, 5 * LANES), (640, WIDE)],
        matrix, *sides, start, low, high,
        scratch=scratch_for(24, 5, 40),
    )
    (near_matrix,) = call(near_matrix_kernel, [(512, WIDE)], matrix, low, high)
    second, first_own, second_own = call(
        second_kernel,
        [(components, 4 * LANES)] + [(components, width)] * 2,
        near_matrix, first, *fetch_three(first, first, first, -1),
        scratch=scratch_for(20, 4, 32),
    )
    (third,) = call(
        third_kernel,
        [(components, 3 * LANES)],
        far_matrix, second, *fetch_three(second, second, second, 1),
        scratch=scratch_for(16, 3, 40),
    )
    third_own, message = call(
        fourth_kernel,
        [(components, width), (lax.axis_size("gx"), 4, LANES)],
        near_matrix, third, *fetch_three(third, third, third, -1), start, first_own, second_own,
        scratch=scratch_for(12, 2, 32),
    )
    rest = lax.axis_size("gy") * lax.axis_size("gz")
    message = lax.all_to_all(message, "gx", 0, 0, tiled=True)
    (message,) = call(relay_kernel, [(rest, 4, LANES)], message)
    message = lax.all_to_all(message, ("gy", "gz"), 0, 0, tiled=True)
    (result,) = call(
        finish_kernel, [start.shape], message, start, first_own, second_own, third_own
    )
    result = result.reshape(components, atoms, columns).transpose(1, 0, 2)
    return result.reshape(rhs.shape)


def solution(mesh):
    return jax.shard_map(
        body,
        mesh=mesh,
        in_specs=(
            P("gx", "gy", "gz", None),
            P("gx", "gy", "gz", None),
            P("gx", "gy", "gz", None, None),
            P("gx", "gy", "gz", None),
        ),
        out_specs=P("gx", "gy", "gz", None),
        check_vma=False,
    )
```

```python
import jax
import jax.numpy as jnp
from jax import lax
from jax.experimental import pallas as pl
from jax.experimental.pallas import tpu as pltpu
from jax.sharding import PartitionSpec as P

ITERS = 2
DEGREE = 2 * ITERS
SHIFT = 2.0
LANES = 128
PAIRS = [(i, j) for i in range(DEGREE + 1) for j in range(i, DEGREE + 1)]
VMEM = pl.BlockSpec(memory_space=pltpu.VMEM)


def two_sum(a, b):
    total = a + b
    part = total - a
    return total, (a - (total - part)) + (b - part)


def quick_sum(a, b):
    total = a + b
    return total, b - (total - a)


def split(a):
    scaled = 4097.0 * a
    head = scaled - (scaled - a)
    return head, a - head


def two_prod(a, b):
    product = a * b
    a_head, a_tail = split(a)
    b_head, b_tail = split(b)
    rest = ((a_head * b_head - product) + a_head * b_tail + a_tail * b_head) + a_tail * b_tail
    return product, rest


def pair_add(a, b):
    head, tail = two_sum(a[0], b[0])
    return quick_sum(head, tail + (a[1] + b[1]))


def pair_mul(a, b):
    head, tail = two_prod(a[0], b[0])
    return quick_sum(head, tail + (a[0] * b[1] + a[1] * b[0]))


def pair_scale(a, factor):
    head, tail = two_prod(a[0], factor)
    return quick_sum(head, tail + a[1] * factor)


def roll_pair(a, amount, axis):
    return pltpu.roll(a[0], amount, axis), pltpu.roll(a[1], amount, axis)


def iota(shape, axis):
    return lax.broadcasted_iota(jnp.int32, shape, axis)


def gram_kernel(fields, out):
    columns = 16
    diagonal_mask = iota((8, LANES), 0) == iota((8, LANES), 1) // columns
    rows = []
    parts = [split(field) for field in fields]
    for i, j in PAIRS:
        product = fields[i] * fields[j]
        (a_head, a_tail), (b_head, b_tail) = parts[i], parts[j]
        rest = ((a_head * b_head - product) + a_head * b_tail + a_tail * b_head) + a_tail * b_tail
        pieces = [
            (product[s : s + 8, t : t + LANES], rest[s : s + 8, t : t + LANES])
            for s in range(0, product.shape[0], 8)
            for t in range(0, product.shape[1], LANES)
        ]
        while len(pieces) > 1:
            pieces = [pair_add(pieces[q], pieces[q + 1]) for q in range(0, len(pieces), 2)]
        total = pieces[0]
        for amount in (4, 2, 1):
            total = pair_add(total, roll_pair(total, amount, 0))
        rows.append((total[0][0:1], total[1][0:1]))
    rows += [(jnp.zeros((1, LANES), jnp.float32),) * 2] * (16 - len(rows))
    packed = [[], []]
    for start in (0, 8):
        total = tuple(
            jnp.concatenate([row[part] for row in rows[start : start + 8]], axis=0)
            for part in (0, 1)
        )
        for amount in (64, 32, 16):
            total = pair_add(total, roll_pair(total, amount, 1))
        for part in (0, 1):
            packed[part].append(
                jnp.sum(jnp.where(diagonal_mask, total[part], 0.0), axis=0, keepdims=True)
            )
    message = jnp.concatenate(packed[0] + packed[1], axis=0)
    for q in range(out.shape[0]):
        out[q] = message


def sum_messages(ref):
    terms = [(ref[q], None) for q in range(ref.shape[0])]
    while len(terms) > 1:
        merged = []
        for q in range(0, len(terms), 2):
            (a, a_rest), (b, b_rest) = terms[q], terms[q + 1]
            total, rest = two_sum(a, b)
            if a_rest is not None:
                rest = rest + (a_rest + b_rest)
            merged.append((total, rest))
        terms = merged
    total, rest = terms[0]
    return quick_sum(total[0:2], rest[0:2] + (total[2:4] + rest[2:4]))


def relay_kernel(ref, out):
    head, tail = sum_messages(ref)
    message = jnp.concatenate([head, tail], axis=0)
    for q in range(out.shape[0]):
        out[q] = message


def finish_kernel(ref, *refs):
    fields, out = refs[:-1], refs[-1]
    columns = 16
    shape = (8, LANES)
    row = iota(shape, 0)
    diagonal_mask = row == iota(shape, 1) // columns
    packed = sum_messages(ref)
    unpacked = []
    for part in (0, 1):
        halves = []
        for half in (0, 1):
            value = jnp.where(
                diagonal_mask, jnp.broadcast_to(packed[part][half : half + 1], shape), 0.0
            )
            for amount in (64, 32, 16):
                value = value + pltpu.roll(value, amount, 1)
            halves.append(value)
        unpacked.append(halves)

    def entry(part, i, j):
        place = PAIRS.index((min(i, j), max(i, j)))
        half = unpacked[part][place // 8]
        return jnp.broadcast_to(half[place % 8 : place % 8 + 1], shape)

    gram = []
    for j in range(DEGREE + 1):
        column = []
        for part in (0, 1):
            value = jnp.zeros(shape, jnp.float32)
            for i in range(DEGREE + 1):
                value = jnp.where(row == i, entry(part, i, j), value)
            column.append(value)
        gram.append(tuple(column))

    def total_rows(a):
        for amount in (4, 2, 1):
            a = pair_add(a, roll_pair(a, amount, 0))
        return a[0]

    def with_start(a):
        return total_rows(pair_mul(gram[0], a))

    def square(a, degree):
        acc = None
        for j in range(degree + 1):
            factor = tuple(jnp.broadcast_to(part[j : j + 1], shape) for part in a)
            term = pair_mul(gram[j], factor)
            acc = term if acc is None else pair_add(acc, term)
        return total_rows(pair_mul(acc, a))

    def apply(a):
        return pair_add((SHIFT * a[0], SHIFT * a[1]), roll_pair(a, 1, 0))

    def shrink(quasi_norm, ratio, step):
        damping = 1.0 / (1.0 + ratio * ratio)
        return quasi_norm * ratio * jnp.sqrt(damping), damping * step

    zero = jnp.zeros(shape, jnp.float32)
    start = (jnp.where(row == 0, 1.0, 0.0), zero)
    inner = entry(0, 0, 0)
    quasi_norm = jnp.sqrt(inner)
    image = apply(start)
    resid = search = start
    direction = total = (zero, zero)
    ratio = weight = zero
    for iteration in range(ITERS):
        step = inner / with_start(image)
        resid = pair_add(resid, pair_scale(image, -step))
        direction = pair_add(search, pair_scale(direction, ratio * ratio * weight / step))
        ratio = jnp.sqrt(square(resid, 2 * iteration + 1)) / quasi_norm
        quasi_norm, weight = shrink(quasi_norm, ratio, step)
        total = pair_add(total, pair_scale(direction, weight))
        search_odd = pair_add(search, pair_scale(image, -step))
        image_odd = apply(search_odd)
        resid = pair_add(resid, pair_scale(image_odd, -step))
        direction = pair_add(search_odd, pair_scale(direction, ratio * ratio * weight / step))
        ratio = jnp.sqrt(square(resid, 2 * iteration + 2)) / quasi_norm
        quasi_norm, weight = shrink(quasi_norm, ratio, step)
        total = pair_add(total, pair_scale(direction, weight))
        if iteration + 1 < ITERS:
            inner_next = with_start(resid)
            mix = inner_next / inner
            search = pair_add(resid, pair_scale(search_odd, mix))
            image = pair_add(
                apply(search), pair_scale(pair_add(image_odd, pair_scale(image, mix)), mix)
            )
            inner = inner_next
    coefficients = total[0] + total[1]
    height, width = fields[0].shape
    acc = None
    for i, field in enumerate(fields):
        factor = jnp.broadcast_to(coefficients[i : i + 1], (height, LANES))
        factor = jnp.concatenate([factor] * (width // LANES), axis=1)
        term = factor * field[...]
        acc = term if acc is None else acc + term
    from_tiles(acc, out)


SLOT_ROWS = 16
WIDE = 512
SELF = 27
CODE = 448
HIGH = lax.Precision.HIGHEST
LENGTHS = (2, 2, 4)
ATOMS = 16
AXES = ("gx", "gy", "gz")


def far_place(x, y, z):
    piece = (x >> 1) * 2 + (y >> 1)
    outside = ((z >> 2) != 0).astype(jnp.int32)
    return (piece * 4 + outside * 2 + (x & 1)) * 8 + (y & 1) * 4 + (z & 3)


def far_slot(x, y, z):
    return (((x - 1) * 2 + y - 1) * 6 + z + 1) & 7


def near_place(x, y, z):
    x, y = x + 1, y + 1
    piece = (x >> 1) * 2 + (y >> 1)
    return (piece * 4 + (x & 1) * 2 + (y & 1)) * 6 + z + 1


def near_slot(x, y, z):
    return (y * 4 + z) & 7


def find_places(matrix, count, atom, place, slot, out):
    rows = [q * SLOT_ROWS for q in range(count)]
    code = jnp.concatenate([matrix[row : row + 1, CODE - 64 : CODE + 64] for row in rows], axis=0)
    code = pltpu.roll(code, 64, 1).astype(jnp.int32)
    x, y, z = atom(iota(code.shape, 0))
    first = (code * 57) >> 9
    rest = code - 9 * first
    second = (rest * 11) >> 5
    where = place(x + first - 1, y + second - 1, z + rest - 3 * second - 1)
    out[...] = (where & ~7) + ((slot(x, y, z) - where) & 7)


def set_tiles(field, pieces):
    count = pieces[0].shape[1] // LANES
    for q, piece in enumerate(pieces):
        for t in range(count):
            tile = piece[:, t * LANES : (t + 1) * LANES]
            for turn in range(8):
                place = (q * count + t) * 8 + turn
                field[place] = pltpu.roll(tile, turn * SLOT_ROWS, 1) if turn else tile


def couple(matrix, field, places, gathered):
    lane_slot = iota((SLOT_ROWS, LANES), 1) >> 4
    groups = matrix.shape[0] // LANES

    def gather(k, carry):
        for q in range(groups):
            acc = None
            for slot in range(8):
                tile = field[places[q * 8 + slot, k]]
                acc = tile if acc is None else jnp.where(lane_slot == slot, tile, acc)
            gathered[q, pl.ds(pl.multiple_of(k * SLOT_ROWS, SLOT_ROWS), SLOT_ROWS), :] = acc
        return carry

    lax.fori_loop(0, SELF + 1, gather, 0, unroll=7)
    tiles = []
    for q in range(groups):
        gathered[q, CODE:WIDE, :] = jnp.zeros((WIDE - CODE, LANES), jnp.float32)
        product = jnp.dot(
            matrix[q * LANES : (q + 1) * LANES, :],
            gathered[q],
            precision=HIGH,
            preferred_element_type=jnp.float32,
        )
        acc = product[0:SLOT_ROWS]
        for slot in range(1, 8):
            piece = product[slot * SLOT_ROWS : (slot + 1) * SLOT_ROWS]
            acc = jnp.where(lane_slot == slot, piece, acc)
        tiles.append(-acc)
    return jnp.concatenate(tiles, axis=1)


def pick_own(field):
    lane_slot = iota((SLOT_ROWS, LANES), 1) >> 4
    tiles = []
    for x in range(2):
        acc = None
        for slot in range(8):
            where = near_place(x, slot >> 2, slot & 3)
            tile = field[(where & ~7) + ((slot - where) & 7)]
            acc = tile if acc is None else jnp.where(lane_slot == slot, tile, acc)
        tiles.append(acc)
    return jnp.concatenate(tiles, axis=1)


def spread_lanes(value):
    for amount in (64, 32, 16):
        value = value + pltpu.roll(value, amount, 1)
    return value


def to_tiles(rows):
    shape = (8, LANES)
    diagonal_mask = iota(shape, 0) == iota(shape, 1) >> 4
    lane_slot = iota(shape, 1) >> 4
    halves = []
    for half in range(2):
        tiles = []
        for x in range(2):
            acc = jnp.zeros(shape, jnp.float32)
            for slot in range(8):
                row = rows(x, slot >> 2, slot & 3)[:, half * LANES : (half + 1) * LANES]
                value = jnp.where(diagonal_mask, jnp.broadcast_to(row, shape), 0.0)
                acc = jnp.where(lane_slot == slot, spread_lanes(value), acc)
            tiles.append(acc)
        halves.append(jnp.concatenate(tiles, axis=1))
    return jnp.concatenate(halves, axis=0)


def from_tiles(value, out):
    shape = (8, LANES)
    diagonal_mask = iota(shape, 0) == iota(shape, 1) >> 4
    lane_slot = iota(shape, 1) >> 4
    for half in range(2):
        for x in range(2):
            tile = value[half * 8 : half * 8 + 8, x * LANES : (x + 1) * LANES]
            for slot in range(8):
                own = spread_lanes(jnp.where(lane_slot == slot, tile, 0.0))
                row = jnp.sum(jnp.where(diagonal_mask, own, 0.0), axis=0, keepdims=True)
                z = slot & 3
                out[x, slot >> 2, z : z + 1, half * LANES : (half + 1) * LANES] = row


def pack_bricks(field):
    return jnp.concatenate([field[0:8], field[8:16]], axis=1)


def unpack_bricks(packed):
    return jnp.concatenate([packed[:, 0 : 2 * LANES], packed[:, 2 * LANES : 4 * LANES]], axis=0)


def pack_kernel(
    rhs_hbm, diagonal_hbm, blocks_hbm, neighbours_hbm,
    matrix, start, to_x, to_y, to_xy,
    rhs, diagonal, blocks, neighbours, sems,
):
    sources = (neighbours_hbm, diagonal_hbm, rhs_hbm, blocks_hbm)
    copies = [
        pltpu.make_async_copy(source, target, sems.at[q])
        for q, (source, target) in enumerate(zip(sources, (neighbours, diagonal, rhs, blocks)))
    ]
    for copy in copies:
        copy.start()
    matrix[:, 384:WIDE] = jnp.zeros((matrix.shape[0], WIDE - 384), jnp.float32)
    eye = iota((SLOT_ROWS, SLOT_ROWS), 0) == iota((SLOT_ROWS, SLOT_ROWS), 1)
    totals = [length * lax.axis_size(axis) for length, axis in zip(LENGTHS, AXES)]
    corner = [length * lax.axis_index(axis) for length, axis in zip(LENGTHS, AXES)]
    bits = [total.bit_length() - 1 for total in totals]
    for copy in copies[:2]:
        copy.wait()
    for x in range(2):
        for y in range(2):
            index = neighbours[x, y]
            along_x = index >> (bits[1] + bits[2])
            along_y = (index >> bits[2]) & (totals[1] - 1)
            along_z = index & (totals[2] - 1)
            z_here = corner[2] + iota(index.shape, 0)
            code = (along_x - (corner[0] + x - 1)) & (totals[0] - 1)
            code = code * 3 + ((along_y - (corner[1] + y - 1)) & (totals[1] - 1))
            code = code * 3 + ((along_z - z_here + 1) & (totals[2] - 1))
            code = code.astype(jnp.float32)
            for z in range(4):
                row = ((x * 2 + y) * 4 + z) * SLOT_ROWS
                matrix[row : row + 1, CODE : CODE + SELF] = code[z : z + 1]
                matrix[row : row + 1, CODE + SELF : CODE + SELF + 1] = jnp.full(
                    (1, 1), 13.0, jnp.float32
                )
                own = SHIFT - jnp.broadcast_to(diagonal[x, y, z : z + 1], eye.shape)
                matrix[row : row + SLOT_ROWS, 432:448] = jnp.where(eye, own, 0.0)
    copies[2].wait()
    value = to_tiles(lambda x, y, z: rhs[x, y, z : z + 1])
    start[...] = value
    bricks = pack_bricks(value)
    copies[3].wait()
    for x in range(2):
        for y in range(2):
            for z in range(4):
                row = ((x * 2 + y) * 4 + z) * SLOT_ROWS
                matrix[row : row + SLOT_ROWS, 0:432] = blocks[x, y, z]
    for out, row in ((to_x, 64), (to_y, 128), (to_xy, 0)):
        out[0:64] = matrix[row : row + 64]
        out[64:72] = bricks


def far_columns(matrix, from_x, from_y, from_xy):
    return (matrix, 192), (from_y, 0), (from_x, 0), (from_xy, 0)


def is_even():
    return lax.rem(lax.axis_index("gz"), 2) == 0


def spread_kernel(matrix, from_x, from_y, from_xy, start, to_first, to_second):
    even = is_even()
    for q, (ref, row) in enumerate(far_columns(matrix, from_x, from_y, from_xy)):
        up, down = ref[row + 48 : row + 64], ref[row : row + 16]
        to_first[q * 16 : q * 16 + 16] = jnp.where(even, up, down)
        to_second[q * 16 : q * 16 + 16] = jnp.where(even, down, up)
    bricks = [pack_bricks(start[...])] + [ref[64:72] for ref in (from_y, from_x, from_xy)]
    for q, brick in enumerate(bricks):
        to_first[64 + q * 8 : 72 + q * 8] = brick
        to_second[64 + q * 8 : 72 + q * 8] = brick


def outside(low, high):
    upper = ((iota(low.shape, 1) >> 4) & 3) < 2
    return jnp.where(upper, high, low)


def far_atom(row):
    column = (row * 43) >> 8
    return 1 + (column >> 1), 1 + (column & 1), row - 6 * column - 1


def near_atom(row):
    return row >> 3, (row >> 2) & 1, row & 3


def join_kernel(
    matrix, from_x, from_y, from_xy, start, first, second,
    wide, places, own, piece_y, piece_x, piece_xy,
):
    even = is_even()
    for q, (ref, row) in enumerate(far_columns(matrix, from_x, from_y, from_xy)):
        one, two = first[q * 16 : q * 16 + 16], second[q * 16 : q * 16 + 16]
        wide[q * 96 : q * 96 + 16] = jnp.where(even, two, one)
        wide[q * 96 + 16 : q * 96 + 80] = ref[row : row + 64]
        wide[q * 96 + 80 : q * 96 + 96] = jnp.where(even, one, two)
    inner = [start[...]] + [unpack_bricks(ref[64:72]) for ref in (from_y, from_x, from_xy)]
    for q, (out, value) in enumerate(zip((own, piece_y, piece_x, piece_xy), inner)):
        one = unpack_bricks(first[64 + q * 8 : 72 + q * 8])
        two = unpack_bricks(second[64 + q * 8 : 72 + q * 8])
        low, high = jnp.where(even, two, one), jnp.where(even, one, two)
        out[:, 0 : 2 * LANES] = value
        out[:, 2 * LANES : 4 * LANES] = outside(low, high)
    find_places(wide, 24, far_atom, far_place, far_slot, places)


def layers_kernel(value, first, second, out):
    even = is_even()
    one, two = first[...], second[...]
    out[:, 0 : 2 * LANES] = value[...]
    low, high = jnp.where(even, two, one), jnp.where(even, one, two)
    out[:, 2 * LANES : 4 * LANES] = outside(low, high)


def near_places_kernel(matrix, places):
    find_places(matrix, ATOMS, near_atom, near_place, near_slot, places)


def with_places(places_in, places, sem, work):
    copy = pltpu.make_async_copy(places_in, places, sem)
    copy.start()
    work()
    copy.wait()


def far_kernel(
    matrix, places_in, own, from_y, from_x, from_xy, out, field, gathered, places, sem
):
    with_places(places_in, places, sem, lambda: set_tiles(field, (own, from_y, from_x, from_xy)))
    out[...] = couple(matrix, field, places, gathered)


def near_kernel(
    matrix, places_in, own, from_y, from_x, from_xy, out, before, field, gathered, places, sem
):
    with_places(places_in, places, sem, lambda: set_tiles(field, (from_xy, from_x, from_y, own)))
    out[...] = couple(matrix, field, places, gathered)
    before[...] = pick_own(field)


def last_kernel(
    matrix, places_in, own, from_y, from_x, from_xy, start, first, second, third_out, out,
    field, gathered, places, sem,
):
    with_places(places_in, places, sem, lambda: set_tiles(field, (from_xy, from_x, from_y, own)))
    fourth = couple(matrix, field, places, gathered)
    third = pick_own(field)
    third_out[...] = third
    gram_kernel([start[...], first[...], second[...], third, fourth], out)


def call(kernel, shapes, *operands, scratch=(), place=VMEM):
    shapes = [
        shape if isinstance(shape, jax.ShapeDtypeStruct) else jax.ShapeDtypeStruct(shape, jnp.float32)
        for shape in shapes
    ]
    return pl.pallas_call(
        kernel,
        out_shape=shapes,
        in_specs=[place] * len(operands),
        out_specs=[VMEM] * len(shapes),
        scratch_shapes=list(scratch),
        compiler_params=pltpu.CompilerParams(vmem_limit_bytes=24 * 1024 * 1024),
    )(*operands)


def scratch_for(tiles, groups):
    return (
        pltpu.VMEM((tiles * 8, SLOT_ROWS, LANES), jnp.float32),
        pltpu.VMEM((groups, WIDE, LANES), jnp.float32),
        pltpu.SMEM((groups * 8, LANES), jnp.int32),
        pltpu.SemaphoreType.DMA,
    )


def fetch(value, first, second):
    sizes = [lax.axis_size(axis) for axis in AXES]
    pairs = []
    for a in range(sizes[0]):
        for b in range(sizes[1]):
            for c in range(sizes[2]):
                source = ((a + first) % sizes[0] * sizes[1] + (b + second) % sizes[1]) * sizes[2] + c
                pairs.append((source, (a * sizes[1] + b) * sizes[2] + c))
    return lax.ppermute(value, AXES, pairs)


def fetch_three(to_x, to_y, to_xy, sign):
    from_x, from_xy = fetch(to_x, sign, 0), fetch(to_xy, sign, sign)
    return fetch(to_y, 0, sign), from_x, from_xy


def swap_layers(to_first, to_second):
    count = lax.axis_size("gz")
    even = [(i, i ^ 1) for i in range(count)]
    odd = [(i, (i + 1 if i % 2 else i - 1) % count) for i in range(count)]
    return lax.ppermute(to_first, "gz", even), lax.ppermute(to_second, "gz", odd)


def body(rhs, diagonal, blocks, neighbours):
    width = rhs.shape[-1]
    flat = (SLOT_ROWS, width)
    matrix, start, *out = call(
        pack_kernel,
        [(ATOMS * SLOT_ROWS, WIDE), flat] + [(72, WIDE)] * 3,
        rhs, diagonal, blocks, neighbours,
        scratch=[
            pltpu.VMEM(rhs.shape, rhs.dtype),
            pltpu.VMEM(diagonal.shape, diagonal.dtype),
            pltpu.VMEM(blocks.shape, blocks.dtype),
            pltpu.VMEM(neighbours.shape, neighbours.dtype),
            pltpu.SemaphoreType.DMA((4,)),
        ],
        place=pl.BlockSpec(memory_space=pl.ANY),
    )
    from_y, from_x, from_xy = fetch_three(*out, 1)
    sides = from_x, from_y, from_xy
    (near_places,) = call(
        near_places_kernel, [jax.ShapeDtypeStruct((ATOMS, LANES), jnp.int32)], matrix
    )
    layers = swap_layers(*call(spread_kernel, [(96, WIDE)] * 2, matrix, *sides, start))
    wide, far_places, *pieces = call(
        join_kernel,
        [(24 * SLOT_ROWS, WIDE), jax.ShapeDtypeStruct((24, LANES), jnp.int32)]
        + [(SLOT_ROWS, 4 * LANES)] * 4,
        matrix, *sides, start, *layers,
    )
    far_scratch, near_scratch = scratch_for(16, 3), scratch_for(12, 2)
    far_shape = (SLOT_ROWS, 3 * LANES)
    (first,) = call(far_kernel, [far_shape], wide, far_places, *pieces, scratch=far_scratch)
    second, first_own = call(
        near_kernel, [flat, flat],
        matrix, near_places, first, *fetch_three(first, first, first, -1),
        scratch=near_scratch,
    )
    (layered,) = call(
        layers_kernel, [(SLOT_ROWS, 4 * LANES)], second, *swap_layers(second, second)
    )
    (third,) = call(
        far_kernel, [far_shape],
        wide, far_places, layered, *fetch_three(layered, layered, layered, 1),
        scratch=far_scratch,
    )
    third_own, message = call(
        last_kernel,
        [flat, (lax.axis_size("gx"), 4, LANES)],
        matrix, near_places, third, *fetch_three(third, third, third, -1),
        start, first_own, second,
        scratch=near_scratch,
    )
    rest = lax.axis_size("gy") * lax.axis_size("gz")
    message = lax.all_to_all(message, "gx", 0, 0, tiled=True)
    (message,) = call(relay_kernel, [(rest, 4, LANES)], message)
    message = lax.all_to_all(message, ("gy", "gz"), 0, 0, tiled=True)
    (result,) = call(finish_kernel, [rhs.shape], message, start, first_own, second, third_own)
    return result


def solution(mesh):
    return jax.shard_map(
        body,
        mesh=mesh,
        in_specs=(
            P("gx", "gy", "gz", None),
            P("gx", "gy", "gz", None),
            P("gx", "gy", "gz", None, None),
            P("gx", "gy", "gz", None),
        ),
        out_specs=P("gx", "gy", "gz", None),
        check_vma=False,
    )
```

```python
import jax
import jax.numpy as jnp
from jax import lax
from jax.experimental import pallas as pl
from jax.experimental.pallas import tpu as pltpu
from jax.sharding import PartitionSpec as P

ITERS = 2
DEGREE = 2 * ITERS
SHIFT = 2.0
LANES = 128
PAIRS = [(i, j) for i in range(DEGREE + 1) for j in range(i, DEGREE + 1)]
VMEM = pl.BlockSpec(memory_space=pltpu.VMEM)


def two_sum(a, b):
    total = a + b
    part = total - a
    return total, (a - (total - part)) + (b - part)


def quick_sum(a, b):
    total = a + b
    return total, b - (total - a)


def split(a):
    scaled = 4097.0 * a
    head = scaled - (scaled - a)
    return head, a - head


def two_prod(a, b):
    product = a * b
    a_head, a_tail = split(a)
    b_head, b_tail = split(b)
    rest = ((a_head * b_head - product) + a_head * b_tail + a_tail * b_head) + a_tail * b_tail
    return product, rest


def pair_add(a, b):
    head, tail = two_sum(a[0], b[0])
    return quick_sum(head, tail + (a[1] + b[1]))


def pair_mul(a, b):
    head, tail = two_prod(a[0], b[0])
    return quick_sum(head, tail + (a[0] * b[1] + a[1] * b[0]))


def pair_scale(a, factor):
    head, tail = two_prod(a[0], factor)
    return quick_sum(head, tail + a[1] * factor)


def roll_pair(a, amount, axis):
    return pltpu.roll(a[0], amount, axis), pltpu.roll(a[1], amount, axis)


def iota(shape, axis):
    return lax.broadcasted_iota(jnp.int32, shape, axis)


def gram_kernel(fields, out):
    columns = 16
    diagonal_mask = iota((8, LANES), 0) == iota((8, LANES), 1) // columns
    rows = []
    parts = [split(field) for field in fields]
    for i, j in PAIRS:
        product = fields[i] * fields[j]
        (a_head, a_tail), (b_head, b_tail) = parts[i], parts[j]
        rest = ((a_head * b_head - product) + a_head * b_tail + a_tail * b_head) + a_tail * b_tail
        pieces = [
            (product[s : s + 8, t : t + LANES], rest[s : s + 8, t : t + LANES])
            for s in range(0, product.shape[0], 8)
            for t in range(0, product.shape[1], LANES)
        ]
        while len(pieces) > 1:
            pieces = [pair_add(pieces[q], pieces[q + 1]) for q in range(0, len(pieces), 2)]
        total = pieces[0]
        for amount in (4, 2, 1):
            total = pair_add(total, roll_pair(total, amount, 0))
        rows.append((total[0][0:1], total[1][0:1]))
    rows += [(jnp.zeros((1, LANES), jnp.float32),) * 2] * (16 - len(rows))
    packed = [[], []]
    for start in (0, 8):
        total = tuple(
            jnp.concatenate([row[part] for row in rows[start : start + 8]], axis=0)
            for part in (0, 1)
        )
        for amount in (64, 32, 16):
            total = pair_add(total, roll_pair(total, amount, 1))
        for part in (0, 1):
            packed[part].append(
                jnp.sum(jnp.where(diagonal_mask, total[part], 0.0), axis=0, keepdims=True)
            )
    message = jnp.concatenate(packed[0] + packed[1], axis=0)
    for q in range(out.shape[0]):
        out[q] = message


def sum_messages(ref):
    terms = [(ref[q], None) for q in range(ref.shape[0])]
    while len(terms) > 1:
        merged = []
        for q in range(0, len(terms), 2):
            (a, a_rest), (b, b_rest) = terms[q], terms[q + 1]
            total, rest = two_sum(a, b)
            if a_rest is not None:
                rest = rest + (a_rest + b_rest)
            merged.append((total, rest))
        terms = merged
    total, rest = terms[0]
    return quick_sum(total[0:2], rest[0:2] + (total[2:4] + rest[2:4]))


def relay_kernel(ref, out):
    head, tail = sum_messages(ref)
    message = jnp.concatenate([head, tail], axis=0)
    for q in range(out.shape[0]):
        out[q] = message


def finish_kernel(ref, *refs):
    fields, out = refs[:-1], refs[-1]
    columns = 16
    shape = (8, LANES)
    row = iota(shape, 0)
    diagonal_mask = row == iota(shape, 1) // columns
    packed = sum_messages(ref)
    unpacked = []
    for part in (0, 1):
        halves = []
        for half in (0, 1):
            value = jnp.where(
                diagonal_mask, jnp.broadcast_to(packed[part][half : half + 1], shape), 0.0
            )
            for amount in (64, 32, 16):
                value = value + pltpu.roll(value, amount, 1)
            halves.append(value)
        unpacked.append(halves)

    def entry(part, i, j):
        place = PAIRS.index((min(i, j), max(i, j)))
        half = unpacked[part][place // 8]
        return jnp.broadcast_to(half[place % 8 : place % 8 + 1], shape)

    gram = []
    for j in range(DEGREE + 1):
        column = []
        for part in (0, 1):
            value = jnp.zeros(shape, jnp.float32)
            for i in range(DEGREE + 1):
                value = jnp.where(row == i, entry(part, i, j), value)
            column.append(value)
        gram.append(tuple(column))

    def total_rows(a):
        for amount in (4, 2, 1):
            a = pair_add(a, roll_pair(a, amount, 0))
        return a[0]

    def with_start(a):
        return total_rows(pair_mul(gram[0], a))

    def square(a, degree):
        acc = None
        for j in range(degree + 1):
            factor = tuple(jnp.broadcast_to(part[j : j + 1], shape) for part in a)
            term = pair_mul(gram[j], factor)
            acc = term if acc is None else pair_add(acc, term)
        return total_rows(pair_mul(acc, a))

    def apply(a):
        return pair_add((SHIFT * a[0], SHIFT * a[1]), roll_pair(a, 1, 0))

    def shrink(quasi_norm, ratio, step):
        damping = 1.0 / (1.0 + ratio * ratio)
        return quasi_norm * ratio * jnp.sqrt(damping), damping * step

    zero = jnp.zeros(shape, jnp.float32)
    start = (jnp.where(row == 0, 1.0, 0.0), zero)
    inner = entry(0, 0, 0)
    quasi_norm = jnp.sqrt(inner)
    image = apply(start)
    resid = search = start
    direction = total = (zero, zero)
    ratio = weight = zero
    for iteration in range(ITERS):
        step = inner / with_start(image)
        resid = pair_add(resid, pair_scale(image, -step))
        direction = pair_add(search, pair_scale(direction, ratio * ratio * weight / step))
        ratio = jnp.sqrt(square(resid, 2 * iteration + 1)) / quasi_norm
        quasi_norm, weight = shrink(quasi_norm, ratio, step)
        total = pair_add(total, pair_scale(direction, weight))
        search_odd = pair_add(search, pair_scale(image, -step))
        image_odd = apply(search_odd)
        resid = pair_add(resid, pair_scale(image_odd, -step))
        direction = pair_add(search_odd, pair_scale(direction, ratio * ratio * weight / step))
        ratio = jnp.sqrt(square(resid, 2 * iteration + 2)) / quasi_norm
        quasi_norm, weight = shrink(quasi_norm, ratio, step)
        total = pair_add(total, pair_scale(direction, weight))
        if iteration + 1 < ITERS:
            inner_next = with_start(resid)
            mix = inner_next / inner
            search = pair_add(resid, pair_scale(search_odd, mix))
            image = pair_add(
                apply(search), pair_scale(pair_add(image_odd, pair_scale(image, mix)), mix)
            )
            inner = inner_next
    coefficients = total[0] + total[1]
    height, width = fields[0].shape
    acc = None
    for i, field in enumerate(fields):
        factor = jnp.broadcast_to(coefficients[i : i + 1], (height, LANES))
        factor = jnp.concatenate([factor] * (width // LANES), axis=1)
        term = factor * field[...]
        acc = term if acc is None else acc + term
    from_tiles(acc, out)


SLOT_ROWS = 16
WIDE = 512
SELF = 27
CODE = 448
HIGH = lax.Precision.HIGHEST
LENGTHS = (2, 2, 4)
ATOMS = 16
AXES = ("gx", "gy", "gz")


def bricks_place(x, y, z):
    brick = ((z + 4) >> 2) * 4 + (x >> 1) * 2 + (y >> 1)
    return (brick * 2 + (x & 1)) * 8 + (y & 1) * 4 + (z & 3)


def pieces_place(origin, run, low):
    def place(x, y, z):
        x, y = x - origin, y - origin
        piece = (x >> 1) * 2 + (y >> 1)
        return (piece * 4 + (x & 1) * 2 + (y & 1)) * run + z - low

    return place


def tall_far_atom(index):
    column = (index * 205) >> 11
    return 1 + (column >> 1), 1 + (column & 1), index - 10 * column - 3


def far_atom(index):
    column = (index * 43) >> 8
    return 1 + (column >> 1), 1 + (column & 1), index - 6 * column - 1


def tall_near_atom(index):
    return index >> 4, (index >> 3) & 1, (index & 7) - 2


def near_atom(index):
    return index >> 3, (index >> 2) & 1, index & 3


FAR_ROWS = [column * 10 + z + 3 for column in range(4) for z in range(-1, 5)]
FIRST_PLACE, SECOND_PLACE = pieces_place(-1, 10, -3), pieces_place(0, 8, -2)
THIRD_PLACE = pieces_place(-1, 6, -1)


def find_places(matrix, rows, atom, place, out):
    rows = [row * SLOT_ROWS for row in rows]
    code = jnp.concatenate([matrix[row : row + 1, CODE - 64 : CODE + 64] for row in rows], axis=0)
    code = pltpu.roll(code, 64, 1).astype(jnp.int32)
    index = iota(code.shape, 0)
    x, y, z = atom(index)
    first = (code * 57) >> 9
    rest = code - 9 * first
    second = (rest * 11) >> 5
    where = place(x + first - 1, y + second - 1, z + rest - 3 * second - 1)
    out[...] = (where & ~7) + ((index - where) & 7)


def set_tiles(field, pieces):
    count = pieces[0].shape[1] // LANES
    for q, piece in enumerate(pieces):
        for t in range(count):
            tile = piece[:, t * LANES : (t + 1) * LANES]
            for turn in range(8):
                place = (q * count + t) * 8 + turn
                field[place] = pltpu.roll(tile, turn * SLOT_ROWS, 1) if turn else tile


def couple(matrix, rows, field, places, gathered):
    lane_slot = iota((SLOT_ROWS, LANES), 1) >> 4
    groups = len(rows) // 8

    def gather(k, carry):
        for q in range(groups):
            acc = None
            for slot in range(8):
                tile = field[places[q * 8 + slot, k]]
                acc = tile if acc is None else jnp.where(lane_slot == slot, tile, acc)
            gathered[q, pl.ds(pl.multiple_of(k * SLOT_ROWS, SLOT_ROWS), SLOT_ROWS), :] = acc
        return carry

    lax.fori_loop(0, SELF + 1, gather, 0, unroll=SELF + 1)
    tiles = []
    for q in range(groups):
        gathered[q, CODE:WIDE, :] = jnp.zeros((WIDE - CODE, LANES), jnp.float32)
        group = rows[q * 8 : q * 8 + 8]
        left, start = [], 0
        for r in range(1, 9):
            if r == 8 or group[r] != group[r - 1] + 1:
                left.append(matrix[group[start] * SLOT_ROWS : (group[r - 1] + 1) * SLOT_ROWS, :])
                start = r
        left = left[0] if len(left) == 1 else jnp.concatenate(left, axis=0)
        product = jnp.dot(
            left, gathered[q], precision=HIGH, preferred_element_type=jnp.float32
        )
        acc = product[0:SLOT_ROWS]
        for slot in range(1, 8):
            piece = product[slot * SLOT_ROWS : (slot + 1) * SLOT_ROWS]
            acc = jnp.where(lane_slot == slot, piece, acc)
        tiles.append(-acc)
    return jnp.concatenate(tiles, axis=1)


def pick_own(pieces, place):
    lane_slot = iota((SLOT_ROWS, LANES), 1) >> 4
    tiles = []
    for x in range(2):
        acc = None
        for slot in range(8):
            where = place(x, slot >> 2, slot & 3)
            count = pieces[0].shape[1] // LANES
            tile, turn = where >> 3, (slot - where) & 7
            lanes = pl.ds(tile % count * LANES, LANES)
            tile = pieces[tile // count][:, lanes]
            tile = pltpu.roll(tile, turn * SLOT_ROWS, 1) if turn else tile
            acc = tile if acc is None else jnp.where(lane_slot == slot, tile, acc)
        tiles.append(acc)
    return jnp.concatenate(tiles, axis=1)


def spread_lanes(value):
    for amount in (64, 32, 16):
        value = value + pltpu.roll(value, amount, 1)
    return value


def to_tiles(rows):
    shape = (8, LANES)
    diagonal_mask = iota(shape, 0) == iota(shape, 1) >> 4
    lane_slot = iota(shape, 1) >> 4
    halves = []
    for half in range(2):
        tiles = []
        for x in range(2):
            acc = jnp.zeros(shape, jnp.float32)
            for slot in range(8):
                row = rows(x, slot >> 2, slot & 3)[:, half * LANES : (half + 1) * LANES]
                value = jnp.where(diagonal_mask, jnp.broadcast_to(row, shape), 0.0)
                acc = jnp.where(lane_slot == slot, spread_lanes(value), acc)
            tiles.append(acc)
        halves.append(jnp.concatenate(tiles, axis=1))
    return jnp.concatenate(halves, axis=0)


def from_tiles(value, out):
    shape = (8, LANES)
    diagonal_mask = iota(shape, 0) == iota(shape, 1) >> 4
    lane_slot = iota(shape, 1) >> 4
    for half in range(2):
        for x in range(2):
            tile = value[half * 8 : half * 8 + 8, x * LANES : (x + 1) * LANES]
            for slot in range(8):
                own = spread_lanes(jnp.where(lane_slot == slot, tile, 0.0))
                row = jnp.sum(jnp.where(diagonal_mask, own, 0.0), axis=0, keepdims=True)
                z = slot & 3
                out[x, slot >> 2, z : z + 1, half * LANES : (half + 1) * LANES] = row


def pack_bricks(field):
    return jnp.concatenate([field[0:8], field[8:16]], axis=1)


def unpack_bricks(packed):
    return jnp.concatenate([packed[:, 0 : 2 * LANES], packed[:, 2 * LANES : 4 * LANES]], axis=0)


def pack_kernel(
    rhs_hbm, diagonal_hbm, blocks_hbm, neighbours_hbm,
    matrix, start, to_x, to_y, to_xy,
    rhs, diagonal, blocks, neighbours, sems,
):
    sources = (neighbours_hbm, diagonal_hbm, rhs_hbm, blocks_hbm)
    copies = [
        pltpu.make_async_copy(source, target, sems.at[q])
        for q, (source, target) in enumerate(zip(sources, (neighbours, diagonal, rhs, blocks)))
    ]
    for copy in copies:
        copy.start()
    matrix[:, 384:WIDE] = jnp.zeros((matrix.shape[0], WIDE - 384), jnp.float32)
    eye = iota((SLOT_ROWS, SLOT_ROWS), 0) == iota((SLOT_ROWS, SLOT_ROWS), 1)
    totals = [length * lax.axis_size(axis) for length, axis in zip(LENGTHS, AXES)]
    corner = [length * lax.axis_index(axis) for length, axis in zip(LENGTHS, AXES)]
    bits = [total.bit_length() - 1 for total in totals]
    for copy in copies[:2]:
        copy.wait()
    for x in range(2):
        for y in range(2):
            index = neighbours[x, y]
            along_x = index >> (bits[1] + bits[2])
            along_y = (index >> bits[2]) & (totals[1] - 1)
            along_z = index & (totals[2] - 1)
            z_here = corner[2] + iota(index.shape, 0)
            code = (along_x - (corner[0] + x - 1)) & (totals[0] - 1)
            code = code * 3 + ((along_y - (corner[1] + y - 1)) & (totals[1] - 1))
            code = code * 3 + ((along_z - z_here + 1) & (totals[2] - 1))
            code = code.astype(jnp.float32)
            for z in range(4):
                row = ((x * 2 + y) * 4 + z) * SLOT_ROWS
                matrix[row : row + 1, CODE : CODE + SELF] = code[z : z + 1]
                matrix[row : row + 1, CODE + SELF : CODE + SELF + 1] = jnp.full(
                    (1, 1), 13.0, jnp.float32
                )
                own = SHIFT - jnp.broadcast_to(diagonal[x, y, z : z + 1], eye.shape)
                matrix[row : row + SLOT_ROWS, 432:448] = jnp.where(eye, own, 0.0)
    copies[2].wait()
    value = to_tiles(lambda x, y, z: rhs[x, y, z : z + 1])
    start[...] = value
    bricks = pack_bricks(value)
    copies[3].wait()
    for x in range(2):
        for y in range(2):
            for z in range(4):
                row = ((x * 2 + y) * 4 + z) * SLOT_ROWS
                matrix[row : row + SLOT_ROWS, 0:432] = blocks[x, y, z]
    for out, row in ((to_x, 64), (to_y, 128), (to_xy, 0)):
        out[0:64] = matrix[row : row + 64]
        out[64:72] = bricks


def far_columns(matrix, from_x, from_y, from_xy):
    return (matrix, 192), (from_y, 0), (from_x, 0), (from_xy, 0)


def is_even():
    return lax.rem(lax.axis_index("gz"), 2) == 0


def spread_kernel(matrix, from_y, from_xy, from_x, start, to_first, to_second):
    even = is_even()
    for q, (ref, row) in enumerate(far_columns(matrix, from_x, from_y, from_xy)):
        up, down = ref[row + 16 : row + 64], ref[row : row + 48]
        to_first[q * 48 : q * 48 + 48] = jnp.where(even, up, down)
        to_second[q * 48 : q * 48 + 48] = jnp.where(even, down, up)
    bricks = [pack_bricks(start[...])] + [ref[64:72] for ref in (from_y, from_x, from_xy)]
    for q, brick in enumerate(bricks):
        to_first[192 + q * 8 : 200 + q * 8] = brick
        to_second[192 + q * 8 : 200 + q * 8] = brick


def spread_near_kernel(matrix, to_first, to_second):
    even = is_even()
    for q in range(3):
        up, down = matrix[q * 64 + 32 : q * 64 + 64], matrix[q * 64 : q * 64 + 32]
        to_first[q * 32 : q * 32 + 32] = jnp.where(even, up, down)
        to_second[q * 32 : q * 32 + 32] = jnp.where(even, down, up)


def join_kernel(matrix, from_y, from_xy, from_x, first, second, wide, places):
    even = is_even()
    for q, (ref, row) in enumerate(far_columns(matrix, from_x, from_y, from_xy)):
        one, two = first[q * 48 : q * 48 + 48], second[q * 48 : q * 48 + 48]
        wide[q * 160 : q * 160 + 48] = jnp.where(even, two, one)
        wide[q * 160 + 48 : q * 160 + 112] = ref[row : row + 64]
        wide[q * 160 + 112 : q * 160 + 160] = jnp.where(even, one, two)
    find_places(wide, range(40), tall_far_atom, bricks_place, places)


def join_near_kernel(matrix, first, second, near_first, near_second, tall, places):
    even = is_even()
    for q in range(4):
        if q < 3:
            one, two = (ref[q * 32 : q * 32 + 32] for ref in (near_first, near_second))
            low, high = jnp.where(even, two, one), jnp.where(even, one, two)
        else:
            low = jnp.where(even, second[16:48], first[16:48])
            high = jnp.where(even, first[0:32], second[0:32])
        tall[q * 128 : q * 128 + 32] = low
        tall[q * 128 + 32 : q * 128 + 96] = matrix[q * 64 : q * 64 + 64]
        tall[q * 128 + 96 : q * 128 + 128] = high
    find_places(tall, range(32), tall_near_atom, FIRST_PLACE, places)


def later_places_kernel(wide, matrix, third_places, fourth_places):
    find_places(wide, FAR_ROWS, far_atom, SECOND_PLACE, third_places)
    find_places(matrix, range(ATOMS), near_atom, THIRD_PLACE, fourth_places)


def first_kernel(
    wide, places, start, from_y, from_xy, from_x, first, second, out, field, gathered
):
    even = is_even()
    inner = [start[...]] + [unpack_bricks(ref[64:72]) for ref in (from_y, from_x, from_xy)]
    outer = [
        [unpack_bricks(ref[192 + q * 8 : 200 + q * 8]) for q in range(4)] for ref in (first, second)
    ]
    low = [jnp.where(even, two, one) for one, two in zip(*outer)]
    high = [jnp.where(even, one, two) for one, two in zip(*outer)]
    set_tiles(field, low + inner + high)
    out[...] = couple(wide, range(40), field, places, gathered)


def second_kernel(tall, places, own, from_x, from_y, from_xy, out, field, gathered):
    set_tiles(field, (from_xy, from_x, from_y, own))
    out[...] = couple(tall, range(32), field, places, gathered)


def third_kernel(wide, places, own, from_x, from_y, from_xy, out, field, gathered):
    set_tiles(field, (own, from_y, from_x, from_xy))
    out[...] = couple(wide, FAR_ROWS, field, places, gathered)


def pick_kernel(own, from_x, from_y, from_xy, second, first_own, second_own):
    first_own[...] = pick_own((from_xy, from_x, from_y, own), FIRST_PLACE)
    second_own[...] = pick_own((second,), SECOND_PLACE)


def last_kernel(
    matrix, places, own, from_x, from_y, from_xy, start, first, second, third_out, out,
    field, gathered,
):
    pieces = from_xy, from_x, from_y, own
    set_tiles(field, pieces)
    fourth = couple(matrix, range(ATOMS), field, places, gathered)
    third = pick_own(pieces, THIRD_PLACE)
    third_out[...] = third
    gram_kernel([start[...], first[...], second[...], third, fourth], out)


SMEM = pl.BlockSpec(memory_space=pltpu.SMEM)


def whole_numbers(rows):
    return jax.ShapeDtypeStruct((rows, LANES), jnp.int32)


def call(kernel, shapes, *operands, scratch=(), place=VMEM):
    shapes = [
        shape if isinstance(shape, jax.ShapeDtypeStruct) else jax.ShapeDtypeStruct(shape, jnp.float32)
        for shape in shapes
    ]
    return pl.pallas_call(
        kernel,
        out_shape=shapes,
        in_specs=[
            SMEM if operand.dtype == jnp.int32 and place is VMEM else place for operand in operands
        ],
        out_specs=[VMEM] * len(shapes),
        scratch_shapes=list(scratch),
        compiler_params=pltpu.CompilerParams(vmem_limit_bytes=24 * 1024 * 1024),
    )(*operands)


def scratch_for(tiles, groups):
    return (
        pltpu.VMEM((tiles * 8, SLOT_ROWS, LANES), jnp.float32),
        pltpu.VMEM((groups, WIDE, LANES), jnp.float32),
    )


def fetch(value, first, second):
    sizes = [lax.axis_size(axis) for axis in AXES]
    pairs = []
    for a in range(sizes[0]):
        for b in range(sizes[1]):
            for c in range(sizes[2]):
                source = ((a + first) % sizes[0] * sizes[1] + (b + second) % sizes[1]) * sizes[2] + c
                pairs.append((source, (a * sizes[1] + b) * sizes[2] + c))
    return lax.ppermute(value, AXES, pairs)


def fetch_three(to_x, to_y, to_xy, sign):
    return fetch(to_x, sign, 0), fetch(to_y, 0, sign), fetch(to_xy, sign, sign)


def swap_layers(to_first, to_second):
    count = lax.axis_size("gz")
    even = [(i, i ^ 1) for i in range(count)]
    odd = [(i, (i + 1 if i % 2 else i - 1) % count) for i in range(count)]
    return lax.ppermute(to_first, "gz", even), lax.ppermute(to_second, "gz", odd)


def body(rhs, diagonal, blocks, neighbours):
    width = rhs.shape[-1]
    flat = (SLOT_ROWS, width)
    matrix, start, *out = call(
        pack_kernel,
        [(ATOMS * SLOT_ROWS, WIDE), flat] + [(72, WIDE)] * 3,
        *(pltpu.with_memory_space_constraint(x, pltpu.HBM) for x in (rhs, diagonal, blocks, neighbours)),
        scratch=[
            pltpu.VMEM(rhs.shape, rhs.dtype),
            pltpu.VMEM(diagonal.shape, diagonal.dtype),
            pltpu.VMEM(blocks.shape, blocks.dtype),
            pltpu.VMEM(neighbours.shape, neighbours.dtype),
            pltpu.SemaphoreType.DMA((4,)),
        ],
        place=pl.BlockSpec(memory_space=pltpu.HBM),
    )
    from_x, from_y, from_xy = fetch_three(*out, 1)
    sides = from_y, from_xy, from_x
    layers = swap_layers(*call(spread_kernel, [(224, WIDE)] * 2, matrix, *sides, start))
    near_layers = swap_layers(*call(spread_near_kernel, [(96, WIDE)] * 2, matrix))
    wide, places = call(
        join_kernel, [(40 * SLOT_ROWS, WIDE), whole_numbers(40)], matrix, *sides, *layers
    )
    (first,) = call(
        first_kernel, [(SLOT_ROWS, 5 * LANES)],
        wide, places, start, *sides, *layers,
        scratch=scratch_for(24, 5),
    )
    tall, places = call(
        join_near_kernel, [(32 * SLOT_ROWS, WIDE), whole_numbers(32)],
        matrix, *layers, *near_layers,
    )
    pieces = fetch_three(first, first, first, -1)
    (second,) = call(
        second_kernel, [(SLOT_ROWS, 4 * LANES)], tall, places, first, *pieces,
        scratch=scratch_for(20, 4),
    )
    first_own, second_own = call(pick_kernel, [flat] * 2, first, *pieces, second)
    third_places, fourth_places = call(
        later_places_kernel, [whole_numbers(24), whole_numbers(ATOMS)], wide, matrix
    )
    (third,) = call(
        third_kernel, [(SLOT_ROWS, 3 * LANES)],
        wide, third_places, second, *fetch_three(second, second, second, 1),
        scratch=scratch_for(16, 3),
    )
    third_own, message = call(
        last_kernel,
        [flat, (lax.axis_size("gx") * lax.axis_size("gy"), 4, LANES)],
        matrix, fourth_places, third, *fetch_three(third, third, third, -1),
        start, first_own, second_own,
        scratch=scratch_for(12, 2),
    )
    message = lax.all_to_all(message, ("gx", "gy"), 0, 0, tiled=True)
    (message,) = call(relay_kernel, [(lax.axis_size("gz"), 4, LANES)], message)
    message = lax.all_to_all(message, "gz", 0, 0, tiled=True)
    (result,) = call(finish_kernel, [rhs.shape], message, start, first_own, second_own, third_own)
    return result


def solution(mesh):
    return jax.shard_map(
        body,
        mesh=mesh,
        in_specs=(
            P("gx", "gy", "gz", None),
            P("gx", "gy", "gz", None),
            P("gx", "gy", "gz", None, None),
            P("gx", "gy", "gz", None),
        ),
        out_specs=P("gx", "gy", "gz", None),
        check_vma=False,
    )
```

```python
import jax
import jax.numpy as jnp
from jax import lax
from jax.experimental import pallas as pl
from jax.experimental.pallas import tpu as pltpu
from jax.sharding import PartitionSpec as P

ITERS = 2
DEGREE = 2 * ITERS
SHIFT = 2.0
LANES = 128
PAIRS = [(i, j) for i in range(DEGREE + 1) for j in range(i, DEGREE + 1)]
VMEM = pl.BlockSpec(memory_space=pltpu.VMEM)


def two_sum(a, b):
    total = a + b
    part = total - a
    return total, (a - (total - part)) + (b - part)


def quick_sum(a, b):
    total = a + b
    return total, b - (total - a)


def split(a):
    scaled = 4097.0 * a
    head = scaled - (scaled - a)
    return head, a - head


def two_prod(a, b):
    product = a * b
    a_head, a_tail = split(a)
    b_head, b_tail = split(b)
    rest = ((a_head * b_head - product) + a_head * b_tail + a_tail * b_head) + a_tail * b_tail
    return product, rest


def pair_add(a, b):
    head, tail = two_sum(a[0], b[0])
    return quick_sum(head, tail + (a[1] + b[1]))


def pair_mul(a, b):
    head, tail = two_prod(a[0], b[0])
    return quick_sum(head, tail + (a[0] * b[1] + a[1] * b[0]))


def pair_scale(a, factor):
    head, tail = two_prod(a[0], factor)
    return quick_sum(head, tail + a[1] * factor)


def roll_pair(a, amount, axis):
    return pltpu.roll(a[0], amount, axis), pltpu.roll(a[1], amount, axis)


def iota(shape, axis):
    return lax.broadcasted_iota(jnp.int32, shape, axis)


def gram_kernel(fields, out):
    columns = 16
    diagonal_mask = iota((8, LANES), 0) == iota((8, LANES), 1) // columns
    rows = []
    parts = [split(field) for field in fields]
    for i, j in PAIRS:
        product = fields[i] * fields[j]
        (a_head, a_tail), (b_head, b_tail) = parts[i], parts[j]
        rest = ((a_head * b_head - product) + a_head * b_tail + a_tail * b_head) + a_tail * b_tail
        pieces = [
            (product[s : s + 8, t : t + LANES], rest[s : s + 8, t : t + LANES])
            for s in range(0, product.shape[0], 8)
            for t in range(0, product.shape[1], LANES)
        ]
        while len(pieces) > 1:
            pieces = [pair_add(pieces[q], pieces[q + 1]) for q in range(0, len(pieces), 2)]
        total = pieces[0]
        for amount in (4, 2, 1):
            total = pair_add(total, roll_pair(total, amount, 0))
        rows.append((total[0][0:1], total[1][0:1]))
    rows += [(jnp.zeros((1, LANES), jnp.float32),) * 2] * (16 - len(rows))
    packed = [[], []]
    for start in (0, 8):
        total = tuple(
            jnp.concatenate([row[part] for row in rows[start : start + 8]], axis=0)
            for part in (0, 1)
        )
        for amount in (64, 32, 16):
            total = pair_add(total, roll_pair(total, amount, 1))
        for part in (0, 1):
            packed[part].append(
                jnp.sum(jnp.where(diagonal_mask, total[part], 0.0), axis=0, keepdims=True)
            )
    message = jnp.concatenate(packed[0] + packed[1], axis=0)
    for q in range(out.shape[0]):
        out[q] = message


def sum_messages(ref):
    terms = [(ref[q], None) for q in range(ref.shape[0])]
    while len(terms) > 1:
        merged = []
        for q in range(0, len(terms), 2):
            (a, a_rest), (b, b_rest) = terms[q], terms[q + 1]
            total, rest = two_sum(a, b)
            if a_rest is not None:
                rest = rest + (a_rest + b_rest)
            merged.append((total, rest))
        terms = merged
    total, rest = terms[0]
    return quick_sum(total[0:2], rest[0:2] + (total[2:4] + rest[2:4]))


def relay_kernel(ref, out):
    head, tail = sum_messages(ref)
    message = jnp.concatenate([head, tail], axis=0)
    for q in range(out.shape[0]):
        out[q] = message


def finish_kernel(ref, *refs):
    fields, out = refs[:-1], refs[-1]
    columns = 16
    shape = (8, LANES)
    row = iota(shape, 0)
    diagonal_mask = row == iota(shape, 1) // columns
    packed = sum_messages(ref)
    unpacked = []
    for part in (0, 1):
        halves = []
        for half in (0, 1):
            value = jnp.where(
                diagonal_mask, jnp.broadcast_to(packed[part][half : half + 1], shape), 0.0
            )
            for amount in (64, 32, 16):
                value = value + pltpu.roll(value, amount, 1)
            halves.append(value)
        unpacked.append(halves)

    def entry(part, i, j):
        place = PAIRS.index((min(i, j), max(i, j)))
        half = unpacked[part][place // 8]
        return jnp.broadcast_to(half[place % 8 : place % 8 + 1], shape)

    gram = []
    for j in range(DEGREE + 1):
        column = []
        for part in (0, 1):
            value = jnp.zeros(shape, jnp.float32)
            for i in range(DEGREE + 1):
                value = jnp.where(row == i, entry(part, i, j), value)
            column.append(value)
        gram.append(tuple(column))

    def total_rows(a):
        for amount in (4, 2, 1):
            a = pair_add(a, roll_pair(a, amount, 0))
        return a[0]

    def with_start(a):
        return total_rows(pair_mul(gram[0], a))

    def square(a, degree):
        acc = None
        for j in range(degree + 1):
            factor = tuple(jnp.broadcast_to(part[j : j + 1], shape) for part in a)
            term = pair_mul(gram[j], factor)
            acc = term if acc is None else pair_add(acc, term)
        return total_rows(pair_mul(acc, a))

    def apply(a):
        return pair_add((SHIFT * a[0], SHIFT * a[1]), roll_pair(a, 1, 0))

    def shrink(quasi_norm, ratio, step):
        damping = 1.0 / (1.0 + ratio * ratio)
        return quasi_norm * ratio * jnp.sqrt(damping), damping * step

    zero = jnp.zeros(shape, jnp.float32)
    start = (jnp.where(row == 0, 1.0, 0.0), zero)
    inner = entry(0, 0, 0)
    quasi_norm = jnp.sqrt(inner)
    image = apply(start)
    resid = search = start
    direction = total = (zero, zero)
    ratio = weight = zero
    for iteration in range(ITERS):
        step = inner / with_start(image)
        resid = pair_add(resid, pair_scale(image, -step))
        direction = pair_add(search, pair_scale(direction, ratio * ratio * weight / step))
        ratio = jnp.sqrt(square(resid, 2 * iteration + 1)) / quasi_norm
        quasi_norm, weight = shrink(quasi_norm, ratio, step)
        total = pair_add(total, pair_scale(direction, weight))
        search_odd = pair_add(search, pair_scale(image, -step))
        image_odd = apply(search_odd)
        resid = pair_add(resid, pair_scale(image_odd, -step))
        direction = pair_add(search_odd, pair_scale(direction, ratio * ratio * weight / step))
        ratio = jnp.sqrt(square(resid, 2 * iteration + 2)) / quasi_norm
        quasi_norm, weight = shrink(quasi_norm, ratio, step)
        total = pair_add(total, pair_scale(direction, weight))
        if iteration + 1 < ITERS:
            inner_next = with_start(resid)
            mix = inner_next / inner
            search = pair_add(resid, pair_scale(search_odd, mix))
            image = pair_add(
                apply(search), pair_scale(pair_add(image_odd, pair_scale(image, mix)), mix)
            )
            inner = inner_next
    coefficients = total[0] + total[1]
    height, width = fields[0].shape
    acc = None
    for i, field in enumerate(fields):
        factor = jnp.broadcast_to(coefficients[i : i + 1], (height, LANES))
        factor = jnp.concatenate([factor] * (width // LANES), axis=1)
        term = factor * field[...]
        acc = term if acc is None else acc + term
    from_tiles(acc, out)


SLOT_ROWS = 16
WIDE = 512
SELF = 27
CODE = 448
HIGH = lax.Precision.HIGHEST
LENGTHS = (2, 2, 4)
ATOMS = 16
AXES = ("gx", "gy", "gz")


def bricks_place(x, y, z):
    brick = ((z + 4) >> 2) * 4 + (x >> 1) * 2 + (y >> 1)
    return (brick * 2 + (x & 1)) * 8 + (y & 1) * 4 + (z & 3)


def pieces_place(origin, run, low):
    def place(x, y, z):
        x, y = x - origin, y - origin
        piece = (x >> 1) * 2 + (y >> 1)
        return (piece * 4 + (x & 1) * 2 + (y & 1)) * run + z - low

    return place


def tall_far_atom(index):
    column = (index * 205) >> 11
    return 1 + (column >> 1), 1 + (column & 1), index - 10 * column - 3


def far_atom(index):
    column = (index * 43) >> 8
    return 1 + (column >> 1), 1 + (column & 1), index - 6 * column - 1


def tall_near_atom(index):
    return index >> 4, (index >> 3) & 1, (index & 7) - 2


def near_atom(index):
    return index >> 3, (index >> 2) & 1, index & 3


FAR_ROWS = [column * 10 + z + 3 for column in range(4) for z in range(-1, 5)]
FIRST_PLACE, SECOND_PLACE = pieces_place(-1, 10, -3), pieces_place(0, 8, -2)
THIRD_PLACE = pieces_place(-1, 6, -1)


def find_places(matrix, rows, atom, place, out):
    rows = [row * SLOT_ROWS for row in rows]
    code = jnp.concatenate([matrix[row : row + 1, CODE - 64 : CODE + 64] for row in rows], axis=0)
    code = pltpu.roll(code, 64, 1).astype(jnp.int32)
    index = iota(code.shape, 0)
    x, y, z = atom(index)
    first = (code * 57) >> 9
    rest = code - 9 * first
    second = (rest * 11) >> 5
    where = place(x + first - 1, y + second - 1, z + rest - 3 * second - 1)
    out[...] = (where & ~7) + ((index - where) & 7)


def set_tiles(field, pieces):
    count = pieces[0].shape[1] // LANES
    for q, piece in enumerate(pieces):
        for t in range(count):
            tile = piece[:, t * LANES : (t + 1) * LANES]
            for turn in range(8):
                place = (q * count + t) * 8 + turn
                field[place] = pltpu.roll(tile, turn * SLOT_ROWS, 1) if turn else tile


def couple(matrix, rows, field, places, gathered):
    lane_slot = iota((SLOT_ROWS, LANES), 1) >> 4
    groups = len(rows) // 8

    def gather(k, carry):
        for q in range(groups):
            acc = None
            for slot in range(8):
                tile = field[places[q * 8 + slot, k]]
                acc = tile if acc is None else jnp.where(lane_slot == slot, tile, acc)
            gathered[q, pl.ds(pl.multiple_of(k * SLOT_ROWS, SLOT_ROWS), SLOT_ROWS), :] = acc
        return carry

    lax.fori_loop(0, SELF + 1, gather, 0, unroll=SELF + 1)
    tiles = []
    for q in range(groups):
        gathered[q, CODE:WIDE, :] = jnp.zeros((WIDE - CODE, LANES), jnp.float32)
        group = rows[q * 8 : q * 8 + 8]
        left, start = [], 0
        for r in range(1, 9):
            if r == 8 or group[r] != group[r - 1] + 1:
                left.append(matrix[group[start] * SLOT_ROWS : (group[r - 1] + 1) * SLOT_ROWS, :])
                start = r
        left = left[0] if len(left) == 1 else jnp.concatenate(left, axis=0)
        product = jnp.dot(
            left, gathered[q], precision=HIGH, preferred_element_type=jnp.float32
        )
        acc = product[0:SLOT_ROWS]
        for slot in range(1, 8):
            piece = product[slot * SLOT_ROWS : (slot + 1) * SLOT_ROWS]
            acc = jnp.where(lane_slot == slot, piece, acc)
        tiles.append(-acc)
    return jnp.concatenate(tiles, axis=1)


def pick_own(pieces, place):
    lane_slot = iota((SLOT_ROWS, LANES), 1) >> 4
    tiles = []
    for x in range(2):
        acc = None
        for slot in range(8):
            where = place(x, slot >> 2, slot & 3)
            count = pieces[0].shape[1] // LANES
            tile, turn = where >> 3, (slot - where) & 7
            lanes = pl.ds(tile % count * LANES, LANES)
            tile = pieces[tile // count][:, lanes]
            tile = pltpu.roll(tile, turn * SLOT_ROWS, 1) if turn else tile
            acc = tile if acc is None else jnp.where(lane_slot == slot, tile, acc)
        tiles.append(acc)
    return jnp.concatenate(tiles, axis=1)


def spread_lanes(value):
    for amount in (64, 32, 16):
        value = value + pltpu.roll(value, amount, 1)
    return value


def to_tiles(rows):
    shape = (8, LANES)
    diagonal_mask = iota(shape, 0) == iota(shape, 1) >> 4
    lane_slot = iota(shape, 1) >> 4
    halves = []
    for half in range(2):
        tiles = []
        for x in range(2):
            acc = jnp.zeros(shape, jnp.float32)
            for slot in range(8):
                row = rows(x, slot >> 2, slot & 3)[:, half * LANES : (half + 1) * LANES]
                value = jnp.where(diagonal_mask, jnp.broadcast_to(row, shape), 0.0)
                acc = jnp.where(lane_slot == slot, spread_lanes(value), acc)
            tiles.append(acc)
        halves.append(jnp.concatenate(tiles, axis=1))
    return jnp.concatenate(halves, axis=0)


def from_tiles(value, out):
    shape = (8, LANES)
    diagonal_mask = iota(shape, 0) == iota(shape, 1) >> 4
    lane_slot = iota(shape, 1) >> 4
    for half in range(2):
        for x in range(2):
            tile = value[half * 8 : half * 8 + 8, x * LANES : (x + 1) * LANES]
            for slot in range(8):
                own = spread_lanes(jnp.where(lane_slot == slot, tile, 0.0))
                row = jnp.sum(jnp.where(diagonal_mask, own, 0.0), axis=0, keepdims=True)
                z = slot & 3
                out[x, slot >> 2, z : z + 1, half * LANES : (half + 1) * LANES] = row


def pack_bricks(field):
    return jnp.concatenate([field[0:8], field[8:16]], axis=1)


def unpack_bricks(packed):
    return jnp.concatenate([packed[:, 0 : 2 * LANES], packed[:, 2 * LANES : 4 * LANES]], axis=0)


def is_even():
    return lax.rem(lax.axis_index("gz"), 2) == 0


def spread_own(matrix, brick, to_first, to_second):
    even = is_even()
    for q in range(4):
        rows = 32 if q < 3 else 48
        up = matrix[q * 64 + 64 - rows : q * 64 + 64]
        down = matrix[q * 64 : q * 64 + rows]
        to_first[q * 32 : q * 32 + rows] = jnp.where(even, up, down)
        to_second[q * 32 : q * 32 + rows] = jnp.where(even, down, up)
    to_first[144:152] = brick
    to_second[144:152] = brick


def pack_kernel(
    rhs_hbm, diagonal_hbm, blocks_hbm, neighbours_hbm,
    matrix, start, to_x, to_y, to_xy, to_first, to_second,
    rhs, diagonal, blocks, neighbours, sems,
):
    sources = (neighbours_hbm, diagonal_hbm, rhs_hbm, blocks_hbm)
    copies = [
        pltpu.make_async_copy(source, target, sems.at[q])
        for q, (source, target) in enumerate(zip(sources, (neighbours, diagonal, rhs, blocks)))
    ]
    for copy in copies:
        copy.start()
    matrix[:, 384:WIDE] = jnp.zeros((matrix.shape[0], WIDE - 384), jnp.float32)
    eye = iota((SLOT_ROWS, SLOT_ROWS), 0) == iota((SLOT_ROWS, SLOT_ROWS), 1)
    totals = [length * lax.axis_size(axis) for length, axis in zip(LENGTHS, AXES)]
    corner = [length * lax.axis_index(axis) for length, axis in zip(LENGTHS, AXES)]
    bits = [total.bit_length() - 1 for total in totals]
    for copy in copies[:2]:
        copy.wait()
    for x in range(2):
        for y in range(2):
            index = neighbours[x, y]
            along_x = index >> (bits[1] + bits[2])
            along_y = (index >> bits[2]) & (totals[1] - 1)
            along_z = index & (totals[2] - 1)
            z_here = corner[2] + iota(index.shape, 0)
            code = (along_x - (corner[0] + x - 1)) & (totals[0] - 1)
            code = code * 3 + ((along_y - (corner[1] + y - 1)) & (totals[1] - 1))
            code = code * 3 + ((along_z - z_here + 1) & (totals[2] - 1))
            code = code.astype(jnp.float32)
            for z in range(4):
                row = ((x * 2 + y) * 4 + z) * SLOT_ROWS
                matrix[row : row + 1, CODE : CODE + SELF] = code[z : z + 1]
                matrix[row : row + 1, CODE + SELF : CODE + SELF + 1] = jnp.full(
                    (1, 1), 13.0, jnp.float32
                )
                own = SHIFT - jnp.broadcast_to(diagonal[x, y, z : z + 1], eye.shape)
                matrix[row : row + SLOT_ROWS, 432:448] = jnp.where(eye, own, 0.0)
    copies[2].wait()
    value = to_tiles(lambda x, y, z: rhs[x, y, z : z + 1])
    start[...] = value
    bricks = pack_bricks(value)
    copies[3].wait()
    for x in range(2):
        for y in range(2):
            for z in range(4):
                row = ((x * 2 + y) * 4 + z) * SLOT_ROWS
                matrix[row : row + SLOT_ROWS, 0:432] = blocks[x, y, z]
    for out, row in ((to_x, 64), (to_y, 128), (to_xy, 0)):
        out[0:64] = matrix[row : row + 64]
        out[64:72] = bricks
    spread_own(matrix, bricks, to_first, to_second)


def far_columns(matrix, from_x, from_y, from_xy):
    return (matrix, 192), (from_y, 0), (from_x, 0), (from_xy, 0)


def spread_kernel(from_y, from_xy, from_x, to_first, to_second):
    even = is_even()
    for q, ref in enumerate((from_y, from_x, from_xy)):
        up, down = ref[16:64], ref[0:48]
        to_first[q * 48 : q * 48 + 48] = jnp.where(even, up, down)
        to_second[q * 48 : q * 48 + 48] = jnp.where(even, down, up)
        to_first[144 + q * 8 : 152 + q * 8] = ref[64:72]
        to_second[144 + q * 8 : 152 + q * 8] = ref[64:72]


def join_kernel(
    matrix, from_y, from_xy, from_x, first, second, own_first, own_second, wide, places
):
    even = is_even()
    for q, (ref, row) in enumerate(far_columns(matrix, from_x, from_y, from_xy)):
        if q == 0:
            one, two = own_first[96:144], own_second[96:144]
        else:
            one, two = (side[q * 48 - 48 : q * 48] for side in (first, second))
        wide[q * 160 : q * 160 + 48] = jnp.where(even, two, one)
        wide[q * 160 + 48 : q * 160 + 112] = ref[row : row + 64]
        wide[q * 160 + 112 : q * 160 + 160] = jnp.where(even, one, two)
    find_places(wide, range(40), tall_far_atom, bricks_place, places)


def join_near_kernel(matrix, own_first, own_second, tall, places):
    even = is_even()
    for q in range(4):
        ends = slice(112, 144) if q == 3 else slice(q * 32, q * 32 + 32)
        starts = slice(q * 32, q * 32 + 32)
        low = jnp.where(even, own_second[ends], own_first[ends])
        high = jnp.where(even, own_first[starts], own_second[starts])
        tall[q * 128 : q * 128 + 32] = low
        tall[q * 128 + 32 : q * 128 + 96] = matrix[q * 64 : q * 64 + 64]
        tall[q * 128 + 96 : q * 128 + 128] = high
    find_places(tall, range(32), tall_near_atom, FIRST_PLACE, places)


def later_places_kernel(wide, matrix, third_places, fourth_places):
    find_places(wide, FAR_ROWS, far_atom, SECOND_PLACE, third_places)
    find_places(matrix, range(ATOMS), near_atom, THIRD_PLACE, fourth_places)


def first_kernel(
    wide, places, start, from_y, from_xy, from_x, first, second, own_first, own_second, out,
    field, gathered,
):
    even = is_even()
    inner = [start[...]] + [unpack_bricks(ref[64:72]) for ref in (from_y, from_x, from_xy)]
    outer = [
        [unpack_bricks(own[144:152])]
        + [unpack_bricks(ref[144 + q * 8 : 152 + q * 8]) for q in range(3)]
        for own, ref in ((own_first, first), (own_second, second))
    ]
    low = [jnp.where(even, two, one) for one, two in zip(*outer)]
    high = [jnp.where(even, one, two) for one, two in zip(*outer)]
    set_tiles(field, low + inner + high)
    out[...] = couple(wide, range(40), field, places, gathered)


def second_kernel(tall, places, own, from_xy, from_y, from_x, out, field, gathered):
    set_tiles(field, (from_xy, from_x, from_y, own))
    out[...] = couple(tall, range(32), field, places, gathered)


def third_kernel(wide, places, own, from_xy, from_y, from_x, out, field, gathered):
    set_tiles(field, (own, from_y, from_x, from_xy))
    out[...] = couple(wide, FAR_ROWS, field, places, gathered)


def pick_kernel(own, from_xy, from_y, from_x, second, first_own, second_own):
    first_own[...] = pick_own((from_xy, from_x, from_y, own), FIRST_PLACE)
    second_own[...] = pick_own((second,), SECOND_PLACE)


def last_kernel(
    matrix, places, own, from_xy, from_y, from_x, start, first, second, third_out, out,
    field, gathered,
):
    pieces = from_xy, from_x, from_y, own
    set_tiles(field, pieces)
    fourth = couple(matrix, range(ATOMS), field, places, gathered)
    third = pick_own(pieces, THIRD_PLACE)
    third_out[...] = third
    gram_kernel([start[...], first[...], second[...], third, fourth], out)


SMEM = pl.BlockSpec(memory_space=pltpu.SMEM)


def whole_numbers(rows):
    return jax.ShapeDtypeStruct((rows, LANES), jnp.int32)


def call(kernel, shapes, *operands, scratch=(), place=VMEM):
    shapes = [
        shape if isinstance(shape, jax.ShapeDtypeStruct) else jax.ShapeDtypeStruct(shape, jnp.float32)
        for shape in shapes
    ]
    return pl.pallas_call(
        kernel,
        out_shape=shapes,
        in_specs=[
            SMEM if operand.dtype == jnp.int32 and place is VMEM else place for operand in operands
        ],
        out_specs=[VMEM] * len(shapes),
        scratch_shapes=list(scratch),
        compiler_params=pltpu.CompilerParams(vmem_limit_bytes=24 * 1024 * 1024),
    )(*operands)


def scratch_for(tiles, groups):
    return (
        pltpu.VMEM((tiles * 8, SLOT_ROWS, LANES), jnp.float32),
        pltpu.VMEM((groups, WIDE, LANES), jnp.float32),
    )


def fetch(value, first, second):
    sizes = [lax.axis_size(axis) for axis in AXES]
    pairs = []
    for a in range(sizes[0]):
        for b in range(sizes[1]):
            for c in range(sizes[2]):
                source = ((a + first) % sizes[0] * sizes[1] + (b + second) % sizes[1]) * sizes[2] + c
                pairs.append((source, (a * sizes[1] + b) * sizes[2] + c))
    return lax.ppermute(value, AXES, pairs)


def fetch_three(to_x, to_y, to_xy, sign):
    return fetch(to_xy, sign, sign), fetch(to_y, 0, sign), fetch(to_x, sign, 0)


def swap_layers(to_first, to_second):
    count = lax.axis_size("gz")
    even = [(i, i ^ 1) for i in range(count)]
    odd = [(i, (i + 1 if i % 2 else i - 1) % count) for i in range(count)]
    return lax.ppermute(to_first, "gz", even), lax.ppermute(to_second, "gz", odd)


def body(rhs, diagonal, blocks, neighbours):
    width = rhs.shape[-1]
    flat = (SLOT_ROWS, width)
    matrix, start, *out = call(
        pack_kernel,
        [(ATOMS * SLOT_ROWS, WIDE), flat] + [(72, WIDE)] * 3 + [(152, WIDE)] * 2,
        *(pltpu.with_memory_space_constraint(x, pltpu.HBM) for x in (rhs, diagonal, blocks, neighbours)),
        scratch=[
            pltpu.VMEM(rhs.shape, rhs.dtype),
            pltpu.VMEM(diagonal.shape, diagonal.dtype),
            pltpu.VMEM(blocks.shape, blocks.dtype),
            pltpu.VMEM(neighbours.shape, neighbours.dtype),
            pltpu.SemaphoreType.DMA((4,)),
        ],
        place=pl.BlockSpec(memory_space=pltpu.HBM),
    )
    from_xy, from_y, from_x = fetch_three(*out[:3], 1)
    own_layers = swap_layers(*out[3:])
    first, second, *sides = lax.optimization_barrier((*own_layers, from_y, from_xy, from_x))
    own_layers = first, second
    layers = swap_layers(*call(spread_kernel, [(168, WIDE)] * 2, *sides))
    wide, places = call(
        join_kernel, [(40 * SLOT_ROWS, WIDE), whole_numbers(40)],
        matrix, *sides, *layers, *own_layers,
    )
    (first,) = call(
        first_kernel, [(SLOT_ROWS, 5 * LANES)],
        wide, places, start, *sides, *layers, *own_layers,
        scratch=scratch_for(24, 5),
    )
    tall, places = call(
        join_near_kernel, [(32 * SLOT_ROWS, WIDE), whole_numbers(32)], matrix, *own_layers
    )
    pieces = fetch_three(first, first, first, -1)
    (second,) = call(
        second_kernel, [(SLOT_ROWS, 4 * LANES)], tall, places, first, *pieces,
        scratch=scratch_for(20, 4),
    )
    first_own, second_own = call(pick_kernel, [flat] * 2, first, *pieces, second)
    third_places, fourth_places = call(
        later_places_kernel, [whole_numbers(24), whole_numbers(ATOMS)], wide, matrix
    )
    (third,) = call(
        third_kernel, [(SLOT_ROWS, 3 * LANES)],
        wide, third_places, second, *fetch_three(second, second, second, 1),
        scratch=scratch_for(16, 3),
    )
    third_own, message = call(
        last_kernel,
        [flat, (lax.axis_size("gx") * lax.axis_size("gy"), 4, LANES)],
        matrix, fourth_places, third, *fetch_three(third, third, third, -1),
        start, first_own, second_own,
        scratch=scratch_for(12, 2),
    )
    message = lax.all_to_all(message, ("gx", "gy"), 0, 0, tiled=True)
    (message,) = call(relay_kernel, [(lax.axis_size("gz"), 4, LANES)], message)
    message = lax.all_to_all(message, "gz", 0, 0, tiled=True)
    (result,) = call(finish_kernel, [rhs.shape], message, start, first_own, second_own, third_own)
    return result


def solution(mesh):
    return jax.shard_map(
        body,
        mesh=mesh,
        in_specs=(
            P("gx", "gy", "gz", None),
            P("gx", "gy", "gz", None),
            P("gx", "gy", "gz", None, None),
            P("gx", "gy", "gz", None),
        ),
        out_specs=P("gx", "gy", "gz", None),
        check_vma=False,
    )
```

```python
import jax
import jax.numpy as jnp
from jax import lax
from jax.experimental import pallas as pl
from jax.experimental.pallas import tpu as pltpu
from jax.sharding import PartitionSpec as P

ITERS = 2
DEGREE = 2 * ITERS
SHIFT = 2.0
LANES = 128
PAIRS = [(i, j) for i in range(DEGREE + 1) for j in range(i, DEGREE + 1)]
VMEM = pl.BlockSpec(memory_space=pltpu.VMEM)


def two_sum(a, b):
    total = a + b
    part = total - a
    return total, (a - (total - part)) + (b - part)


def quick_sum(a, b):
    total = a + b
    return total, b - (total - a)


def split(a):
    scaled = 4097.0 * a
    head = scaled - (scaled - a)
    return head, a - head


def two_prod(a, b):
    product = a * b
    a_head, a_tail = split(a)
    b_head, b_tail = split(b)
    rest = ((a_head * b_head - product) + a_head * b_tail + a_tail * b_head) + a_tail * b_tail
    return product, rest


def pair_add(a, b):
    head, tail = two_sum(a[0], b[0])
    return quick_sum(head, tail + (a[1] + b[1]))


def pair_mul(a, b):
    head, tail = two_prod(a[0], b[0])
    return quick_sum(head, tail + (a[0] * b[1] + a[1] * b[0]))


def pair_scale(a, factor):
    head, tail = two_prod(a[0], factor)
    return quick_sum(head, tail + a[1] * factor)


def roll_pair(a, amount, axis):
    return pltpu.roll(a[0], amount, axis), pltpu.roll(a[1], amount, axis)


def iota(shape, axis):
    return lax.broadcasted_iota(jnp.int32, shape, axis)


def gram_kernel(fields, out):
    columns = 16
    diagonal_mask = iota((8, LANES), 0) == iota((8, LANES), 1) // columns
    rows = []
    parts = [split(field) for field in fields]
    for i, j in PAIRS:
        product = fields[i] * fields[j]
        (a_head, a_tail), (b_head, b_tail) = parts[i], parts[j]
        rest = ((a_head * b_head - product) + a_head * b_tail + a_tail * b_head) + a_tail * b_tail
        pieces = [
            (product[s : s + 8, t : t + LANES], rest[s : s + 8, t : t + LANES])
            for s in range(0, product.shape[0], 8)
            for t in range(0, product.shape[1], LANES)
        ]
        while len(pieces) > 1:
            pieces = [pair_add(pieces[q], pieces[q + 1]) for q in range(0, len(pieces), 2)]
        total = pieces[0]
        for amount in (4, 2, 1):
            total = pair_add(total, roll_pair(total, amount, 0))
        rows.append((total[0][0:1], total[1][0:1]))
    rows += [(jnp.zeros((1, LANES), jnp.float32),) * 2] * (16 - len(rows))
    packed = [[], []]
    for start in (0, 8):
        total = tuple(
            jnp.concatenate([row[part] for row in rows[start : start + 8]], axis=0)
            for part in (0, 1)
        )
        for amount in (64, 32, 16):
            total = pair_add(total, roll_pair(total, amount, 1))
        for part in (0, 1):
            packed[part].append(
                jnp.sum(jnp.where(diagonal_mask, total[part], 0.0), axis=0, keepdims=True)
            )
    message = jnp.concatenate(packed[0] + packed[1], axis=0)
    for q in range(out.shape[0]):
        out[q] = message


def sum_messages(ref):
    terms = [(ref[q], None) for q in range(ref.shape[0])]
    while len(terms) > 1:
        merged = []
        for q in range(0, len(terms), 2):
            (a, a_rest), (b, b_rest) = terms[q], terms[q + 1]
            total, rest = two_sum(a, b)
            if a_rest is not None:
                rest = rest + (a_rest + b_rest)
            merged.append((total, rest))
        terms = merged
    total, rest = terms[0]
    return quick_sum(total[0:2], rest[0:2] + (total[2:4] + rest[2:4]))


def relay_kernel(ref, out):
    head, tail = sum_messages(ref)
    message = jnp.concatenate([head, tail], axis=0)
    for q in range(out.shape[0]):
        out[q] = message


def finish_kernel(ref, *refs):
    fields, out = refs[:-1], refs[-1]
    columns = 16
    shape = (8, LANES)
    row = iota(shape, 0)
    diagonal_mask = row == iota(shape, 1) // columns
    packed = sum_messages(ref)
    unpacked = []
    for part in (0, 1):
        halves = []
        for half in (0, 1):
            value = jnp.where(
                diagonal_mask, jnp.broadcast_to(packed[part][half : half + 1], shape), 0.0
            )
            for amount in (64, 32, 16):
                value = value + pltpu.roll(value, amount, 1)
            halves.append(value)
        unpacked.append(halves)

    def entry(part, i, j):
        place = PAIRS.index((min(i, j), max(i, j)))
        half = unpacked[part][place // 8]
        return jnp.broadcast_to(half[place % 8 : place % 8 + 1], shape)

    gram = []
    for j in range(DEGREE + 1):
        column = []
        for part in (0, 1):
            value = jnp.zeros(shape, jnp.float32)
            for i in range(DEGREE + 1):
                value = jnp.where(row == i, entry(part, i, j), value)
            column.append(value)
        gram.append(tuple(column))

    def total_rows(a):
        for amount in (4, 2, 1):
            a = pair_add(a, roll_pair(a, amount, 0))
        return a[0]

    def with_start(a):
        return total_rows(pair_mul(gram[0], a))

    def square(a, degree):
        acc = None
        for j in range(degree + 1):
            factor = tuple(jnp.broadcast_to(part[j : j + 1], shape) for part in a)
            term = pair_mul(gram[j], factor)
            acc = term if acc is None else pair_add(acc, term)
        return total_rows(pair_mul(acc, a))

    def apply(a):
        return pair_add((SHIFT * a[0], SHIFT * a[1]), roll_pair(a, 1, 0))

    def shrink(quasi_norm, ratio, step):
        damping = 1.0 / (1.0 + ratio * ratio)
        return quasi_norm * ratio * jnp.sqrt(damping), damping * step

    zero = jnp.zeros(shape, jnp.float32)
    start = (jnp.where(row == 0, 1.0, 0.0), zero)
    inner = entry(0, 0, 0)
    quasi_norm = jnp.sqrt(inner)
    image = apply(start)
    resid = search = start
    direction = total = (zero, zero)
    ratio = weight = zero
    for iteration in range(ITERS):
        step = inner / with_start(image)
        resid = pair_add(resid, pair_scale(image, -step))
        direction = pair_add(search, pair_scale(direction, ratio * ratio * weight / step))
        ratio = jnp.sqrt(square(resid, 2 * iteration + 1)) / quasi_norm
        quasi_norm, weight = shrink(quasi_norm, ratio, step)
        total = pair_add(total, pair_scale(direction, weight))
        search_odd = pair_add(search, pair_scale(image, -step))
        image_odd = apply(search_odd)
        resid = pair_add(resid, pair_scale(image_odd, -step))
        direction = pair_add(search_odd, pair_scale(direction, ratio * ratio * weight / step))
        ratio = jnp.sqrt(square(resid, 2 * iteration + 2)) / quasi_norm
        quasi_norm, weight = shrink(quasi_norm, ratio, step)
        total = pair_add(total, pair_scale(direction, weight))
        if iteration + 1 < ITERS:
            inner_next = with_start(resid)
            mix = inner_next / inner
            search = pair_add(resid, pair_scale(search_odd, mix))
            image = pair_add(
                apply(search), pair_scale(pair_add(image_odd, pair_scale(image, mix)), mix)
            )
            inner = inner_next
    coefficients = total[0] + total[1]
    height, width = fields[0].shape
    acc = None
    for i, field in enumerate(fields):
        factor = jnp.broadcast_to(coefficients[i : i + 1], (height, LANES))
        factor = jnp.concatenate([factor] * (width // LANES), axis=1)
        term = factor * field[...]
        acc = term if acc is None else acc + term
    from_tiles(acc, out)


SLOT_ROWS = 16
WIDE = 512
SELF = 27
CODE = 448
HIGH = lax.Precision.HIGHEST
LENGTHS = (2, 2, 4)
ATOMS = 16
AXES = ("gx", "gy", "gz")


def bricks_place(x, y, z):
    layer = ((z >> 2) != 0).astype(jnp.int32)
    brick = layer * 4 + (x >> 1) * 2 + (y >> 1)
    return (brick * 2 + (x & 1)) * 8 + (y & 1) * 4 + (z & 3)


def pieces_place(origin, run, low):
    def place(x, y, z):
        x, y = x - origin, y - origin
        piece = (x >> 1) * 2 + (y >> 1)
        return (piece * 4 + (x & 1) * 2 + (y & 1)) * run + z - low

    return place


def far_atom(index):
    column = (index * 43) >> 8
    return 1 + (column >> 1), 1 + (column & 1), index - 6 * column - 1


def tall_near_atom(index):
    return index >> 4, (index >> 3) & 1, (index & 7) - 2


def near_atom(index):
    return index >> 3, (index >> 2) & 1, index & 3


def first_spans(even):
    if isinstance(even, bool):
        return (1, -3) if even else (-3, 3)
    return jnp.where(even, 1, -3), jnp.where(even, -3, 3)


def first_place(even):
    wide_low, slim_low = first_spans(even)

    def place(x, y, z):
        x, y = x + 1, y + 1
        piece = (x >> 1) * 2 + (y >> 1)
        column = (x & 1) * 2 + (y & 1)
        layer = z - wide_low
        wide, slim = column * 6 + layer, 24 + column * 4 + z - slim_low
        if isinstance(z, int):
            return piece * 40 + (wide if 0 <= layer < 6 else slim)
        return piece * 40 + jnp.where((layer >= 0) & (layer < 6), wide, slim)

    return place


SECOND_PLACE, THIRD_PLACE = pieces_place(0, 8, -2), pieces_place(-1, 6, -1)


def find_places(matrix, rows, atom, place, out):
    rows = [row * SLOT_ROWS for row in rows]
    code = jnp.concatenate([matrix[row : row + 1, CODE - 64 : CODE + 64] for row in rows], axis=0)
    code = pltpu.roll(code, 64, 1).astype(jnp.int32)
    index = iota(code.shape, 0)
    x, y, z = atom(index)
    first = (code * 57) >> 9
    rest = code - 9 * first
    second = (rest * 11) >> 5
    where = place(x + first - 1, y + second - 1, z + rest - 3 * second - 1)
    out[...] = (where & ~7) + ((index - where) & 7)


def set_tiles(field, pieces):
    count = pieces[0].shape[1] // LANES
    for q, piece in enumerate(pieces):
        for t in range(count):
            tile = piece[:, t * LANES : (t + 1) * LANES]
            for turn in range(8):
                place = (q * count + t) * 8 + turn
                field[place] = pltpu.roll(tile, turn * SLOT_ROWS, 1) if turn else tile


def couple(matrix, rows, field, places, gathered):
    lane_slot = iota((SLOT_ROWS, LANES), 1) >> 4
    groups = len(rows) // 8

    def gather(k, carry):
        for q in range(groups):
            acc = None
            for slot in range(8):
                tile = field[places[q * 8 + slot, k]]
                acc = tile if acc is None else jnp.where(lane_slot == slot, tile, acc)
            gathered[q, pl.ds(pl.multiple_of(k * SLOT_ROWS, SLOT_ROWS), SLOT_ROWS), :] = acc
        return carry

    lax.fori_loop(0, SELF + 1, gather, 0, unroll=SELF + 1)
    tiles = []
    for q in range(groups):
        gathered[q, CODE:WIDE, :] = jnp.zeros((WIDE - CODE, LANES), jnp.float32)
        group = rows[q * 8 : q * 8 + 8]
        left, start = [], 0
        for r in range(1, 9):
            if r == 8 or group[r] != group[r - 1] + 1:
                left.append(matrix[group[start] * SLOT_ROWS : (group[r - 1] + 1) * SLOT_ROWS, :])
                start = r
        left = left[0] if len(left) == 1 else jnp.concatenate(left, axis=0)
        product = jnp.dot(
            left, gathered[q], precision=HIGH, preferred_element_type=jnp.float32
        )
        acc = product[0:SLOT_ROWS]
        for slot in range(1, 8):
            piece = product[slot * SLOT_ROWS : (slot + 1) * SLOT_ROWS]
            acc = jnp.where(lane_slot == slot, piece, acc)
        tiles.append(-acc)
    return jnp.concatenate(tiles, axis=1)


def pick_own(pieces, place):
    lane_slot = iota((SLOT_ROWS, LANES), 1) >> 4
    tiles = []
    for x in range(2):
        acc = None
        for slot in range(8):
            where = place(x, slot >> 2, slot & 3)
            count = pieces[0].shape[1] // LANES
            tile, turn = where >> 3, (slot - where) & 7
            lanes = pl.ds(tile % count * LANES, LANES)
            tile = pieces[tile // count][:, lanes]
            tile = pltpu.roll(tile, turn * SLOT_ROWS, 1) if turn else tile
            acc = tile if acc is None else jnp.where(lane_slot == slot, tile, acc)
        tiles.append(acc)
    return jnp.concatenate(tiles, axis=1)


def spread_lanes(value):
    for amount in (64, 32, 16):
        value = value + pltpu.roll(value, amount, 1)
    return value


def to_tiles(rows):
    shape = (8, LANES)
    diagonal_mask = iota(shape, 0) == iota(shape, 1) >> 4
    lane_slot = iota(shape, 1) >> 4
    halves = []
    for half in range(2):
        tiles = []
        for x in range(2):
            acc = jnp.zeros(shape, jnp.float32)
            for slot in range(8):
                row = rows(x, slot >> 2, slot & 3)[:, half * LANES : (half + 1) * LANES]
                value = jnp.where(diagonal_mask, jnp.broadcast_to(row, shape), 0.0)
                acc = jnp.where(lane_slot == slot, spread_lanes(value), acc)
            tiles.append(acc)
        halves.append(jnp.concatenate(tiles, axis=1))
    return jnp.concatenate(halves, axis=0)


def from_tiles(value, out):
    shape = (8, LANES)
    diagonal_mask = iota(shape, 0) == iota(shape, 1) >> 4
    lane_slot = iota(shape, 1) >> 4
    for half in range(2):
        for x in range(2):
            tile = value[half * 8 : half * 8 + 8, x * LANES : (x + 1) * LANES]
            for slot in range(8):
                own = spread_lanes(jnp.where(lane_slot == slot, tile, 0.0))
                row = jnp.sum(jnp.where(diagonal_mask, own, 0.0), axis=0, keepdims=True)
                z = slot & 3
                out[x, slot >> 2, z : z + 1, half * LANES : (half + 1) * LANES] = row


def pack_bricks(field):
    return jnp.concatenate([field[0:8], field[8:16]], axis=1)


def unpack_bricks(packed):
    return jnp.concatenate([packed[:, 0 : 2 * LANES], packed[:, 2 * LANES : 4 * LANES]], axis=0)


def pack_kernel(
    rhs_hbm, diagonal_hbm, blocks_hbm, neighbours_hbm,
    matrix, start, to_x, to_y, to_xy,
    rhs, diagonal, blocks, neighbours, sems,
):
    sources = (neighbours_hbm, diagonal_hbm, rhs_hbm, blocks_hbm)
    copies = [
        pltpu.make_async_copy(source, target, sems.at[q])
        for q, (source, target) in enumerate(zip(sources, (neighbours, diagonal, rhs, blocks)))
    ]
    for copy in copies:
        copy.start()
    matrix[:, 384:WIDE] = jnp.zeros((matrix.shape[0], WIDE - 384), jnp.float32)
    eye = iota((SLOT_ROWS, SLOT_ROWS), 0) == iota((SLOT_ROWS, SLOT_ROWS), 1)
    totals = [length * lax.axis_size(axis) for length, axis in zip(LENGTHS, AXES)]
    corner = [length * lax.axis_index(axis) for length, axis in zip(LENGTHS, AXES)]
    bits = [total.bit_length() - 1 for total in totals]
    for copy in copies[:2]:
        copy.wait()
    for x in range(2):
        for y in range(2):
            index = neighbours[x, y]
            along_x = index >> (bits[1] + bits[2])
            along_y = (index >> bits[2]) & (totals[1] - 1)
            along_z = index & (totals[2] - 1)
            z_here = corner[2] + iota(index.shape, 0)
            code = (along_x - (corner[0] + x - 1)) & (totals[0] - 1)
            code = code * 3 + ((along_y - (corner[1] + y - 1)) & (totals[1] - 1))
            code = code * 3 + ((along_z - z_here + 1) & (totals[2] - 1))
            code = code.astype(jnp.float32)
            for z in range(4):
                row = ((x * 2 + y) * 4 + z) * SLOT_ROWS
                matrix[row : row + 1, CODE : CODE + SELF] = code[z : z + 1]
                matrix[row : row + 1, CODE + SELF : CODE + SELF + 1] = jnp.full(
                    (1, 1), 13.0, jnp.float32
                )
                own = SHIFT - jnp.broadcast_to(diagonal[x, y, z : z + 1], eye.shape)
                matrix[row : row + SLOT_ROWS, 432:448] = jnp.where(eye, own, 0.0)
    copies[2].wait()
    value = to_tiles(lambda x, y, z: rhs[x, y, z : z + 1])
    start[...] = value
    bricks = pack_bricks(value)
    copies[3].wait()
    for x in range(2):
        for y in range(2):
            for z in range(4):
                row = ((x * 2 + y) * 4 + z) * SLOT_ROWS
                matrix[row : row + SLOT_ROWS, 0:432] = blocks[x, y, z]
    for out, row in ((to_x, 64), (to_y, 128), (to_xy, 0)):
        out[0:64] = matrix[row : row + 64]
        out[64:72] = bricks


def far_columns(matrix, from_x, from_y, from_xy):
    return (matrix, 192), (from_y, 0), (from_x, 0), (from_xy, 0)


def is_even():
    return lax.rem(lax.axis_index("gz"), 2) == 0


def spread_kernel(matrix, from_y, from_xy, from_x, start, to_first, to_second):
    even = is_even()
    for q, (ref, row) in enumerate(far_columns(matrix, from_x, from_y, from_xy)):
        up, down = ref[row + 16 : row + 64], ref[row : row + 48]
        to_first[q * 48 : q * 48 + 48] = jnp.where(even, up, down)
        to_second[q * 48 : q * 48 + 48] = jnp.where(even, down, up)
    bricks = [pack_bricks(start[...])] + [ref[64:72] for ref in (from_y, from_x, from_xy)]
    for q, brick in enumerate(bricks):
        to_first[192 + q * 8 : 200 + q * 8] = brick
        to_second[192 + q * 8 : 200 + q * 8] = brick


def spread_near_kernel(matrix, to_first, to_second):
    even = is_even()
    for q in range(3):
        up, down = matrix[q * 64 + 32 : q * 64 + 64], matrix[q * 64 : q * 64 + 32]
        to_first[q * 32 : q * 32 + 32] = jnp.where(even, up, down)
        to_second[q * 32 : q * 32 + 32] = jnp.where(even, down, up)


def join_wide_kernel(matrix, from_y, from_xy, from_x, first, wide, places):
    even = is_even()
    for q, (ref, row) in enumerate(far_columns(matrix, from_x, from_y, from_xy)):
        other = first[q * 48 : q * 48 + 48]
        wide[q * 96 : q * 96 + 48] = jnp.where(even, ref[row + 16 : row + 64], other)
        wide[q * 96 + 48 : q * 96 + 96] = jnp.where(even, other, ref[row : row + 48])
    low, _ = first_spans(even)

    def atom(index):
        x, y, z = far_atom(index)
        return x, y, z + 1 + low

    find_places(wide, range(24), atom, bricks_place, places)


def join_slim_kernel(matrix, from_y, from_xy, from_x, second, slim, places):
    even = is_even()
    for q, (ref, row) in enumerate(far_columns(matrix, from_x, from_y, from_xy)):
        other = second[q * 48 : q * 48 + 48]
        below = jnp.concatenate([other, ref[row : row + 16]], axis=0)
        above = jnp.concatenate([ref[row + 48 : row + 64], other], axis=0)
        slim[q * 64 : q * 64 + 64] = jnp.where(even, below, above)
    _, low = first_spans(even)

    def atom(index):
        return 1 + (index >> 3), 1 + ((index >> 2) & 1), (index & 3) + low

    find_places(slim, range(16), atom, bricks_place, places)


def join_near_kernel(matrix, first, second, near_first, near_second, tall, places):
    even = is_even()
    for q in range(4):
        if q < 3:
            one, two = (ref[q * 32 : q * 32 + 32] for ref in (near_first, near_second))
            low, high = jnp.where(even, two, one), jnp.where(even, one, two)
        else:
            low = jnp.where(even, second[16:48], first[16:48])
            high = jnp.where(even, first[0:32], second[0:32])
        tall[q * 128 : q * 128 + 32] = low
        tall[q * 128 + 32 : q * 128 + 96] = matrix[q * 64 : q * 64 + 64]
        tall[q * 128 + 96 : q * 128 + 128] = high
    find_places(tall, range(32), tall_near_atom, first_place(even), places)


def later_kernel(wide, slim, matrix, far, third_places, fourth_places):
    even = is_even()
    for q in range(4):
        one, two = wide[q * 96 : q * 96 + 96], slim[q * 64 : q * 64 + 64]
        below = jnp.concatenate([two[32:64], one[0:64]], axis=0)
        above = jnp.concatenate([one[32:96], two[0:32]], axis=0)
        far[q * 96 : q * 96 + 96] = jnp.where(even, below, above)
    find_places(far, range(24), far_atom, SECOND_PLACE, third_places)
    find_places(matrix, range(ATOMS), near_atom, THIRD_PLACE, fourth_places)


WIDE_FLOPS = 1 << 28


def first_tiles(rows, places, start, from_y, from_xy, from_x, side, field, gathered):
    pieces = [start[...]] + [unpack_bricks(ref[64:72]) for ref in (from_y, from_x, from_xy)]
    pieces += [unpack_bricks(side[192 + q * 8 : 200 + q * 8]) for q in range(4)]
    set_tiles(field, pieces)
    return couple(rows, range(rows.shape[0] // SLOT_ROWS), field, places, gathered)


def first_wide_kernel(
    wide, places, start, from_y, from_xy, from_x, first, out, field, gathered
):
    out[...] = first_tiles(wide, places, start, from_y, from_xy, from_x, first, field, gathered)


def first_slim_kernel(
    slim, places, start, from_y, from_xy, from_x, second, before, out, field, gathered
):
    out[:, 0 : 3 * LANES] = before[...]
    out[:, 3 * LANES : 5 * LANES] = first_tiles(
        slim, places, start, from_y, from_xy, from_x, second, field, gathered
    )


def second_kernel(tall, places, own, from_x, from_y, from_xy, out, field, gathered):
    set_tiles(field, (from_xy, from_x, from_y, own))
    out[...] = couple(tall, range(32), field, places, gathered)


def third_kernel(wide, places, own, from_x, from_y, from_xy, out, field, gathered):
    set_tiles(field, (own, from_y, from_x, from_xy))
    out[...] = couple(wide, range(24), field, places, gathered)


def pick_kernel(own, from_x, from_y, from_xy, second, first_own, second_own):
    pieces = from_xy, from_x, from_y, own
    first_own[...] = jnp.where(
        is_even(), pick_own(pieces, first_place(True)), pick_own(pieces, first_place(False))
    )
    second_own[...] = pick_own((second,), SECOND_PLACE)


def last_kernel(
    matrix, places, own, from_x, from_y, from_xy, start, first, second, third_out, out,
    field, gathered,
):
    pieces = from_xy, from_x, from_y, own
    set_tiles(field, pieces)
    fourth = couple(matrix, range(ATOMS), field, places, gathered)
    third = pick_own(pieces, THIRD_PLACE)
    third_out[...] = third
    gram_kernel([start[...], first[...], second[...], third, fourth], out)


SMEM = pl.BlockSpec(memory_space=pltpu.SMEM)


def whole_numbers(rows):
    return jax.ShapeDtypeStruct((rows, LANES), jnp.int32)


def call(kernel, shapes, *operands, scratch=(), place=VMEM, flops=0):
    shapes = [
        shape if isinstance(shape, jax.ShapeDtypeStruct) else jax.ShapeDtypeStruct(shape, jnp.float32)
        for shape in shapes
    ]
    return pl.pallas_call(
        kernel,
        out_shape=shapes,
        in_specs=[
            SMEM if operand.dtype == jnp.int32 and place is VMEM else place for operand in operands
        ],
        out_specs=[VMEM] * len(shapes),
        scratch_shapes=list(scratch),
        cost_estimate=pl.CostEstimate(flops=flops, bytes_accessed=flops // 64, transcendentals=0)
        if flops
        else None,
        compiler_params=pltpu.CompilerParams(vmem_limit_bytes=24 * 1024 * 1024),
    )(*operands)


def scratch_for(tiles, groups):
    return (
        pltpu.VMEM((tiles * 8, SLOT_ROWS, LANES), jnp.float32),
        pltpu.VMEM((groups, WIDE, LANES), jnp.float32),
    )


def fetch(value, first, second):
    sizes = [lax.axis_size(axis) for axis in AXES]
    pairs = []
    for a in range(sizes[0]):
        for b in range(sizes[1]):
            for c in range(sizes[2]):
                source = ((a + first) % sizes[0] * sizes[1] + (b + second) % sizes[1]) * sizes[2] + c
                pairs.append((source, (a * sizes[1] + b) * sizes[2] + c))
    return lax.ppermute(value, AXES, pairs)


def fetch_three(to_x, to_y, to_xy, sign):
    return fetch(to_x, sign, 0), fetch(to_y, 0, sign), fetch(to_xy, sign, sign)


def swap_layers(to_first, to_second):
    count = lax.axis_size("gz")
    even = [(i, i ^ 1) for i in range(count)]
    odd = [(i, (i + 1 if i % 2 else i - 1) % count) for i in range(count)]
    return lax.ppermute(to_first, "gz", even), lax.ppermute(to_second, "gz", odd)


def body(rhs, diagonal, blocks, neighbours):
    width = rhs.shape[-1]
    flat = (SLOT_ROWS, width)
    matrix, start, *out = call(
        pack_kernel,
        [(ATOMS * SLOT_ROWS, WIDE), flat] + [(72, WIDE)] * 3,
        *(pltpu.with_memory_space_constraint(x, pltpu.HBM) for x in (rhs, diagonal, blocks, neighbours)),
        scratch=[
            pltpu.VMEM(rhs.shape, rhs.dtype),
            pltpu.VMEM(diagonal.shape, diagonal.dtype),
            pltpu.VMEM(blocks.shape, blocks.dtype),
            pltpu.VMEM(neighbours.shape, neighbours.dtype),
            pltpu.SemaphoreType.DMA((4,)),
        ],
        place=pl.BlockSpec(memory_space=pltpu.HBM),
    )
    from_x, from_y, from_xy = fetch_three(*out, 1)
    sides = from_y, from_xy, from_x
    layers = swap_layers(*call(spread_kernel, [(224, WIDE)] * 2, matrix, *sides, start))
    near_layers = swap_layers(*call(spread_near_kernel, [(96, WIDE)] * 2, matrix))
    wide, wide_places = call(
        join_wide_kernel, [(24 * SLOT_ROWS, WIDE), whole_numbers(24)], matrix, *sides, layers[0]
    )
    (first,) = call(
        first_wide_kernel, [(SLOT_ROWS, 3 * LANES)],
        wide, wide_places, start, *sides, layers[0],
        scratch=scratch_for(16, 3),
        flops=WIDE_FLOPS,
    )
    first, last_layers = lax.optimization_barrier((first, layers[1]))
    layers = layers[0], last_layers
    slim, slim_places = call(
        join_slim_kernel, [(16 * SLOT_ROWS, WIDE), whole_numbers(16)], matrix, *sides, layers[1]
    )
    (first,) = call(
        first_slim_kernel, [(SLOT_ROWS, 5 * LANES)],
        slim, slim_places, start, *sides, layers[1], first,
        scratch=scratch_for(16, 2),
    )
    tall, places = call(
        join_near_kernel, [(32 * SLOT_ROWS, WIDE), whole_numbers(32)],
        matrix, *layers, *near_layers,
    )
    pieces = fetch_three(first, first, first, -1)
    (second,) = call(
        second_kernel, [(SLOT_ROWS, 4 * LANES)], tall, places, first, *pieces,
        scratch=scratch_for(20, 4),
    )
    first_own, second_own = call(pick_kernel, [flat] * 2, first, *pieces, second)
    far, third_places, fourth_places = call(
        later_kernel,
        [(24 * SLOT_ROWS, WIDE), whole_numbers(24), whole_numbers(ATOMS)],
        wide, slim, matrix,
    )
    (third,) = call(
        third_kernel, [(SLOT_ROWS, 3 * LANES)],
        far, third_places, second, *fetch_three(second, second, second, 1),
        scratch=scratch_for(16, 3),
    )
    third_own, message = call(
        last_kernel,
        [flat, (lax.axis_size("gx") * lax.axis_size("gy"), 4, LANES)],
        matrix, fourth_places, third, *fetch_three(third, third, third, -1),
        start, first_own, second_own,
        scratch=scratch_for(12, 2),
    )
    message = lax.all_to_all(message, ("gx", "gy"), 0, 0, tiled=True)
    (message,) = call(relay_kernel, [(lax.axis_size("gz"), 4, LANES)], message)
    message = lax.all_to_all(message, "gz", 0, 0, tiled=True)
    (result,) = call(finish_kernel, [rhs.shape], message, start, first_own, second_own, third_own)
    return result


def solution(mesh):
    return jax.shard_map(
        body,
        mesh=mesh,
        in_specs=(
            P("gx", "gy", "gz", None),
            P("gx", "gy", "gz", None),
            P("gx", "gy", "gz", None, None),
            P("gx", "gy", "gz", None),
        ),
        out_specs=P("gx", "gy", "gz", None),
        check_vma=False,
    )
```

```python
import jax
import jax.numpy as jnp
from jax import lax
from jax.experimental import pallas as pl
from jax.experimental.pallas import tpu as pltpu
from jax.sharding import PartitionSpec as P

ITERS = 2
DEGREE = 2 * ITERS
SHIFT = 2.0
LANES = 128
PAIRS = [(i, j) for i in range(DEGREE + 1) for j in range(i, DEGREE + 1)]
VMEM = pl.BlockSpec(memory_space=pltpu.VMEM)


def two_sum(a, b):
    total = a + b
    part = total - a
    return total, (a - (total - part)) + (b - part)


def quick_sum(a, b):
    total = a + b
    return total, b - (total - a)


def split(a):
    scaled = 4097.0 * a
    head = scaled - (scaled - a)
    return head, a - head


def two_prod(a, b):
    product = a * b
    a_head, a_tail = split(a)
    b_head, b_tail = split(b)
    rest = ((a_head * b_head - product) + a_head * b_tail + a_tail * b_head) + a_tail * b_tail
    return product, rest


def pair_add(a, b):
    head, tail = two_sum(a[0], b[0])
    return quick_sum(head, tail + (a[1] + b[1]))


def pair_mul(a, b):
    head, tail = two_prod(a[0], b[0])
    return quick_sum(head, tail + (a[0] * b[1] + a[1] * b[0]))


def pair_scale(a, factor):
    head, tail = two_prod(a[0], factor)
    return quick_sum(head, tail + a[1] * factor)


def roll_pair(a, amount, axis):
    return pltpu.roll(a[0], amount, axis), pltpu.roll(a[1], amount, axis)


def iota(shape, axis):
    return lax.broadcasted_iota(jnp.int32, shape, axis)


def gram_kernel(fields, out):
    columns = 16
    diagonal_mask = iota((8, LANES), 0) == iota((8, LANES), 1) // columns
    rows = []
    parts = [split(field) for field in fields]
    for i, j in PAIRS:
        product = fields[i] * fields[j]
        (a_head, a_tail), (b_head, b_tail) = parts[i], parts[j]
        rest = ((a_head * b_head - product) + a_head * b_tail + a_tail * b_head) + a_tail * b_tail
        pieces = [
            (product[s : s + 8, t : t + LANES], rest[s : s + 8, t : t + LANES])
            for s in range(0, product.shape[0], 8)
            for t in range(0, product.shape[1], LANES)
        ]
        while len(pieces) > 1:
            pieces = [pair_add(pieces[q], pieces[q + 1]) for q in range(0, len(pieces), 2)]
        total = pieces[0]
        for amount in (4, 2, 1):
            total = pair_add(total, roll_pair(total, amount, 0))
        rows.append((total[0][0:1], total[1][0:1]))
    rows += [(jnp.zeros((1, LANES), jnp.float32),) * 2] * (16 - len(rows))
    packed = [[], []]
    for start in (0, 8):
        total = tuple(
            jnp.concatenate([row[part] for row in rows[start : start + 8]], axis=0)
            for part in (0, 1)
        )
        for amount in (64, 32, 16):
            total = pair_add(total, roll_pair(total, amount, 1))
        for part in (0, 1):
            packed[part].append(
                jnp.sum(jnp.where(diagonal_mask, total[part], 0.0), axis=0, keepdims=True)
            )
    message = jnp.concatenate(packed[0] + packed[1], axis=0)
    for q in range(out.shape[0]):
        out[q] = message


def sum_messages(ref):
    terms = [(ref[q], None) for q in range(ref.shape[0])]
    while len(terms) > 1:
        merged = []
        for q in range(0, len(terms), 2):
            (a, a_rest), (b, b_rest) = terms[q], terms[q + 1]
            total, rest = two_sum(a, b)
            if a_rest is not None:
                rest = rest + (a_rest + b_rest)
            merged.append((total, rest))
        terms = merged
    total, rest = terms[0]
    return quick_sum(total[0:2], rest[0:2] + (total[2:4] + rest[2:4]))


def relay_kernel(ref, out):
    head, tail = sum_messages(ref)
    message = jnp.concatenate([head, tail], axis=0)
    for q in range(out.shape[0]):
        out[q] = message


def finish_kernel(ref, *refs):
    fields, out = refs[:-1], refs[-1]
    columns = 16
    shape = (8, LANES)
    row = iota(shape, 0)
    diagonal_mask = row == iota(shape, 1) // columns
    packed = sum_messages(ref)
    unpacked = []
    for part in (0, 1):
        halves = []
        for half in (0, 1):
            value = jnp.where(
                diagonal_mask, jnp.broadcast_to(packed[part][half : half + 1], shape), 0.0
            )
            for amount in (64, 32, 16):
                value = value + pltpu.roll(value, amount, 1)
            halves.append(value)
        unpacked.append(halves)

    def entry(part, i, j):
        place = PAIRS.index((min(i, j), max(i, j)))
        half = unpacked[part][place // 8]
        return jnp.broadcast_to(half[place % 8 : place % 8 + 1], shape)

    gram = []
    for j in range(DEGREE + 1):
        column = []
        for part in (0, 1):
            value = jnp.zeros(shape, jnp.float32)
            for i in range(DEGREE + 1):
                value = jnp.where(row == i, entry(part, i, j), value)
            column.append(value)
        gram.append(tuple(column))

    def total_rows(a):
        for amount in (4, 2, 1):
            a = pair_add(a, roll_pair(a, amount, 0))
        return a[0]

    def with_start(a):
        return total_rows(pair_mul(gram[0], a))

    def square(a, degree):
        acc = None
        for j in range(degree + 1):
            factor = tuple(jnp.broadcast_to(part[j : j + 1], shape) for part in a)
            term = pair_mul(gram[j], factor)
            acc = term if acc is None else pair_add(acc, term)
        return total_rows(pair_mul(acc, a))

    def apply(a):
        return pair_add((SHIFT * a[0], SHIFT * a[1]), roll_pair(a, 1, 0))

    def shrink(quasi_norm, ratio, step):
        damping = 1.0 / (1.0 + ratio * ratio)
        return quasi_norm * ratio * jnp.sqrt(damping), damping * step

    zero = jnp.zeros(shape, jnp.float32)
    start = (jnp.where(row == 0, 1.0, 0.0), zero)
    inner = entry(0, 0, 0)
    quasi_norm = jnp.sqrt(inner)
    image = apply(start)
    resid = search = start
    direction = total = (zero, zero)
    ratio = weight = zero
    for iteration in range(ITERS):
        step = inner / with_start(image)
        resid = pair_add(resid, pair_scale(image, -step))
        direction = pair_add(search, pair_scale(direction, ratio * ratio * weight / step))
        ratio = jnp.sqrt(square(resid, 2 * iteration + 1)) / quasi_norm
        quasi_norm, weight = shrink(quasi_norm, ratio, step)
        total = pair_add(total, pair_scale(direction, weight))
        search_odd = pair_add(search, pair_scale(image, -step))
        image_odd = apply(search_odd)
        resid = pair_add(resid, pair_scale(image_odd, -step))
        direction = pair_add(search_odd, pair_scale(direction, ratio * ratio * weight / step))
        ratio = jnp.sqrt(square(resid, 2 * iteration + 2)) / quasi_norm
        quasi_norm, weight = shrink(quasi_norm, ratio, step)
        total = pair_add(total, pair_scale(direction, weight))
        if iteration + 1 < ITERS:
            inner_next = with_start(resid)
            mix = inner_next / inner
            search = pair_add(resid, pair_scale(search_odd, mix))
            image = pair_add(
                apply(search), pair_scale(pair_add(image_odd, pair_scale(image, mix)), mix)
            )
            inner = inner_next
    coefficients = total[0] + total[1]
    height, width = fields[0].shape
    acc = None
    for i, field in enumerate(fields):
        factor = jnp.broadcast_to(coefficients[i : i + 1], (height, LANES))
        factor = jnp.concatenate([factor] * (width // LANES), axis=1)
        term = factor * field[...]
        acc = term if acc is None else acc + term
    from_tiles(acc, out)


SLOT_ROWS = 16
WIDE = 512
SELF = 27
CODE = 448
HIGH = lax.Precision.HIGHEST
LENGTHS = (2, 2, 4)
ATOMS = 16
AXES = ("gx", "gy", "gz")


def bricks_place(x, y, z):
    layer = ((z >> 2) != 0).astype(jnp.int32)
    brick = layer * 4 + (x >> 1) * 2 + (y >> 1)
    return (brick * 2 + (x & 1)) * 8 + (y & 1) * 4 + (z & 3)


def pieces_place(origin, run, low):
    def place(x, y, z):
        x, y = x - origin, y - origin
        piece = (x >> 1) * 2 + (y >> 1)
        return (piece * 4 + (x & 1) * 2 + (y & 1)) * run + z - low

    return place


def far_atom(index):
    column = (index * 43) >> 8
    return 1 + (column >> 1), 1 + (column & 1), index - 6 * column - 1


def tall_near_atom(index):
    return index >> 4, (index >> 3) & 1, (index & 7) - 2


def near_atom(index):
    return index >> 3, (index >> 2) & 1, index & 3


def first_spans(even):
    if isinstance(even, bool):
        return (1, -3) if even else (-3, 3)
    return jnp.where(even, 1, -3), jnp.where(even, -3, 3)


def first_place(even):
    wide_low, slim_low = first_spans(even)

    def place(x, y, z):
        x, y = x + 1, y + 1
        piece = (x >> 1) * 2 + (y >> 1)
        column = (x & 1) * 2 + (y & 1)
        layer = z - wide_low
        wide, slim = column * 6 + layer, 24 + column * 4 + z - slim_low
        if isinstance(z, int):
            return piece * 40 + (wide if 0 <= layer < 6 else slim)
        return piece * 40 + jnp.where((layer >= 0) & (layer < 6), wide, slim)

    return place


SECOND_PLACE, THIRD_PLACE = pieces_place(0, 8, -2), pieces_place(-1, 6, -1)


def find_places(matrix, rows, atom, place, out):
    rows = [row * SLOT_ROWS for row in rows]
    code = jnp.concatenate([matrix[row : row + 1, CODE - 64 : CODE + 64] for row in rows], axis=0)
    code = pltpu.roll(code, 64, 1).astype(jnp.int32)
    index = iota(code.shape, 0)
    x, y, z = atom(index)
    first = (code * 57) >> 9
    rest = code - 9 * first
    second = (rest * 11) >> 5
    where = place(x + first - 1, y + second - 1, z + rest - 3 * second - 1)
    out[...] = (where & ~7) + ((index - where) & 7)


def set_tiles(field, pieces):
    count = pieces[0].shape[1] // LANES
    for q, piece in enumerate(pieces):
        for t in range(count):
            tile = piece[:, t * LANES : (t + 1) * LANES]
            for turn in range(8):
                place = (q * count + t) * 8 + turn
                field[place] = pltpu.roll(tile, turn * SLOT_ROWS, 1) if turn else tile


def couple(matrix, rows, field, places, gathered):
    lane_slot = iota((SLOT_ROWS, LANES), 1) >> 4
    groups = len(rows) // 8

    def gather(k, carry):
        for q in range(groups):
            acc = None
            for slot in range(8):
                tile = field[places[q * 8 + slot, k]]
                acc = tile if acc is None else jnp.where(lane_slot == slot, tile, acc)
            gathered[q, pl.ds(pl.multiple_of(k * SLOT_ROWS, SLOT_ROWS), SLOT_ROWS), :] = acc
        return carry

    lax.fori_loop(0, SELF + 1, gather, 0, unroll=SELF + 1)
    tiles = []
    for q in range(groups):
        gathered[q, CODE:WIDE, :] = jnp.zeros((WIDE - CODE, LANES), jnp.float32)
        group = rows[q * 8 : q * 8 + 8]
        left, start = [], 0
        for r in range(1, 9):
            if r == 8 or group[r] != group[r - 1] + 1:
                left.append(matrix[group[start] * SLOT_ROWS : (group[r - 1] + 1) * SLOT_ROWS, :])
                start = r
        left = left[0] if len(left) == 1 else jnp.concatenate(left, axis=0)
        product = jnp.dot(
            left, gathered[q], precision=HIGH, preferred_element_type=jnp.float32
        )
        acc = product[0:SLOT_ROWS]
        for slot in range(1, 8):
            piece = product[slot * SLOT_ROWS : (slot + 1) * SLOT_ROWS]
            acc = jnp.where(lane_slot == slot, piece, acc)
        tiles.append(-acc)
    return jnp.concatenate(tiles, axis=1)


def pick_own(pieces, place):
    lane_slot = iota((SLOT_ROWS, LANES), 1) >> 4
    tiles = []
    for x in range(2):
        acc = None
        for slot in range(8):
            where = place(x, slot >> 2, slot & 3)
            count = pieces[0].shape[1] // LANES
            tile, turn = where >> 3, (slot - where) & 7
            lanes = pl.ds(tile % count * LANES, LANES)
            tile = pieces[tile // count][:, lanes]
            tile = pltpu.roll(tile, turn * SLOT_ROWS, 1) if turn else tile
            acc = tile if acc is None else jnp.where(lane_slot == slot, tile, acc)
        tiles.append(acc)
    return jnp.concatenate(tiles, axis=1)


def spread_lanes(value):
    for amount in (64, 32, 16):
        value = value + pltpu.roll(value, amount, 1)
    return value


def to_tiles(rows):
    shape = (8, LANES)
    diagonal_mask = iota(shape, 0) == iota(shape, 1) >> 4
    lane_slot = iota(shape, 1) >> 4
    halves = []
    for half in range(2):
        tiles = []
        for x in range(2):
            acc = jnp.zeros(shape, jnp.float32)
            for slot in range(8):
                row = rows(x, slot >> 2, slot & 3)[:, half * LANES : (half + 1) * LANES]
                value = jnp.where(diagonal_mask, jnp.broadcast_to(row, shape), 0.0)
                acc = jnp.where(lane_slot == slot, spread_lanes(value), acc)
            tiles.append(acc)
        halves.append(jnp.concatenate(tiles, axis=1))
    return jnp.concatenate(halves, axis=0)


def from_tiles(value, out):
    shape = (8, LANES)
    diagonal_mask = iota(shape, 0) == iota(shape, 1) >> 4
    lane_slot = iota(shape, 1) >> 4
    for half in range(2):
        for x in range(2):
            tile = value[half * 8 : half * 8 + 8, x * LANES : (x + 1) * LANES]
            for slot in range(8):
                own = spread_lanes(jnp.where(lane_slot == slot, tile, 0.0))
                row = jnp.sum(jnp.where(diagonal_mask, own, 0.0), axis=0, keepdims=True)
                z = slot & 3
                out[x, slot >> 2, z : z + 1, half * LANES : (half + 1) * LANES] = row


def pack_bricks(field):
    return jnp.concatenate([field[0:8], field[8:16]], axis=1)


def unpack_bricks(packed):
    return jnp.concatenate([packed[:, 0 : 2 * LANES], packed[:, 2 * LANES : 4 * LANES]], axis=0)


def pack_kernel(
    rhs_hbm, diagonal_hbm, blocks_hbm, neighbours_hbm,
    matrix, start, to_x, to_y, to_xy,
    rhs, diagonal, blocks, neighbours, sems,
):
    sources = (neighbours_hbm, diagonal_hbm, rhs_hbm, blocks_hbm)
    copies = [
        pltpu.make_async_copy(source, target, sems.at[q])
        for q, (source, target) in enumerate(zip(sources, (neighbours, diagonal, rhs, blocks)))
    ]
    for copy in copies:
        copy.start()
    matrix[:, 384:WIDE] = jnp.zeros((matrix.shape[0], WIDE - 384), jnp.float32)
    eye = iota((SLOT_ROWS, SLOT_ROWS), 0) == iota((SLOT_ROWS, SLOT_ROWS), 1)
    totals = [length * lax.axis_size(axis) for length, axis in zip(LENGTHS, AXES)]
    corner = [length * lax.axis_index(axis) for length, axis in zip(LENGTHS, AXES)]
    bits = [total.bit_length() - 1 for total in totals]
    for copy in copies[:2]:
        copy.wait()
    for x in range(2):
        for y in range(2):
            index = neighbours[x, y]
            along_x = index >> (bits[1] + bits[2])
            along_y = (index >> bits[2]) & (totals[1] - 1)
            along_z = index & (totals[2] - 1)
            z_here = corner[2] + iota(index.shape, 0)
            code = (along_x - (corner[0] + x - 1)) & (totals[0] - 1)
            code = code * 3 + ((along_y - (corner[1] + y - 1)) & (totals[1] - 1))
            code = code * 3 + ((along_z - z_here + 1) & (totals[2] - 1))
            code = code.astype(jnp.float32)
            for z in range(4):
                row = ((x * 2 + y) * 4 + z) * SLOT_ROWS
                matrix[row : row + 1, CODE : CODE + SELF] = code[z : z + 1]
                matrix[row : row + 1, CODE + SELF : CODE + SELF + 1] = jnp.full(
                    (1, 1), 13.0, jnp.float32
                )
                own = SHIFT - jnp.broadcast_to(diagonal[x, y, z : z + 1], eye.shape)
                matrix[row : row + SLOT_ROWS, 432:448] = jnp.where(eye, own, 0.0)
    copies[2].wait()
    value = to_tiles(lambda x, y, z: rhs[x, y, z : z + 1])
    start[...] = value
    bricks = pack_bricks(value)
    copies[3].wait()
    for x in range(2):
        for y in range(2):
            for z in range(4):
                row = ((x * 2 + y) * 4 + z) * SLOT_ROWS
                matrix[row : row + SLOT_ROWS, 0:432] = blocks[x, y, z]
    for out, row in ((to_x, 64), (to_y, 128), (to_xy, 0)):
        out[0:64] = matrix[row : row + 64]
        out[64:72] = bricks


def far_columns(matrix, from_x, from_y, from_xy):
    return (matrix, 192), (from_y, 0), (from_x, 0), (from_xy, 0)


def is_even():
    return lax.rem(lax.axis_index("gz"), 2) == 0


def spread_second_kernel(matrix, from_y, from_xy, from_x, start, out):
    even = is_even()
    for q, (ref, row) in enumerate(far_columns(matrix, from_x, from_y, from_xy)):
        up, down = ref[row + 16 : row + 64], ref[row : row + 48]
        out[q * 48 : q * 48 + 48] = jnp.where(even, down, up)
    bricks = [pack_bricks(start[...])] + [ref[64:72] for ref in (from_y, from_x, from_xy)]
    for q, brick in enumerate(bricks):
        out[192 + q * 8 : 200 + q * 8] = brick


def spread_first_kernel(from_y, from_xy, from_x, out):
    even = is_even()
    for q, ref in enumerate((from_y, from_x, from_xy)):
        out[q * 48 : q * 48 + 48] = jnp.where(even, ref[16:64], ref[0:48])
        out[144 + q * 8 : 152 + q * 8] = ref[64:72]


def spread_own_kernel(matrix, start, to_first, to_second):
    even = is_even()
    for q in range(4):
        rows = 32 if q < 3 else 48
        up = matrix[q * 64 + 64 - rows : q * 64 + 64]
        down = matrix[q * 64 : q * 64 + rows]
        to_first[q * 32 : q * 32 + rows] = jnp.where(even, up, down)
        if q < 3:
            to_second[q * 32 : q * 32 + rows] = jnp.where(even, down, up)
    to_first[144:152] = pack_bricks(start[...])


def join_wide_kernel(matrix, from_y, from_xy, from_x, first, own_first, wide, places):
    even = is_even()
    for q, (ref, row) in enumerate(far_columns(matrix, from_x, from_y, from_xy)):
        other = first[q * 48 - 48 : q * 48] if q else own_first[96:144]
        wide[q * 96 : q * 96 + 48] = jnp.where(even, ref[row + 16 : row + 64], other)
        wide[q * 96 + 48 : q * 96 + 96] = jnp.where(even, other, ref[row : row + 48])
    low, _ = first_spans(even)

    def atom(index):
        x, y, z = far_atom(index)
        return x, y, z + 1 + low

    find_places(wide, range(24), atom, bricks_place, places)


def join_slim_kernel(matrix, from_y, from_xy, from_x, second, slim, places):
    even = is_even()
    for q, (ref, row) in enumerate(far_columns(matrix, from_x, from_y, from_xy)):
        other = second[q * 48 : q * 48 + 48]
        below = jnp.concatenate([other, ref[row : row + 16]], axis=0)
        above = jnp.concatenate([ref[row + 48 : row + 64], other], axis=0)
        slim[q * 64 : q * 64 + 64] = jnp.where(even, below, above)
    _, low = first_spans(even)

    def atom(index):
        return 1 + (index >> 3), 1 + ((index >> 2) & 1), (index & 3) + low

    find_places(slim, range(16), atom, bricks_place, places)


def join_near_kernel(matrix, second, own_first, near_second, tall, places):
    even = is_even()
    for q in range(4):
        if q < 3:
            one, two = (ref[q * 32 : q * 32 + 32] for ref in (own_first, near_second))
            low, high = jnp.where(even, two, one), jnp.where(even, one, two)
        else:
            low = jnp.where(even, second[16:48], own_first[112:144])
            high = jnp.where(even, own_first[96:128], second[0:32])
        tall[q * 128 : q * 128 + 32] = low
        tall[q * 128 + 32 : q * 128 + 96] = matrix[q * 64 : q * 64 + 64]
        tall[q * 128 + 96 : q * 128 + 128] = high
    find_places(tall, range(32), tall_near_atom, first_place(even), places)


def later_kernel(wide, slim, matrix, far, third_places, fourth_places):
    even = is_even()
    for q in range(4):
        one, two = wide[q * 96 : q * 96 + 96], slim[q * 64 : q * 64 + 64]
        below = jnp.concatenate([two[32:64], one[0:64]], axis=0)
        above = jnp.concatenate([one[32:96], two[0:32]], axis=0)
        far[q * 96 : q * 96 + 96] = jnp.where(even, below, above)
    find_places(far, range(24), far_atom, SECOND_PLACE, third_places)
    find_places(matrix, range(ATOMS), near_atom, THIRD_PLACE, fourth_places)


WIDE_FLOPS = 1 << 28


def first_tiles(rows, places, start, from_y, from_xy, from_x, bricks, field, gathered):
    pieces = [start[...]] + [unpack_bricks(ref[64:72]) for ref in (from_y, from_x, from_xy)]
    set_tiles(field, pieces + [unpack_bricks(brick) for brick in bricks])
    return couple(rows, range(rows.shape[0] // SLOT_ROWS), field, places, gathered)


def first_wide_kernel(
    wide, places, start, from_y, from_xy, from_x, first, own_first, out, field, gathered
):
    bricks = [own_first[144:152]] + [first[144 + q * 8 : 152 + q * 8] for q in range(3)]
    out[...] = first_tiles(wide, places, start, from_y, from_xy, from_x, bricks, field, gathered)


def first_slim_kernel(
    slim, places, start, from_y, from_xy, from_x, second, before, out, field, gathered
):
    bricks = [second[192 + q * 8 : 200 + q * 8] for q in range(4)]
    out[:, 0 : 3 * LANES] = before[...]
    out[:, 3 * LANES : 5 * LANES] = first_tiles(
        slim, places, start, from_y, from_xy, from_x, bricks, field, gathered
    )


def second_kernel(tall, places, own, from_x, from_y, from_xy, out, field, gathered):
    set_tiles(field, (from_xy, from_x, from_y, own))
    out[...] = couple(tall, range(32), field, places, gathered)


def third_kernel(wide, places, own, from_x, from_y, from_xy, out, field, gathered):
    set_tiles(field, (own, from_y, from_x, from_xy))
    out[...] = couple(wide, range(24), field, places, gathered)


def pick_kernel(own, from_x, from_y, from_xy, second, first_own, second_own):
    pieces = from_xy, from_x, from_y, own
    first_own[...] = jnp.where(
        is_even(), pick_own(pieces, first_place(True)), pick_own(pieces, first_place(False))
    )
    second_own[...] = pick_own((second,), SECOND_PLACE)


def last_kernel(
    matrix, places, own, from_x, from_y, from_xy, start, first, second, third_out, out,
    field, gathered,
):
    pieces = from_xy, from_x, from_y, own
    set_tiles(field, pieces)
    fourth = couple(matrix, range(ATOMS), field, places, gathered)
    third = pick_own(pieces, THIRD_PLACE)
    third_out[...] = third
    gram_kernel([start[...], first[...], second[...], third, fourth], out)


SMEM = pl.BlockSpec(memory_space=pltpu.SMEM)


def whole_numbers(rows):
    return jax.ShapeDtypeStruct((rows, LANES), jnp.int32)


def call(kernel, shapes, *operands, scratch=(), place=VMEM, flops=0):
    shapes = [
        shape if isinstance(shape, jax.ShapeDtypeStruct) else jax.ShapeDtypeStruct(shape, jnp.float32)
        for shape in shapes
    ]
    return pl.pallas_call(
        kernel,
        out_shape=shapes,
        in_specs=[
            SMEM if operand.dtype == jnp.int32 and place is VMEM else place for operand in operands
        ],
        out_specs=[VMEM] * len(shapes),
        scratch_shapes=list(scratch),
        cost_estimate=pl.CostEstimate(flops=flops, bytes_accessed=flops // 64, transcendentals=0)
        if flops
        else None,
        compiler_params=pltpu.CompilerParams(vmem_limit_bytes=24 * 1024 * 1024),
    )(*operands)


def scratch_for(tiles, groups):
    return (
        pltpu.VMEM((tiles * 8, SLOT_ROWS, LANES), jnp.float32),
        pltpu.VMEM((groups, WIDE, LANES), jnp.float32),
    )


def fetch(value, first, second):
    sizes = [lax.axis_size(axis) for axis in AXES]
    pairs = []
    for a in range(sizes[0]):
        for b in range(sizes[1]):
            for c in range(sizes[2]):
                source = ((a + first) % sizes[0] * sizes[1] + (b + second) % sizes[1]) * sizes[2] + c
                pairs.append((source, (a * sizes[1] + b) * sizes[2] + c))
    return lax.ppermute(value, AXES, pairs)


def fetch_three(to_x, to_y, to_xy, sign):
    return fetch(to_x, sign, 0), fetch(to_y, 0, sign), fetch(to_xy, sign, sign)


def swap_layers(to_first, to_second):
    count = lax.axis_size("gz")
    even = [(i, i ^ 1) for i in range(count)]
    odd = [(i, (i + 1 if i % 2 else i - 1) % count) for i in range(count)]
    return lax.ppermute(to_first, "gz", even), lax.ppermute(to_second, "gz", odd)


def body(rhs, diagonal, blocks, neighbours):
    width = rhs.shape[-1]
    flat = (SLOT_ROWS, width)
    matrix, start, *out = call(
        pack_kernel,
        [(ATOMS * SLOT_ROWS, WIDE), flat] + [(72, WIDE)] * 3,
        *(pltpu.with_memory_space_constraint(x, pltpu.HBM) for x in (rhs, diagonal, blocks, neighbours)),
        scratch=[
            pltpu.VMEM(rhs.shape, rhs.dtype),
            pltpu.VMEM(diagonal.shape, diagonal.dtype),
            pltpu.VMEM(blocks.shape, blocks.dtype),
            pltpu.VMEM(neighbours.shape, neighbours.dtype),
            pltpu.SemaphoreType.DMA((4,)),
        ],
        place=pl.BlockSpec(memory_space=pltpu.HBM),
    )
    from_x, from_y, from_xy = fetch_three(*out, 1)
    sides = from_y, from_xy, from_x
    (to_second,) = call(spread_second_kernel, [(224, WIDE)], matrix, *sides, start)
    (to_first,) = call(spread_first_kernel, [(168, WIDE)], *sides)
    first_layers, second_layers = swap_layers(to_first, to_second)
    own_layers, near_layers = swap_layers(
        *call(spread_own_kernel, [(152, WIDE), (96, WIDE)], matrix, start)
    )
    wide, wide_places = call(
        join_wide_kernel, [(24 * SLOT_ROWS, WIDE), whole_numbers(24)],
        matrix, *sides, first_layers, own_layers,
    )
    (first,) = call(
        first_wide_kernel, [(SLOT_ROWS, 3 * LANES)],
        wide, wide_places, start, *sides, first_layers, own_layers,
        scratch=scratch_for(16, 3),
        flops=WIDE_FLOPS,
    )
    first, second_layers = lax.optimization_barrier((first, second_layers))
    slim, slim_places = call(
        join_slim_kernel, [(16 * SLOT_ROWS, WIDE), whole_numbers(16)], matrix, *sides, second_layers
    )
    (first,) = call(
        first_slim_kernel, [(SLOT_ROWS, 5 * LANES)],
        slim, slim_places, start, *sides, second_layers, first,
        scratch=scratch_for(16, 2),
    )
    tall, places = call(
        join_near_kernel, [(32 * SLOT_ROWS, WIDE), whole_numbers(32)],
        matrix, second_layers, own_layers, near_layers,
    )
    pieces = fetch_three(first, first, first, -1)
    (second,) = call(
        second_kernel, [(SLOT_ROWS, 4 * LANES)], tall, places, first, *pieces,
        scratch=scratch_for(20, 4),
    )
    first_own, second_own = call(pick_kernel, [flat] * 2, first, *pieces, second)
    far, third_places, fourth_places = call(
        later_kernel,
        [(24 * SLOT_ROWS, WIDE), whole_numbers(24), whole_numbers(ATOMS)],
        wide, slim, matrix,
    )
    (third,) = call(
        third_kernel, [(SLOT_ROWS, 3 * LANES)],
        far, third_places, second, *fetch_three(second, second, second, 1),
        scratch=scratch_for(16, 3),
    )
    third_own, message = call(
        last_kernel,
        [flat, (lax.axis_size("gx") * lax.axis_size("gy"), 4, LANES)],
        matrix, fourth_places, third, *fetch_three(third, third, third, -1),
        start, first_own, second_own,
        scratch=scratch_for(12, 2),
    )
    message = lax.all_to_all(message, ("gx", "gy"), 0, 0, tiled=True)
    (message,) = call(relay_kernel, [(lax.axis_size("gz"), 4, LANES)], message)
    message = lax.all_to_all(message, "gz", 0, 0, tiled=True)
    (result,) = call(finish_kernel, [rhs.shape], message, start, first_own, second_own, third_own)
    return result


def solution(mesh):
    return jax.shard_map(
        body,
        mesh=mesh,
        in_specs=(
            P("gx", "gy", "gz", None),
            P("gx", "gy", "gz", None),
            P("gx", "gy", "gz", None, None),
            P("gx", "gy", "gz", None),
        ),
        out_specs=P("gx", "gy", "gz", None),
        check_vma=False,
    )
```

```python
import jax
import jax.numpy as jnp
from jax import lax
from jax.experimental import pallas as pl
from jax.experimental.pallas import tpu as pltpu
from jax.sharding import PartitionSpec as P

ITERS = 2
DEGREE = 2 * ITERS
SHIFT = 2.0
LANES = 128
PAIRS = [(i, j) for i in range(DEGREE + 1) for j in range(i, DEGREE + 1)]
VMEM = pl.BlockSpec(memory_space=pltpu.VMEM)


def two_sum(a, b):
    total = a + b
    part = total - a
    return total, (a - (total - part)) + (b - part)


def quick_sum(a, b):
    total = a + b
    return total, b - (total - a)


def split(a):
    scaled = 4097.0 * a
    head = scaled - (scaled - a)
    return head, a - head


def two_prod(a, b):
    product = a * b
    a_head, a_tail = split(a)
    b_head, b_tail = split(b)
    rest = ((a_head * b_head - product) + a_head * b_tail + a_tail * b_head) + a_tail * b_tail
    return product, rest


def pair_add(a, b):
    head, tail = two_sum(a[0], b[0])
    return quick_sum(head, tail + (a[1] + b[1]))


def pair_mul(a, b):
    head, tail = two_prod(a[0], b[0])
    return quick_sum(head, tail + (a[0] * b[1] + a[1] * b[0]))


def pair_scale(a, factor):
    head, tail = two_prod(a[0], factor)
    return quick_sum(head, tail + a[1] * factor)


def roll_pair(a, amount, axis):
    return pltpu.roll(a[0], amount, axis), pltpu.roll(a[1], amount, axis)


def iota(shape, axis):
    return lax.broadcasted_iota(jnp.int32, shape, axis)


def gram_kernel(fields, out):
    columns = 16
    diagonal_mask = iota((8, LANES), 0) == iota((8, LANES), 1) // columns
    rows = []
    parts = [split(field) for field in fields]
    for i, j in PAIRS:
        product = fields[i] * fields[j]
        (a_head, a_tail), (b_head, b_tail) = parts[i], parts[j]
        rest = ((a_head * b_head - product) + a_head * b_tail + a_tail * b_head) + a_tail * b_tail
        pieces = [
            (product[s : s + 8, t : t + LANES], rest[s : s + 8, t : t + LANES])
            for s in range(0, product.shape[0], 8)
            for t in range(0, product.shape[1], LANES)
        ]
        while len(pieces) > 1:
            pieces = [pair_add(pieces[q], pieces[q + 1]) for q in range(0, len(pieces), 2)]
        total = pieces[0]
        for amount in (4, 2, 1):
            total = pair_add(total, roll_pair(total, amount, 0))
        rows.append((total[0][0:1], total[1][0:1]))
    rows += [(jnp.zeros((1, LANES), jnp.float32),) * 2] * (16 - len(rows))
    packed = [[], []]
    for start in (0, 8):
        total = tuple(
            jnp.concatenate([row[part] for row in rows[start : start + 8]], axis=0)
            for part in (0, 1)
        )
        for amount in (64, 32, 16):
            total = pair_add(total, roll_pair(total, amount, 1))
        for part in (0, 1):
            packed[part].append(
                jnp.sum(jnp.where(diagonal_mask, total[part], 0.0), axis=0, keepdims=True)
            )
    message = jnp.concatenate(packed[0] + packed[1], axis=0)
    for q in range(out.shape[0]):
        out[q] = message


def sum_messages(ref):
    terms = [(ref[q], None) for q in range(ref.shape[0])]
    while len(terms) > 1:
        merged = []
        for q in range(0, len(terms), 2):
            (a, a_rest), (b, b_rest) = terms[q], terms[q + 1]
            total, rest = two_sum(a, b)
            if a_rest is not None:
                rest = rest + (a_rest + b_rest)
            merged.append((total, rest))
        terms = merged
    total, rest = terms[0]
    return quick_sum(total[0:2], rest[0:2] + (total[2:4] + rest[2:4]))


def relay_kernel(ref, out):
    head, tail = sum_messages(ref)
    message = jnp.concatenate([head, tail], axis=0)
    for q in range(out.shape[0]):
        out[q] = message


def finish_kernel(ref, *refs):
    fields, out = refs[:-1], refs[-1]
    columns = 16
    shape = (8, LANES)
    row = iota(shape, 0)
    diagonal_mask = row == iota(shape, 1) // columns
    packed = sum_messages(ref)
    unpacked = []
    for part in (0, 1):
        halves = []
        for half in (0, 1):
            value = jnp.where(
                diagonal_mask, jnp.broadcast_to(packed[part][half : half + 1], shape), 0.0
            )
            for amount in (64, 32, 16):
                value = value + pltpu.roll(value, amount, 1)
            halves.append(value)
        unpacked.append(halves)

    def entry(part, i, j):
        place = PAIRS.index((min(i, j), max(i, j)))
        half = unpacked[part][place // 8]
        return jnp.broadcast_to(half[place % 8 : place % 8 + 1], shape)

    gram = []
    for j in range(DEGREE + 1):
        column = []
        for part in (0, 1):
            value = jnp.zeros(shape, jnp.float32)
            for i in range(DEGREE + 1):
                value = jnp.where(row == i, entry(part, i, j), value)
            column.append(value)
        gram.append(tuple(column))

    def total_rows(a):
        for amount in (4, 2, 1):
            a = pair_add(a, roll_pair(a, amount, 0))
        return a[0]

    def with_start(a):
        return total_rows(pair_mul(gram[0], a))

    def square(a, degree):
        acc = None
        for j in range(degree + 1):
            factor = tuple(jnp.broadcast_to(part[j : j + 1], shape) for part in a)
            term = pair_mul(gram[j], factor)
            acc = term if acc is None else pair_add(acc, term)
        return total_rows(pair_mul(acc, a))

    def apply(a):
        return pair_add((SHIFT * a[0], SHIFT * a[1]), roll_pair(a, 1, 0))

    def shrink(quasi_norm, ratio, step):
        damping = 1.0 / (1.0 + ratio * ratio)
        return quasi_norm * ratio * jnp.sqrt(damping), damping * step

    zero = jnp.zeros(shape, jnp.float32)
    start = (jnp.where(row == 0, 1.0, 0.0), zero)
    inner = entry(0, 0, 0)
    quasi_norm = jnp.sqrt(inner)
    image = apply(start)
    resid = search = start
    direction = total = (zero, zero)
    ratio = weight = zero
    for iteration in range(ITERS):
        step = inner / with_start(image)
        resid = pair_add(resid, pair_scale(image, -step))
        direction = pair_add(search, pair_scale(direction, ratio * ratio * weight / step))
        ratio = jnp.sqrt(square(resid, 2 * iteration + 1)) / quasi_norm
        quasi_norm, weight = shrink(quasi_norm, ratio, step)
        total = pair_add(total, pair_scale(direction, weight))
        search_odd = pair_add(search, pair_scale(image, -step))
        image_odd = apply(search_odd)
        resid = pair_add(resid, pair_scale(image_odd, -step))
        direction = pair_add(search_odd, pair_scale(direction, ratio * ratio * weight / step))
        ratio = jnp.sqrt(square(resid, 2 * iteration + 2)) / quasi_norm
        quasi_norm, weight = shrink(quasi_norm, ratio, step)
        total = pair_add(total, pair_scale(direction, weight))
        if iteration + 1 < ITERS:
            inner_next = with_start(resid)
            mix = inner_next / inner
            search = pair_add(resid, pair_scale(search_odd, mix))
            image = pair_add(
                apply(search), pair_scale(pair_add(image_odd, pair_scale(image, mix)), mix)
            )
            inner = inner_next
    coefficients = total[0] + total[1]
    height, width = fields[0].shape
    acc = None
    for i, field in enumerate(fields):
        factor = jnp.broadcast_to(coefficients[i : i + 1], (height, LANES))
        factor = jnp.concatenate([factor] * (width // LANES), axis=1)
        term = factor * field[...]
        acc = term if acc is None else acc + term
    from_tiles(acc, out)


SLOT_ROWS = 16
WIDE = 512
SELF = 27
CODE = 448
HIGH = lax.Precision.HIGHEST
LENGTHS = (2, 2, 4)
ATOMS = 16
AXES = ("gx", "gy", "gz")


def bricks_place(x, y, z):
    layer = ((z >> 2) != 0).astype(jnp.int32)
    brick = layer * 4 + (x >> 1) * 2 + (y >> 1)
    return (brick * 2 + (x & 1)) * 8 + (y & 1) * 4 + (z & 3)


def pieces_place(origin, run, low):
    def place(x, y, z):
        x, y = x - origin, y - origin
        piece = (x >> 1) * 2 + (y >> 1)
        return (piece * 4 + (x & 1) * 2 + (y & 1)) * run + z - low

    return place


def far_atom(index):
    column = (index * 43) >> 8
    return 1 + (column >> 1), 1 + (column & 1), index - 6 * column - 1


def tall_near_atom(index):
    return index >> 4, (index >> 3) & 1, (index & 7) - 2


def near_atom(index):
    return index >> 3, (index >> 2) & 1, index & 3


def first_spans(even):
    if isinstance(even, bool):
        return (1, -3) if even else (-3, 3)
    return jnp.where(even, 1, -3), jnp.where(even, -3, 3)


def first_place(even):
    wide_low, slim_low = first_spans(even)

    def place(x, y, z):
        x, y = x + 1, y + 1
        piece = (x >> 1) * 2 + (y >> 1)
        column = (x & 1) * 2 + (y & 1)
        layer = z - wide_low
        wide, slim = column * 6 + layer, 24 + column * 4 + z - slim_low
        if isinstance(z, int):
            return piece * 40 + (wide if 0 <= layer < 6 else slim)
        return piece * 40 + jnp.where((layer >= 0) & (layer < 6), wide, slim)

    return place


SECOND_PLACE, THIRD_PLACE = pieces_place(0, 8, -2), pieces_place(-1, 6, -1)


def find_places(matrix, rows, atom, place, out):
    rows = [row * SLOT_ROWS for row in rows]
    code = jnp.concatenate([matrix[row : row + 1, CODE - 64 : CODE + 64] for row in rows], axis=0)
    code = pltpu.roll(code, 64, 1).astype(jnp.int32)
    index = iota(code.shape, 0)
    x, y, z = atom(index)
    first = (code * 57) >> 9
    rest = code - 9 * first
    second = (rest * 11) >> 5
    where = place(x + first - 1, y + second - 1, z + rest - 3 * second - 1)
    out[...] = (where & ~7) + ((index - where) & 7)


def set_tiles(field, pieces):
    count = pieces[0].shape[1] // LANES
    for q, piece in enumerate(pieces):
        for t in range(count):
            tile = piece[:, t * LANES : (t + 1) * LANES]
            for turn in range(8):
                place = (q * count + t) * 8 + turn
                field[place] = pltpu.roll(tile, turn * SLOT_ROWS, 1) if turn else tile


def couple(matrix, rows, field, places, gathered):
    lane_slot = iota((SLOT_ROWS, LANES), 1) >> 4
    groups = len(rows) // 8

    def gather(k, carry):
        for q in range(groups):
            acc = None
            for slot in range(8):
                tile = field[places[q * 8 + slot, k]]
                acc = tile if acc is None else jnp.where(lane_slot == slot, tile, acc)
            gathered[q, pl.ds(pl.multiple_of(k * SLOT_ROWS, SLOT_ROWS), SLOT_ROWS), :] = acc
        return carry

    lax.fori_loop(0, SELF + 1, gather, 0, unroll=SELF + 1)
    tiles = []
    for q in range(groups):
        gathered[q, CODE:WIDE, :] = jnp.zeros((WIDE - CODE, LANES), jnp.float32)
        group = rows[q * 8 : q * 8 + 8]
        left, start = [], 0
        for r in range(1, 9):
            if r == 8 or group[r] != group[r - 1] + 1:
                left.append(matrix[group[start] * SLOT_ROWS : (group[r - 1] + 1) * SLOT_ROWS, :])
                start = r
        left = left[0] if len(left) == 1 else jnp.concatenate(left, axis=0)
        product = jnp.dot(
            left, gathered[q], precision=HIGH, preferred_element_type=jnp.float32
        )
        acc = product[0:SLOT_ROWS]
        for slot in range(1, 8):
            piece = product[slot * SLOT_ROWS : (slot + 1) * SLOT_ROWS]
            acc = jnp.where(lane_slot == slot, piece, acc)
        tiles.append(-acc)
    return jnp.concatenate(tiles, axis=1)


def pick_own(pieces, place):
    lane_slot = iota((SLOT_ROWS, LANES), 1) >> 4
    tiles = []
    for x in range(2):
        acc = None
        for slot in range(8):
            where = place(x, slot >> 2, slot & 3)
            count = pieces[0].shape[1] // LANES
            tile, turn = where >> 3, (slot - where) & 7
            lanes = pl.ds(tile % count * LANES, LANES)
            tile = pieces[tile // count][:, lanes]
            tile = pltpu.roll(tile, turn * SLOT_ROWS, 1) if turn else tile
            acc = tile if acc is None else jnp.where(lane_slot == slot, tile, acc)
        tiles.append(acc)
    return jnp.concatenate(tiles, axis=1)


def spread_lanes(value):
    for amount in (64, 32, 16):
        value = value + pltpu.roll(value, amount, 1)
    return value


def to_tiles(rows):
    shape = (8, LANES)
    diagonal_mask = iota(shape, 0) == iota(shape, 1) >> 4
    lane_slot = iota(shape, 1) >> 4
    halves = []
    for half in range(2):
        tiles = []
        for x in range(2):
            acc = jnp.zeros(shape, jnp.float32)
            for slot in range(8):
                row = rows(x, slot >> 2, slot & 3)[:, half * LANES : (half + 1) * LANES]
                value = jnp.where(diagonal_mask, jnp.broadcast_to(row, shape), 0.0)
                acc = jnp.where(lane_slot == slot, spread_lanes(value), acc)
            tiles.append(acc)
        halves.append(jnp.concatenate(tiles, axis=1))
    return jnp.concatenate(halves, axis=0)


def from_tiles(value, out):
    shape = (8, LANES)
    diagonal_mask = iota(shape, 0) == iota(shape, 1) >> 4
    lane_slot = iota(shape, 1) >> 4
    for half in range(2):
        for x in range(2):
            tile = value[half * 8 : half * 8 + 8, x * LANES : (x + 1) * LANES]
            for slot in range(8):
                own = spread_lanes(jnp.where(lane_slot == slot, tile, 0.0))
                row = jnp.sum(jnp.where(diagonal_mask, own, 0.0), axis=0, keepdims=True)
                z = slot & 3
                out[x, slot >> 2, z : z + 1, half * LANES : (half + 1) * LANES] = row


def pack_bricks(field):
    return jnp.concatenate([field[0:8], field[8:16]], axis=1)


def unpack_bricks(packed):
    return jnp.concatenate([packed[:, 0 : 2 * LANES], packed[:, 2 * LANES : 4 * LANES]], axis=0)


def pack_kernel(
    rhs_hbm, diagonal_hbm, blocks_hbm, neighbours_hbm,
    matrix, start, to_x, to_y, to_xy,
    rhs, diagonal, blocks, neighbours, sems,
):
    sources = (neighbours_hbm, diagonal_hbm, rhs_hbm, blocks_hbm)
    copies = [
        pltpu.make_async_copy(source, target, sems.at[q])
        for q, (source, target) in enumerate(zip(sources, (neighbours, diagonal, rhs, blocks)))
    ]
    for copy in copies:
        copy.start()
    matrix[:, 384:WIDE] = jnp.zeros((matrix.shape[0], WIDE - 384), jnp.float32)
    eye = iota((SLOT_ROWS, SLOT_ROWS), 0) == iota((SLOT_ROWS, SLOT_ROWS), 1)
    totals = [length * lax.axis_size(axis) for length, axis in zip(LENGTHS, AXES)]
    corner = [length * lax.axis_index(axis) for length, axis in zip(LENGTHS, AXES)]
    bits = [total.bit_length() - 1 for total in totals]
    for copy in copies[:2]:
        copy.wait()
    for x in range(2):
        for y in range(2):
            index = neighbours[x, y]
            along_x = index >> (bits[1] + bits[2])
            along_y = (index >> bits[2]) & (totals[1] - 1)
            along_z = index & (totals[2] - 1)
            z_here = corner[2] + iota(index.shape, 0)
            code = (along_x - (corner[0] + x - 1)) & (totals[0] - 1)
            code = code * 3 + ((along_y - (corner[1] + y - 1)) & (totals[1] - 1))
            code = code * 3 + ((along_z - z_here + 1) & (totals[2] - 1))
            code = code.astype(jnp.float32)
            for z in range(4):
                row = ((x * 2 + y) * 4 + z) * SLOT_ROWS
                matrix[row : row + 1, CODE : CODE + SELF] = code[z : z + 1]
                matrix[row : row + 1, CODE + SELF : CODE + SELF + 1] = jnp.full(
                    (1, 1), 13.0, jnp.float32
                )
                own = SHIFT - jnp.broadcast_to(diagonal[x, y, z : z + 1], eye.shape)
                matrix[row : row + SLOT_ROWS, 432:448] = jnp.where(eye, own, 0.0)
    copies[2].wait()
    value = to_tiles(lambda x, y, z: rhs[x, y, z : z + 1])
    start[...] = value
    bricks = pack_bricks(value)
    copies[3].wait()
    for x in range(2):
        for y in range(2):
            for z in range(4):
                row = ((x * 2 + y) * 4 + z) * SLOT_ROWS
                matrix[row : row + SLOT_ROWS, 0:432] = blocks[x, y, z]
    for out, row in ((to_x, 64), (to_y, 128), (to_xy, 0)):
        out[0:64] = matrix[row : row + 64]
        out[64:72] = bricks


def far_columns(matrix, from_x, from_y, from_xy):
    return (matrix, 192), (from_y, 0), (from_x, 0), (from_xy, 0)


def is_even():
    return lax.rem(lax.axis_index("gz"), 2) == 0


def spread_early_kernel(matrix, out):
    out[...] = jnp.where(is_even(), matrix[192:240], matrix[208:256])


def spread_second_kernel(from_y, from_xy, from_x, start, out):
    even = is_even()
    for q, ref in enumerate((from_y, from_x, from_xy)):
        out[q * 48 : q * 48 + 48] = jnp.where(even, ref[0:48], ref[16:64])
    bricks = [pack_bricks(start[...])] + [ref[64:72] for ref in (from_y, from_x, from_xy)]
    for q, brick in enumerate(bricks):
        out[144 + q * 8 : 152 + q * 8] = brick


def spread_first_kernel(from_y, from_xy, from_x, out):
    even = is_even()
    for q, ref in enumerate((from_y, from_x, from_xy)):
        out[q * 48 : q * 48 + 48] = jnp.where(even, ref[16:64], ref[0:48])
        out[144 + q * 8 : 152 + q * 8] = ref[64:72]


def spread_own_kernel(matrix, start, to_first, to_second):
    even = is_even()
    for q in range(4):
        rows = 32 if q < 3 else 48
        up = matrix[q * 64 + 64 - rows : q * 64 + 64]
        down = matrix[q * 64 : q * 64 + rows]
        to_first[q * 32 : q * 32 + rows] = jnp.where(even, up, down)
        if q < 3:
            to_second[q * 32 : q * 32 + rows] = jnp.where(even, down, up)
    to_first[144:152] = pack_bricks(start[...])


def join_wide_kernel(matrix, from_y, from_xy, from_x, first, own_first, wide, places):
    even = is_even()
    for q, (ref, row) in enumerate(far_columns(matrix, from_x, from_y, from_xy)):
        other = first[q * 48 - 48 : q * 48] if q else own_first[96:144]
        wide[q * 96 : q * 96 + 48] = jnp.where(even, ref[row + 16 : row + 64], other)
        wide[q * 96 + 48 : q * 96 + 96] = jnp.where(even, other, ref[row : row + 48])
    low, _ = first_spans(even)

    def atom(index):
        x, y, z = far_atom(index)
        return x, y, z + 1 + low

    find_places(wide, range(24), atom, bricks_place, places)


def join_slim_kernel(matrix, from_y, from_xy, from_x, second, early, slim, places):
    even = is_even()
    for q, (ref, row) in enumerate(far_columns(matrix, from_x, from_y, from_xy)):
        other = second[q * 48 - 48 : q * 48] if q else early[...]
        below = jnp.concatenate([other, ref[row : row + 16]], axis=0)
        above = jnp.concatenate([ref[row + 48 : row + 64], other], axis=0)
        slim[q * 64 : q * 64 + 64] = jnp.where(even, below, above)
    _, low = first_spans(even)

    def atom(index):
        return 1 + (index >> 3), 1 + ((index >> 2) & 1), (index & 3) + low

    find_places(slim, range(16), atom, bricks_place, places)


def join_near_kernel(matrix, early, own_first, near_second, tall, places):
    even = is_even()
    for q in range(4):
        if q < 3:
            one, two = (ref[q * 32 : q * 32 + 32] for ref in (own_first, near_second))
            low, high = jnp.where(even, two, one), jnp.where(even, one, two)
        else:
            low = jnp.where(even, early[16:48], own_first[112:144])
            high = jnp.where(even, own_first[96:128], early[0:32])
        tall[q * 128 : q * 128 + 32] = low
        tall[q * 128 + 32 : q * 128 + 96] = matrix[q * 64 : q * 64 + 64]
        tall[q * 128 + 96 : q * 128 + 128] = high
    find_places(tall, range(32), tall_near_atom, first_place(even), places)


def later_kernel(wide, slim, matrix, far, third_places, fourth_places):
    even = is_even()
    for q in range(4):
        one, two = wide[q * 96 : q * 96 + 96], slim[q * 64 : q * 64 + 64]
        below = jnp.concatenate([two[32:64], one[0:64]], axis=0)
        above = jnp.concatenate([one[32:96], two[0:32]], axis=0)
        far[q * 96 : q * 96 + 96] = jnp.where(even, below, above)
    find_places(far, range(24), far_atom, SECOND_PLACE, third_places)
    find_places(matrix, range(ATOMS), near_atom, THIRD_PLACE, fourth_places)


def first_tiles(rows, places, start, from_y, from_xy, from_x, bricks, field, gathered):
    pieces = [start[...]] + [unpack_bricks(ref[64:72]) for ref in (from_y, from_x, from_xy)]
    set_tiles(field, pieces + [unpack_bricks(brick) for brick in bricks])
    return couple(rows, range(rows.shape[0] // SLOT_ROWS), field, places, gathered)


def first_wide_kernel(
    wide, places, start, from_y, from_xy, from_x, first, own_first, out, field, gathered
):
    bricks = [own_first[144:152]] + [first[144 + q * 8 : 152 + q * 8] for q in range(3)]
    out[...] = first_tiles(wide, places, start, from_y, from_xy, from_x, bricks, field, gathered)


def first_slim_kernel(
    slim, places, start, from_y, from_xy, from_x, second, before, out, field, gathered
):
    bricks = [second[144 + q * 8 : 152 + q * 8] for q in range(4)]
    out[:, 0 : 3 * LANES] = before[...]
    out[:, 3 * LANES : 5 * LANES] = first_tiles(
        slim, places, start, from_y, from_xy, from_x, bricks, field, gathered
    )


def second_kernel(tall, places, own, from_x, from_y, from_xy, out, field, gathered):
    set_tiles(field, (from_xy, from_x, from_y, own))
    out[...] = couple(tall, range(32), field, places, gathered)


def third_kernel(wide, places, own, from_x, from_y, from_xy, out, field, gathered):
    set_tiles(field, (own, from_y, from_x, from_xy))
    out[...] = couple(wide, range(24), field, places, gathered)


def pick_kernel(own, from_x, from_y, from_xy, second, first_own, second_own):
    pieces = from_xy, from_x, from_y, own
    first_own[...] = jnp.where(
        is_even(), pick_own(pieces, first_place(True)), pick_own(pieces, first_place(False))
    )
    second_own[...] = pick_own((second,), SECOND_PLACE)


def last_kernel(
    matrix, places, own, from_x, from_y, from_xy, start, first, second, third_out, out,
    field, gathered,
):
    pieces = from_xy, from_x, from_y, own
    set_tiles(field, pieces)
    fourth = couple(matrix, range(ATOMS), field, places, gathered)
    third = pick_own(pieces, THIRD_PLACE)
    third_out[...] = third
    gram_kernel([start[...], first[...], second[...], third, fourth], out)


SMEM = pl.BlockSpec(memory_space=pltpu.SMEM)


def whole_numbers(rows):
    return jax.ShapeDtypeStruct((rows, LANES), jnp.int32)


def call(kernel, shapes, *operands, scratch=(), place=VMEM):
    shapes = [
        shape if isinstance(shape, jax.ShapeDtypeStruct) else jax.ShapeDtypeStruct(shape, jnp.float32)
        for shape in shapes
    ]
    return pl.pallas_call(
        kernel,
        out_shape=shapes,
        in_specs=[
            SMEM if operand.dtype == jnp.int32 and place is VMEM else place for operand in operands
        ],
        out_specs=[VMEM] * len(shapes),
        scratch_shapes=list(scratch),
        compiler_params=pltpu.CompilerParams(vmem_limit_bytes=24 * 1024 * 1024),
    )(*operands)


def scratch_for(tiles, groups):
    return (
        pltpu.VMEM((tiles * 8, SLOT_ROWS, LANES), jnp.float32),
        pltpu.VMEM((groups, WIDE, LANES), jnp.float32),
    )


def fetch(value, first, second):
    sizes = [lax.axis_size(axis) for axis in AXES]
    pairs = []
    for a in range(sizes[0]):
        for b in range(sizes[1]):
            for c in range(sizes[2]):
                source = ((a + first) % sizes[0] * sizes[1] + (b + second) % sizes[1]) * sizes[2] + c
                pairs.append((source, (a * sizes[1] + b) * sizes[2] + c))
    return lax.ppermute(value, AXES, pairs)


def fetch_three(to_x, to_y, to_xy, sign):
    return fetch(to_x, sign, 0), fetch(to_y, 0, sign), fetch(to_xy, sign, sign)


def swap_layers(to_first, to_second):
    even = [(i, i ^ 1) for i in range(lax.axis_size("gz"))]
    return lax.ppermute(to_first, "gz", even), swap_odd(to_second)


def swap_odd(value):
    count = lax.axis_size("gz")
    return lax.ppermute(
        value, "gz", [(i, (i + 1 if i % 2 else i - 1) % count) for i in range(count)]
    )


def body(rhs, diagonal, blocks, neighbours):
    width = rhs.shape[-1]
    flat = (SLOT_ROWS, width)
    matrix, start, *out = call(
        pack_kernel,
        [(ATOMS * SLOT_ROWS, WIDE), flat] + [(72, WIDE)] * 3,
        *(pltpu.with_memory_space_constraint(x, pltpu.HBM) for x in (rhs, diagonal, blocks, neighbours)),
        scratch=[
            pltpu.VMEM(rhs.shape, rhs.dtype),
            pltpu.VMEM(diagonal.shape, diagonal.dtype),
            pltpu.VMEM(blocks.shape, blocks.dtype),
            pltpu.VMEM(neighbours.shape, neighbours.dtype),
            pltpu.SemaphoreType.DMA((4,)),
        ],
        place=pl.BlockSpec(memory_space=pltpu.HBM),
    )
    from_x, from_y, from_xy = fetch_three(*out, 1)
    early = swap_odd(*call(spread_early_kernel, [(48, WIDE)], matrix))
    *sides, early = lax.optimization_barrier((from_y, from_xy, from_x, early))
    (to_second,) = call(spread_second_kernel, [(176, WIDE)], *sides, start)
    (to_first,) = call(spread_first_kernel, [(168, WIDE)], *sides)
    first_layers, second_layers = swap_layers(to_first, to_second)
    own_layers, near_layers = swap_layers(
        *call(spread_own_kernel, [(152, WIDE), (96, WIDE)], matrix, start)
    )
    wide, wide_places = call(
        join_wide_kernel, [(24 * SLOT_ROWS, WIDE), whole_numbers(24)],
        matrix, *sides, first_layers, own_layers,
    )
    (first,) = call(
        first_wide_kernel, [(SLOT_ROWS, 3 * LANES)],
        wide, wide_places, start, *sides, first_layers, own_layers,
        scratch=scratch_for(16, 3),
    )
    first, second_layers = lax.optimization_barrier((first, second_layers))
    slim, slim_places = call(
        join_slim_kernel, [(16 * SLOT_ROWS, WIDE), whole_numbers(16)], matrix, *sides, second_layers, early
    )
    (first,) = call(
        first_slim_kernel, [(SLOT_ROWS, 5 * LANES)],
        slim, slim_places, start, *sides, second_layers, first,
        scratch=scratch_for(16, 2),
    )
    tall, places = call(
        join_near_kernel, [(32 * SLOT_ROWS, WIDE), whole_numbers(32)],
        matrix, early, own_layers, near_layers,
    )
    pieces = fetch_three(first, first, first, -1)
    (second,) = call(
        second_kernel, [(SLOT_ROWS, 4 * LANES)], tall, places, first, *pieces,
        scratch=scratch_for(20, 4),
    )
    first_own, second_own = call(pick_kernel, [flat] * 2, first, *pieces, second)
    far, third_places, fourth_places = call(
        later_kernel,
        [(24 * SLOT_ROWS, WIDE), whole_numbers(24), whole_numbers(ATOMS)],
        wide, slim, matrix,
    )
    (third,) = call(
        third_kernel, [(SLOT_ROWS, 3 * LANES)],
        far, third_places, second, *fetch_three(second, second, second, 1),
        scratch=scratch_for(16, 3),
    )
    third_own, message = call(
        last_kernel,
        [flat, (lax.axis_size("gx") * lax.axis_size("gy"), 4, LANES)],
        matrix, fourth_places, third, *fetch_three(third, third, third, -1),
        start, first_own, second_own,
        scratch=scratch_for(12, 2),
    )
    message = lax.all_to_all(message, ("gx", "gy"), 0, 0, tiled=True)
    (message,) = call(relay_kernel, [(lax.axis_size("gz"), 4, LANES)], message)
    message = lax.all_to_all(message, "gz", 0, 0, tiled=True)
    (result,) = call(finish_kernel, [rhs.shape], message, start, first_own, second_own, third_own)
    return result


def solution(mesh):
    return jax.shard_map(
        body,
        mesh=mesh,
        in_specs=(
            P("gx", "gy", "gz", None),
            P("gx", "gy", "gz", None),
            P("gx", "gy", "gz", None, None),
            P("gx", "gy", "gz", None),
        ),
        out_specs=P("gx", "gy", "gz", None),
        check_vma=False,
    )
```

```python
import jax
import jax.numpy as jnp
from jax import lax
from jax.experimental import pallas as pl
from jax.experimental.pallas import tpu as pltpu
from jax.sharding import PartitionSpec as P

ITERS = 2
DEGREE = 2 * ITERS
SHIFT = 2.0
RESOLUTION = 1e-14
LANES = 128
PAIRS = [(i, j) for i in range(DEGREE + 1) for j in range(i, DEGREE + 1)]
VMEM = pl.BlockSpec(memory_space=pltpu.VMEM)


def two_sum(a, b):
    total = a + b
    part = total - a
    return total, (a - (total - part)) + (b - part)


def quick_sum(a, b):
    total = a + b
    return total, b - (total - a)


def split(a):
    scaled = 4097.0 * a
    head = scaled - (scaled - a)
    return head, a - head


def two_prod(a, b):
    product = a * b
    a_head, a_tail = split(a)
    b_head, b_tail = split(b)
    rest = ((a_head * b_head - product) + a_head * b_tail + a_tail * b_head) + a_tail * b_tail
    return product, rest


def pair_add(a, b):
    head, tail = two_sum(a[0], b[0])
    return quick_sum(head, tail + (a[1] + b[1]))


def pair_mul(a, b):
    head, tail = two_prod(a[0], b[0])
    return quick_sum(head, tail + (a[0] * b[1] + a[1] * b[0]))


def pair_scale(a, factor):
    head, tail = two_prod(a[0], factor)
    return quick_sum(head, tail + a[1] * factor)


def roll_pair(a, amount, axis):
    return pltpu.roll(a[0], amount, axis), pltpu.roll(a[1], amount, axis)


def iota(shape, axis):
    return lax.broadcasted_iota(jnp.int32, shape, axis)


def gram_kernel(fields, out):
    columns = 16
    diagonal_mask = iota((8, LANES), 0) == iota((8, LANES), 1) // columns
    rows = []
    parts = [split(field) for field in fields]
    for i, j in PAIRS:
        product = fields[i] * fields[j]
        (a_head, a_tail), (b_head, b_tail) = parts[i], parts[j]
        rest = ((a_head * b_head - product) + a_head * b_tail + a_tail * b_head) + a_tail * b_tail
        pieces = [
            (product[s : s + 8, t : t + LANES], rest[s : s + 8, t : t + LANES])
            for s in range(0, product.shape[0], 8)
            for t in range(0, product.shape[1], LANES)
        ]
        while len(pieces) > 1:
            pieces = [pair_add(pieces[q], pieces[q + 1]) for q in range(0, len(pieces), 2)]
        total = pieces[0]
        for amount in (4, 2, 1):
            total = pair_add(total, roll_pair(total, amount, 0))
        rows.append((total[0][0:1], total[1][0:1]))
    rows += [(jnp.zeros((1, LANES), jnp.float32),) * 2] * (16 - len(rows))
    packed = [[], []]
    for start in (0, 8):
        total = tuple(
            jnp.concatenate([row[part] for row in rows[start : start + 8]], axis=0)
            for part in (0, 1)
        )
        for amount in (64, 32, 16):
            total = pair_add(total, roll_pair(total, amount, 1))
        for part in (0, 1):
            packed[part].append(
                jnp.sum(jnp.where(diagonal_mask, total[part], 0.0), axis=0, keepdims=True)
            )
    message = jnp.concatenate(packed[0] + packed[1], axis=0)
    for q in range(out.shape[0]):
        out[q] = message


def sum_messages(ref):
    terms = [(ref[q], None) for q in range(ref.shape[0])]
    while len(terms) > 1:
        merged = []
        for q in range(0, len(terms), 2):
            (a, a_rest), (b, b_rest) = terms[q], terms[q + 1]
            total, rest = two_sum(a, b)
            if a_rest is not None:
                rest = rest + (a_rest + b_rest)
            merged.append((total, rest))
        terms = merged
    total, rest = terms[0]
    return quick_sum(total[0:2], rest[0:2] + (total[2:4] + rest[2:4]))


def relay_kernel(ref, out):
    head, tail = sum_messages(ref)
    message = jnp.concatenate([head, tail], axis=0)
    for q in range(out.shape[0]):
        out[q] = message


def finish_kernel(ref, *refs):
    fields, out = refs[:-1], refs[-1]
    columns = 16
    shape = (8, LANES)
    row = iota(shape, 0)
    diagonal_mask = row == iota(shape, 1) // columns
    packed = sum_messages(ref)
    unpacked = []
    for part in (0, 1):
        halves = []
        for half in (0, 1):
            value = jnp.where(
                diagonal_mask, jnp.broadcast_to(packed[part][half : half + 1], shape), 0.0
            )
            for amount in (64, 32, 16):
                value = value + pltpu.roll(value, amount, 1)
            halves.append(value)
        unpacked.append(halves)

    def entry(part, i, j):
        place = PAIRS.index((min(i, j), max(i, j)))
        half = unpacked[part][place // 8]
        return jnp.broadcast_to(half[place % 8 : place % 8 + 1], shape)

    gram = []
    for j in range(DEGREE + 1):
        column = []
        for part in (0, 1):
            value = jnp.zeros(shape, jnp.float32)
            for i in range(DEGREE + 1):
                value = jnp.where(row == i, entry(part, i, j), value)
            column.append(value)
        gram.append(tuple(column))

    def total_rows(a):
        for amount in (4, 2, 1):
            a = pair_add(a, roll_pair(a, amount, 0))
        return a[0]

    def with_start(a):
        return total_rows(pair_mul(gram[0], a))

    def square(a, degree):
        acc = None
        for j in range(degree + 1):
            factor = tuple(jnp.broadcast_to(part[j : j + 1], shape) for part in a)
            term = pair_mul(gram[j], factor)
            acc = term if acc is None else pair_add(acc, term)
        return total_rows(pair_mul(acc, a))

    def apply(a):
        return pair_add((SHIFT * a[0], SHIFT * a[1]), roll_pair(a, 1, 0))

    def shrink(quasi_norm, ratio, step):
        damping = 1.0 / (1.0 + ratio * ratio)
        return quasi_norm * ratio * jnp.sqrt(damping), damping * step

    zero = jnp.zeros(shape, jnp.float32)
    start = (jnp.where(row == 0, 1.0, 0.0), zero)
    inner = entry(0, 0, 0)
    least = RESOLUTION * inner
    quasi_norm = jnp.sqrt(inner)
    image = apply(start)
    resid = search = start
    direction = total = (zero, zero)
    ratio = weight = zero
    for iteration in range(ITERS):
        step = inner / with_start(image)
        resid = pair_add(resid, pair_scale(image, -step))
        direction = pair_add(search, pair_scale(direction, ratio * ratio * weight / step))
        ratio = jnp.sqrt(jnp.maximum(square(resid, 2 * iteration + 1), least)) / quasi_norm
        quasi_norm, weight = shrink(quasi_norm, ratio, step)
        total = pair_add(total, pair_scale(direction, weight))
        search_odd = pair_add(search, pair_scale(image, -step))
        image_odd = apply(search_odd)
        resid = pair_add(resid, pair_scale(image_odd, -step))
        direction = pair_add(search_odd, pair_scale(direction, ratio * ratio * weight / step))
        ratio = jnp.sqrt(jnp.maximum(square(resid, 2 * iteration + 2), least)) / quasi_norm
        quasi_norm, weight = shrink(quasi_norm, ratio, step)
        total = pair_add(total, pair_scale(direction, weight))
        if iteration + 1 < ITERS:
            inner_next = with_start(resid)
            mix = inner_next / inner
            search = pair_add(resid, pair_scale(search_odd, mix))
            image = pair_add(
                apply(search), pair_scale(pair_add(image_odd, pair_scale(image, mix)), mix)
            )
            inner = inner_next
    coefficients = total[0] + total[1]
    height, width = fields[0].shape
    acc = None
    for i, field in enumerate(fields):
        factor = jnp.broadcast_to(coefficients[i : i + 1], (height, LANES))
        factor = jnp.concatenate([factor] * (width // LANES), axis=1)
        term = factor * field[...]
        acc = term if acc is None else acc + term
    from_tiles(acc, out)


SLOT_ROWS = 16
WIDE = 512
SELF = 27
CODE = 448
HIGH = lax.Precision.HIGHEST
LENGTHS = (2, 2, 4)
ATOMS = 16
AXES = ("gx", "gy", "gz")


def bricks_place(x, y, z):
    layer = ((z >> 2) != 0).astype(jnp.int32)
    brick = layer * 4 + (x >> 1) * 2 + (y >> 1)
    return (brick * 2 + (x & 1)) * 8 + (y & 1) * 4 + (z & 3)


def pieces_place(origin, run, low):
    def place(x, y, z):
        x, y = x - origin, y - origin
        piece = (x >> 1) * 2 + (y >> 1)
        return (piece * 4 + (x & 1) * 2 + (y & 1)) * run + z - low

    return place


def far_atom(index):
    column = (index * 43) >> 8
    return 1 + (column >> 1), 1 + (column & 1), index - 6 * column - 1


def tall_near_atom(index):
    return index >> 4, (index >> 3) & 1, (index & 7) - 2


def near_atom(index):
    return index >> 3, (index >> 2) & 1, index & 3


def first_spans(even):
    if isinstance(even, bool):
        return (1, -3) if even else (-3, 3)
    return jnp.where(even, 1, -3), jnp.where(even, -3, 3)


def first_place(even):
    wide_low, slim_low = first_spans(even)

    def place(x, y, z):
        x, y = x + 1, y + 1
        piece = (x >> 1) * 2 + (y >> 1)
        column = (x & 1) * 2 + (y & 1)
        layer = z - wide_low
        wide, slim = column * 6 + layer, 24 + column * 4 + z - slim_low
        if isinstance(z, int):
            return piece * 40 + (wide if 0 <= layer < 6 else slim)
        return piece * 40 + jnp.where((layer >= 0) & (layer < 6), wide, slim)

    return place


SECOND_PLACE, THIRD_PLACE = pieces_place(0, 8, -2), pieces_place(-1, 6, -1)


def find_places(matrix, rows, atom, place, out):
    rows = [row * SLOT_ROWS for row in rows]
    code = jnp.concatenate([matrix[row : row + 1, CODE - 64 : CODE + 64] for row in rows], axis=0)
    code = pltpu.roll(code, 64, 1).astype(jnp.int32)
    index = iota(code.shape, 0)
    x, y, z = atom(index)
    first = (code * 57) >> 9
    rest = code - 9 * first
    second = (rest * 11) >> 5
    where = place(x + first - 1, y + second - 1, z + rest - 3 * second - 1)
    out[...] = (where & ~7) + ((index - where) & 7)


def set_tiles(field, pieces):
    count = pieces[0].shape[1] // LANES
    for q, piece in enumerate(pieces):
        for t in range(count):
            tile = piece[:, t * LANES : (t + 1) * LANES]
            for turn in range(8):
                place = (q * count + t) * 8 + turn
                field[place] = pltpu.roll(tile, turn * SLOT_ROWS, 1) if turn else tile


def couple(matrix, rows, field, places, gathered):
    lane_slot = iota((SLOT_ROWS, LANES), 1) >> 4
    groups = len(rows) // 8

    def gather(k, carry):
        for q in range(groups):
            acc = None
            for slot in range(8):
                tile = field[places[q * 8 + slot, k]]
                acc = tile if acc is None else jnp.where(lane_slot == slot, tile, acc)
            gathered[q, pl.ds(pl.multiple_of(k * SLOT_ROWS, SLOT_ROWS), SLOT_ROWS), :] = acc
        return carry

    lax.fori_loop(0, SELF + 1, gather, 0, unroll=SELF + 1)
    tiles = []
    for q in range(groups):
        gathered[q, CODE:WIDE, :] = jnp.zeros((WIDE - CODE, LANES), jnp.float32)
        group = rows[q * 8 : q * 8 + 8]
        left, start = [], 0
        for r in range(1, 9):
            if r == 8 or group[r] != group[r - 1] + 1:
                left.append(matrix[group[start] * SLOT_ROWS : (group[r - 1] + 1) * SLOT_ROWS, :])
                start = r
        left = left[0] if len(left) == 1 else jnp.concatenate(left, axis=0)
        product = jnp.dot(
            left, gathered[q], precision=HIGH, preferred_element_type=jnp.float32
        )
        acc = product[0:SLOT_ROWS]
        for slot in range(1, 8):
            piece = product[slot * SLOT_ROWS : (slot + 1) * SLOT_ROWS]
            acc = jnp.where(lane_slot == slot, piece, acc)
        tiles.append(-acc)
    return jnp.concatenate(tiles, axis=1)


def pick_own(pieces, place):
    lane_slot = iota((SLOT_ROWS, LANES), 1) >> 4
    tiles = []
    for x in range(2):
        acc = None
        for slot in range(8):
            where = place(x, slot >> 2, slot & 3)
            count = pieces[0].shape[1] // LANES
            tile, turn = where >> 3, (slot - where) & 7
            lanes = pl.ds(tile % count * LANES, LANES)
            tile = pieces[tile // count][:, lanes]
            tile = pltpu.roll(tile, turn * SLOT_ROWS, 1) if turn else tile
            acc = tile if acc is None else jnp.where(lane_slot == slot, tile, acc)
        tiles.append(acc)
    return jnp.concatenate(tiles, axis=1)


def turn_blocks(value):
    row, group = iota(value.shape, 0), iota(value.shape, 1) >> 4
    for bit in (1, 2, 4):
        lanes = bit * SLOT_ROWS
        later = pltpu.roll(pltpu.roll(value, 8 - bit, 0), lanes, 1)
        earlier = pltpu.roll(pltpu.roll(value, bit, 0), LANES - lanes, 1)
        swapped = jnp.where((group & bit) != 0, later, earlier)
        value = jnp.where((row & bit) == (group & bit), value, swapped)
    return value


def to_tiles(field):
    halves = []
    for half in range(2):
        lanes = slice(half * LANES, (half + 1) * LANES)
        tiles = [
            turn_blocks(jnp.concatenate([field[x, y, :, lanes] for y in range(2)], axis=0))
            for x in range(2)
        ]
        halves.append(jnp.concatenate(tiles, axis=1))
    return jnp.concatenate(halves, axis=0)


def from_tiles(value, out):
    for half in range(2):
        for x in range(2):
            rows = turn_blocks(value[half * 8 : half * 8 + 8, x * LANES : (x + 1) * LANES])
            for y in range(2):
                out[x, y, :, half * LANES : (half + 1) * LANES] = rows[y * 4 : y * 4 + 4]


def pack_bricks(field):
    return jnp.concatenate([field[0:8], field[8:16]], axis=1)


def unpack_bricks(packed):
    return jnp.concatenate([packed[:, 0 : 2 * LANES], packed[:, 2 * LANES : 4 * LANES]], axis=0)


def pack_kernel(
    rhs_hbm, diagonal_hbm, blocks_hbm, neighbours_hbm,
    matrix, start, to_x, to_y, to_xy,
    rhs, diagonal, blocks, neighbours, sems,
):
    sources = (neighbours_hbm, diagonal_hbm, rhs_hbm, blocks_hbm)
    copies = [
        pltpu.make_async_copy(source, target, sems.at[q])
        for q, (source, target) in enumerate(zip(sources, (neighbours, diagonal, rhs, blocks)))
    ]
    for copy in copies:
        copy.start()
    matrix[:, 384:WIDE] = jnp.zeros((matrix.shape[0], WIDE - 384), jnp.float32)
    eye = iota((SLOT_ROWS, SLOT_ROWS), 0) == iota((SLOT_ROWS, SLOT_ROWS), 1)
    totals = [length * lax.axis_size(axis) for length, axis in zip(LENGTHS, AXES)]
    corner = [length * lax.axis_index(axis) for length, axis in zip(LENGTHS, AXES)]
    bits = [total.bit_length() - 1 for total in totals]
    for copy in copies[:2]:
        copy.wait()
    for x in range(2):
        for y in range(2):
            index = neighbours[x, y]
            along_x = index >> (bits[1] + bits[2])
            along_y = (index >> bits[2]) & (totals[1] - 1)
            along_z = index & (totals[2] - 1)
            z_here = corner[2] + iota(index.shape, 0)
            code = (along_x - (corner[0] + x - 1)) & (totals[0] - 1)
            code = code * 3 + ((along_y - (corner[1] + y - 1)) & (totals[1] - 1))
            code = code * 3 + ((along_z - z_here + 1) & (totals[2] - 1))
            code = code.astype(jnp.float32)
            for z in range(4):
                row = ((x * 2 + y) * 4 + z) * SLOT_ROWS
                matrix[row : row + 1, CODE : CODE + SELF] = code[z : z + 1]
                matrix[row : row + 1, CODE + SELF : CODE + SELF + 1] = jnp.full(
                    (1, 1), 13.0, jnp.float32
                )
                own = SHIFT - jnp.broadcast_to(diagonal[x, y, z : z + 1], eye.shape)
                matrix[row : row + SLOT_ROWS, 432:448] = jnp.where(eye, own, 0.0)
    copies[2].wait()
    value = to_tiles(rhs)
    start[...] = value
    bricks = pack_bricks(value)
    copies[3].wait()
    for x in range(2):
        for y in range(2):
            for z in range(4):
                row = ((x * 2 + y) * 4 + z) * SLOT_ROWS
                matrix[row : row + SLOT_ROWS, 0:432] = blocks[x, y, z]
    for out, row in ((to_x, 64), (to_y, 128), (to_xy, 0)):
        out[0:64] = matrix[row : row + 64]
        out[64:72] = bricks


def far_columns(matrix, from_x, from_y, from_xy):
    return (matrix, 192), (from_y, 0), (from_x, 0), (from_xy, 0)


def is_even():
    return lax.rem(lax.axis_index("gz"), 2) == 0


def spread_second_kernel(matrix, from_y, from_xy, from_x, start, out):
    even = is_even()
    for q, (ref, row) in enumerate(far_columns(matrix, from_x, from_y, from_xy)):
        up, down = ref[row + 16 : row + 64], ref[row : row + 48]
        out[q * 48 : q * 48 + 48] = jnp.where(even, down, up)
    bricks = [pack_bricks(start[...])] + [ref[64:72] for ref in (from_y, from_x, from_xy)]
    for q, brick in enumerate(bricks):
        out[192 + q * 8 : 200 + q * 8] = brick


def spread_first_kernel(from_y, from_xy, from_x, out):
    even = is_even()
    for q, ref in enumerate((from_y, from_x, from_xy)):
        out[q * 48 : q * 48 + 48] = jnp.where(even, ref[16:64], ref[0:48])
        out[144 + q * 8 : 152 + q * 8] = ref[64:72]


def spread_own_kernel(matrix, start, to_first, to_second):
    even = is_even()
    for q in range(4):
        rows = 32 if q < 3 else 48
        up = matrix[q * 64 + 64 - rows : q * 64 + 64]
        down = matrix[q * 64 : q * 64 + rows]
        to_first[q * 32 : q * 32 + rows] = jnp.where(even, up, down)
        if q < 3:
            to_second[q * 32 : q * 32 + rows] = jnp.where(even, down, up)
    to_first[144:152] = pack_bricks(start[...])


def join_wide_kernel(matrix, from_y, from_xy, from_x, first, own_first, wide, places):
    even = is_even()
    for q, (ref, row) in enumerate(far_columns(matrix, from_x, from_y, from_xy)):
        other = first[q * 48 - 48 : q * 48] if q else own_first[96:144]
        wide[q * 96 : q * 96 + 48] = jnp.where(even, ref[row + 16 : row + 64], other)
        wide[q * 96 + 48 : q * 96 + 96] = jnp.where(even, other, ref[row : row + 48])
    low, _ = first_spans(even)

    def atom(index):
        x, y, z = far_atom(index)
        return x, y, z + 1 + low

    find_places(wide, range(24), atom, bricks_place, places)


def join_slim_kernel(matrix, from_y, from_xy, from_x, second, slim, places):
    even = is_even()
    for q, (ref, row) in enumerate(far_columns(matrix, from_x, from_y, from_xy)):
        other = second[q * 48 : q * 48 + 48]
        below = jnp.concatenate([other, ref[row : row + 16]], axis=0)
        above = jnp.concatenate([ref[row + 48 : row + 64], other], axis=0)
        slim[q * 64 : q * 64 + 64] = jnp.where(even, below, above)
    _, low = first_spans(even)

    def atom(index):
        return 1 + (index >> 3), 1 + ((index >> 2) & 1), (index & 3) + low

    find_places(slim, range(16), atom, bricks_place, places)


def join_near_kernel(matrix, second, own_first, near_second, tall, places):
    even = is_even()
    for q in range(4):
        if q < 3:
            one, two = (ref[q * 32 : q * 32 + 32] for ref in (own_first, near_second))
            low, high = jnp.where(even, two, one), jnp.where(even, one, two)
        else:
            low = jnp.where(even, second[16:48], own_first[112:144])
            high = jnp.where(even, own_first[96:128], second[0:32])
        tall[q * 128 : q * 128 + 32] = low
        tall[q * 128 + 32 : q * 128 + 96] = matrix[q * 64 : q * 64 + 64]
        tall[q * 128 + 96 : q * 128 + 128] = high
    find_places(tall, range(32), tall_near_atom, first_place(even), places)


def later_kernel(wide, slim, matrix, far, third_places, fourth_places):
    even = is_even()
    for q in range(4):
        one, two = wide[q * 96 : q * 96 + 96], slim[q * 64 : q * 64 + 64]
        below = jnp.concatenate([two[32:64], one[0:64]], axis=0)
        above = jnp.concatenate([one[32:96], two[0:32]], axis=0)
        far[q * 96 : q * 96 + 96] = jnp.where(even, below, above)
    find_places(far, range(24), far_atom, SECOND_PLACE, third_places)
    find_places(matrix, range(ATOMS), near_atom, THIRD_PLACE, fourth_places)


WIDE_FLOPS = 1 << 28


def first_tiles(rows, places, start, from_y, from_xy, from_x, bricks, field, gathered):
    pieces = [start[...]] + [unpack_bricks(ref[64:72]) for ref in (from_y, from_x, from_xy)]
    set_tiles(field, pieces + [unpack_bricks(brick) for brick in bricks])
    return couple(rows, range(rows.shape[0] // SLOT_ROWS), field, places, gathered)


def first_wide_kernel(
    wide, places, start, from_y, from_xy, from_x, first, own_first, out, field, gathered
):
    bricks = [own_first[144:152]] + [first[144 + q * 8 : 152 + q * 8] for q in range(3)]
    out[...] = first_tiles(wide, places, start, from_y, from_xy, from_x, bricks, field, gathered)


def first_slim_kernel(
    slim, places, start, from_y, from_xy, from_x, second, before, out, field, gathered
):
    bricks = [second[192 + q * 8 : 200 + q * 8] for q in range(4)]
    out[:, 0 : 3 * LANES] = before[...]
    out[:, 3 * LANES : 5 * LANES] = first_tiles(
        slim, places, start, from_y, from_xy, from_x, bricks, field, gathered
    )


def second_kernel(tall, places, own, from_x, from_y, from_xy, out, field, gathered):
    set_tiles(field, (from_xy, from_x, from_y, own))
    out[...] = couple(tall, range(32), field, places, gathered)


def third_kernel(wide, places, own, from_x, from_y, from_xy, out, field, gathered):
    set_tiles(field, (own, from_y, from_x, from_xy))
    out[...] = couple(wide, range(24), field, places, gathered)


def pick_kernel(own, from_x, from_y, from_xy, second, first_own, second_own):
    pieces = from_xy, from_x, from_y, own
    first_own[...] = jnp.where(
        is_even(), pick_own(pieces, first_place(True)), pick_own(pieces, first_place(False))
    )
    second_own[...] = pick_own((second,), SECOND_PLACE)


def last_kernel(
    matrix, places, own, from_x, from_y, from_xy, start, first, second, third_out, out,
    field, gathered,
):
    pieces = from_xy, from_x, from_y, own
    set_tiles(field, pieces)
    fourth = couple(matrix, range(ATOMS), field, places, gathered)
    third = pick_own(pieces, THIRD_PLACE)
    third_out[...] = third
    gram_kernel([start[...], first[...], second[...], third, fourth], out)


SMEM = pl.BlockSpec(memory_space=pltpu.SMEM)


def whole_numbers(rows):
    return jax.ShapeDtypeStruct((rows, LANES), jnp.int32)


def call(kernel, shapes, *operands, scratch=(), place=VMEM, flops=0):
    shapes = [
        shape if isinstance(shape, jax.ShapeDtypeStruct) else jax.ShapeDtypeStruct(shape, jnp.float32)
        for shape in shapes
    ]
    return pl.pallas_call(
        kernel,
        out_shape=shapes,
        in_specs=[
            SMEM if operand.dtype == jnp.int32 and place is VMEM else place for operand in operands
        ],
        out_specs=[VMEM] * len(shapes),
        scratch_shapes=list(scratch),
        cost_estimate=pl.CostEstimate(flops=flops, bytes_accessed=flops // 64, transcendentals=0)
        if flops
        else None,
        compiler_params=pltpu.CompilerParams(vmem_limit_bytes=24 * 1024 * 1024),
    )(*operands)


def scratch_for(tiles, groups):
    return (
        pltpu.VMEM((tiles * 8, SLOT_ROWS, LANES), jnp.float32),
        pltpu.VMEM((groups, WIDE, LANES), jnp.float32),
    )


def fetch(value, first, second):
    sizes = [lax.axis_size(axis) for axis in AXES]
    pairs = []
    for a in range(sizes[0]):
        for b in range(sizes[1]):
            for c in range(sizes[2]):
                source = ((a + first) % sizes[0] * sizes[1] + (b + second) % sizes[1]) * sizes[2] + c
                pairs.append((source, (a * sizes[1] + b) * sizes[2] + c))
    return lax.ppermute(value, AXES, pairs)


def fetch_three(to_x, to_y, to_xy, sign):
    return fetch(to_x, sign, 0), fetch(to_y, 0, sign), fetch(to_xy, sign, sign)


def swap_layers(to_first, to_second):
    count = lax.axis_size("gz")
    even = [(i, i ^ 1) for i in range(count)]
    odd = [(i, (i + 1 if i % 2 else i - 1) % count) for i in range(count)]
    return lax.ppermute(to_first, "gz", even), lax.ppermute(to_second, "gz", odd)


def body(rhs, diagonal, blocks, neighbours):
    width = rhs.shape[-1]
    flat = (SLOT_ROWS, width)
    matrix, start, *out = call(
        pack_kernel,
        [(ATOMS * SLOT_ROWS, WIDE), flat] + [(72, WIDE)] * 3,
        *(pltpu.with_memory_space_constraint(x, pltpu.HBM) for x in (rhs, diagonal, blocks, neighbours)),
        scratch=[
            pltpu.VMEM(rhs.shape, rhs.dtype),
            pltpu.VMEM(diagonal.shape, diagonal.dtype),
            pltpu.VMEM(blocks.shape, blocks.dtype),
            pltpu.VMEM(neighbours.shape, neighbours.dtype),
            pltpu.SemaphoreType.DMA((4,)),
        ],
        place=pl.BlockSpec(memory_space=pltpu.HBM),
    )
    from_x, from_y, from_xy = fetch_three(*out, 1)
    sides = from_y, from_xy, from_x
    (to_second,) = call(spread_second_kernel, [(224, WIDE)], matrix, *sides, start)
    (to_first,) = call(spread_first_kernel, [(168, WIDE)], *sides)
    first_layers, second_layers = swap_layers(to_first, to_second)
    own_layers, near_layers = swap_layers(
        *call(spread_own_kernel, [(152, WIDE), (96, WIDE)], matrix, start)
    )
    wide, wide_places = call(
        join_wide_kernel, [(24 * SLOT_ROWS, WIDE), whole_numbers(24)],
        matrix, *sides, first_layers, own_layers,
    )
    (first,) = call(
        first_wide_kernel, [(SLOT_ROWS, 3 * LANES)],
        wide, wide_places, start, *sides, first_layers, own_layers,
        scratch=scratch_for(16, 3),
        flops=WIDE_FLOPS,
    )
    first, second_layers = lax.optimization_barrier((first, second_layers))
    slim, slim_places = call(
        join_slim_kernel, [(16 * SLOT_ROWS, WIDE), whole_numbers(16)], matrix, *sides, second_layers
    )
    (first,) = call(
        first_slim_kernel, [(SLOT_ROWS, 5 * LANES)],
        slim, slim_places, start, *sides, second_layers, first,
        scratch=scratch_for(16, 2),
    )
    tall, places = call(
        join_near_kernel, [(32 * SLOT_ROWS, WIDE), whole_numbers(32)],
        matrix, second_layers, own_layers, near_layers,
    )
    pieces = fetch_three(first, first, first, -1)
    (second,) = call(
        second_kernel, [(SLOT_ROWS, 4 * LANES)], tall, places, first, *pieces,
        scratch=scratch_for(20, 4),
    )
    first_own, second_own = call(pick_kernel, [flat] * 2, first, *pieces, second)
    far, third_places, fourth_places = call(
        later_kernel,
        [(24 * SLOT_ROWS, WIDE), whole_numbers(24), whole_numbers(ATOMS)],
        wide, slim, matrix,
    )
    (third,) = call(
        third_kernel, [(SLOT_ROWS, 3 * LANES)],
        far, third_places, second, *fetch_three(second, second, second, 1),
        scratch=scratch_for(16, 3),
    )
    third_own, message = call(
        last_kernel,
        [flat, (lax.axis_size("gx") * lax.axis_size("gy"), 4, LANES)],
        matrix, fourth_places, third, *fetch_three(third, third, third, -1),
        start, first_own, second_own,
        scratch=scratch_for(12, 2),
    )
    message = lax.all_to_all(message, ("gx", "gy"), 0, 0, tiled=True)
    (message,) = call(relay_kernel, [(lax.axis_size("gz"), 4, LANES)], message)
    message = lax.all_to_all(message, "gz", 0, 0, tiled=True)
    (result,) = call(finish_kernel, [rhs.shape], message, start, first_own, second_own, third_own)
    return result


def solution(mesh):
    return jax.shard_map(
        body,
        mesh=mesh,
        in_specs=(
            P("gx", "gy", "gz", None),
            P("gx", "gy", "gz", None),
            P("gx", "gy", "gz", None, None),
            P("gx", "gy", "gz", None),
        ),
        out_specs=P("gx", "gy", "gz", None),
        check_vma=False,
    )
```

```python
import jax
import jax.numpy as jnp
from jax import lax
from jax.experimental import pallas as pl
from jax.experimental.pallas import tpu as pltpu
from jax.sharding import PartitionSpec as P

ITERS = 2
DEGREE = 2 * ITERS
SHIFT = 2.0
RESOLUTION = 1e-14
LANES = 128
PAIRS = [(i, j) for i in range(DEGREE + 1) for j in range(i, DEGREE + 1)]
VMEM = pl.BlockSpec(memory_space=pltpu.VMEM)


def two_sum(a, b):
    total = a + b
    part = total - a
    return total, (a - (total - part)) + (b - part)


def quick_sum(a, b):
    total = a + b
    return total, b - (total - a)


def split(a):
    scaled = 4097.0 * a
    head = scaled - (scaled - a)
    return head, a - head


def two_prod(a, b):
    product = a * b
    a_head, a_tail = split(a)
    b_head, b_tail = split(b)
    rest = ((a_head * b_head - product) + a_head * b_tail + a_tail * b_head) + a_tail * b_tail
    return product, rest


def pair_add(a, b):
    head, tail = two_sum(a[0], b[0])
    return quick_sum(head, tail + (a[1] + b[1]))


def pair_mul(a, b):
    head, tail = two_prod(a[0], b[0])
    return quick_sum(head, tail + (a[0] * b[1] + a[1] * b[0]))


def pair_scale(a, factor):
    head, tail = two_prod(a[0], factor)
    return quick_sum(head, tail + a[1] * factor)


def roll_pair(a, amount, axis):
    return pltpu.roll(a[0], amount, axis), pltpu.roll(a[1], amount, axis)


def iota(shape, axis):
    return lax.broadcasted_iota(jnp.int32, shape, axis)


def gram_kernel(fields, out):
    columns = 16
    diagonal_mask = iota((8, LANES), 0) == iota((8, LANES), 1) // columns
    rows = []
    parts = [split(field) for field in fields]
    for i, j in PAIRS:
        product = fields[i] * fields[j]
        (a_head, a_tail), (b_head, b_tail) = parts[i], parts[j]
        rest = ((a_head * b_head - product) + a_head * b_tail + a_tail * b_head) + a_tail * b_tail
        pieces = [
            (product[s : s + 8, t : t + LANES], rest[s : s + 8, t : t + LANES])
            for s in range(0, product.shape[0], 8)
            for t in range(0, product.shape[1], LANES)
        ]
        while len(pieces) > 1:
            pieces = [pair_add(pieces[q], pieces[q + 1]) for q in range(0, len(pieces), 2)]
        total = pieces[0]
        for amount in (4, 2, 1):
            total = pair_add(total, roll_pair(total, amount, 0))
        rows.append((total[0][0:1], total[1][0:1]))
    rows += [(jnp.zeros((1, LANES), jnp.float32),) * 2] * (16 - len(rows))
    packed = [[], []]
    for start in (0, 8):
        total = tuple(
            jnp.concatenate([row[part] for row in rows[start : start + 8]], axis=0)
            for part in (0, 1)
        )
        for amount in (64, 32, 16):
            total = pair_add(total, roll_pair(total, amount, 1))
        for part in (0, 1):
            packed[part].append(
                jnp.sum(jnp.where(diagonal_mask, total[part], 0.0), axis=0, keepdims=True)
            )
    message = jnp.concatenate(packed[0] + packed[1], axis=0)
    for q in range(out.shape[0]):
        out[q] = message


def sum_messages(ref):
    terms = [(ref[q], None) for q in range(ref.shape[0])]
    while len(terms) > 1:
        merged = []
        for q in range(0, len(terms), 2):
            (a, a_rest), (b, b_rest) = terms[q], terms[q + 1]
            total, rest = two_sum(a, b)
            if a_rest is not None:
                rest = rest + (a_rest + b_rest)
            merged.append((total, rest))
        terms = merged
    total, rest = terms[0]
    return quick_sum(total[0:2], rest[0:2] + (total[2:4] + rest[2:4]))


def relay_kernel(ref, out):
    head, tail = sum_messages(ref)
    message = jnp.concatenate([head, tail], axis=0)
    for q in range(out.shape[0]):
        out[q] = message


def finish_kernel(ref, *refs):
    fields, out = refs[:-1], refs[-1]
    columns = 16
    shape = (8, LANES)
    row = iota(shape, 0)
    diagonal_mask = row == iota(shape, 1) // columns
    packed = sum_messages(ref)
    unpacked = []
    for part in (0, 1):
        halves = []
        for half in (0, 1):
            value = jnp.where(
                diagonal_mask, jnp.broadcast_to(packed[part][half : half + 1], shape), 0.0
            )
            for amount in (64, 32, 16):
                value = value + pltpu.roll(value, amount, 1)
            halves.append(value)
        unpacked.append(halves)

    def entry(part, i, j):
        place = PAIRS.index((min(i, j), max(i, j)))
        half = unpacked[part][place // 8]
        return jnp.broadcast_to(half[place % 8 : place % 8 + 1], shape)

    gram = []
    for j in range(DEGREE + 1):
        column = []
        for part in (0, 1):
            value = jnp.zeros(shape, jnp.float32)
            for i in range(DEGREE + 1):
                value = jnp.where(row == i, entry(part, i, j), value)
            column.append(value)
        gram.append(tuple(column))

    def total_rows(a):
        for amount in (4, 2, 1):
            a = pair_add(a, roll_pair(a, amount, 0))
        return a[0]

    def with_start(a):
        return total_rows(pair_mul(gram[0], a))

    def square(a, degree):
        acc = None
        for j in range(degree + 1):
            factor = tuple(jnp.broadcast_to(part[j : j + 1], shape) for part in a)
            term = pair_mul(gram[j], factor)
            acc = term if acc is None else pair_add(acc, term)
        return total_rows(pair_mul(acc, a))

    def apply(a):
        return pair_add((SHIFT * a[0], SHIFT * a[1]), roll_pair(a, 1, 0))

    def shrink(quasi_norm, ratio, step):
        damping = 1.0 / (1.0 + ratio * ratio)
        return quasi_norm * ratio * jnp.sqrt(damping), damping * step

    zero = jnp.zeros(shape, jnp.float32)
    start = (jnp.where(row == 0, 1.0, 0.0), zero)
    inner = entry(0, 0, 0)
    least = RESOLUTION * inner
    quasi_norm = jnp.sqrt(inner)
    image = apply(start)
    resid = search = start
    direction = total = (zero, zero)
    ratio = weight = zero
    for iteration in range(ITERS):
        step = inner / with_start(image)
        resid = pair_add(resid, pair_scale(image, -step))
        direction = pair_add(search, pair_scale(direction, ratio * ratio * weight / step))
        ratio = jnp.sqrt(jnp.maximum(square(resid, 2 * iteration + 1), least)) / quasi_norm
        quasi_norm, weight = shrink(quasi_norm, ratio, step)
        total = pair_add(total, pair_scale(direction, weight))
        search_odd = pair_add(search, pair_scale(image, -step))
        image_odd = apply(search_odd)
        resid = pair_add(resid, pair_scale(image_odd, -step))
        direction = pair_add(search_odd, pair_scale(direction, ratio * ratio * weight / step))
        ratio = jnp.sqrt(jnp.maximum(square(resid, 2 * iteration + 2), least)) / quasi_norm
        quasi_norm, weight = shrink(quasi_norm, ratio, step)
        total = pair_add(total, pair_scale(direction, weight))
        if iteration + 1 < ITERS:
            inner_next = with_start(resid)
            mix = inner_next / inner
            search = pair_add(resid, pair_scale(search_odd, mix))
            image = pair_add(
                apply(search), pair_scale(pair_add(image_odd, pair_scale(image, mix)), mix)
            )
            inner = inner_next
    coefficients = total[0] + total[1]
    height, width = fields[0].shape
    acc = None
    for i, field in enumerate(fields):
        factor = jnp.broadcast_to(coefficients[i : i + 1], (height, LANES))
        factor = jnp.concatenate([factor] * (width // LANES), axis=1)
        term = factor * field[...]
        acc = term if acc is None else acc + term
    from_tiles(acc, out)


SLOT_ROWS = 16
WIDE = 512
SELF = 27
CODE = 448
HIGH = lax.Precision.HIGHEST
LENGTHS = (2, 2, 4)
ATOMS = 16
AXES = ("gx", "gy", "gz")


def bricks_place(x, y, z):
    layer = ((z >> 2) != 0).astype(jnp.int32)
    brick = layer * 4 + (x >> 1) * 2 + (y >> 1)
    return (brick * 2 + (x & 1)) * 8 + (y & 1) * 4 + (z & 3)


def pieces_place(origin, run, low):
    def place(x, y, z):
        x, y = x - origin, y - origin
        piece = (x >> 1) * 2 + (y >> 1)
        return (piece * 4 + (x & 1) * 2 + (y & 1)) * run + z - low

    return place


def far_atom(index):
    column = (index * 43) >> 8
    return 1 + (column >> 1), 1 + (column & 1), index - 6 * column - 1


def tall_near_atom(index):
    return index >> 4, (index >> 3) & 1, (index & 7) - 2


def near_atom(index):
    return index >> 3, (index >> 2) & 1, index & 3


def first_spans(even):
    if isinstance(even, bool):
        return (1, -3) if even else (-3, 3)
    return jnp.where(even, 1, -3), jnp.where(even, -3, 3)


def first_place(even):
    wide_low, slim_low = first_spans(even)

    def place(x, y, z):
        x, y = x + 1, y + 1
        piece = (x >> 1) * 2 + (y >> 1)
        column = (x & 1) * 2 + (y & 1)
        layer = z - wide_low
        wide, slim = column * 6 + layer, 24 + column * 4 + z - slim_low
        if isinstance(z, int):
            return piece * 40 + (wide if 0 <= layer < 6 else slim)
        return piece * 40 + jnp.where((layer >= 0) & (layer < 6), wide, slim)

    return place


SECOND_PLACE, THIRD_PLACE = pieces_place(0, 8, -2), pieces_place(-1, 6, -1)


def find_places(matrix, rows, atom, place, out):
    rows = [row * SLOT_ROWS for row in rows]
    code = jnp.concatenate([matrix[row : row + 1, CODE - 64 : CODE + 64] for row in rows], axis=0)
    code = pltpu.roll(code, 64, 1).astype(jnp.int32)
    index = iota(code.shape, 0)
    x, y, z = atom(index)
    first = (code * 57) >> 9
    rest = code - 9 * first
    second = (rest * 11) >> 5
    where = place(x + first - 1, y + second - 1, z + rest - 3 * second - 1)
    out[...] = (where & ~7) + ((index - where) & 7)


def set_tiles(field, pieces):
    count = pieces[0].shape[1] // LANES
    for q, piece in enumerate(pieces):
        for t in range(count):
            tile = piece[:, t * LANES : (t + 1) * LANES]
            for turn in range(8):
                place = (q * count + t) * 8 + turn
                field[place] = pltpu.roll(tile, turn * SLOT_ROWS, 1) if turn else tile


def thirds(value):
    head = value.astype(jnp.bfloat16)
    rest = value - head.astype(jnp.float32)
    middle = rest.astype(jnp.bfloat16)
    return head, middle, (rest - middle.astype(jnp.float32)).astype(jnp.bfloat16)


def multiply(matrix, rows, right):
    right = right[0:CODE]
    if not isinstance(matrix, tuple):
        return jnp.dot(
            matrix[rows, 0:CODE], right, precision=HIGH, preferred_element_type=jnp.float32
        )
    head, middle, tail = (part[rows, 0:CODE] for part in matrix)
    right = jnp.concatenate(thirds(right), axis=1)
    by_head = jnp.dot(head, right, preferred_element_type=jnp.float32)
    by_middle = jnp.dot(middle, right[:, 0 : 2 * LANES], preferred_element_type=jnp.float32)
    by_tail = jnp.dot(tail, right[:, 0:LANES], preferred_element_type=jnp.float32)
    small = by_head[:, 2 * LANES : 3 * LANES] + by_middle[:, LANES : 2 * LANES] + by_tail
    return small + (by_head[:, LANES : 2 * LANES] + by_middle[:, 0:LANES]) + by_head[:, 0:LANES]


def couple(matrix, atoms, field, places, gathered):
    lane_slot = iota((SLOT_ROWS, LANES), 1) >> 4
    groups = atoms // 8

    def gather(k, carry):
        for q in range(groups):
            acc = None
            for slot in range(8):
                tile = field[places[q * 8 + slot, k]]
                acc = tile if acc is None else jnp.where(lane_slot == slot, tile, acc)
            gathered[q, pl.ds(pl.multiple_of(k * SLOT_ROWS, SLOT_ROWS), SLOT_ROWS), :] = acc
        return carry

    lax.fori_loop(0, SELF + 1, gather, 0, unroll=SELF + 1)
    tiles = []
    for q in range(groups):
        product = multiply(matrix, slice(q * LANES, (q + 1) * LANES), gathered[q])
        acc = product[0:SLOT_ROWS]
        for slot in range(1, 8):
            piece = product[slot * SLOT_ROWS : (slot + 1) * SLOT_ROWS]
            acc = jnp.where(lane_slot == slot, piece, acc)
        tiles.append(-acc)
    return jnp.concatenate(tiles, axis=1)


def pick_own(pieces, place):
    lane_slot = iota((SLOT_ROWS, LANES), 1) >> 4
    tiles = []
    for x in range(2):
        acc = None
        for slot in range(8):
            where = place(x, slot >> 2, slot & 3)
            count = pieces[0].shape[1] // LANES
            tile, turn = where >> 3, (slot - where) & 7
            lanes = pl.ds(tile % count * LANES, LANES)
            tile = pieces[tile // count][:, lanes]
            tile = pltpu.roll(tile, turn * SLOT_ROWS, 1) if turn else tile
            acc = tile if acc is None else jnp.where(lane_slot == slot, tile, acc)
        tiles.append(acc)
    return jnp.concatenate(tiles, axis=1)


def turn_blocks(value):
    row, group = iota(value.shape, 0), iota(value.shape, 1) >> 4
    for bit in (1, 2, 4):
        lanes = bit * SLOT_ROWS
        later = pltpu.roll(pltpu.roll(value, 8 - bit, 0), lanes, 1)
        earlier = pltpu.roll(pltpu.roll(value, bit, 0), LANES - lanes, 1)
        swapped = jnp.where((group & bit) != 0, later, earlier)
        value = jnp.where((row & bit) == (group & bit), value, swapped)
    return value


def to_tiles(field):
    halves = []
    for half in range(2):
        lanes = slice(half * LANES, (half + 1) * LANES)
        tiles = [
            turn_blocks(jnp.concatenate([field[x, y, :, lanes] for y in range(2)], axis=0))
            for x in range(2)
        ]
        halves.append(jnp.concatenate(tiles, axis=1))
    return jnp.concatenate(halves, axis=0)


def from_tiles(value, out):
    for half in range(2):
        for x in range(2):
            rows = turn_blocks(value[half * 8 : half * 8 + 8, x * LANES : (x + 1) * LANES])
            for y in range(2):
                out[x, y, :, half * LANES : (half + 1) * LANES] = rows[y * 4 : y * 4 + 4]


def pack_bricks(field):
    return jnp.concatenate([field[0:8], field[8:16]], axis=1)


def unpack_bricks(packed):
    return jnp.concatenate([packed[:, 0 : 2 * LANES], packed[:, 2 * LANES : 4 * LANES]], axis=0)


def pack_kernel(
    rhs_hbm, diagonal_hbm, blocks_hbm, neighbours_hbm,
    matrix, start, to_x, to_y, to_xy,
    rhs, diagonal, blocks, neighbours, sems,
):
    sources = (neighbours_hbm, diagonal_hbm, rhs_hbm, blocks_hbm)
    copies = [
        pltpu.make_async_copy(source, target, sems.at[q])
        for q, (source, target) in enumerate(zip(sources, (neighbours, diagonal, rhs, blocks)))
    ]
    for copy in copies:
        copy.start()
    matrix[:, 384:WIDE] = jnp.zeros((matrix.shape[0], WIDE - 384), jnp.float32)
    eye = iota((SLOT_ROWS, SLOT_ROWS), 0) == iota((SLOT_ROWS, SLOT_ROWS), 1)
    totals = [length * lax.axis_size(axis) for length, axis in zip(LENGTHS, AXES)]
    corner = [length * lax.axis_index(axis) for length, axis in zip(LENGTHS, AXES)]
    bits = [total.bit_length() - 1 for total in totals]
    for copy in copies[:2]:
        copy.wait()
    for x in range(2):
        for y in range(2):
            index = neighbours[x, y]
            along_x = index >> (bits[1] + bits[2])
            along_y = (index >> bits[2]) & (totals[1] - 1)
            along_z = index & (totals[2] - 1)
            z_here = corner[2] + iota(index.shape, 0)
            code = (along_x - (corner[0] + x - 1)) & (totals[0] - 1)
            code = code * 3 + ((along_y - (corner[1] + y - 1)) & (totals[1] - 1))
            code = code * 3 + ((along_z - z_here + 1) & (totals[2] - 1))
            code = code.astype(jnp.float32)
            for z in range(4):
                row = ((x * 2 + y) * 4 + z) * SLOT_ROWS
                matrix[row : row + 1, CODE : CODE + SELF] = code[z : z + 1]
                matrix[row : row + 1, CODE + SELF : CODE + SELF + 1] = jnp.full(
                    (1, 1), 13.0, jnp.float32
                )
                own = SHIFT - jnp.broadcast_to(diagonal[x, y, z : z + 1], eye.shape)
                matrix[row : row + SLOT_ROWS, 432:448] = jnp.where(eye, own, 0.0)
    copies[2].wait()
    value = to_tiles(rhs)
    start[...] = value
    bricks = pack_bricks(value)
    copies[3].wait()
    for x in range(2):
        for y in range(2):
            for z in range(4):
                row = ((x * 2 + y) * 4 + z) * SLOT_ROWS
                matrix[row : row + SLOT_ROWS, 0:432] = blocks[x, y, z]
    for out, row in ((to_x, 64), (to_y, 128), (to_xy, 0)):
        out[0:64] = matrix[row : row + 64]
        out[64:72] = bricks


def far_columns(matrix, from_x, from_y, from_xy):
    return (matrix, 192), (from_y, 0), (from_x, 0), (from_xy, 0)


def is_even():
    return lax.rem(lax.axis_index("gz"), 2) == 0


def spread_second_kernel(matrix, from_y, from_xy, from_x, start, out):
    even = is_even()
    for q, (ref, row) in enumerate(far_columns(matrix, from_x, from_y, from_xy)):
        up, down = ref[row + 16 : row + 64], ref[row : row + 48]
        out[q * 48 : q * 48 + 48] = jnp.where(even, down, up)
    bricks = [pack_bricks(start[...])] + [ref[64:72] for ref in (from_y, from_x, from_xy)]
    for q, brick in enumerate(bricks):
        out[192 + q * 8 : 200 + q * 8] = brick


def spread_first_kernel(from_y, from_xy, from_x, out):
    even = is_even()
    for q, ref in enumerate((from_y, from_x, from_xy)):
        out[q * 48 : q * 48 + 48] = jnp.where(even, ref[16:64], ref[0:48])
        out[144 + q * 8 : 152 + q * 8] = ref[64:72]


def spread_own_kernel(matrix, start, to_first, to_second):
    even = is_even()
    for q in range(4):
        rows = 32 if q < 3 else 48
        up = matrix[q * 64 + 64 - rows : q * 64 + 64]
        down = matrix[q * 64 : q * 64 + rows]
        to_first[q * 32 : q * 32 + rows] = jnp.where(even, up, down)
        if q < 3:
            to_second[q * 32 : q * 32 + rows] = jnp.where(even, down, up)
    to_first[144:152] = pack_bricks(start[...])


def join_wide_kernel(matrix, from_y, from_xy, from_x, first, own_first, wide, places):
    even = is_even()
    for q, (ref, row) in enumerate(far_columns(matrix, from_x, from_y, from_xy)):
        other = first[q * 48 - 48 : q * 48] if q else own_first[96:144]
        wide[q * 96 : q * 96 + 48] = jnp.where(even, ref[row + 16 : row + 64], other)
        wide[q * 96 + 48 : q * 96 + 96] = jnp.where(even, other, ref[row : row + 48])
    low, _ = first_spans(even)

    def atom(index):
        x, y, z = far_atom(index)
        return x, y, z + 1 + low

    find_places(wide, range(24), atom, bricks_place, places)


def join_slim_kernel(matrix, from_y, from_xy, from_x, second, slim, places):
    even = is_even()
    for q, (ref, row) in enumerate(far_columns(matrix, from_x, from_y, from_xy)):
        other = second[q * 48 : q * 48 + 48]
        below = jnp.concatenate([other, ref[row : row + 16]], axis=0)
        above = jnp.concatenate([ref[row + 48 : row + 64], other], axis=0)
        slim[q * 64 : q * 64 + 64] = jnp.where(even, below, above)
    _, low = first_spans(even)

    def atom(index):
        return 1 + (index >> 3), 1 + ((index >> 2) & 1), (index & 3) + low

    find_places(slim, range(16), atom, bricks_place, places)


def join_near_kernel(matrix, second, own_first, near_second, head, middle, tail, places, tall):
    even = is_even()
    for q in range(4):
        if q < 3:
            one, two = (ref[q * 32 : q * 32 + 32] for ref in (own_first, near_second))
            low, high = jnp.where(even, two, one), jnp.where(even, one, two)
        else:
            low = jnp.where(even, second[16:48], own_first[112:144])
            high = jnp.where(even, own_first[96:128], second[0:32])
        tall[q * 128 : q * 128 + 32] = low
        tall[q * 128 + 32 : q * 128 + 96] = matrix[q * 64 : q * 64 + 64]
        tall[q * 128 + 96 : q * 128 + 128] = high
    find_places(tall, range(32), tall_near_atom, first_place(even), places)
    head[...], middle[...], tail[...] = thirds(tall[...])


def later_kernel(
    wide, slim, matrix, far_head, far_middle, far_tail, head, middle, tail,
    third_places, fourth_places, far,
):
    even = is_even()
    for q in range(4):
        one, two = wide[q * 96 : q * 96 + 96], slim[q * 64 : q * 64 + 64]
        below = jnp.concatenate([two[32:64], one[0:64]], axis=0)
        above = jnp.concatenate([one[32:96], two[0:32]], axis=0)
        far[q * 96 : q * 96 + 96] = jnp.where(even, below, above)
    find_places(far, range(24), far_atom, SECOND_PLACE, third_places)
    find_places(matrix, range(ATOMS), near_atom, THIRD_PLACE, fourth_places)
    far_head[...], far_middle[...], far_tail[...] = thirds(far[...])
    head[...], middle[...], tail[...] = thirds(matrix[...])


WIDE_FLOPS = 1 << 28


def first_tiles(rows, places, start, from_y, from_xy, from_x, bricks, field, gathered):
    pieces = [start[...]] + [unpack_bricks(ref[64:72]) for ref in (from_y, from_x, from_xy)]
    set_tiles(field, pieces + [unpack_bricks(brick) for brick in bricks])
    return couple(rows, rows.shape[0] // SLOT_ROWS, field, places, gathered)


def first_wide_kernel(
    wide, places, start, from_y, from_xy, from_x, first, own_first, out, field, gathered
):
    bricks = [own_first[144:152]] + [first[144 + q * 8 : 152 + q * 8] for q in range(3)]
    out[...] = first_tiles(wide, places, start, from_y, from_xy, from_x, bricks, field, gathered)


def first_slim_kernel(
    slim, places, start, from_y, from_xy, from_x, second, before, out, field, gathered
):
    bricks = [second[192 + q * 8 : 200 + q * 8] for q in range(4)]
    out[:, 0 : 3 * LANES] = before[...]
    out[:, 3 * LANES : 5 * LANES] = first_tiles(
        slim, places, start, from_y, from_xy, from_x, bricks, field, gathered
    )


def second_kernel(
    head, middle, tail, places, own, from_x, from_y, from_xy, out, field, gathered
):
    set_tiles(field, (from_xy, from_x, from_y, own))
    out[...] = couple((head, middle, tail), 32, field, places, gathered)


def third_kernel(
    head, middle, tail, places, own, from_x, from_y, from_xy, out, field, gathered
):
    set_tiles(field, (own, from_y, from_x, from_xy))
    out[...] = couple((head, middle, tail), 24, field, places, gathered)


def pick_kernel(own, from_x, from_y, from_xy, second, first_own, second_own):
    pieces = from_xy, from_x, from_y, own
    first_own[...] = jnp.where(
        is_even(), pick_own(pieces, first_place(True)), pick_own(pieces, first_place(False))
    )
    second_own[...] = pick_own((second,), SECOND_PLACE)


def last_kernel(
    head, middle, tail, places, own, from_x, from_y, from_xy, start, first, second,
    third_out, out,
    field, gathered,
):
    pieces = from_xy, from_x, from_y, own
    set_tiles(field, pieces)
    fourth = couple((head, middle, tail), ATOMS, field, places, gathered)
    third = pick_own(pieces, THIRD_PLACE)
    third_out[...] = third
    gram_kernel([start[...], first[...], second[...], third, fourth], out)


SMEM = pl.BlockSpec(memory_space=pltpu.SMEM)


def cut(atoms):
    return jax.ShapeDtypeStruct((atoms * SLOT_ROWS, WIDE), jnp.bfloat16)


def whole_numbers(rows):
    return jax.ShapeDtypeStruct((rows, LANES), jnp.int32)


def call(kernel, shapes, *operands, scratch=(), place=VMEM, flops=0):
    shapes = [
        shape if isinstance(shape, jax.ShapeDtypeStruct) else jax.ShapeDtypeStruct(shape, jnp.float32)
        for shape in shapes
    ]
    return pl.pallas_call(
        kernel,
        out_shape=shapes,
        in_specs=[
            SMEM if operand.dtype == jnp.int32 and place is VMEM else place for operand in operands
        ],
        out_specs=[VMEM] * len(shapes),
        scratch_shapes=list(scratch),
        cost_estimate=pl.CostEstimate(flops=flops, bytes_accessed=flops // 64, transcendentals=0)
        if flops
        else None,
        compiler_params=pltpu.CompilerParams(vmem_limit_bytes=24 * 1024 * 1024),
    )(*operands)


def scratch_for(tiles, groups):
    return (
        pltpu.VMEM((tiles * 8, SLOT_ROWS, LANES), jnp.float32),
        pltpu.VMEM((groups, CODE, LANES), jnp.float32),
    )


def fetch(value, first, second):
    sizes = [lax.axis_size(axis) for axis in AXES]
    pairs = []
    for a in range(sizes[0]):
        for b in range(sizes[1]):
            for c in range(sizes[2]):
                source = ((a + first) % sizes[0] * sizes[1] + (b + second) % sizes[1]) * sizes[2] + c
                pairs.append((source, (a * sizes[1] + b) * sizes[2] + c))
    return lax.ppermute(value, AXES, pairs)


def fetch_three(to_x, to_y, to_xy, sign):
    return fetch(to_x, sign, 0), fetch(to_y, 0, sign), fetch(to_xy, sign, sign)


def swap_layers(to_first, to_second):
    count = lax.axis_size("gz")
    even = [(i, i ^ 1) for i in range(count)]
    odd = [(i, (i + 1 if i % 2 else i - 1) % count) for i in range(count)]
    return lax.ppermute(to_first, "gz", even), lax.ppermute(to_second, "gz", odd)


def body(rhs, diagonal, blocks, neighbours):
    width = rhs.shape[-1]
    flat = (SLOT_ROWS, width)
    matrix, start, *out = call(
        pack_kernel,
        [(ATOMS * SLOT_ROWS, WIDE), flat] + [(72, WIDE)] * 3,
        *(pltpu.with_memory_space_constraint(x, pltpu.HBM) for x in (rhs, diagonal, blocks, neighbours)),
        scratch=[
            pltpu.VMEM(rhs.shape, rhs.dtype),
            pltpu.VMEM(diagonal.shape, diagonal.dtype),
            pltpu.VMEM(blocks.shape, blocks.dtype),
            pltpu.VMEM(neighbours.shape, neighbours.dtype),
            pltpu.SemaphoreType.DMA((4,)),
        ],
        place=pl.BlockSpec(memory_space=pltpu.HBM),
    )
    from_x, from_y, from_xy = fetch_three(*out, 1)
    sides = from_y, from_xy, from_x
    (to_second,) = call(spread_second_kernel, [(224, WIDE)], matrix, *sides, start)
    (to_first,) = call(spread_first_kernel, [(168, WIDE)], *sides)
    first_layers, second_layers = swap_layers(to_first, to_second)
    own_layers, near_layers = swap_layers(
        *call(spread_own_kernel, [(152, WIDE), (96, WIDE)], matrix, start)
    )
    wide, wide_places = call(
        join_wide_kernel, [(24 * SLOT_ROWS, WIDE), whole_numbers(24)],
        matrix, *sides, first_layers, own_layers,
    )
    (first,) = call(
        first_wide_kernel, [(SLOT_ROWS, 3 * LANES)],
        wide, wide_places, start, *sides, first_layers, own_layers,
        scratch=scratch_for(16, 3),
        flops=WIDE_FLOPS,
    )
    first, second_layers = lax.optimization_barrier((first, second_layers))
    slim, slim_places = call(
        join_slim_kernel, [(16 * SLOT_ROWS, WIDE), whole_numbers(16)], matrix, *sides, second_layers
    )
    (first,) = call(
        first_slim_kernel, [(SLOT_ROWS, 5 * LANES)],
        slim, slim_places, start, *sides, second_layers, first,
        scratch=scratch_for(16, 2),
    )
    *tall, places = call(
        join_near_kernel, [cut(32)] * 3 + [whole_numbers(32)],
        matrix, second_layers, own_layers, near_layers,
        scratch=[pltpu.VMEM((32 * SLOT_ROWS, WIDE), jnp.float32)],
    )
    pieces = fetch_three(first, first, first, -1)
    (second,) = call(
        second_kernel, [(SLOT_ROWS, 4 * LANES)], *tall, places, first, *pieces,
        scratch=scratch_for(20, 4),
    )
    first_own, second_own = call(pick_kernel, [flat] * 2, first, *pieces, second)
    *parts, third_places, fourth_places = call(
        later_kernel,
        [cut(24)] * 3 + [cut(ATOMS)] * 3 + [whole_numbers(24), whole_numbers(ATOMS)],
        wide, slim, matrix,
        scratch=[pltpu.VMEM((24 * SLOT_ROWS, WIDE), jnp.float32)],
    )
    (third,) = call(
        third_kernel, [(SLOT_ROWS, 3 * LANES)],
        *parts[:3], third_places, second, *fetch_three(second, second, second, 1),
        scratch=scratch_for(16, 3),
    )
    third_own, message = call(
        last_kernel,
        [flat, (lax.axis_size("gx") * lax.axis_size("gy"), 4, LANES)],
        *parts[3:], fourth_places, third, *fetch_three(third, third, third, -1),
        start, first_own, second_own,
        scratch=scratch_for(12, 2),
    )
    message = lax.all_to_all(message, ("gx", "gy"), 0, 0, tiled=True)
    (message,) = call(relay_kernel, [(lax.axis_size("gz"), 4, LANES)], message)
    message = lax.all_to_all(message, "gz", 0, 0, tiled=True)
    (result,) = call(finish_kernel, [rhs.shape], message, start, first_own, second_own, third_own)
    return result


def solution(mesh):
    return jax.shard_map(
        body,
        mesh=mesh,
        in_specs=(
            P("gx", "gy", "gz", None),
            P("gx", "gy", "gz", None),
            P("gx", "gy", "gz", None, None),
            P("gx", "gy", "gz", None),
        ),
        out_specs=P("gx", "gy", "gz", None),
        check_vma=False,
    )
```

```python
import jax
import jax.numpy as jnp
from jax import lax
from jax.experimental import pallas as pl
from jax.experimental.pallas import tpu as pltpu
from jax.sharding import PartitionSpec as P

ITERS = 2
DEGREE = 2 * ITERS
SHIFT = 2.0
RESOLUTION = 1e-14
LANES = 128
PAIRS = [(i, j) for i in range(DEGREE + 1) for j in range(i, DEGREE + 1)]
VMEM = pl.BlockSpec(memory_space=pltpu.VMEM)


def two_sum(a, b):
    total = a + b
    part = total - a
    return total, (a - (total - part)) + (b - part)


def quick_sum(a, b):
    total = a + b
    return total, b - (total - a)


def split(a):
    scaled = 4097.0 * a
    head = scaled - (scaled - a)
    return head, a - head


def two_prod(a, b):
    product = a * b
    a_head, a_tail = split(a)
    b_head, b_tail = split(b)
    rest = ((a_head * b_head - product) + a_head * b_tail + a_tail * b_head) + a_tail * b_tail
    return product, rest


def pair_add(a, b):
    head, tail = two_sum(a[0], b[0])
    return quick_sum(head, tail + (a[1] + b[1]))


def pair_mul(a, b):
    head, tail = two_prod(a[0], b[0])
    return quick_sum(head, tail + (a[0] * b[1] + a[1] * b[0]))


def pair_scale(a, factor):
    head, tail = two_prod(a[0], factor)
    return quick_sum(head, tail + a[1] * factor)


def roll_pair(a, amount, axis):
    return pltpu.roll(a[0], amount, axis), pltpu.roll(a[1], amount, axis)


def iota(shape, axis):
    return lax.broadcasted_iota(jnp.int32, shape, axis)


def gram_kernel(fields, out):
    columns = 16
    diagonal_mask = iota((8, LANES), 0) == iota((8, LANES), 1) // columns
    rows = []
    parts = [split(field) for field in fields]
    for i, j in PAIRS:
        product = fields[i] * fields[j]
        (a_head, a_tail), (b_head, b_tail) = parts[i], parts[j]
        rest = ((a_head * b_head - product) + a_head * b_tail + a_tail * b_head) + a_tail * b_tail
        pieces = [
            (product[s : s + 8, t : t + LANES], rest[s : s + 8, t : t + LANES])
            for s in range(0, product.shape[0], 8)
            for t in range(0, product.shape[1], LANES)
        ]
        while len(pieces) > 1:
            pieces = [pair_add(pieces[q], pieces[q + 1]) for q in range(0, len(pieces), 2)]
        total = pieces[0]
        for amount in (4, 2, 1):
            total = pair_add(total, roll_pair(total, amount, 0))
        rows.append((total[0][0:1], total[1][0:1]))
    rows += [(jnp.zeros((1, LANES), jnp.float32),) * 2] * (16 - len(rows))
    packed = [[], []]
    for start in (0, 8):
        total = tuple(
            jnp.concatenate([row[part] for row in rows[start : start + 8]], axis=0)
            for part in (0, 1)
        )
        for amount in (64, 32, 16):
            total = pair_add(total, roll_pair(total, amount, 1))
        for part in (0, 1):
            packed[part].append(
                jnp.sum(jnp.where(diagonal_mask, total[part], 0.0), axis=0, keepdims=True)
            )
    message = jnp.concatenate(packed[0] + packed[1], axis=0)
    for q in range(out.shape[0]):
        out[q] = message


def sum_messages(ref):
    terms = [(ref[q], None) for q in range(ref.shape[0])]
    while len(terms) > 1:
        merged = []
        for q in range(0, len(terms), 2):
            (a, a_rest), (b, b_rest) = terms[q], terms[q + 1]
            total, rest = two_sum(a, b)
            if a_rest is not None:
                rest = rest + (a_rest + b_rest)
            merged.append((total, rest))
        terms = merged
    total, rest = terms[0]
    return quick_sum(total[0:2], rest[0:2] + (total[2:4] + rest[2:4]))


def relay_kernel(ref, out):
    head, tail = sum_messages(ref)
    message = jnp.concatenate([head, tail], axis=0)
    for q in range(out.shape[0]):
        out[q] = message


def finish_kernel(ref, *refs):
    fields, out = refs[:-1], refs[-1]
    columns = 16
    shape = (8, LANES)
    row = iota(shape, 0)
    diagonal_mask = row == iota(shape, 1) // columns
    packed = sum_messages(ref)
    unpacked = []
    for part in (0, 1):
        halves = []
        for half in (0, 1):
            value = jnp.where(
                diagonal_mask, jnp.broadcast_to(packed[part][half : half + 1], shape), 0.0
            )
            for amount in (64, 32, 16):
                value = value + pltpu.roll(value, amount, 1)
            halves.append(value)
        unpacked.append(halves)

    def entry(part, i, j):
        place = PAIRS.index((min(i, j), max(i, j)))
        half = unpacked[part][place // 8]
        return jnp.broadcast_to(half[place % 8 : place % 8 + 1], shape)

    gram = []
    for j in range(DEGREE + 1):
        column = []
        for part in (0, 1):
            value = jnp.zeros(shape, jnp.float32)
            for i in range(DEGREE + 1):
                value = jnp.where(row == i, entry(part, i, j), value)
            column.append(value)
        gram.append(tuple(column))

    def total_rows(a):
        for amount in (4, 2, 1):
            a = pair_add(a, roll_pair(a, amount, 0))
        return a[0]

    def with_start(a):
        return total_rows(pair_mul(gram[0], a))

    def square(a, degree):
        acc = None
        for j in range(degree + 1):
            factor = tuple(jnp.broadcast_to(part[j : j + 1], shape) for part in a)
            term = pair_mul(gram[j], factor)
            acc = term if acc is None else pair_add(acc, term)
        return total_rows(pair_mul(acc, a))

    def apply(a):
        return pair_add((SHIFT * a[0], SHIFT * a[1]), roll_pair(a, 1, 0))

    def shrink(quasi_norm, ratio, step):
        damping = 1.0 / (1.0 + ratio * ratio)
        return quasi_norm * ratio * jnp.sqrt(damping), damping * step

    zero = jnp.zeros(shape, jnp.float32)
    start = (jnp.where(row == 0, 1.0, 0.0), zero)
    inner = entry(0, 0, 0)
    least = RESOLUTION * inner
    quasi_norm = jnp.sqrt(inner)
    image = apply(start)
    resid = search = start
    direction = total = (zero, zero)
    ratio = weight = zero
    for iteration in range(ITERS):
        step = inner / with_start(image)
        resid = pair_add(resid, pair_scale(image, -step))
        direction = pair_add(search, pair_scale(direction, ratio * ratio * weight / step))
        ratio = jnp.sqrt(jnp.maximum(square(resid, 2 * iteration + 1), least)) / quasi_norm
        quasi_norm, weight = shrink(quasi_norm, ratio, step)
        total = pair_add(total, pair_scale(direction, weight))
        search_odd = pair_add(search, pair_scale(image, -step))
        image_odd = apply(search_odd)
        resid = pair_add(resid, pair_scale(image_odd, -step))
        direction = pair_add(search_odd, pair_scale(direction, ratio * ratio * weight / step))
        ratio = jnp.sqrt(jnp.maximum(square(resid, 2 * iteration + 2), least)) / quasi_norm
        quasi_norm, weight = shrink(quasi_norm, ratio, step)
        total = pair_add(total, pair_scale(direction, weight))
        if iteration + 1 < ITERS:
            inner_next = with_start(resid)
            mix = inner_next / inner
            search = pair_add(resid, pair_scale(search_odd, mix))
            image = pair_add(
                apply(search), pair_scale(pair_add(image_odd, pair_scale(image, mix)), mix)
            )
            inner = inner_next
    coefficients = total[0] + total[1]
    height, width = fields[0].shape
    acc = None
    for i, field in enumerate(fields):
        factor = jnp.broadcast_to(coefficients[i : i + 1], (height, LANES))
        factor = jnp.concatenate([factor] * (width // LANES), axis=1)
        term = factor * field[...]
        acc = term if acc is None else acc + term
    from_tiles(acc, out)


SLOT_ROWS = 16
WIDE = 512
SELF = 27
CODE = 448
HIGH = lax.Precision.HIGHEST
LENGTHS = (2, 2, 4)
ATOMS = 16
AXES = ("gx", "gy", "gz")


def bricks_place(x, y, z):
    layer = ((z >> 2) != 0).astype(jnp.int32)
    brick = layer * 4 + (x >> 1) * 2 + (y >> 1)
    return (brick * 2 + (x & 1)) * 8 + (y & 1) * 4 + (z & 3)


def pieces_place(origin, run, low):
    def place(x, y, z):
        x, y = x - origin, y - origin
        piece = (x >> 1) * 2 + (y >> 1)
        return (piece * 4 + (x & 1) * 2 + (y & 1)) * run + z - low

    return place


def far_atom(index):
    column = (index * 43) >> 8
    return 1 + (column >> 1), 1 + (column & 1), index - 6 * column - 1


def tall_near_atom(index):
    return index >> 4, (index >> 3) & 1, (index & 7) - 2


def near_atom(index):
    return index >> 3, (index >> 2) & 1, index & 3


def first_spans(even):
    if isinstance(even, bool):
        return (1, -3) if even else (-3, 3)
    return jnp.where(even, 1, -3), jnp.where(even, -3, 3)


def first_place(even):
    wide_low, slim_low = first_spans(even)

    def place(x, y, z):
        x, y = x + 1, y + 1
        piece = (x >> 1) * 2 + (y >> 1)
        column = (x & 1) * 2 + (y & 1)
        layer = z - wide_low
        wide, slim = column * 6 + layer, 24 + column * 4 + z - slim_low
        if isinstance(z, int):
            return piece * 40 + (wide if 0 <= layer < 6 else slim)
        return piece * 40 + jnp.where((layer >= 0) & (layer < 6), wide, slim)

    return place


SECOND_PLACE, THIRD_PLACE = pieces_place(0, 8, -2), pieces_place(-1, 6, -1)


def find_places(matrix, rows, atom, place, out):
    rows = [row * SLOT_ROWS for row in rows]
    code = jnp.concatenate([matrix[row : row + 1, CODE - 64 : CODE + 64] for row in rows], axis=0)
    code = pltpu.roll(code, 64, 1).astype(jnp.int32)
    index = iota(code.shape, 0)
    x, y, z = atom(index)
    first = (code * 57) >> 9
    rest = code - 9 * first
    second = (rest * 11) >> 5
    where = place(x + first - 1, y + second - 1, z + rest - 3 * second - 1)
    out[...] = (where & ~7) + ((index - where) & 7)


def set_tiles(field, pieces):
    count = pieces[0].shape[1] // LANES
    for q, piece in enumerate(pieces):
        for t in range(count):
            tile = piece[:, t * LANES : (t + 1) * LANES]
            for turn in range(8):
                place = (q * count + t) * 8 + turn
                field[place] = pltpu.roll(tile, turn * SLOT_ROWS, 1) if turn else tile


def thirds(value):
    head = value.astype(jnp.bfloat16)
    rest = value - head.astype(jnp.float32)
    middle = rest.astype(jnp.bfloat16)
    return head, middle, (rest - middle.astype(jnp.float32)).astype(jnp.bfloat16)


def multiply(matrix, rows, right):
    right = right[0:CODE]
    if not isinstance(matrix, tuple):
        return jnp.dot(
            matrix[rows, 0:CODE], right, precision=HIGH, preferred_element_type=jnp.float32
        )
    head, middle, tail = (part[rows, 0:CODE] for part in matrix)
    right = jnp.concatenate(thirds(right), axis=1)
    by_head = jnp.dot(head, right, preferred_element_type=jnp.float32)
    by_middle = jnp.dot(middle, right[:, 0 : 2 * LANES], preferred_element_type=jnp.float32)
    by_tail = jnp.dot(tail, right[:, 0:LANES], preferred_element_type=jnp.float32)
    small = by_head[:, 2 * LANES : 3 * LANES] + by_middle[:, LANES : 2 * LANES] + by_tail
    return small + (by_head[:, LANES : 2 * LANES] + by_middle[:, 0:LANES]) + by_head[:, 0:LANES]


def couple(matrix, atoms, field, places, gathered):
    lane_slot = iota((SLOT_ROWS, LANES), 1) >> 4
    groups = atoms // 8

    def gather(k, carry):
        for q in range(groups):
            acc = None
            for slot in range(8):
                tile = field[places[q * 8 + slot, k]]
                acc = tile if acc is None else jnp.where(lane_slot == slot, tile, acc)
            gathered[q, pl.ds(pl.multiple_of(k * SLOT_ROWS, SLOT_ROWS), SLOT_ROWS), :] = acc
        return carry

    lax.fori_loop(0, SELF + 1, gather, 0, unroll=SELF + 1)
    tiles = []
    for q in range(groups):
        product = multiply(matrix, slice(q * LANES, (q + 1) * LANES), gathered[q])
        acc = product[0:SLOT_ROWS]
        for slot in range(1, 8):
            piece = product[slot * SLOT_ROWS : (slot + 1) * SLOT_ROWS]
            acc = jnp.where(lane_slot == slot, piece, acc)
        tiles.append(-acc)
    return jnp.concatenate(tiles, axis=1)


def pick_own(pieces, place):
    lane_slot = iota((SLOT_ROWS, LANES), 1) >> 4
    tiles = []
    for x in range(2):
        acc = None
        for slot in range(8):
            where = place(x, slot >> 2, slot & 3)
            count = pieces[0].shape[1] // LANES
            tile, turn = where >> 3, (slot - where) & 7
            lanes = pl.ds(tile % count * LANES, LANES)
            tile = pieces[tile // count][:, lanes]
            tile = pltpu.roll(tile, turn * SLOT_ROWS, 1) if turn else tile
            acc = tile if acc is None else jnp.where(lane_slot == slot, tile, acc)
        tiles.append(acc)
    return jnp.concatenate(tiles, axis=1)


def turn_blocks(value):
    row, group = iota(value.shape, 0), iota(value.shape, 1) >> 4
    for bit in (1, 2, 4):
        lanes = bit * SLOT_ROWS
        later = pltpu.roll(pltpu.roll(value, 8 - bit, 0), lanes, 1)
        earlier = pltpu.roll(pltpu.roll(value, bit, 0), LANES - lanes, 1)
        swapped = jnp.where((group & bit) != 0, later, earlier)
        value = jnp.where((row & bit) == (group & bit), value, swapped)
    return value


def to_tiles(field):
    halves = []
    for half in range(2):
        lanes = slice(half * LANES, (half + 1) * LANES)
        tiles = [
            turn_blocks(jnp.concatenate([field[x, y, :, lanes] for y in range(2)], axis=0))
            for x in range(2)
        ]
        halves.append(jnp.concatenate(tiles, axis=1))
    return jnp.concatenate(halves, axis=0)


def from_tiles(value, out):
    for half in range(2):
        for x in range(2):
            rows = turn_blocks(value[half * 8 : half * 8 + 8, x * LANES : (x + 1) * LANES])
            for y in range(2):
                out[x, y, :, half * LANES : (half + 1) * LANES] = rows[y * 4 : y * 4 + 4]


def pack_bricks(field):
    return jnp.concatenate([field[0:8], field[8:16]], axis=1)


def unpack_bricks(packed):
    return jnp.concatenate([packed[:, 0 : 2 * LANES], packed[:, 2 * LANES : 4 * LANES]], axis=0)


def pack_kernel(
    rhs_hbm, diagonal_hbm, blocks_hbm, neighbours_hbm,
    matrix, start, to_x, to_y, to_xy,
    rhs, diagonal, blocks, neighbours, sems,
):
    sources = (neighbours_hbm, diagonal_hbm, rhs_hbm, blocks_hbm)
    copies = [
        pltpu.make_async_copy(source, target, sems.at[q])
        for q, (source, target) in enumerate(zip(sources, (neighbours, diagonal, rhs, blocks)))
    ]
    for copy in copies:
        copy.start()
    matrix[:, 384:WIDE] = jnp.zeros((matrix.shape[0], WIDE - 384), jnp.float32)
    eye = iota((SLOT_ROWS, SLOT_ROWS), 0) == iota((SLOT_ROWS, SLOT_ROWS), 1)
    totals = [length * lax.axis_size(axis) for length, axis in zip(LENGTHS, AXES)]
    corner = [length * lax.axis_index(axis) for length, axis in zip(LENGTHS, AXES)]
    bits = [total.bit_length() - 1 for total in totals]
    for copy in copies[:2]:
        copy.wait()
    for x in range(2):
        for y in range(2):
            index = neighbours[x, y]
            along_x = index >> (bits[1] + bits[2])
            along_y = (index >> bits[2]) & (totals[1] - 1)
            along_z = index & (totals[2] - 1)
            z_here = corner[2] + iota(index.shape, 0)
            code = (along_x - (corner[0] + x - 1)) & (totals[0] - 1)
            code = code * 3 + ((along_y - (corner[1] + y - 1)) & (totals[1] - 1))
            code = code * 3 + ((along_z - z_here + 1) & (totals[2] - 1))
            code = code.astype(jnp.float32)
            for z in range(4):
                row = ((x * 2 + y) * 4 + z) * SLOT_ROWS
                matrix[row : row + 1, CODE : CODE + SELF] = code[z : z + 1]
                matrix[row : row + 1, CODE + SELF : CODE + SELF + 1] = jnp.full(
                    (1, 1), 13.0, jnp.float32
                )
                own = SHIFT - jnp.broadcast_to(diagonal[x, y, z : z + 1], eye.shape)
                matrix[row : row + SLOT_ROWS, 432:448] = jnp.where(eye, own, 0.0)
    copies[2].wait()
    value = to_tiles(rhs)
    start[...] = value
    bricks = pack_bricks(value)
    copies[3].wait()
    for x in range(2):
        for y in range(2):
            for z in range(4):
                row = ((x * 2 + y) * 4 + z) * SLOT_ROWS
                matrix[row : row + SLOT_ROWS, 0:432] = blocks[x, y, z]
    for out, row in ((to_x, 64), (to_y, 128), (to_xy, 0)):
        out[0:64] = matrix[row : row + 64]
        out[64:72] = bricks


def far_columns(matrix, from_x, from_y, from_xy):
    return (matrix, 192), (from_y, 0), (from_x, 0), (from_xy, 0)


def is_even():
    return lax.rem(lax.axis_index("gz"), 2) == 0


def spread_second_kernel(matrix, from_y, from_xy, from_x, start, out):
    even = is_even()
    for q, (ref, row) in enumerate(far_columns(matrix, from_x, from_y, from_xy)):
        up, down = ref[row + 16 : row + 64], ref[row : row + 48]
        out[q * 48 : q * 48 + 48] = jnp.where(even, down, up)
    bricks = [pack_bricks(start[...])] + [ref[64:72] for ref in (from_y, from_x, from_xy)]
    for q, brick in enumerate(bricks):
        out[192 + q * 8 : 200 + q * 8] = brick


def spread_first_kernel(from_y, from_xy, from_x, out):
    even = is_even()
    for q, ref in enumerate((from_y, from_x, from_xy)):
        out[q * 48 : q * 48 + 48] = jnp.where(even, ref[16:64], ref[0:48])
        out[144 + q * 8 : 152 + q * 8] = ref[64:72]


def spread_own_kernel(matrix, start, to_first, to_second):
    even = is_even()
    for q in range(4):
        rows = 32 if q < 3 else 48
        up = matrix[q * 64 + 64 - rows : q * 64 + 64]
        down = matrix[q * 64 : q * 64 + rows]
        to_first[q * 32 : q * 32 + rows] = jnp.where(even, up, down)
        if q < 3:
            to_second[q * 32 : q * 32 + rows] = jnp.where(even, down, up)
    to_first[144:152] = pack_bricks(start[...])


def join_wide_kernel(matrix, from_y, from_xy, from_x, first, own_first, wide, places):
    even = is_even()
    for q, (ref, row) in enumerate(far_columns(matrix, from_x, from_y, from_xy)):
        other = first[q * 48 - 48 : q * 48] if q else own_first[96:144]
        wide[q * 96 : q * 96 + 48] = jnp.where(even, ref[row + 16 : row + 64], other)
        wide[q * 96 + 48 : q * 96 + 96] = jnp.where(even, other, ref[row : row + 48])
    low, _ = first_spans(even)

    def atom(index):
        x, y, z = far_atom(index)
        return x, y, z + 1 + low

    find_places(wide, range(24), atom, bricks_place, places)


def join_slim_kernel(matrix, from_y, from_xy, from_x, second, slim, places):
    even = is_even()
    for q, (ref, row) in enumerate(far_columns(matrix, from_x, from_y, from_xy)):
        other = second[q * 48 : q * 48 + 48]
        below = jnp.concatenate([other, ref[row : row + 16]], axis=0)
        above = jnp.concatenate([ref[row + 48 : row + 64], other], axis=0)
        slim[q * 64 : q * 64 + 64] = jnp.where(even, below, above)
    _, low = first_spans(even)

    def atom(index):
        return 1 + (index >> 3), 1 + ((index >> 2) & 1), (index & 3) + low

    find_places(slim, range(16), atom, bricks_place, places)


def join_near_kernel(matrix, second, own_first, near_second, head, middle, tail, places, tall):
    even = is_even()
    for q in range(4):
        if q < 3:
            one, two = (ref[q * 32 : q * 32 + 32] for ref in (own_first, near_second))
            low, high = jnp.where(even, two, one), jnp.where(even, one, two)
        else:
            low = jnp.where(even, second[16:48], own_first[112:144])
            high = jnp.where(even, own_first[96:128], second[0:32])
        tall[q * 128 : q * 128 + 32] = low
        tall[q * 128 + 32 : q * 128 + 96] = matrix[q * 64 : q * 64 + 64]
        tall[q * 128 + 96 : q * 128 + 128] = high
    find_places(tall, range(32), tall_near_atom, first_place(even), places)
    head[...], middle[...], tail[...] = thirds(tall[...])


def later_kernel(
    wide, slim, matrix, far_head, far_middle, far_tail, head, middle, tail,
    third_places, fourth_places, far,
):
    even = is_even()
    for q in range(4):
        one, two = wide[q * 96 : q * 96 + 96], slim[q * 64 : q * 64 + 64]
        below = jnp.concatenate([two[32:64], one[0:64]], axis=0)
        above = jnp.concatenate([one[32:96], two[0:32]], axis=0)
        far[q * 96 : q * 96 + 96] = jnp.where(even, below, above)
    find_places(far, range(24), far_atom, SECOND_PLACE, third_places)
    find_places(matrix, range(ATOMS), near_atom, THIRD_PLACE, fourth_places)
    far_head[...], far_middle[...], far_tail[...] = thirds(far[...])
    head[...], middle[...], tail[...] = thirds(matrix[...])


WIDE_FLOPS = 1 << 28


def first_tiles(rows, places, start, from_y, from_xy, from_x, bricks, field, gathered):
    pieces = [start[...]] + [unpack_bricks(ref[64:72]) for ref in (from_y, from_x, from_xy)]
    set_tiles(field, pieces + [unpack_bricks(brick) for brick in bricks])
    return couple(rows, rows.shape[0] // SLOT_ROWS, field, places, gathered)


def first_wide_kernel(
    wide, places, start, from_y, from_xy, from_x, first, own_first, out, field, gathered
):
    bricks = [own_first[144:152]] + [first[144 + q * 8 : 152 + q * 8] for q in range(3)]
    out[...] = first_tiles(wide, places, start, from_y, from_xy, from_x, bricks, field, gathered)


def first_slim_kernel(
    slim, places, start, from_y, from_xy, from_x, second, before, out, field, gathered
):
    bricks = [second[192 + q * 8 : 200 + q * 8] for q in range(4)]
    out[:, 0 : 3 * LANES] = before[...]
    out[:, 3 * LANES : 5 * LANES] = first_tiles(
        slim, places, start, from_y, from_xy, from_x, bricks, field, gathered
    )


def second_kernel(
    head, middle, tail, places, own, from_x, from_xy, from_y, out, field, gathered
):
    set_tiles(field, (from_xy, from_x, from_y, own))
    out[...] = couple((head, middle, tail), 32, field, places, gathered)


def third_kernel(
    head, middle, tail, places, own, from_x, from_xy, from_y, out, field, gathered
):
    set_tiles(field, (own, from_y, from_x, from_xy))
    out[...] = couple((head, middle, tail), 24, field, places, gathered)


def pick_kernel(own, from_x, from_xy, from_y, second, first_own, second_own):
    pieces = from_xy, from_x, from_y, own
    first_own[...] = jnp.where(
        is_even(), pick_own(pieces, first_place(True)), pick_own(pieces, first_place(False))
    )
    second_own[...] = pick_own((second,), SECOND_PLACE)


def last_kernel(
    head, middle, tail, places, own, from_x, from_xy, from_y, start, first, second,
    third_out, out,
    field, gathered,
):
    pieces = from_xy, from_x, from_y, own
    set_tiles(field, pieces)
    fourth = couple((head, middle, tail), ATOMS, field, places, gathered)
    third = pick_own(pieces, THIRD_PLACE)
    third_out[...] = third
    gram_kernel([start[...], first[...], second[...], third, fourth], out)


SMEM = pl.BlockSpec(memory_space=pltpu.SMEM)


def cut(atoms):
    return jax.ShapeDtypeStruct((atoms * SLOT_ROWS, WIDE), jnp.bfloat16)


def whole_numbers(rows):
    return jax.ShapeDtypeStruct((rows, LANES), jnp.int32)


def call(kernel, shapes, *operands, scratch=(), place=VMEM, flops=0):
    shapes = [
        shape if isinstance(shape, jax.ShapeDtypeStruct) else jax.ShapeDtypeStruct(shape, jnp.float32)
        for shape in shapes
    ]
    return pl.pallas_call(
        kernel,
        out_shape=shapes,
        in_specs=[
            SMEM if operand.dtype == jnp.int32 and place is VMEM else place for operand in operands
        ],
        out_specs=[VMEM] * len(shapes),
        scratch_shapes=list(scratch),
        cost_estimate=pl.CostEstimate(flops=flops, bytes_accessed=flops // 64, transcendentals=0)
        if flops
        else None,
        compiler_params=pltpu.CompilerParams(vmem_limit_bytes=24 * 1024 * 1024),
    )(*operands)


def scratch_for(tiles, groups):
    return (
        pltpu.VMEM((tiles * 8, SLOT_ROWS, LANES), jnp.float32),
        pltpu.VMEM((groups, CODE, LANES), jnp.float32),
    )


def fetch(value, first, second):
    sizes = [lax.axis_size(axis) for axis in AXES]
    pairs = []
    for a in range(sizes[0]):
        for b in range(sizes[1]):
            for c in range(sizes[2]):
                source = ((a + first) % sizes[0] * sizes[1] + (b + second) % sizes[1]) * sizes[2] + c
                pairs.append((source, (a * sizes[1] + b) * sizes[2] + c))
    return lax.ppermute(value, AXES, pairs)


def fetch_three(to_x, to_y, to_xy, sign):
    return fetch(to_x, sign, 0), fetch(to_xy, sign, sign), fetch(to_y, 0, sign)


def swap_layers(to_first, to_second):
    count = lax.axis_size("gz")
    even = [(i, i ^ 1) for i in range(count)]
    odd = [(i, (i + 1 if i % 2 else i - 1) % count) for i in range(count)]
    return lax.ppermute(to_first, "gz", even), lax.ppermute(to_second, "gz", odd)


def body(rhs, diagonal, blocks, neighbours):
    width = rhs.shape[-1]
    flat = (SLOT_ROWS, width)
    matrix, start, *out = call(
        pack_kernel,
        [(ATOMS * SLOT_ROWS, WIDE), flat] + [(72, WIDE)] * 3,
        *(pltpu.with_memory_space_constraint(x, pltpu.HBM) for x in (rhs, diagonal, blocks, neighbours)),
        scratch=[
            pltpu.VMEM(rhs.shape, rhs.dtype),
            pltpu.VMEM(diagonal.shape, diagonal.dtype),
            pltpu.VMEM(blocks.shape, blocks.dtype),
            pltpu.VMEM(neighbours.shape, neighbours.dtype),
            pltpu.SemaphoreType.DMA((4,)),
        ],
        place=pl.BlockSpec(memory_space=pltpu.HBM),
    )
    from_x, from_xy, from_y = fetch_three(*out, 1)
    sides = from_y, from_xy, from_x
    (to_second,) = call(spread_second_kernel, [(224, WIDE)], matrix, *sides, start)
    (to_first,) = call(spread_first_kernel, [(168, WIDE)], *sides)
    first_layers, second_layers = swap_layers(to_first, to_second)
    own_layers, near_layers = swap_layers(
        *call(spread_own_kernel, [(152, WIDE), (96, WIDE)], matrix, start)
    )
    wide, wide_places = call(
        join_wide_kernel, [(24 * SLOT_ROWS, WIDE), whole_numbers(24)],
        matrix, *sides, first_layers, own_layers,
    )
    (first,) = call(
        first_wide_kernel, [(SLOT_ROWS, 3 * LANES)],
        wide, wide_places, start, *sides, first_layers, own_layers,
        scratch=scratch_for(16, 3),
        flops=WIDE_FLOPS,
    )
    first, second_layers = lax.optimization_barrier((first, second_layers))
    slim, slim_places = call(
        join_slim_kernel, [(16 * SLOT_ROWS, WIDE), whole_numbers(16)], matrix, *sides, second_layers
    )
    (first,) = call(
        first_slim_kernel, [(SLOT_ROWS, 5 * LANES)],
        slim, slim_places, start, *sides, second_layers, first,
        scratch=scratch_for(16, 2),
    )
    *tall, places = call(
        join_near_kernel, [cut(32)] * 3 + [whole_numbers(32)],
        matrix, second_layers, own_layers, near_layers,
        scratch=[pltpu.VMEM((32 * SLOT_ROWS, WIDE), jnp.float32)],
    )
    pieces = fetch_three(first, first, first, -1)
    (second,) = call(
        second_kernel, [(SLOT_ROWS, 4 * LANES)], *tall, places, first, *pieces,
        scratch=scratch_for(20, 4),
    )
    first_own, second_own = call(pick_kernel, [flat] * 2, first, *pieces, second)
    *parts, third_places, fourth_places = call(
        later_kernel,
        [cut(24)] * 3 + [cut(ATOMS)] * 3 + [whole_numbers(24), whole_numbers(ATOMS)],
        wide, slim, matrix,
        scratch=[pltpu.VMEM((24 * SLOT_ROWS, WIDE), jnp.float32)],
    )
    (third,) = call(
        third_kernel, [(SLOT_ROWS, 3 * LANES)],
        *parts[:3], third_places, second, *fetch_three(second, second, second, 1),
        scratch=scratch_for(16, 3),
    )
    third_own, message = call(
        last_kernel,
        [flat, (lax.axis_size("gx") * lax.axis_size("gy"), 4, LANES)],
        *parts[3:], fourth_places, third, *fetch_three(third, third, third, -1),
        start, first_own, second_own,
        scratch=scratch_for(12, 2),
    )
    message = lax.all_to_all(message, ("gx", "gy"), 0, 0, tiled=True)
    (message,) = call(relay_kernel, [(lax.axis_size("gz"), 4, LANES)], message)
    message = lax.all_to_all(message, "gz", 0, 0, tiled=True)
    (result,) = call(finish_kernel, [rhs.shape], message, start, first_own, second_own, third_own)
    return result


def solution(mesh):
    return jax.shard_map(
        body,
        mesh=mesh,
        in_specs=(
            P("gx", "gy", "gz", None),
            P("gx", "gy", "gz", None),
            P("gx", "gy", "gz", None, None),
            P("gx", "gy", "gz", None),
        ),
        out_specs=P("gx", "gy", "gz", None),
        check_vma=False,
    )
```

```python
import jax
import jax.numpy as jnp
from jax import lax
from jax.experimental import pallas as pl
from jax.experimental.pallas import tpu as pltpu
from jax.sharding import PartitionSpec as P

ITERS = 2
DEGREE = 2 * ITERS
SHIFT = 2.0
RESOLUTION = 1e-14
LANES = 128
PAIRS = [(i, j) for i in range(DEGREE + 1) for j in range(i, DEGREE + 1)]
VMEM = pl.BlockSpec(memory_space=pltpu.VMEM)


def two_sum(a, b):
    total = a + b
    part = total - a
    return total, (a - (total - part)) + (b - part)


def quick_sum(a, b):
    total = a + b
    return total, b - (total - a)


def split(a):
    scaled = 4097.0 * a
    head = scaled - (scaled - a)
    return head, a - head


def two_prod(a, b):
    product = a * b
    a_head, a_tail = split(a)
    b_head, b_tail = split(b)
    rest = ((a_head * b_head - product) + a_head * b_tail + a_tail * b_head) + a_tail * b_tail
    return product, rest


def pair_add(a, b):
    head, tail = two_sum(a[0], b[0])
    return quick_sum(head, tail + (a[1] + b[1]))


def pair_mul(a, b):
    head, tail = two_prod(a[0], b[0])
    return quick_sum(head, tail + (a[0] * b[1] + a[1] * b[0]))


def pair_scale(a, factor):
    head, tail = two_prod(a[0], factor)
    return quick_sum(head, tail + a[1] * factor)


def roll_pair(a, amount, axis):
    return pltpu.roll(a[0], amount, axis), pltpu.roll(a[1], amount, axis)


def iota(shape, axis):
    return lax.broadcasted_iota(jnp.int32, shape, axis)


def gram_kernel(fields, out):
    columns = 16
    diagonal_mask = iota((8, LANES), 0) == iota((8, LANES), 1) // columns
    rows = []
    parts = [split(field) for field in fields]
    for i, j in PAIRS:
        product = fields[i] * fields[j]
        (a_head, a_tail), (b_head, b_tail) = parts[i], parts[j]
        rest = ((a_head * b_head - product) + a_head * b_tail + a_tail * b_head) + a_tail * b_tail
        pieces = [
            (product[s : s + 8, t : t + LANES], rest[s : s + 8, t : t + LANES])
            for s in range(0, product.shape[0], 8)
            for t in range(0, product.shape[1], LANES)
        ]
        while len(pieces) > 1:
            pieces = [pair_add(pieces[q], pieces[q + 1]) for q in range(0, len(pieces), 2)]
        total = pieces[0]
        for amount in (4, 2, 1):
            total = pair_add(total, roll_pair(total, amount, 0))
        rows.append((total[0][0:1], total[1][0:1]))
    rows += [(jnp.zeros((1, LANES), jnp.float32),) * 2] * (16 - len(rows))
    packed = [[], []]
    for start in (0, 8):
        total = tuple(
            jnp.concatenate([row[part] for row in rows[start : start + 8]], axis=0)
            for part in (0, 1)
        )
        for amount in (64, 32, 16):
            total = pair_add(total, roll_pair(total, amount, 1))
        for part in (0, 1):
            packed[part].append(
                jnp.sum(jnp.where(diagonal_mask, total[part], 0.0), axis=0, keepdims=True)
            )
    message = jnp.concatenate(packed[0] + packed[1], axis=0)
    for q in range(out.shape[0]):
        out[q] = message


def sum_messages(ref):
    terms = [(ref[q], None) for q in range(ref.shape[0])]
    while len(terms) > 1:
        merged = []
        for q in range(0, len(terms), 2):
            (a, a_rest), (b, b_rest) = terms[q], terms[q + 1]
            total, rest = two_sum(a, b)
            if a_rest is not None:
                rest = rest + (a_rest + b_rest)
            merged.append((total, rest))
        terms = merged
    total, rest = terms[0]
    return quick_sum(total[0:2], rest[0:2] + (total[2:4] + rest[2:4]))


def relay_kernel(ref, out):
    head, tail = sum_messages(ref)
    message = jnp.concatenate([head, tail], axis=0)
    for q in range(out.shape[0]):
        out[q] = message


def finish_kernel(ref, *refs):
    fields, out = refs[:-1], refs[-1]
    columns = 16
    shape = (8, LANES)
    row = iota(shape, 0)
    diagonal_mask = row == iota(shape, 1) // columns
    packed = sum_messages(ref)
    unpacked = []
    for part in (0, 1):
        halves = []
        for half in (0, 1):
            value = jnp.where(
                diagonal_mask, jnp.broadcast_to(packed[part][half : half + 1], shape), 0.0
            )
            for amount in (64, 32, 16):
                value = value + pltpu.roll(value, amount, 1)
            halves.append(value)
        unpacked.append(halves)

    def entry(part, i, j):
        place = PAIRS.index((min(i, j), max(i, j)))
        half = unpacked[part][place // 8]
        return jnp.broadcast_to(half[place % 8 : place % 8 + 1], shape)

    gram = []
    for j in range(DEGREE + 1):
        column = []
        for part in (0, 1):
            value = jnp.zeros(shape, jnp.float32)
            for i in range(DEGREE + 1):
                value = jnp.where(row == i, entry(part, i, j), value)
            column.append(value)
        gram.append(tuple(column))

    def total_rows(a):
        for amount in (4, 2, 1):
            a = pair_add(a, roll_pair(a, amount, 0))
        return a[0]

    def with_start(a):
        return total_rows(pair_mul(gram[0], a))

    def square(a, degree):
        acc = None
        for j in range(degree + 1):
            factor = tuple(jnp.broadcast_to(part[j : j + 1], shape) for part in a)
            term = pair_mul(gram[j], factor)
            acc = term if acc is None else pair_add(acc, term)
        return total_rows(pair_mul(acc, a))

    def apply(a):
        return pair_add((SHIFT * a[0], SHIFT * a[1]), roll_pair(a, 1, 0))

    def shrink(quasi_norm, ratio, step):
        damping = 1.0 / (1.0 + ratio * ratio)
        return quasi_norm * ratio * jnp.sqrt(damping), damping * step

    zero = jnp.zeros(shape, jnp.float32)
    start = (jnp.where(row == 0, 1.0, 0.0), zero)
    inner = entry(0, 0, 0)
    least = RESOLUTION * inner
    quasi_norm = jnp.sqrt(inner)
    image = apply(start)
    resid = search = start
    direction = total = (zero, zero)
    ratio = weight = zero
    for iteration in range(ITERS):
        step = inner / with_start(image)
        resid = pair_add(resid, pair_scale(image, -step))
        direction = pair_add(search, pair_scale(direction, ratio * ratio * weight / step))
        ratio = jnp.sqrt(jnp.maximum(square(resid, 2 * iteration + 1), least)) / quasi_norm
        quasi_norm, weight = shrink(quasi_norm, ratio, step)
        total = pair_add(total, pair_scale(direction, weight))
        search_odd = pair_add(search, pair_scale(image, -step))
        image_odd = apply(search_odd)
        resid = pair_add(resid, pair_scale(image_odd, -step))
        direction = pair_add(search_odd, pair_scale(direction, ratio * ratio * weight / step))
        ratio = jnp.sqrt(jnp.maximum(square(resid, 2 * iteration + 2), least)) / quasi_norm
        quasi_norm, weight = shrink(quasi_norm, ratio, step)
        total = pair_add(total, pair_scale(direction, weight))
        if iteration + 1 < ITERS:
            inner_next = with_start(resid)
            mix = inner_next / inner
            search = pair_add(resid, pair_scale(search_odd, mix))
            image = pair_add(
                apply(search), pair_scale(pair_add(image_odd, pair_scale(image, mix)), mix)
            )
            inner = inner_next
    coefficients = total[0] + total[1]
    height, width = fields[0].shape
    acc = None
    for i, field in enumerate(fields):
        factor = jnp.broadcast_to(coefficients[i : i + 1], (height, LANES))
        factor = jnp.concatenate([factor] * (width // LANES), axis=1)
        term = factor * field[...]
        acc = term if acc is None else acc + term
    from_tiles(acc, out)


SLOT_ROWS = 16
WIDE = 512
SELF = 27
CODE = 448
HIGH = lax.Precision.HIGHEST
LENGTHS = (2, 2, 4)
ATOMS = 16
AXES = ("gx", "gy", "gz")


def bricks_place(x, y, z):
    layer = ((z >> 2) != 0).astype(jnp.int32)
    brick = layer * 4 + (x >> 1) * 2 + (y >> 1)
    return (brick * 2 + (x & 1)) * 8 + (y & 1) * 4 + (z & 3)


def pieces_place(origin, run, low):
    def place(x, y, z):
        x, y = x - origin, y - origin
        piece = (x >> 1) * 2 + (y >> 1)
        return (piece * 4 + (x & 1) * 2 + (y & 1)) * run + z - low

    return place


def far_atom(index):
    column = (index * 43) >> 8
    return 1 + (column >> 1), 1 + (column & 1), index - 6 * column - 1


def tall_near_atom(index):
    return index >> 4, (index >> 3) & 1, (index & 7) - 2


def near_atom(index):
    return index >> 3, (index >> 2) & 1, index & 3


def first_spans(even):
    if isinstance(even, bool):
        return (1, -3) if even else (-3, 3)
    return jnp.where(even, 1, -3), jnp.where(even, -3, 3)


def first_place(even):
    wide_low, slim_low = first_spans(even)

    def place(x, y, z):
        x, y = x + 1, y + 1
        piece = (x >> 1) * 2 + (y >> 1)
        column = (x & 1) * 2 + (y & 1)
        layer = z - wide_low
        wide, slim = column * 6 + layer, 24 + column * 4 + z - slim_low
        if isinstance(z, int):
            return piece * 40 + (wide if 0 <= layer < 6 else slim)
        return piece * 40 + jnp.where((layer >= 0) & (layer < 6), wide, slim)

    return place


SECOND_PLACE, THIRD_PLACE = pieces_place(0, 8, -2), pieces_place(-1, 6, -1)


def find_places(matrix, rows, atom, place, out):
    rows = [row * SLOT_ROWS for row in rows]
    code = jnp.concatenate([matrix[row : row + 1, CODE - 64 : CODE + 64] for row in rows], axis=0)
    code = pltpu.roll(code, 64, 1).astype(jnp.int32)
    index = iota(code.shape, 0)
    x, y, z = atom(index)
    first = (code * 57) >> 9
    rest = code - 9 * first
    second = (rest * 11) >> 5
    where = place(x + first - 1, y + second - 1, z + rest - 3 * second - 1)
    out[...] = (where & ~7) + ((index - where) & 7)


def set_tiles(field, pieces):
    count = pieces[0].shape[1] // LANES
    for q, piece in enumerate(pieces):
        for t in range(count):
            tile = piece[:, t * LANES : (t + 1) * LANES]
            for turn in range(8):
                place = (q * count + t) * 8 + turn
                field[place] = pltpu.roll(tile, turn * SLOT_ROWS, 1) if turn else tile


def thirds(value):
    head = value.astype(jnp.bfloat16)
    rest = value - head.astype(jnp.float32)
    middle = rest.astype(jnp.bfloat16)
    return head, middle, (rest - middle.astype(jnp.float32)).astype(jnp.bfloat16)


def multiply(matrix, rows, right):
    right = right[0:CODE]
    if not isinstance(matrix, tuple):
        return jnp.dot(
            matrix[rows, 0:CODE], right, precision=HIGH, preferred_element_type=jnp.float32
        )
    head, middle, tail = (part[rows, 0:CODE] for part in matrix)
    right = jnp.concatenate(thirds(right), axis=1)
    by_head = jnp.dot(head, right, preferred_element_type=jnp.float32)
    by_middle = jnp.dot(middle, right[:, 0 : 2 * LANES], preferred_element_type=jnp.float32)
    by_tail = jnp.dot(tail, right[:, 0:LANES], preferred_element_type=jnp.float32)
    small = by_head[:, 2 * LANES : 3 * LANES] + by_middle[:, LANES : 2 * LANES] + by_tail
    return small + (by_head[:, LANES : 2 * LANES] + by_middle[:, 0:LANES]) + by_head[:, 0:LANES]


def couple(matrix, atoms, field, places, gathered):
    lane_slot = iota((SLOT_ROWS, LANES), 1) >> 4
    groups = atoms // 8

    def gather(k, carry):
        for q in range(groups):
            acc = None
            for slot in range(8):
                tile = field[places[q * 8 + slot, k]]
                acc = tile if acc is None else jnp.where(lane_slot == slot, tile, acc)
            gathered[q, pl.ds(pl.multiple_of(k * SLOT_ROWS, SLOT_ROWS), SLOT_ROWS), :] = acc
        return carry

    lax.fori_loop(0, SELF + 1, gather, 0, unroll=SELF + 1)
    tiles = []
    for q in range(groups):
        product = multiply(matrix, slice(q * LANES, (q + 1) * LANES), gathered[q])
        acc = product[0:SLOT_ROWS]
        for slot in range(1, 8):
            piece = product[slot * SLOT_ROWS : (slot + 1) * SLOT_ROWS]
            acc = jnp.where(lane_slot == slot, piece, acc)
        tiles.append(-acc)
    return jnp.concatenate(tiles, axis=1)


def pick_own(pieces, place):
    lane_slot = iota((SLOT_ROWS, LANES), 1) >> 4
    tiles = []
    for x in range(2):
        acc = None
        for slot in range(8):
            where = place(x, slot >> 2, slot & 3)
            count = pieces[0].shape[1] // LANES
            tile, turn = where >> 3, (slot - where) & 7
            lanes = pl.ds(tile % count * LANES, LANES)
            tile = pieces[tile // count][:, lanes]
            tile = pltpu.roll(tile, turn * SLOT_ROWS, 1) if turn else tile
            acc = tile if acc is None else jnp.where(lane_slot == slot, tile, acc)
        tiles.append(acc)
    return jnp.concatenate(tiles, axis=1)


def turn_blocks(value):
    row, group = iota(value.shape, 0), iota(value.shape, 1) >> 4
    for bit in (1, 2, 4):
        lanes = bit * SLOT_ROWS
        later = pltpu.roll(pltpu.roll(value, 8 - bit, 0), lanes, 1)
        earlier = pltpu.roll(pltpu.roll(value, bit, 0), LANES - lanes, 1)
        swapped = jnp.where((group & bit) != 0, later, earlier)
        value = jnp.where((row & bit) == (group & bit), value, swapped)
    return value


def to_tiles(field):
    halves = []
    for half in range(2):
        lanes = slice(half * LANES, (half + 1) * LANES)
        tiles = [
            turn_blocks(jnp.concatenate([field[x, y, :, lanes] for y in range(2)], axis=0))
            for x in range(2)
        ]
        halves.append(jnp.concatenate(tiles, axis=1))
    return jnp.concatenate(halves, axis=0)


def from_tiles(value, out):
    for half in range(2):
        for x in range(2):
            rows = turn_blocks(value[half * 8 : half * 8 + 8, x * LANES : (x + 1) * LANES])
            for y in range(2):
                out[x, y, :, half * LANES : (half + 1) * LANES] = rows[y * 4 : y * 4 + 4]


def pack_bricks(field):
    return jnp.concatenate([field[0:8], field[8:16]], axis=1)


def unpack_bricks(packed):
    return jnp.concatenate([packed[:, 0 : 2 * LANES], packed[:, 2 * LANES : 4 * LANES]], axis=0)


def pack_kernel(
    rhs_hbm, diagonal_hbm, blocks_hbm, neighbours_hbm,
    matrix, start, to_x, to_y, to_xy,
    rhs, diagonal, blocks, neighbours, sems,
):
    sources = (neighbours_hbm, diagonal_hbm, rhs_hbm, blocks_hbm)
    copies = [
        pltpu.make_async_copy(source, target, sems.at[q])
        for q, (source, target) in enumerate(zip(sources, (neighbours, diagonal, rhs, blocks)))
    ]
    for copy in copies:
        copy.start()
    matrix[:, 384:WIDE] = jnp.zeros((matrix.shape[0], WIDE - 384), jnp.float32)
    eye = iota((SLOT_ROWS, SLOT_ROWS), 0) == iota((SLOT_ROWS, SLOT_ROWS), 1)
    totals = [length * lax.axis_size(axis) for length, axis in zip(LENGTHS, AXES)]
    corner = [length * lax.axis_index(axis) for length, axis in zip(LENGTHS, AXES)]
    bits = [total.bit_length() - 1 for total in totals]
    for copy in copies[:2]:
        copy.wait()
    for x in range(2):
        for y in range(2):
            index = neighbours[x, y]
            along_x = index >> (bits[1] + bits[2])
            along_y = (index >> bits[2]) & (totals[1] - 1)
            along_z = index & (totals[2] - 1)
            z_here = corner[2] + iota(index.shape, 0)
            code = (along_x - (corner[0] + x - 1)) & (totals[0] - 1)
            code = code * 3 + ((along_y - (corner[1] + y - 1)) & (totals[1] - 1))
            code = code * 3 + ((along_z - z_here + 1) & (totals[2] - 1))
            code = code.astype(jnp.float32)
            for z in range(4):
                row = ((x * 2 + y) * 4 + z) * SLOT_ROWS
                matrix[row : row + 1, CODE : CODE + SELF] = code[z : z + 1]
                matrix[row : row + 1, CODE + SELF : CODE + SELF + 1] = jnp.full(
                    (1, 1), 13.0, jnp.float32
                )
                own = SHIFT - jnp.broadcast_to(diagonal[x, y, z : z + 1], eye.shape)
                matrix[row : row + SLOT_ROWS, 432:448] = jnp.where(eye, own, 0.0)
    copies[2].wait()
    value = to_tiles(rhs)
    start[...] = value
    bricks = pack_bricks(value)
    copies[3].wait()
    for x in range(2):
        for y in range(2):
            for z in range(4):
                row = ((x * 2 + y) * 4 + z) * SLOT_ROWS
                matrix[row : row + SLOT_ROWS, 0:432] = blocks[x, y, z]
    for out, row in ((to_x, 64), (to_y, 128), (to_xy, 0)):
        out[0:64] = matrix[row : row + 64]
        out[64:72] = bricks


def far_columns(matrix, from_x, from_y, from_xy):
    return (matrix, 192), (from_y, 0), (from_x, 0), (from_xy, 0)


def is_even():
    return lax.rem(lax.axis_index("gz"), 2) == 0


def spread_second_kernel(matrix, from_y, from_xy, from_x, start, out):
    even = is_even()
    for q, (ref, row) in enumerate(far_columns(matrix, from_x, from_y, from_xy)):
        up, down = ref[row + 16 : row + 64], ref[row : row + 48]
        out[q * 48 : q * 48 + 48] = jnp.where(even, down, up)
    bricks = [pack_bricks(start[...])] + [ref[64:72] for ref in (from_y, from_x, from_xy)]
    for q, brick in enumerate(bricks):
        out[192 + q * 8 : 200 + q * 8] = brick


def spread_first_kernel(from_y, from_xy, from_x, out):
    even = is_even()
    for q, ref in enumerate((from_y, from_x, from_xy)):
        out[q * 48 : q * 48 + 48] = jnp.where(even, ref[16:64], ref[0:48])
        out[144 + q * 8 : 152 + q * 8] = ref[64:72]


def spread_own_kernel(matrix, start, to_first, to_second):
    even = is_even()
    for q in range(4):
        rows = 32 if q < 3 else 48
        up = matrix[q * 64 + 64 - rows : q * 64 + 64]
        down = matrix[q * 64 : q * 64 + rows]
        to_first[q * 32 : q * 32 + rows] = jnp.where(even, up, down)
        if q < 3:
            to_second[q * 32 : q * 32 + rows] = jnp.where(even, down, up)
    to_first[144:152] = pack_bricks(start[...])


def join_wide_kernel(matrix, from_y, from_xy, from_x, first, own_first, wide, places):
    even = is_even()
    for q, (ref, row) in enumerate(far_columns(matrix, from_x, from_y, from_xy)):
        other = first[q * 48 - 48 : q * 48] if q else own_first[96:144]
        wide[q * 96 : q * 96 + 48] = jnp.where(even, ref[row + 16 : row + 64], other)
        wide[q * 96 + 48 : q * 96 + 96] = jnp.where(even, other, ref[row : row + 48])
    low, _ = first_spans(even)

    def atom(index):
        x, y, z = far_atom(index)
        return x, y, z + 1 + low

    find_places(wide, range(24), atom, bricks_place, places)


def join_slim_kernel(matrix, from_y, from_xy, from_x, second, slim, places):
    even = is_even()
    for q, (ref, row) in enumerate(far_columns(matrix, from_x, from_y, from_xy)):
        other = second[q * 48 : q * 48 + 48]
        below = jnp.concatenate([other, ref[row : row + 16]], axis=0)
        above = jnp.concatenate([ref[row + 48 : row + 64], other], axis=0)
        slim[q * 64 : q * 64 + 64] = jnp.where(even, below, above)
    _, low = first_spans(even)

    def atom(index):
        return 1 + (index >> 3), 1 + ((index >> 2) & 1), (index & 3) + low

    find_places(slim, range(16), atom, bricks_place, places)


def join_near_kernel(matrix, second, own_first, near_second, head, middle, tail, places, tall):
    even = is_even()
    for q in range(4):
        if q < 3:
            one, two = (ref[q * 32 : q * 32 + 32] for ref in (own_first, near_second))
            low, high = jnp.where(even, two, one), jnp.where(even, one, two)
        else:
            low = jnp.where(even, second[16:48], own_first[112:144])
            high = jnp.where(even, own_first[96:128], second[0:32])
        tall[q * 128 : q * 128 + 32] = low
        tall[q * 128 + 32 : q * 128 + 96] = matrix[q * 64 : q * 64 + 64]
        tall[q * 128 + 96 : q * 128 + 128] = high
    find_places(tall, range(32), tall_near_atom, first_place(even), places)
    head[...], middle[...], tail[...] = thirds(tall[...])


def later_kernel(
    wide, slim, matrix, far_head, far_middle, far_tail, head, middle, tail,
    third_places, fourth_places, far,
):
    even = is_even()
    for q in range(4):
        one, two = wide[q * 96 : q * 96 + 96], slim[q * 64 : q * 64 + 64]
        below = jnp.concatenate([two[32:64], one[0:64]], axis=0)
        above = jnp.concatenate([one[32:96], two[0:32]], axis=0)
        far[q * 96 : q * 96 + 96] = jnp.where(even, below, above)
    find_places(far, range(24), far_atom, SECOND_PLACE, third_places)
    find_places(matrix, range(ATOMS), near_atom, THIRD_PLACE, fourth_places)
    far_head[...], far_middle[...], far_tail[...] = thirds(far[...])
    head[...], middle[...], tail[...] = thirds(matrix[...])


WIDE_FLOPS = 1 << 28


def first_tiles(rows, places, start, from_y, from_xy, from_x, bricks, field, gathered):
    pieces = [start[...]] + [unpack_bricks(ref[64:72]) for ref in (from_y, from_x, from_xy)]
    set_tiles(field, pieces + [unpack_bricks(brick) for brick in bricks])
    return couple(rows, rows.shape[0] // SLOT_ROWS, field, places, gathered)


def first_wide_kernel(
    wide, places, start, from_y, from_xy, from_x, first, own_first, out, field, gathered
):
    bricks = [own_first[144:152]] + [first[144 + q * 8 : 152 + q * 8] for q in range(3)]
    out[...] = first_tiles(wide, places, start, from_y, from_xy, from_x, bricks, field, gathered)


def first_slim_kernel(
    slim, places, start, from_y, from_xy, from_x, second, before, out, field, gathered
):
    bricks = [second[192 + q * 8 : 200 + q * 8] for q in range(4)]
    out[:, 0 : 3 * LANES] = before[...]
    out[:, 3 * LANES : 5 * LANES] = first_tiles(
        slim, places, start, from_y, from_xy, from_x, bricks, field, gathered
    )


def second_kernel(
    head, middle, tail, places, own, from_x, from_y, from_xy, out, field, gathered
):
    set_tiles(field, (from_xy, from_x, from_y, own))
    out[...] = couple((head, middle, tail), 32, field, places, gathered)


def third_kernel(
    head, middle, tail, places, own, from_x, from_y, from_xy, out, field, gathered
):
    set_tiles(field, (own, from_y, from_x, from_xy))
    out[...] = couple((head, middle, tail), 24, field, places, gathered)


def pick_kernel(own, from_x, from_y, from_xy, second, first_own, second_own):
    pieces = from_xy, from_x, from_y, own
    first_own[...] = jnp.where(
        is_even(), pick_own(pieces, first_place(True)), pick_own(pieces, first_place(False))
    )
    second_own[...] = pick_own((second,), SECOND_PLACE)


def last_kernel(
    head, middle, tail, places, own, from_x, from_y, from_xy, start, first, second,
    third_out, out,
    field, gathered,
):
    pieces = from_xy, from_x, from_y, own
    set_tiles(field, pieces)
    fourth = couple((head, middle, tail), ATOMS, field, places, gathered)
    third = pick_own(pieces, THIRD_PLACE)
    third_out[...] = third
    gram_kernel([start[...], first[...], second[...], third, fourth], out)


SMEM = pl.BlockSpec(memory_space=pltpu.SMEM)


def cut(atoms):
    return jax.ShapeDtypeStruct((atoms * SLOT_ROWS, WIDE), jnp.bfloat16)


def whole_numbers(rows):
    return jax.ShapeDtypeStruct((rows, LANES), jnp.int32)


def call(kernel, shapes, *operands, scratch=(), place=VMEM, flops=0):
    shapes = [
        shape if isinstance(shape, jax.ShapeDtypeStruct) else jax.ShapeDtypeStruct(shape, jnp.float32)
        for shape in shapes
    ]
    return pl.pallas_call(
        kernel,
        out_shape=shapes,
        in_specs=[
            SMEM if operand.dtype == jnp.int32 and place is VMEM else place for operand in operands
        ],
        out_specs=[VMEM] * len(shapes),
        scratch_shapes=list(scratch),
        cost_estimate=pl.CostEstimate(flops=flops, bytes_accessed=flops // 64, transcendentals=0)
        if flops
        else None,
        compiler_params=pltpu.CompilerParams(vmem_limit_bytes=24 * 1024 * 1024),
    )(*operands)


def scratch_for(tiles, groups):
    return (
        pltpu.VMEM((tiles * 8, SLOT_ROWS, LANES), jnp.float32),
        pltpu.VMEM((groups, CODE, LANES), jnp.float32),
    )


def fetch(value, first, second):
    sizes = [lax.axis_size(axis) for axis in AXES]
    pairs = []
    for a in range(sizes[0]):
        for b in range(sizes[1]):
            for c in range(sizes[2]):
                source = ((a + first) % sizes[0] * sizes[1] + (b + second) % sizes[1]) * sizes[2] + c
                pairs.append((source, (a * sizes[1] + b) * sizes[2] + c))
    return lax.ppermute(value, AXES, pairs)


def fetch_three(to_x, to_y, to_xy, sign):
    return fetch(to_x, sign, 0), fetch(to_y, 0, sign), fetch(to_xy, sign, sign)


def swap_layers(to_first, to_second):
    count = lax.axis_size("gz")
    even = [(i, i ^ 1) for i in range(count)]
    odd = [(i, (i + 1 if i % 2 else i - 1) % count) for i in range(count)]
    return lax.ppermute(to_first, "gz", even), lax.ppermute(to_second, "gz", odd)


def body(rhs, diagonal, blocks, neighbours):
    width = rhs.shape[-1]
    flat = (SLOT_ROWS, width)
    matrix, start, *out = call(
        pack_kernel,
        [(ATOMS * SLOT_ROWS, WIDE), flat] + [(72, WIDE)] * 3,
        *(pltpu.with_memory_space_constraint(x, pltpu.HBM) for x in (rhs, diagonal, blocks, neighbours)),
        scratch=[
            pltpu.VMEM(rhs.shape, rhs.dtype),
            pltpu.VMEM(diagonal.shape, diagonal.dtype),
            pltpu.VMEM(blocks.shape, blocks.dtype),
            pltpu.VMEM(neighbours.shape, neighbours.dtype),
            pltpu.SemaphoreType.DMA((4,)),
        ],
        place=pl.BlockSpec(memory_space=pltpu.HBM),
    )
    from_x, from_y, from_xy = fetch_three(*out, 1)
    sides = from_y, from_xy, from_x
    (to_second,) = call(spread_second_kernel, [(224, WIDE)], matrix, *sides, start)
    (to_first,) = call(spread_first_kernel, [(168, WIDE)], *sides)
    first_layers, second_layers = swap_layers(to_first, to_second)
    own_layers, near_layers = swap_layers(
        *call(spread_own_kernel, [(152, WIDE), (96, WIDE)], matrix, start)
    )
    wide, wide_places = call(
        join_wide_kernel, [(24 * SLOT_ROWS, WIDE), whole_numbers(24)],
        matrix, *sides, first_layers, own_layers,
    )
    (first,) = call(
        first_wide_kernel, [(SLOT_ROWS, 3 * LANES)],
        wide, wide_places, start, *sides, first_layers, own_layers,
        scratch=scratch_for(16, 3),
        flops=WIDE_FLOPS,
    )
    first, second_layers = lax.optimization_barrier((first, second_layers))
    slim, slim_places = call(
        join_slim_kernel, [(16 * SLOT_ROWS, WIDE), whole_numbers(16)], matrix, *sides, second_layers
    )
    (first,) = call(
        first_slim_kernel, [(SLOT_ROWS, 5 * LANES)],
        slim, slim_places, start, *sides, second_layers, first,
        scratch=scratch_for(16, 2),
    )
    *tall, places = call(
        join_near_kernel, [cut(32)] * 3 + [whole_numbers(32)],
        matrix, second_layers, own_layers, near_layers,
        scratch=[pltpu.VMEM((32 * SLOT_ROWS, WIDE), jnp.float32)],
    )
    pieces = fetch_three(first, first, first, -1)
    (second,) = call(
        second_kernel, [(SLOT_ROWS, 4 * LANES)], *tall, places, first, *pieces,
        scratch=scratch_for(20, 4),
    )
    first_own, second_own = call(pick_kernel, [flat] * 2, first, *pieces, second)
    *parts, third_places, fourth_places = call(
        later_kernel,
        [cut(24)] * 3 + [cut(ATOMS)] * 3 + [whole_numbers(24), whole_numbers(ATOMS)],
        wide, slim, matrix,
        scratch=[pltpu.VMEM((24 * SLOT_ROWS, WIDE), jnp.float32)],
    )
    (third,) = call(
        third_kernel, [(SLOT_ROWS, 3 * LANES)],
        *parts[:3], third_places, second, *fetch_three(second, second, second, 1),
        scratch=scratch_for(16, 3),
    )
    third_own, message = call(
        last_kernel,
        [flat, (lax.axis_size("gx") * lax.axis_size("gy"), 4, LANES)],
        *parts[3:], fourth_places, third, *fetch_three(third, third, third, -1),
        start, first_own, second_own,
        scratch=scratch_for(12, 2),
    )
    message = lax.all_to_all(message, ("gy", "gx"), 0, 0, tiled=True)
    (message,) = call(relay_kernel, [(lax.axis_size("gz"), 4, LANES)], message)
    message = lax.all_to_all(message, "gz", 0, 0, tiled=True)
    (result,) = call(finish_kernel, [rhs.shape], message, start, first_own, second_own, third_own)
    return result


def solution(mesh):
    return jax.shard_map(
        body,
        mesh=mesh,
        in_specs=(
            P("gx", "gy", "gz", None),
            P("gx", "gy", "gz", None),
            P("gx", "gy", "gz", None, None),
            P("gx", "gy", "gz", None),
        ),
        out_specs=P("gx", "gy", "gz", None),
        check_vma=False,
    )
```

```python
import jax
import jax.numpy as jnp
from jax import lax
from jax.experimental import pallas as pl
from jax.experimental.pallas import tpu as pltpu
from jax.sharding import PartitionSpec as P

ITERS = 2
DEGREE = 2 * ITERS
SHIFT = 2.0
RESOLUTION = 1e-14
LANES = 128
PAIRS = [(i, j) for i in range(DEGREE + 1) for j in range(i, DEGREE + 1)]
VMEM = pl.BlockSpec(memory_space=pltpu.VMEM)


def two_sum(a, b):
    total = a + b
    part = total - a
    return total, (a - (total - part)) + (b - part)


def quick_sum(a, b):
    total = a + b
    return total, b - (total - a)


def split(a):
    scaled = 4097.0 * a
    head = scaled - (scaled - a)
    return head, a - head


def two_prod(a, b):
    product = a * b
    a_head, a_tail = split(a)
    b_head, b_tail = split(b)
    rest = ((a_head * b_head - product) + a_head * b_tail + a_tail * b_head) + a_tail * b_tail
    return product, rest


def pair_add(a, b):
    head, tail = two_sum(a[0], b[0])
    return quick_sum(head, tail + (a[1] + b[1]))


def pair_mul(a, b):
    head, tail = two_prod(a[0], b[0])
    return quick_sum(head, tail + (a[0] * b[1] + a[1] * b[0]))


def pair_scale(a, factor):
    head, tail = two_prod(a[0], factor)
    return quick_sum(head, tail + a[1] * factor)


def roll_pair(a, amount, axis):
    return pltpu.roll(a[0], amount, axis), pltpu.roll(a[1], amount, axis)


def iota(shape, axis):
    return lax.broadcasted_iota(jnp.int32, shape, axis)


EARLY = [pair for pair in PAIRS if pair[1] <= 2]


def gram_rows(fields, pairs):
    rows = {}
    parts = [split(field) for field in fields]
    for i, j in pairs:
        product = fields[i] * fields[j]
        (a_head, a_tail), (b_head, b_tail) = parts[i], parts[j]
        rest = ((a_head * b_head - product) + a_head * b_tail + a_tail * b_head) + a_tail * b_tail
        pieces = [
            (product[s : s + 8, t : t + LANES], rest[s : s + 8, t : t + LANES])
            for s in range(0, product.shape[0], 8)
            for t in range(0, product.shape[1], LANES)
        ]
        while len(pieces) > 1:
            pieces = [pair_add(pieces[q], pieces[q + 1]) for q in range(0, len(pieces), 2)]
        total = pieces[0]
        for amount in (4, 2, 1):
            total = pair_add(total, roll_pair(total, amount, 0))
        rows[i, j] = total[0][0:1], total[1][0:1]
    return rows


def gram_kernel(fields, early, out):
    columns = 16
    diagonal_mask = iota((8, LANES), 0) == iota((8, LANES), 1) // columns
    found = gram_rows(fields, [pair for pair in PAIRS if pair not in EARLY])
    for q, pair in enumerate(EARLY):
        found[pair] = early[q : q + 1], early[8 + q : 9 + q]
    rows = [found[pair] for pair in PAIRS]
    rows += [(jnp.zeros((1, LANES), jnp.float32),) * 2] * (16 - len(rows))
    packed = [[], []]
    for start in (0, 8):
        total = tuple(
            jnp.concatenate([row[part] for row in rows[start : start + 8]], axis=0)
            for part in (0, 1)
        )
        for amount in (64, 32, 16):
            total = pair_add(total, roll_pair(total, amount, 1))
        for part in (0, 1):
            packed[part].append(
                jnp.sum(jnp.where(diagonal_mask, total[part], 0.0), axis=0, keepdims=True)
            )
    message = jnp.concatenate(packed[0] + packed[1], axis=0)
    for q in range(out.shape[0]):
        out[q] = message


def sum_messages(ref):
    terms = [(ref[q], None) for q in range(ref.shape[0])]
    while len(terms) > 1:
        merged = []
        for q in range(0, len(terms), 2):
            (a, a_rest), (b, b_rest) = terms[q], terms[q + 1]
            total, rest = two_sum(a, b)
            if a_rest is not None:
                rest = rest + (a_rest + b_rest)
            merged.append((total, rest))
        terms = merged
    total, rest = terms[0]
    return quick_sum(total[0:2], rest[0:2] + (total[2:4] + rest[2:4]))


def relay_kernel(ref, out):
    head, tail = sum_messages(ref)
    message = jnp.concatenate([head, tail], axis=0)
    for q in range(out.shape[0]):
        out[q] = message


def finish_kernel(ref, *refs):
    fields, out = refs[:-1], refs[-1]
    columns = 16
    shape = (8, LANES)
    row = iota(shape, 0)
    diagonal_mask = row == iota(shape, 1) // columns
    packed = sum_messages(ref)
    unpacked = []
    for part in (0, 1):
        halves = []
        for half in (0, 1):
            value = jnp.where(
                diagonal_mask, jnp.broadcast_to(packed[part][half : half + 1], shape), 0.0
            )
            for amount in (64, 32, 16):
                value = value + pltpu.roll(value, amount, 1)
            halves.append(value)
        unpacked.append(halves)

    def entry(part, i, j):
        place = PAIRS.index((min(i, j), max(i, j)))
        half = unpacked[part][place // 8]
        return jnp.broadcast_to(half[place % 8 : place % 8 + 1], shape)

    gram = []
    for j in range(DEGREE + 1):
        column = []
        for part in (0, 1):
            value = jnp.zeros(shape, jnp.float32)
            for i in range(DEGREE + 1):
                value = jnp.where(row == i, entry(part, i, j), value)
            column.append(value)
        gram.append(tuple(column))

    def total_rows(a):
        for amount in (4, 2, 1):
            a = pair_add(a, roll_pair(a, amount, 0))
        return a[0]

    def with_start(a):
        return total_rows(pair_mul(gram[0], a))

    def square(a, degree):
        acc = None
        for j in range(degree + 1):
            factor = tuple(jnp.broadcast_to(part[j : j + 1], shape) for part in a)
            term = pair_mul(gram[j], factor)
            acc = term if acc is None else pair_add(acc, term)
        return total_rows(pair_mul(acc, a))

    def apply(a):
        return pair_add((SHIFT * a[0], SHIFT * a[1]), roll_pair(a, 1, 0))

    def shrink(quasi_norm, ratio, step):
        damping = 1.0 / (1.0 + ratio * ratio)
        return quasi_norm * ratio * jnp.sqrt(damping), damping * step

    zero = jnp.zeros(shape, jnp.float32)
    start = (jnp.where(row == 0, 1.0, 0.0), zero)
    inner = entry(0, 0, 0)
    least = RESOLUTION * inner
    quasi_norm = jnp.sqrt(inner)
    image = apply(start)
    resid = search = start
    direction = total = (zero, zero)
    ratio = weight = zero
    for iteration in range(ITERS):
        step = inner / with_start(image)
        resid = pair_add(resid, pair_scale(image, -step))
        direction = pair_add(search, pair_scale(direction, ratio * ratio * weight / step))
        ratio = jnp.sqrt(jnp.maximum(square(resid, 2 * iteration + 1), least)) / quasi_norm
        quasi_norm, weight = shrink(quasi_norm, ratio, step)
        total = pair_add(total, pair_scale(direction, weight))
        search_odd = pair_add(search, pair_scale(image, -step))
        image_odd = apply(search_odd)
        resid = pair_add(resid, pair_scale(image_odd, -step))
        direction = pair_add(search_odd, pair_scale(direction, ratio * ratio * weight / step))
        ratio = jnp.sqrt(jnp.maximum(square(resid, 2 * iteration + 2), least)) / quasi_norm
        quasi_norm, weight = shrink(quasi_norm, ratio, step)
        total = pair_add(total, pair_scale(direction, weight))
        if iteration + 1 < ITERS:
            inner_next = with_start(resid)
            mix = inner_next / inner
            search = pair_add(resid, pair_scale(search_odd, mix))
            image = pair_add(
                apply(search), pair_scale(pair_add(image_odd, pair_scale(image, mix)), mix)
            )
            inner = inner_next
    coefficients = total[0] + total[1]
    height, width = fields[0].shape
    acc = None
    for i, field in enumerate(fields):
        factor = jnp.broadcast_to(coefficients[i : i + 1], (height, LANES))
        factor = jnp.concatenate([factor] * (width // LANES), axis=1)
        term = factor * field[...]
        acc = term if acc is None else acc + term
    from_tiles(acc, out)


SLOT_ROWS = 16
WIDE = 512
SELF = 27
CODE = 448
HIGH = lax.Precision.HIGHEST
LENGTHS = (2, 2, 4)
ATOMS = 16
AXES = ("gx", "gy", "gz")


def bricks_place(x, y, z):
    layer = ((z >> 2) != 0).astype(jnp.int32)
    brick = layer * 4 + (x >> 1) * 2 + (y >> 1)
    return (brick * 2 + (x & 1)) * 8 + (y & 1) * 4 + (z & 3)


def pieces_place(origin, run, low):
    def place(x, y, z):
        x, y = x - origin, y - origin
        piece = (x >> 1) * 2 + (y >> 1)
        return (piece * 4 + (x & 1) * 2 + (y & 1)) * run + z - low

    return place


def far_atom(index):
    column = (index * 43) >> 8
    return 1 + (column >> 1), 1 + (column & 1), index - 6 * column - 1


def tall_near_atom(index):
    return index >> 4, (index >> 3) & 1, (index & 7) - 2


def near_atom(index):
    return index >> 3, (index >> 2) & 1, index & 3


def first_spans(even):
    if isinstance(even, bool):
        return (1, -3) if even else (-3, 3)
    return jnp.where(even, 1, -3), jnp.where(even, -3, 3)


def first_place(even):
    wide_low, slim_low = first_spans(even)

    def place(x, y, z):
        x, y = x + 1, y + 1
        piece = (x >> 1) * 2 + (y >> 1)
        column = (x & 1) * 2 + (y & 1)
        layer = z - wide_low
        wide, slim = column * 6 + layer, 24 + column * 4 + z - slim_low
        if isinstance(z, int):
            return piece * 40 + (wide if 0 <= layer < 6 else slim)
        return piece * 40 + jnp.where((layer >= 0) & (layer < 6), wide, slim)

    return place


SECOND_PLACE, THIRD_PLACE = pieces_place(0, 8, -2), pieces_place(-1, 6, -1)


def find_places(matrix, rows, atom, place, out):
    rows = [row * SLOT_ROWS for row in rows]
    code = jnp.concatenate([matrix[row : row + 1, CODE - 64 : CODE + 64] for row in rows], axis=0)
    code = pltpu.roll(code, 64, 1).astype(jnp.int32)
    index = iota(code.shape, 0)
    x, y, z = atom(index)
    first = (code * 57) >> 9
    rest = code - 9 * first
    second = (rest * 11) >> 5
    where = place(x + first - 1, y + second - 1, z + rest - 3 * second - 1)
    out[...] = (where & ~7) + ((index - where) & 7)


def set_tiles(field, pieces):
    count = pieces[0].shape[1] // LANES
    for q, piece in enumerate(pieces):
        for t in range(count):
            tile = piece[:, t * LANES : (t + 1) * LANES]
            for turn in range(8):
                place = (q * count + t) * 8 + turn
                field[place] = pltpu.roll(tile, turn * SLOT_ROWS, 1) if turn else tile


def thirds(value):
    head = value.astype(jnp.bfloat16)
    rest = value - head.astype(jnp.float32)
    middle = rest.astype(jnp.bfloat16)
    return head, middle, (rest - middle.astype(jnp.float32)).astype(jnp.bfloat16)


def multiply(matrix, rows, right):
    right = right[0:CODE]
    if not isinstance(matrix, tuple):
        return jnp.dot(
            matrix[rows, 0:CODE], right, precision=HIGH, preferred_element_type=jnp.float32
        )
    head, middle, tail = (part[rows, 0:CODE] for part in matrix)
    right = jnp.concatenate(thirds(right), axis=1)
    by_head = jnp.dot(head, right, preferred_element_type=jnp.float32)
    by_middle = jnp.dot(middle, right[:, 0 : 2 * LANES], preferred_element_type=jnp.float32)
    by_tail = jnp.dot(tail, right[:, 0:LANES], preferred_element_type=jnp.float32)
    small = by_head[:, 2 * LANES : 3 * LANES] + by_middle[:, LANES : 2 * LANES] + by_tail
    return small + (by_head[:, LANES : 2 * LANES] + by_middle[:, 0:LANES]) + by_head[:, 0:LANES]


def couple(matrix, atoms, field, places, gathered):
    lane_slot = iota((SLOT_ROWS, LANES), 1) >> 4
    groups = atoms // 8

    def gather(k, carry):
        for q in range(groups):
            acc = None
            for slot in range(8):
                tile = field[places[q * 8 + slot, k]]
                acc = tile if acc is None else jnp.where(lane_slot == slot, tile, acc)
            gathered[q, pl.ds(pl.multiple_of(k * SLOT_ROWS, SLOT_ROWS), SLOT_ROWS), :] = acc
        return carry

    lax.fori_loop(0, SELF + 1, gather, 0, unroll=SELF + 1)
    tiles = []
    for q in range(groups):
        product = multiply(matrix, slice(q * LANES, (q + 1) * LANES), gathered[q])
        acc = product[0:SLOT_ROWS]
        for slot in range(1, 8):
            piece = product[slot * SLOT_ROWS : (slot + 1) * SLOT_ROWS]
            acc = jnp.where(lane_slot == slot, piece, acc)
        tiles.append(-acc)
    return jnp.concatenate(tiles, axis=1)


def pick_own(pieces, place):
    lane_slot = iota((SLOT_ROWS, LANES), 1) >> 4
    tiles = []
    for x in range(2):
        acc = None
        for slot in range(8):
            where = place(x, slot >> 2, slot & 3)
            count = pieces[0].shape[1] // LANES
            tile, turn = where >> 3, (slot - where) & 7
            lanes = pl.ds(tile % count * LANES, LANES)
            tile = pieces[tile // count][:, lanes]
            tile = pltpu.roll(tile, turn * SLOT_ROWS, 1) if turn else tile
            acc = tile if acc is None else jnp.where(lane_slot == slot, tile, acc)
        tiles.append(acc)
    return jnp.concatenate(tiles, axis=1)


def turn_blocks(value):
    row, group = iota(value.shape, 0), iota(value.shape, 1) >> 4
    for bit in (1, 2, 4):
        lanes = bit * SLOT_ROWS
        later = pltpu.roll(pltpu.roll(value, 8 - bit, 0), lanes, 1)
        earlier = pltpu.roll(pltpu.roll(value, bit, 0), LANES - lanes, 1)
        swapped = jnp.where((group & bit) != 0, later, earlier)
        value = jnp.where((row & bit) == (group & bit), value, swapped)
    return value


def to_tiles(field):
    halves = []
    for half in range(2):
        lanes = slice(half * LANES, (half + 1) * LANES)
        tiles = [
            turn_blocks(jnp.concatenate([field[x, y, :, lanes] for y in range(2)], axis=0))
            for x in range(2)
        ]
        halves.append(jnp.concatenate(tiles, axis=1))
    return jnp.concatenate(halves, axis=0)


def from_tiles(value, out):
    for half in range(2):
        for x in range(2):
            rows = turn_blocks(value[half * 8 : half * 8 + 8, x * LANES : (x + 1) * LANES])
            for y in range(2):
                out[x, y, :, half * LANES : (half + 1) * LANES] = rows[y * 4 : y * 4 + 4]


def pack_bricks(field):
    return jnp.concatenate([field[0:8], field[8:16]], axis=1)


def unpack_bricks(packed):
    return jnp.concatenate([packed[:, 0 : 2 * LANES], packed[:, 2 * LANES : 4 * LANES]], axis=0)


def pack_kernel(
    rhs_hbm, diagonal_hbm, blocks_hbm, neighbours_hbm,
    matrix, start, to_x, to_y, to_xy,
    rhs, diagonal, blocks, neighbours, sems,
):
    sources = (neighbours_hbm, diagonal_hbm, rhs_hbm, blocks_hbm)
    copies = [
        pltpu.make_async_copy(source, target, sems.at[q])
        for q, (source, target) in enumerate(zip(sources, (neighbours, diagonal, rhs, blocks)))
    ]
    for copy in copies:
        copy.start()
    matrix[:, 384:WIDE] = jnp.zeros((matrix.shape[0], WIDE - 384), jnp.float32)
    eye = iota((SLOT_ROWS, SLOT_ROWS), 0) == iota((SLOT_ROWS, SLOT_ROWS), 1)
    totals = [length * lax.axis_size(axis) for length, axis in zip(LENGTHS, AXES)]
    corner = [length * lax.axis_index(axis) for length, axis in zip(LENGTHS, AXES)]
    bits = [total.bit_length() - 1 for total in totals]
    for copy in copies[:2]:
        copy.wait()
    for x in range(2):
        for y in range(2):
            index = neighbours[x, y]
            along_x = index >> (bits[1] + bits[2])
            along_y = (index >> bits[2]) & (totals[1] - 1)
            along_z = index & (totals[2] - 1)
            z_here = corner[2] + iota(index.shape, 0)
            code = (along_x - (corner[0] + x - 1)) & (totals[0] - 1)
            code = code * 3 + ((along_y - (corner[1] + y - 1)) & (totals[1] - 1))
            code = code * 3 + ((along_z - z_here + 1) & (totals[2] - 1))
            code = code.astype(jnp.float32)
            for z in range(4):
                row = ((x * 2 + y) * 4 + z) * SLOT_ROWS
                matrix[row : row + 1, CODE : CODE + SELF] = code[z : z + 1]
                matrix[row : row + 1, CODE + SELF : CODE + SELF + 1] = jnp.full(
                    (1, 1), 13.0, jnp.float32
                )
                own = SHIFT - jnp.broadcast_to(diagonal[x, y, z : z + 1], eye.shape)
                matrix[row : row + SLOT_ROWS, 432:448] = jnp.where(eye, own, 0.0)
    copies[2].wait()
    value = to_tiles(rhs)
    start[...] = value
    bricks = pack_bricks(value)
    copies[3].wait()
    for x in range(2):
        for y in range(2):
            for z in range(4):
                row = ((x * 2 + y) * 4 + z) * SLOT_ROWS
                matrix[row : row + SLOT_ROWS, 0:432] = blocks[x, y, z]
    for out, row in ((to_x, 64), (to_y, 128), (to_xy, 0)):
        out[0:64] = matrix[row : row + 64]
        out[64:72] = bricks


def far_columns(matrix, from_x, from_y, from_xy):
    return (matrix, 192), (from_y, 0), (from_x, 0), (from_xy, 0)


def is_even():
    return lax.rem(lax.axis_index("gz"), 2) == 0


def spread_second_kernel(matrix, from_y, from_xy, from_x, start, out):
    even = is_even()
    for q, (ref, row) in enumerate(far_columns(matrix, from_x, from_y, from_xy)):
        up, down = ref[row + 16 : row + 64], ref[row : row + 48]
        out[q * 48 : q * 48 + 48] = jnp.where(even, down, up)
    bricks = [pack_bricks(start[...])] + [ref[64:72] for ref in (from_y, from_x, from_xy)]
    for q, brick in enumerate(bricks):
        out[192 + q * 8 : 200 + q * 8] = brick


def spread_first_kernel(from_y, from_xy, from_x, out):
    even = is_even()
    for q, ref in enumerate((from_y, from_x, from_xy)):
        out[q * 48 : q * 48 + 48] = jnp.where(even, ref[16:64], ref[0:48])
        out[144 + q * 8 : 152 + q * 8] = ref[64:72]


def spread_own_kernel(matrix, start, to_first, to_second):
    even = is_even()
    for q in range(4):
        rows = 32 if q < 3 else 48
        up = matrix[q * 64 + 64 - rows : q * 64 + 64]
        down = matrix[q * 64 : q * 64 + rows]
        to_first[q * 32 : q * 32 + rows] = jnp.where(even, up, down)
        if q < 3:
            to_second[q * 32 : q * 32 + rows] = jnp.where(even, down, up)
    to_first[144:152] = pack_bricks(start[...])


def join_wide_kernel(matrix, from_y, from_xy, from_x, first, own_first, wide, places):
    even = is_even()
    for q, (ref, row) in enumerate(far_columns(matrix, from_x, from_y, from_xy)):
        other = first[q * 48 - 48 : q * 48] if q else own_first[96:144]
        wide[q * 96 : q * 96 + 48] = jnp.where(even, ref[row + 16 : row + 64], other)
        wide[q * 96 + 48 : q * 96 + 96] = jnp.where(even, other, ref[row : row + 48])
    low, _ = first_spans(even)

    def atom(index):
        x, y, z = far_atom(index)
        return x, y, z + 1 + low

    find_places(wide, range(24), atom, bricks_place, places)


def join_slim_kernel(matrix, from_y, from_xy, from_x, second, slim, places):
    even = is_even()
    for q, (ref, row) in enumerate(far_columns(matrix, from_x, from_y, from_xy)):
        other = second[q * 48 : q * 48 + 48]
        below = jnp.concatenate([other, ref[row : row + 16]], axis=0)
        above = jnp.concatenate([ref[row + 48 : row + 64], other], axis=0)
        slim[q * 64 : q * 64 + 64] = jnp.where(even, below, above)
    _, low = first_spans(even)

    def atom(index):
        return 1 + (index >> 3), 1 + ((index >> 2) & 1), (index & 3) + low

    find_places(slim, range(16), atom, bricks_place, places)


def join_near_kernel(matrix, second, own_first, near_second, head, middle, tail, places, tall):
    even = is_even()
    for q in range(4):
        if q < 3:
            one, two = (ref[q * 32 : q * 32 + 32] for ref in (own_first, near_second))
            low, high = jnp.where(even, two, one), jnp.where(even, one, two)
        else:
            low = jnp.where(even, second[16:48], own_first[112:144])
            high = jnp.where(even, own_first[96:128], second[0:32])
        tall[q * 128 : q * 128 + 32] = low
        tall[q * 128 + 32 : q * 128 + 96] = matrix[q * 64 : q * 64 + 64]
        tall[q * 128 + 96 : q * 128 + 128] = high
    find_places(tall, range(32), tall_near_atom, first_place(even), places)
    head[...], middle[...], tail[...] = thirds(tall[...])


def later_kernel(
    wide, slim, matrix, far_head, far_middle, far_tail, head, middle, tail,
    third_places, fourth_places, far,
):
    even = is_even()
    for q in range(4):
        one, two = wide[q * 96 : q * 96 + 96], slim[q * 64 : q * 64 + 64]
        below = jnp.concatenate([two[32:64], one[0:64]], axis=0)
        above = jnp.concatenate([one[32:96], two[0:32]], axis=0)
        far[q * 96 : q * 96 + 96] = jnp.where(even, below, above)
    find_places(far, range(24), far_atom, SECOND_PLACE, third_places)
    find_places(matrix, range(ATOMS), near_atom, THIRD_PLACE, fourth_places)
    far_head[...], far_middle[...], far_tail[...] = thirds(far[...])
    head[...], middle[...], tail[...] = thirds(matrix[...])


WIDE_FLOPS = 1 << 28


def first_tiles(rows, places, start, from_y, from_xy, from_x, bricks, field, gathered):
    pieces = [start[...]] + [unpack_bricks(ref[64:72]) for ref in (from_y, from_x, from_xy)]
    set_tiles(field, pieces + [unpack_bricks(brick) for brick in bricks])
    return couple(rows, rows.shape[0] // SLOT_ROWS, field, places, gathered)


def first_wide_kernel(
    wide, places, start, from_y, from_xy, from_x, first, own_first, out, field, gathered
):
    bricks = [own_first[144:152]] + [first[144 + q * 8 : 152 + q * 8] for q in range(3)]
    out[...] = first_tiles(wide, places, start, from_y, from_xy, from_x, bricks, field, gathered)


def first_slim_kernel(
    slim, places, start, from_y, from_xy, from_x, second, before, out, field, gathered
):
    bricks = [second[192 + q * 8 : 200 + q * 8] for q in range(4)]
    out[:, 0 : 3 * LANES] = before[...]
    out[:, 3 * LANES : 5 * LANES] = first_tiles(
        slim, places, start, from_y, from_xy, from_x, bricks, field, gathered
    )


def second_kernel(
    head, middle, tail, places, own, from_x, from_y, from_xy, out, field, gathered
):
    set_tiles(field, (from_xy, from_x, from_y, own))
    out[...] = couple((head, middle, tail), 32, field, places, gathered)


def third_kernel(
    head, middle, tail, places, own, from_x, from_y, from_xy, out, field, gathered
):
    set_tiles(field, (own, from_y, from_x, from_xy))
    out[...] = couple((head, middle, tail), 24, field, places, gathered)


def pick_kernel(own, from_x, from_y, from_xy, second, start, first_own, second_own, early):
    pieces = from_xy, from_x, from_y, own
    first_own[...] = jnp.where(
        is_even(), pick_own(pieces, first_place(True)), pick_own(pieces, first_place(False))
    )
    second_own[...] = pick_own((second,), SECOND_PLACE)
    early[...] = jnp.zeros_like(early)
    rows = gram_rows([start[...], first_own[...], second_own[...]], EARLY)
    for q, pair in enumerate(EARLY):
        early[q : q + 1], early[8 + q : 9 + q] = rows[pair]


def last_kernel(
    head, middle, tail, places, own, from_x, from_y, from_xy, start, first, second, early,
    third_out, out,
    field, gathered,
):
    pieces = from_xy, from_x, from_y, own
    set_tiles(field, pieces)
    fourth = couple((head, middle, tail), ATOMS, field, places, gathered)
    third = pick_own(pieces, THIRD_PLACE)
    third_out[...] = third
    gram_kernel([start[...], first[...], second[...], third, fourth], early, out)


SMEM = pl.BlockSpec(memory_space=pltpu.SMEM)


def cut(atoms):
    return jax.ShapeDtypeStruct((atoms * SLOT_ROWS, WIDE), jnp.bfloat16)


def whole_numbers(rows):
    return jax.ShapeDtypeStruct((rows, LANES), jnp.int32)


def call(kernel, shapes, *operands, scratch=(), place=VMEM, flops=0):
    shapes = [
        shape if isinstance(shape, jax.ShapeDtypeStruct) else jax.ShapeDtypeStruct(shape, jnp.float32)
        for shape in shapes
    ]
    return pl.pallas_call(
        kernel,
        out_shape=shapes,
        in_specs=[
            SMEM if operand.dtype == jnp.int32 and place is VMEM else place for operand in operands
        ],
        out_specs=[VMEM] * len(shapes),
        scratch_shapes=list(scratch),
        cost_estimate=pl.CostEstimate(flops=flops, bytes_accessed=flops // 64, transcendentals=0)
        if flops
        else None,
        compiler_params=pltpu.CompilerParams(vmem_limit_bytes=24 * 1024 * 1024),
    )(*operands)


def scratch_for(tiles, groups):
    return (
        pltpu.VMEM((tiles * 8, SLOT_ROWS, LANES), jnp.float32),
        pltpu.VMEM((groups, CODE, LANES), jnp.float32),
    )


def fetch(value, first, second):
    sizes = [lax.axis_size(axis) for axis in AXES]
    pairs = []
    for a in range(sizes[0]):
        for b in range(sizes[1]):
            for c in range(sizes[2]):
                source = ((a + first) % sizes[0] * sizes[1] + (b + second) % sizes[1]) * sizes[2] + c
                pairs.append((source, (a * sizes[1] + b) * sizes[2] + c))
    return lax.ppermute(value, AXES, pairs)


def fetch_three(to_x, to_y, to_xy, sign):
    return fetch(to_x, sign, 0), fetch(to_y, 0, sign), fetch(to_xy, sign, sign)


def swap_layers(to_first, to_second):
    count = lax.axis_size("gz")
    even = [(i, i ^ 1) for i in range(count)]
    odd = [(i, (i + 1 if i % 2 else i - 1) % count) for i in range(count)]
    return lax.ppermute(to_first, "gz", even), lax.ppermute(to_second, "gz", odd)


def body(rhs, diagonal, blocks, neighbours):
    width = rhs.shape[-1]
    flat = (SLOT_ROWS, width)
    matrix, start, *out = call(
        pack_kernel,
        [(ATOMS * SLOT_ROWS, WIDE), flat] + [(72, WIDE)] * 3,
        *(pltpu.with_memory_space_constraint(x, pltpu.HBM) for x in (rhs, diagonal, blocks, neighbours)),
        scratch=[
            pltpu.VMEM(rhs.shape, rhs.dtype),
            pltpu.VMEM(diagonal.shape, diagonal.dtype),
            pltpu.VMEM(blocks.shape, blocks.dtype),
            pltpu.VMEM(neighbours.shape, neighbours.dtype),
            pltpu.SemaphoreType.DMA((4,)),
        ],
        place=pl.BlockSpec(memory_space=pltpu.HBM),
    )
    from_x, from_y, from_xy = fetch_three(*out, 1)
    sides = from_y, from_xy, from_x
    (to_second,) = call(spread_second_kernel, [(224, WIDE)], matrix, *sides, start)
    (to_first,) = call(spread_first_kernel, [(168, WIDE)], *sides)
    first_layers, second_layers = swap_layers(to_first, to_second)
    own_layers, near_layers = swap_layers(
        *call(spread_own_kernel, [(152, WIDE), (96, WIDE)], matrix, start)
    )
    wide, wide_places = call(
        join_wide_kernel, [(24 * SLOT_ROWS, WIDE), whole_numbers(24)],
        matrix, *sides, first_layers, own_layers,
    )
    (first,) = call(
        first_wide_kernel, [(SLOT_ROWS, 3 * LANES)],
        wide, wide_places, start, *sides, first_layers, own_layers,
        scratch=scratch_for(16, 3),
        flops=WIDE_FLOPS,
    )
    first, second_layers = lax.optimization_barrier((first, second_layers))
    slim, slim_places = call(
        join_slim_kernel, [(16 * SLOT_ROWS, WIDE), whole_numbers(16)], matrix, *sides, second_layers
    )
    (first,) = call(
        first_slim_kernel, [(SLOT_ROWS, 5 * LANES)],
        slim, slim_places, start, *sides, second_layers, first,
        scratch=scratch_for(16, 2),
    )
    *tall, places = call(
        join_near_kernel, [cut(32)] * 3 + [whole_numbers(32)],
        matrix, second_layers, own_layers, near_layers,
        scratch=[pltpu.VMEM((32 * SLOT_ROWS, WIDE), jnp.float32)],
    )
    pieces = fetch_three(first, first, first, -1)
    (second,) = call(
        second_kernel, [(SLOT_ROWS, 4 * LANES)], *tall, places, first, *pieces,
        scratch=scratch_for(20, 4),
    )
    first_own, second_own, early = call(
        pick_kernel, [flat] * 2 + [(16, LANES)], first, *pieces, second, start
    )
    *parts, third_places, fourth_places = call(
        later_kernel,
        [cut(24)] * 3 + [cut(ATOMS)] * 3 + [whole_numbers(24), whole_numbers(ATOMS)],
        wide, slim, matrix,
        scratch=[pltpu.VMEM((24 * SLOT_ROWS, WIDE), jnp.float32)],
    )
    (third,) = call(
        third_kernel, [(SLOT_ROWS, 3 * LANES)],
        *parts[:3], third_places, second, *fetch_three(second, second, second, 1),
        scratch=scratch_for(16, 3),
    )
    third_own, message = call(
        last_kernel,
        [flat, (lax.axis_size("gx") * lax.axis_size("gy"), 4, LANES)],
        *parts[3:], fourth_places, third, *fetch_three(third, third, third, -1),
        start, first_own, second_own, early,
        scratch=scratch_for(12, 2),
    )
    message = lax.all_to_all(message, ("gx", "gy"), 0, 0, tiled=True)
    (message,) = call(relay_kernel, [(lax.axis_size("gz"), 4, LANES)], message)
    message = lax.all_to_all(message, "gz", 0, 0, tiled=True)
    (result,) = call(finish_kernel, [rhs.shape], message, start, first_own, second_own, third_own)
    return result


def solution(mesh):
    return jax.shard_map(
        body,
        mesh=mesh,
        in_specs=(
            P("gx", "gy", "gz", None),
            P("gx", "gy", "gz", None),
            P("gx", "gy", "gz", None, None),
            P("gx", "gy", "gz", None),
        ),
        out_specs=P("gx", "gy", "gz", None),
        check_vma=False,
    )
```

```python
import jax
import jax.numpy as jnp
from jax import lax
from jax.experimental import pallas as pl
from jax.experimental.pallas import tpu as pltpu
from jax.sharding import PartitionSpec as P

ITERS = 2
DEGREE = 2 * ITERS
SHIFT = 2.0
RESOLUTION = 1e-14
LANES = 128
PAIRS = [(i, j) for i in range(DEGREE + 1) for j in range(i, DEGREE + 1)]
VMEM = pl.BlockSpec(memory_space=pltpu.VMEM)


def two_sum(a, b):
    total = a + b
    part = total - a
    return total, (a - (total - part)) + (b - part)


def quick_sum(a, b):
    total = a + b
    return total, b - (total - a)


def split(a):
    scaled = 4097.0 * a
    head = scaled - (scaled - a)
    return head, a - head


def two_prod(a, b):
    product = a * b
    a_head, a_tail = split(a)
    b_head, b_tail = split(b)
    rest = ((a_head * b_head - product) + a_head * b_tail + a_tail * b_head) + a_tail * b_tail
    return product, rest


def pair_add(a, b):
    head, tail = two_sum(a[0], b[0])
    return quick_sum(head, tail + (a[1] + b[1]))


def pair_mul(a, b):
    head, tail = two_prod(a[0], b[0])
    return quick_sum(head, tail + (a[0] * b[1] + a[1] * b[0]))


def pair_scale(a, factor):
    head, tail = two_prod(a[0], factor)
    return quick_sum(head, tail + a[1] * factor)


def roll_pair(a, amount, axis):
    return pltpu.roll(a[0], amount, axis), pltpu.roll(a[1], amount, axis)


def iota(shape, axis):
    return lax.broadcasted_iota(jnp.int32, shape, axis)


EARLY = [pair for pair in PAIRS if pair[1] <= 2]


def gram_rows(fields, pairs):
    rows = {}
    parts = [split(field) for field in fields]
    for i, j in pairs:
        product = fields[i] * fields[j]
        (a_head, a_tail), (b_head, b_tail) = parts[i], parts[j]
        rest = ((a_head * b_head - product) + a_head * b_tail + a_tail * b_head) + a_tail * b_tail
        pieces = [
            (product[s : s + 8, t : t + LANES], rest[s : s + 8, t : t + LANES])
            for s in range(0, product.shape[0], 8)
            for t in range(0, product.shape[1], LANES)
        ]
        while len(pieces) > 1:
            pieces = [pair_add(pieces[q], pieces[q + 1]) for q in range(0, len(pieces), 2)]
        total = pieces[0]
        for amount in (4, 2, 1):
            total = pair_add(total, roll_pair(total, amount, 0))
        rows[i, j] = total[0][0:1], total[1][0:1]
    return rows


def gram_kernel(fields, early, out):
    columns = 16
    diagonal_mask = iota((8, LANES), 0) == iota((8, LANES), 1) // columns
    found = gram_rows(fields, [pair for pair in PAIRS if pair not in EARLY])
    for q, pair in enumerate(EARLY):
        found[pair] = early[q : q + 1], early[8 + q : 9 + q]
    rows = [found[pair] for pair in PAIRS]
    rows += [(jnp.zeros((1, LANES), jnp.float32),) * 2] * (16 - len(rows))
    packed = [[], []]
    for start in (0, 8):
        total = tuple(
            jnp.concatenate([row[part] for row in rows[start : start + 8]], axis=0)
            for part in (0, 1)
        )
        for amount in (64, 32, 16):
            total = pair_add(total, roll_pair(total, amount, 1))
        for part in (0, 1):
            packed[part].append(
                jnp.sum(jnp.where(diagonal_mask, total[part], 0.0), axis=0, keepdims=True)
            )
    message = jnp.concatenate(packed[0] + packed[1], axis=0)
    for q in range(out.shape[0]):
        out[q] = message


def sum_messages(ref):
    terms = [(ref[q], None) for q in range(ref.shape[0])]
    while len(terms) > 1:
        merged = []
        for q in range(0, len(terms), 2):
            (a, a_rest), (b, b_rest) = terms[q], terms[q + 1]
            total, rest = two_sum(a, b)
            if a_rest is not None:
                rest = rest + (a_rest + b_rest)
            merged.append((total, rest))
        terms = merged
    total, rest = terms[0]
    return quick_sum(total[0:2], rest[0:2] + (total[2:4] + rest[2:4]))


def relay_kernel(ref, out):
    head, tail = sum_messages(ref)
    message = jnp.concatenate([head, tail], axis=0)
    for q in range(out.shape[0]):
        out[q] = message


def finish_kernel(ref, *refs):
    fields, out = refs[:-1], refs[-1]
    columns = 16
    shape = (8, LANES)
    row = iota(shape, 0)
    diagonal_mask = row == iota(shape, 1) // columns
    packed = sum_messages(ref)
    unpacked = []
    for part in (0, 1):
        halves = []
        for half in (0, 1):
            value = jnp.where(
                diagonal_mask, jnp.broadcast_to(packed[part][half : half + 1], shape), 0.0
            )
            for amount in (64, 32, 16):
                value = value + pltpu.roll(value, amount, 1)
            halves.append(value)
        unpacked.append(halves)

    def entry(part, i, j):
        place = PAIRS.index((min(i, j), max(i, j)))
        half = unpacked[part][place // 8]
        return jnp.broadcast_to(half[place % 8 : place % 8 + 1], shape)

    gram = []
    for j in range(DEGREE + 1):
        column = []
        for part in (0, 1):
            value = jnp.zeros(shape, jnp.float32)
            for i in range(DEGREE + 1):
                value = jnp.where(row == i, entry(part, i, j), value)
            column.append(value)
        gram.append(tuple(column))

    def total_rows(a):
        for amount in (4, 2, 1):
            a = pair_add(a, roll_pair(a, amount, 0))
        return a[0]

    def with_start(a):
        return total_rows(pair_mul(gram[0], a))

    def square(a, degree):
        acc = None
        for j in range(degree + 1):
            factor = tuple(jnp.broadcast_to(part[j : j + 1], shape) for part in a)
            term = pair_mul(gram[j], factor)
            acc = term if acc is None else pair_add(acc, term)
        return total_rows(pair_mul(acc, a))

    def apply(a):
        return pair_add((SHIFT * a[0], SHIFT * a[1]), roll_pair(a, 1, 0))

    def shrink(quasi_norm, ratio, step):
        damping = 1.0 / (1.0 + ratio * ratio)
        return quasi_norm * ratio * jnp.sqrt(damping), damping * step

    zero = jnp.zeros(shape, jnp.float32)
    start = (jnp.where(row == 0, 1.0, 0.0), zero)
    inner = entry(0, 0, 0)
    least = RESOLUTION * inner
    quasi_norm = jnp.sqrt(inner)
    image = apply(start)
    resid = search = start
    direction = total = (zero, zero)
    ratio = weight = zero
    for iteration in range(ITERS):
        step = inner / with_start(image)
        resid = pair_add(resid, pair_scale(image, -step))
        direction = pair_add(search, pair_scale(direction, ratio * ratio * weight / step))
        ratio = jnp.sqrt(jnp.maximum(square(resid, 2 * iteration + 1), least)) / quasi_norm
        quasi_norm, weight = shrink(quasi_norm, ratio, step)
        total = pair_add(total, pair_scale(direction, weight))
        search_odd = pair_add(search, pair_scale(image, -step))
        image_odd = apply(search_odd)
        resid = pair_add(resid, pair_scale(image_odd, -step))
        direction = pair_add(search_odd, pair_scale(direction, ratio * ratio * weight / step))
        ratio = jnp.sqrt(jnp.maximum(square(resid, 2 * iteration + 2), least)) / quasi_norm
        quasi_norm, weight = shrink(quasi_norm, ratio, step)
        total = pair_add(total, pair_scale(direction, weight))
        if iteration + 1 < ITERS:
            inner_next = with_start(resid)
            mix = inner_next / inner
            search = pair_add(resid, pair_scale(search_odd, mix))
            image = pair_add(
                apply(search), pair_scale(pair_add(image_odd, pair_scale(image, mix)), mix)
            )
            inner = inner_next
    coefficients = total[0] + total[1]
    height, width = fields[0].shape
    acc = None
    for i, field in enumerate(fields):
        factor = jnp.broadcast_to(coefficients[i : i + 1], (height, LANES))
        factor = jnp.concatenate([factor] * (width // LANES), axis=1)
        term = factor * field[...]
        acc = term if acc is None else acc + term
    from_tiles(acc, out)


SLOT_ROWS = 16
WIDE = 512
SELF = 27
CODE = 448
HIGH = lax.Precision.HIGHEST
LENGTHS = (2, 2, 4)
ATOMS = 16
AXES = ("gx", "gy", "gz")


def bricks_place(x, y, z):
    layer = ((z >> 2) != 0).astype(jnp.int32)
    brick = layer * 4 + (x >> 1) * 2 + (y >> 1)
    return (brick * 2 + (x & 1)) * 8 + (y & 1) * 4 + (z & 3)


def pieces_place(origin, run, low):
    def place(x, y, z):
        x, y = x - origin, y - origin
        piece = (x >> 1) * 2 + (y >> 1)
        return (piece * 4 + (x & 1) * 2 + (y & 1)) * run + z - low

    return place


def far_atom(index):
    column = (index * 43) >> 8
    return 1 + (column >> 1), 1 + (column & 1), index - 6 * column - 1


def tall_near_atom(index):
    return index >> 4, (index >> 3) & 1, (index & 7) - 2


def near_atom(index):
    return index >> 3, (index >> 2) & 1, index & 3


def first_spans(even):
    if isinstance(even, bool):
        return (1, -3) if even else (-3, 3)
    return jnp.where(even, 1, -3), jnp.where(even, -3, 3)


def first_place(even):
    wide_low, slim_low = first_spans(even)

    def place(x, y, z):
        x, y = x + 1, y + 1
        piece = (x >> 1) * 2 + (y >> 1)
        column = (x & 1) * 2 + (y & 1)
        layer = z - wide_low
        wide, slim = column * 6 + layer, 24 + column * 4 + z - slim_low
        if isinstance(z, int):
            return piece * 40 + (wide if 0 <= layer < 6 else slim)
        return piece * 40 + jnp.where((layer >= 0) & (layer < 6), wide, slim)

    return place


SECOND_PLACE, THIRD_PLACE = pieces_place(0, 8, -2), pieces_place(-1, 6, -1)


def find_places(matrix, rows, atom, place, out):
    rows = [row * SLOT_ROWS for row in rows]
    code = jnp.concatenate([matrix[row : row + 1, CODE - 64 : CODE + 64] for row in rows], axis=0)
    code = pltpu.roll(code, 64, 1).astype(jnp.int32)
    index = iota(code.shape, 0)
    x, y, z = atom(index)
    first = (code * 57) >> 9
    rest = code - 9 * first
    second = (rest * 11) >> 5
    where = place(x + first - 1, y + second - 1, z + rest - 3 * second - 1)
    out[...] = (where & ~7) + ((index - where) & 7)


def set_tiles(field, pieces):
    count = pieces[0].shape[1] // LANES
    for q, piece in enumerate(pieces):
        for t in range(count):
            tile = piece[:, t * LANES : (t + 1) * LANES]
            for turn in range(8):
                place = (q * count + t) * 8 + turn
                field[place] = pltpu.roll(tile, turn * SLOT_ROWS, 1) if turn else tile


def thirds(value):
    head = value.astype(jnp.bfloat16)
    rest = value - head.astype(jnp.float32)
    middle = rest.astype(jnp.bfloat16)
    return head, middle, (rest - middle.astype(jnp.float32)).astype(jnp.bfloat16)


def multiply(matrix, rows, right):
    right = right[0:CODE]
    if not isinstance(matrix, tuple):
        return jnp.dot(
            matrix[rows, 0:CODE], right, precision=HIGH, preferred_element_type=jnp.float32
        )
    head, middle, tail = (part[rows, 0:CODE] for part in matrix)
    right = jnp.concatenate(thirds(right), axis=1)
    by_head = jnp.dot(head, right, preferred_element_type=jnp.float32)
    by_middle = jnp.dot(middle, right[:, 0 : 2 * LANES], preferred_element_type=jnp.float32)
    by_tail = jnp.dot(tail, right[:, 0:LANES], preferred_element_type=jnp.float32)
    small = by_head[:, 2 * LANES : 3 * LANES] + by_middle[:, LANES : 2 * LANES] + by_tail
    return small + (by_head[:, LANES : 2 * LANES] + by_middle[:, 0:LANES]) + by_head[:, 0:LANES]


def couple(matrix, atoms, field, places, gathered):
    lane_slot = iota((SLOT_ROWS, LANES), 1) >> 4
    groups = atoms // 8

    def gather(k, carry):
        for q in range(groups):
            acc = None
            for slot in range(8):
                tile = field[places[q * 8 + slot, k]]
                acc = tile if acc is None else jnp.where(lane_slot == slot, tile, acc)
            gathered[q, pl.ds(pl.multiple_of(k * SLOT_ROWS, SLOT_ROWS), SLOT_ROWS), :] = acc
        return carry

    lax.fori_loop(0, SELF + 1, gather, 0, unroll=SELF + 1)
    tiles = []
    for q in range(groups):
        product = multiply(matrix, slice(q * LANES, (q + 1) * LANES), gathered[q])
        acc = product[0:SLOT_ROWS]
        for slot in range(1, 8):
            piece = product[slot * SLOT_ROWS : (slot + 1) * SLOT_ROWS]
            acc = jnp.where(lane_slot == slot, piece, acc)
        tiles.append(-acc)
    return jnp.concatenate(tiles, axis=1)


def pick_own(pieces, place):
    lane_slot = iota((SLOT_ROWS, LANES), 1) >> 4
    tiles = []
    for x in range(2):
        acc = None
        for slot in range(8):
            where = place(x, slot >> 2, slot & 3)
            count = pieces[0].shape[1] // LANES
            tile, turn = where >> 3, (slot - where) & 7
            lanes = pl.ds(tile % count * LANES, LANES)
            tile = pieces[tile // count][:, lanes]
            tile = pltpu.roll(tile, turn * SLOT_ROWS, 1) if turn else tile
            acc = tile if acc is None else jnp.where(lane_slot == slot, tile, acc)
        tiles.append(acc)
    return jnp.concatenate(tiles, axis=1)


def turn_blocks(value):
    row, group = iota(value.shape, 0), iota(value.shape, 1) >> 4
    for bit in (1, 2, 4):
        lanes = bit * SLOT_ROWS
        later = pltpu.roll(pltpu.roll(value, 8 - bit, 0), lanes, 1)
        earlier = pltpu.roll(pltpu.roll(value, bit, 0), LANES - lanes, 1)
        swapped = jnp.where((group & bit) != 0, later, earlier)
        value = jnp.where((row & bit) == (group & bit), value, swapped)
    return value


def to_tiles(field):
    halves = []
    for half in range(2):
        lanes = slice(half * LANES, (half + 1) * LANES)
        tiles = [
            turn_blocks(jnp.concatenate([field[x, y, :, lanes] for y in range(2)], axis=0))
            for x in range(2)
        ]
        halves.append(jnp.concatenate(tiles, axis=1))
    return jnp.concatenate(halves, axis=0)


def from_tiles(value, out):
    for half in range(2):
        for x in range(2):
            rows = turn_blocks(value[half * 8 : half * 8 + 8, x * LANES : (x + 1) * LANES])
            for y in range(2):
                out[x, y, :, half * LANES : (half + 1) * LANES] = rows[y * 4 : y * 4 + 4]


def pack_bricks(field):
    return jnp.concatenate([field[0:8], field[8:16]], axis=1)


def unpack_bricks(packed):
    return jnp.concatenate([packed[:, 0 : 2 * LANES], packed[:, 2 * LANES : 4 * LANES]], axis=0)


def pack_kernel(
    rhs_hbm, diagonal_hbm, blocks_hbm, neighbours_hbm,
    matrix, start, to_x, to_y, to_xy,
    rhs, diagonal, blocks, neighbours, sems,
):
    sources = (neighbours_hbm, diagonal_hbm, rhs_hbm, blocks_hbm)
    copies = [
        pltpu.make_async_copy(source, target, sems.at[q])
        for q, (source, target) in enumerate(zip(sources, (neighbours, diagonal, rhs, blocks)))
    ]
    for copy in copies:
        copy.start()
    matrix[:, 384:WIDE] = jnp.zeros((matrix.shape[0], WIDE - 384), jnp.float32)
    eye = iota((SLOT_ROWS, SLOT_ROWS), 0) == iota((SLOT_ROWS, SLOT_ROWS), 1)
    totals = [length * lax.axis_size(axis) for length, axis in zip(LENGTHS, AXES)]
    corner = [length * lax.axis_index(axis) for length, axis in zip(LENGTHS, AXES)]
    bits = [total.bit_length() - 1 for total in totals]
    for copy in copies[:2]:
        copy.wait()
    for x in range(2):
        for y in range(2):
            index = neighbours[x, y]
            along_x = index >> (bits[1] + bits[2])
            along_y = (index >> bits[2]) & (totals[1] - 1)
            along_z = index & (totals[2] - 1)
            z_here = corner[2] + iota(index.shape, 0)
            code = (along_x - (corner[0] + x - 1)) & (totals[0] - 1)
            code = code * 3 + ((along_y - (corner[1] + y - 1)) & (totals[1] - 1))
            code = code * 3 + ((along_z - z_here + 1) & (totals[2] - 1))
            code = code.astype(jnp.float32)
            for z in range(4):
                row = ((x * 2 + y) * 4 + z) * SLOT_ROWS
                matrix[row : row + 1, CODE : CODE + SELF] = code[z : z + 1]
                matrix[row : row + 1, CODE + SELF : CODE + SELF + 1] = jnp.full(
                    (1, 1), 13.0, jnp.float32
                )
                own = SHIFT - jnp.broadcast_to(diagonal[x, y, z : z + 1], eye.shape)
                matrix[row : row + SLOT_ROWS, 432:448] = jnp.where(eye, own, 0.0)
    copies[2].wait()
    value = to_tiles(rhs)
    start[...] = value
    bricks = pack_bricks(value)
    copies[3].wait()
    for x in range(2):
        for y in range(2):
            for z in range(4):
                row = ((x * 2 + y) * 4 + z) * SLOT_ROWS
                matrix[row : row + SLOT_ROWS, 0:432] = blocks[x, y, z]
    for out, row in ((to_x, 64), (to_y, 128), (to_xy, 0)):
        out[0:64] = matrix[row : row + 64]
        out[64:72] = bricks


def far_columns(matrix, from_x, from_y, from_xy):
    return (matrix, 192), (from_y, 0), (from_x, 0), (from_xy, 0)


def is_even():
    return lax.rem(lax.axis_index("gz"), 2) == 0


def spread_second_kernel(matrix, from_y, from_xy, from_x, start, out):
    even = is_even()
    for q, (ref, row) in enumerate(far_columns(matrix, from_x, from_y, from_xy)):
        up, down = ref[row + 16 : row + 64], ref[row : row + 48]
        out[q * 48 : q * 48 + 48] = jnp.where(even, down, up)
    bricks = [pack_bricks(start[...])] + [ref[64:72] for ref in (from_y, from_x, from_xy)]
    for q, brick in enumerate(bricks):
        out[192 + q * 8 : 200 + q * 8] = brick


def spread_first_kernel(from_y, from_xy, from_x, out):
    even = is_even()
    for q, ref in enumerate((from_y, from_x, from_xy)):
        out[q * 48 : q * 48 + 48] = jnp.where(even, ref[16:64], ref[0:48])
        out[144 + q * 8 : 152 + q * 8] = ref[64:72]


def spread_own_kernel(matrix, start, to_first, to_second):
    even = is_even()
    for q in range(4):
        rows = 32 if q < 3 else 48
        up = matrix[q * 64 + 64 - rows : q * 64 + 64]
        down = matrix[q * 64 : q * 64 + rows]
        to_first[q * 32 : q * 32 + rows] = jnp.where(even, up, down)
        if q < 3:
            to_second[q * 32 : q * 32 + rows] = jnp.where(even, down, up)
    to_first[144:152] = pack_bricks(start[...])


def join_wide_kernel(matrix, from_y, from_xy, from_x, first, own_first, wide, places):
    even = is_even()
    for q, (ref, row) in enumerate(far_columns(matrix, from_x, from_y, from_xy)):
        other = first[q * 48 - 48 : q * 48] if q else own_first[96:144]
        wide[q * 96 : q * 96 + 48] = jnp.where(even, ref[row + 16 : row + 64], other)
        wide[q * 96 + 48 : q * 96 + 96] = jnp.where(even, other, ref[row : row + 48])
    low, _ = first_spans(even)

    def atom(index):
        x, y, z = far_atom(index)
        return x, y, z + 1 + low

    find_places(wide, range(24), atom, bricks_place, places)


def join_slim_kernel(matrix, from_y, from_xy, from_x, second, slim, places):
    even = is_even()
    for q, (ref, row) in enumerate(far_columns(matrix, from_x, from_y, from_xy)):
        other = second[q * 48 : q * 48 + 48]
        below = jnp.concatenate([other, ref[row : row + 16]], axis=0)
        above = jnp.concatenate([ref[row + 48 : row + 64], other], axis=0)
        slim[q * 64 : q * 64 + 64] = jnp.where(even, below, above)
    _, low = first_spans(even)

    def atom(index):
        return 1 + (index >> 3), 1 + ((index >> 2) & 1), (index & 3) + low

    find_places(slim, range(16), atom, bricks_place, places)


def join_near_kernel(matrix, second, own_first, near_second, head, middle, tail, places, tall):
    even = is_even()
    for q in range(4):
        if q < 3:
            one, two = (ref[q * 32 : q * 32 + 32] for ref in (own_first, near_second))
            low, high = jnp.where(even, two, one), jnp.where(even, one, two)
        else:
            low = jnp.where(even, second[16:48], own_first[112:144])
            high = jnp.where(even, own_first[96:128], second[0:32])
        tall[q * 128 : q * 128 + 32] = low
        tall[q * 128 + 32 : q * 128 + 96] = matrix[q * 64 : q * 64 + 64]
        tall[q * 128 + 96 : q * 128 + 128] = high
    find_places(tall, range(32), tall_near_atom, first_place(even), places)
    head[...], middle[...], tail[...] = thirds(tall[...])


def later_kernel(
    wide, slim, matrix, far_head, far_middle, far_tail, head, middle, tail,
    third_places, fourth_places, far,
):
    even = is_even()
    for q in range(4):
        one, two = wide[q * 96 : q * 96 + 96], slim[q * 64 : q * 64 + 64]
        below = jnp.concatenate([two[32:64], one[0:64]], axis=0)
        above = jnp.concatenate([one[32:96], two[0:32]], axis=0)
        far[q * 96 : q * 96 + 96] = jnp.where(even, below, above)
    find_places(far, range(24), far_atom, SECOND_PLACE, third_places)
    find_places(matrix, range(ATOMS), near_atom, THIRD_PLACE, fourth_places)
    far_head[...], far_middle[...], far_tail[...] = thirds(far[...])
    head[...], middle[...], tail[...] = thirds(matrix[...])


WIDE_FLOPS = 1 << 28


def first_tiles(rows, places, start, from_y, from_xy, from_x, bricks, field, gathered, listed, sem):
    pieces = [start[...]] + [unpack_bricks(ref[64:72]) for ref in (from_y, from_x, from_xy)]
    copy = pltpu.make_async_copy(places, listed, sem)
    copy.start()
    set_tiles(field, pieces + [unpack_bricks(brick) for brick in bricks])
    copy.wait()
    return couple(rows, rows.shape[0] // SLOT_ROWS, field, listed, gathered)


def first_wide_kernel(
    wide, places, start, from_y, from_xy, from_x, first, own_first, out, field, gathered, listed, sem
):
    bricks = [own_first[144:152]] + [first[144 + q * 8 : 152 + q * 8] for q in range(3)]
    out[...] = first_tiles(wide, places, start, from_y, from_xy, from_x, bricks, field, gathered, listed, sem)


def first_slim_kernel(
    slim, places, start, from_y, from_xy, from_x, second, before, out, field, gathered, listed, sem
):
    bricks = [second[192 + q * 8 : 200 + q * 8] for q in range(4)]
    out[:, 0 : 3 * LANES] = before[...]
    out[:, 3 * LANES : 5 * LANES] = first_tiles(
        slim, places, start, from_y, from_xy, from_x, bricks, field, gathered, listed, sem
    )


def second_kernel(
    head, middle, tail, places, own, from_x, from_y, from_xy, out, field, gathered, listed, sem
):
    copy = pltpu.make_async_copy(places, listed, sem)
    copy.start()
    set_tiles(field, (from_xy, from_x, from_y, own))
    copy.wait()
    out[...] = couple((head, middle, tail), 32, field, listed, gathered)


def third_kernel(
    head, middle, tail, places, own, from_x, from_y, from_xy, out, field, gathered, listed, sem
):
    copy = pltpu.make_async_copy(places, listed, sem)
    copy.start()
    set_tiles(field, (own, from_y, from_x, from_xy))
    copy.wait()
    out[...] = couple((head, middle, tail), 24, field, listed, gathered)


def pick_kernel(own, from_x, from_y, from_xy, second, start, first_own, second_own, early):
    pieces = from_xy, from_x, from_y, own
    first_own[...] = jnp.where(
        is_even(), pick_own(pieces, first_place(True)), pick_own(pieces, first_place(False))
    )
    second_own[...] = pick_own((second,), SECOND_PLACE)
    early[...] = jnp.zeros_like(early)
    rows = gram_rows([start[...], first_own[...], second_own[...]], EARLY)
    for q, pair in enumerate(EARLY):
        early[q : q + 1], early[8 + q : 9 + q] = rows[pair]


def last_kernel(
    head, middle, tail, places, own, from_x, from_y, from_xy, start, first, second, early,
    third_out, out,
    field, gathered, listed, sem,
):
    pieces = from_xy, from_x, from_y, own
    copy = pltpu.make_async_copy(places, listed, sem)
    copy.start()
    set_tiles(field, pieces)
    copy.wait()
    fourth = couple((head, middle, tail), ATOMS, field, listed, gathered)
    third = pick_own(pieces, THIRD_PLACE)
    third_out[...] = third
    gram_kernel([start[...], first[...], second[...], third, fourth], early, out)


def cut(atoms):
    return jax.ShapeDtypeStruct((atoms * SLOT_ROWS, WIDE), jnp.bfloat16)


def whole_numbers(rows):
    return jax.ShapeDtypeStruct((rows, LANES), jnp.int32)


def call(kernel, shapes, *operands, scratch=(), place=VMEM, flops=0):
    shapes = [
        shape if isinstance(shape, jax.ShapeDtypeStruct) else jax.ShapeDtypeStruct(shape, jnp.float32)
        for shape in shapes
    ]
    return pl.pallas_call(
        kernel,
        out_shape=shapes,
        in_specs=[place] * len(operands),
        out_specs=[VMEM] * len(shapes),
        scratch_shapes=list(scratch),
        cost_estimate=pl.CostEstimate(flops=flops, bytes_accessed=flops // 64, transcendentals=0)
        if flops
        else None,
        compiler_params=pltpu.CompilerParams(vmem_limit_bytes=24 * 1024 * 1024),
    )(*operands)


def scratch_for(tiles, groups):
    return (
        pltpu.VMEM((tiles * 8, SLOT_ROWS, LANES), jnp.float32),
        pltpu.VMEM((groups, CODE, LANES), jnp.float32),
        pltpu.SMEM((groups * 8, LANES), jnp.int32),
        pltpu.SemaphoreType.DMA,
    )


def fetch(value, first, second):
    sizes = [lax.axis_size(axis) for axis in AXES]
    pairs = []
    for a in range(sizes[0]):
        for b in range(sizes[1]):
            for c in range(sizes[2]):
                source = ((a + first) % sizes[0] * sizes[1] + (b + second) % sizes[1]) * sizes[2] + c
                pairs.append((source, (a * sizes[1] + b) * sizes[2] + c))
    return lax.ppermute(value, AXES, pairs)


def fetch_three(to_x, to_y, to_xy, sign):
    return fetch(to_x, sign, 0), fetch(to_y, 0, sign), fetch(to_xy, sign, sign)


def swap_layers(to_first, to_second):
    count = lax.axis_size("gz")
    even = [(i, i ^ 1) for i in range(count)]
    odd = [(i, (i + 1 if i % 2 else i - 1) % count) for i in range(count)]
    return lax.ppermute(to_first, "gz", even), lax.ppermute(to_second, "gz", odd)


def body(rhs, diagonal, blocks, neighbours):
    width = rhs.shape[-1]
    flat = (SLOT_ROWS, width)
    matrix, start, *out = call(
        pack_kernel,
        [(ATOMS * SLOT_ROWS, WIDE), flat] + [(72, WIDE)] * 3,
        *(pltpu.with_memory_space_constraint(x, pltpu.HBM) for x in (rhs, diagonal, blocks, neighbours)),
        scratch=[
            pltpu.VMEM(rhs.shape, rhs.dtype),
            pltpu.VMEM(diagonal.shape, diagonal.dtype),
            pltpu.VMEM(blocks.shape, blocks.dtype),
            pltpu.VMEM(neighbours.shape, neighbours.dtype),
            pltpu.SemaphoreType.DMA((4,)),
        ],
        place=pl.BlockSpec(memory_space=pltpu.HBM),
    )
    from_x, from_y, from_xy = fetch_three(*out, 1)
    sides = from_y, from_xy, from_x
    (to_second,) = call(spread_second_kernel, [(224, WIDE)], matrix, *sides, start)
    (to_first,) = call(spread_first_kernel, [(168, WIDE)], *sides)
    first_layers, second_layers = swap_layers(to_first, to_second)
    own_layers, near_layers = swap_layers(
        *call(spread_own_kernel, [(152, WIDE), (96, WIDE)], matrix, start)
    )
    wide, wide_places = call(
        join_wide_kernel, [(24 * SLOT_ROWS, WIDE), whole_numbers(24)],
        matrix, *sides, first_layers, own_layers,
    )
    (first,) = call(
        first_wide_kernel, [(SLOT_ROWS, 3 * LANES)],
        wide, wide_places, start, *sides, first_layers, own_layers,
        scratch=scratch_for(16, 3),
        flops=WIDE_FLOPS,
    )
    first, second_layers = lax.optimization_barrier((first, second_layers))
    slim, slim_places = call(
        join_slim_kernel, [(16 * SLOT_ROWS, WIDE), whole_numbers(16)], matrix, *sides, second_layers
    )
    (first,) = call(
        first_slim_kernel, [(SLOT_ROWS, 5 * LANES)],
        slim, slim_places, start, *sides, second_layers, first,
        scratch=scratch_for(16, 2),
    )
    *tall, places = call(
        join_near_kernel, [cut(32)] * 3 + [whole_numbers(32)],
        matrix, second_layers, own_layers, near_layers,
        scratch=[pltpu.VMEM((32 * SLOT_ROWS, WIDE), jnp.float32)],
    )
    pieces = fetch_three(first, first, first, -1)
    (second,) = call(
        second_kernel, [(SLOT_ROWS, 4 * LANES)], *tall, places, first, *pieces,
        scratch=scratch_for(20, 4),
    )
    first_own, second_own, early = call(
        pick_kernel, [flat] * 2 + [(16, LANES)], first, *pieces, second, start
    )
    *parts, third_places, fourth_places = call(
        later_kernel,
        [cut(24)] * 3 + [cut(ATOMS)] * 3 + [whole_numbers(24), whole_numbers(ATOMS)],
        wide, slim, matrix,
        scratch=[pltpu.VMEM((24 * SLOT_ROWS, WIDE), jnp.float32)],
    )
    (third,) = call(
        third_kernel, [(SLOT_ROWS, 3 * LANES)],
        *parts[:3], third_places, second, *fetch_three(second, second, second, 1),
        scratch=scratch_for(16, 3),
    )
    third_own, message = call(
        last_kernel,
        [flat, (lax.axis_size("gx") * lax.axis_size("gy"), 4, LANES)],
        *parts[3:], fourth_places, third, *fetch_three(third, third, third, -1),
        start, first_own, second_own, early,
        scratch=scratch_for(12, 2),
    )
    message = lax.all_to_all(message, ("gx", "gy"), 0, 0, tiled=True)
    (message,) = call(relay_kernel, [(lax.axis_size("gz"), 4, LANES)], message)
    message = lax.all_to_all(message, "gz", 0, 0, tiled=True)
    (result,) = call(finish_kernel, [rhs.shape], message, start, first_own, second_own, third_own)
    return result


def solution(mesh):
    return jax.shard_map(
        body,
        mesh=mesh,
        in_specs=(
            P("gx", "gy", "gz", None),
            P("gx", "gy", "gz", None),
            P("gx", "gy", "gz", None, None),
            P("gx", "gy", "gz", None),
        ),
        out_specs=P("gx", "gy", "gz", None),
        check_vma=False,
    )
```
